32 devices in a mesh: dp: 16 (over z, y, x), tensor: 2 (over core).
Axes of the slice: x: 2, y: 2, z: 4, core: 2. Of those that a mesh axis runs over, the one named last changes fastest.
Arguments:
- images: bfloat16 [16, 16, 16, 1024], P('dp'), may hold values from -4 to 4
- t_index: int32 [16], P('dp'), may hold values from 0 to 999
- cotangent: bfloat16 [16, 64, 2048], P('dp'), may hold values from -4 to 4
- norm_params: float32 [2, 1024], P(None, 'dp'), may hold values from -1 to 1.6
- norm_params_avg: float32 [2, 1024], P(None, 'dp'), may hold values from -0.0004272461 to 0.0004272461
- norm_params_sq: float32 [2, 1024], P(None, 'dp'), may hold values from 5.615713e-09 to 2.2462851e-08
- first_conv: float32 [3, 3, 1024, 1024], P(None, None, 'dp', 'tensor'), may hold values from -0.0625 to 0.0625
- first_conv_avg: float32 [3, 3, 1024, 1024], P(None, None, 'dp', 'tensor'), may hold values from -0.00061035156 to 0.00061035156
- first_conv_sq: float32 [3, 3, 1024, 1024], P(None, None, 'dp', 'tensor'), may hold values from 1.0766219e-08 to 4.3064876e-08
- resnet_mod: float32 [256, 2, 1024], P('dp', None, 'tensor'), may hold values from -0.1875 to 0.1875
- resnet_mod_avg: float32 [256, 2, 1024], P('dp', None, 'tensor'), may hold values from -0.0004272461 to 0.0004272461
- resnet_mod_sq: float32 [256, 2, 1024], P('dp', None, 'tensor'), may hold values from 5.615713e-09 to 2.2462851e-08
- second_conv: float32 [3, 3, 1024, 1024], P(None, None, 'tensor', 'dp'), may hold values from -0.0625 to 0.0625
- second_kernel_first_moment: float32 [3, 3, 1024, 1024], P(None, None, 'tensor', 'dp'), may hold values from -0.0008544922 to 0.0008544922
- second_conv_sq: float32 [3, 3, 1024, 1024], P(None, None, 'tensor', 'dp'), may hold values from 1.7578179e-08 to 7.0312716e-08
- down_conv: float32 [3, 3, 1024, 2048], P(None, None, 'dp', 'tensor'), may hold values from -0.0625 to 0.0625
- down_conv_avg: float32 [3, 3, 1024, 2048], P(None, None, 'dp', 'tensor'), may hold values from -0.0009765625 to 0.0009765625
- down_conv_sq: float32 [3, 3, 1024, 2048], P(None, None, 'dp', 'tensor'), may hold values from 2.9906165e-08 to 1.1962466e-07
- ada_proj: float32 [256, 6, 2048], P('dp'), may hold values from -0.1875 to 0.1875
- ada_proj_avg: float32 [256, 6, 2048], P('dp'), may hold values from -0.0004272461 to 0.0004272461
- ada_proj_sq: float32 [256, 6, 2048], P('dp'), may hold values from 4.784986e-09 to 1.9139945e-08
- qkv_proj: float32 [2048, 3, 16, 128], P('dp', None, 'tensor'), may hold values from -0.125 to 0.125
- qkv_proj_avg: float32 [2048, 3, 16, 128], P('dp', None, 'tensor'), may hold values from -0.00048828125 to 0.00048828125
- qkv_proj_sq: float32 [2048, 3, 16, 128], P('dp', None, 'tensor'), may hold values from 7.476541e-09 to 2.9906165e-08
- out_proj: float32 [16, 128, 2048], P('tensor', None, 'dp'), may hold values from -0.75 to 0.75
- out_proj_avg: float32 [16, 128, 2048], P('tensor', None, 'dp'), may hold values from -7.6293945e-05 to 7.6293945e-05
- out_proj_sq: float32 [16, 128, 2048], P('tensor', None, 'dp'), may hold values from 1.9139944e-10 to 7.6559775e-10
- hidden_in: float32 [2048, 8192], P('dp', 'tensor'), may hold values from -0.125 to 0.125
- hidden_in_avg: float32 [2048, 8192], P('dp', 'tensor'), may hold values from -0.00018310547 to 0.00018310547
- hidden_in_sq: float32 [2048, 8192], P('dp', 'tensor'), may hold values from 8.3072677e-10 to 3.322907e-09
- hidden_out: float32 [8192, 2048], P('tensor', 'dp'), may hold values from -0.0625 to 0.0625
- hidden_out_avg: float32 [8192, 2048], P('tensor', 'dp'), may hold values from -0.00024414062 to 0.00024414062
- hidden_out_sq: float32 [8192, 2048], P('tensor', 'dp'), may hold values from 1.9701516e-09 to 7.880606e-09
Outputs:
- block_out: bfloat16 [16, 64, 2048], P('dp')
- images_grad: float32 [16, 16, 16, 1024], P('dp')
- grad_norm: float32 [1], replicated
- new_norm_params: float32 [2, 1024], P(None, 'dp')
- new_norm_params_avg: float32 [2, 1024], P(None, 'dp')
- new_norm_params_sq: float32 [2, 1024], P(None, 'dp')
- new_first_conv: float32 [3, 3, 1024, 1024], P(None, None, 'dp', 'tensor')
- new_first_conv_avg: float32 [3, 3, 1024, 1024], P(None, None, 'dp', 'tensor')
- new_first_conv_sq: float32 [3, 3, 1024, 1024], P(None, None, 'dp', 'tensor')
- new_resnet_mod: float32 [256, 2, 1024], P('dp', None, 'tensor')
- new_resnet_mod_avg: float32 [256, 2, 1024], P('dp', None, 'tensor')
- new_resnet_mod_sq: float32 [256, 2, 1024], P('dp', None, 'tensor')
- new_second_conv: float32 [3, 3, 1024, 1024], P(None, None, 'tensor', 'dp')
- new_second_conv_avg: float32 [3, 3, 1024, 1024], P(None, None, 'tensor', 'dp')
- new_second_conv_sq: float32 [3, 3, 1024, 1024], P(None, None, 'tensor', 'dp')
- new_down_conv: float32 [3, 3, 1024, 2048], P(None, None, 'dp', 'tensor')
- new_down_conv_avg: float32 [3, 3, 1024, 2048], P(None, None, 'dp', 'tensor')
- new_down_conv_sq: float32 [3, 3, 1024, 2048], P(None, None, 'dp', 'tensor')
- new_ada_proj: float32 [256, 6, 2048], P('dp')
- new_ada_proj_avg: float32 [256, 6, 2048], P('dp')
- new_ada_proj_sq: float32 [256, 6, 2048], P('dp')
- new_qkv_proj: float32 [2048, 3, 16, 128], P('dp', None, 'tensor')
- new_qkv_proj_avg: float32 [2048, 3, 16, 128], P('dp', None, 'tensor')
- new_qkv_proj_sq: float32 [2048, 3, 16, 128], P('dp', None, 'tensor')
- new_out_proj: float32 [16, 128, 2048], P('tensor', None, 'dp')
- new_out_proj_avg: float32 [16, 128, 2048], P('tensor', None, 'dp')
- new_out_proj_sq: float32 [16, 128, 2048], P('tensor', None, 'dp')
- new_hidden_in: float32 [2048, 8192], P('dp', 'tensor')
- new_hidden_in_avg: float32 [2048, 8192], P('dp', 'tensor')
- new_hidden_in_sq: float32 [2048, 8192], P('dp', 'tensor')
- new_hidden_out: float32 [8192, 2048], P('tensor', 'dp')
- new_hidden_out_avg: float32 [8192, 2048], P('tensor', 'dp')
- new_hidden_out_sq: float32 [8192, 2048], P('tensor', 'dp')
The draws below stay inside these ranges and needn't reach their ends.
All inputs are finite; a program needn't handle non-finite values.
Results may differ from the reference program's by a relative error of at most 0.035.
Values may be sent and summed in bfloat16 or wider, within the bound.
A program may use at most 448 MiB of HBM per device.

```python
import math
import jax
import jax.numpy as jnp
from jax import lax

C = 1024
D = 2048
HEADS = 16
HDIM = 128
FF = 8192
GROUPS = 32
FREQ = 256
HGT = 16
WID = 16
STEP = 5
SEQ = 64
IMAGES = 16


def rising_scale(entries, highest):
    return 1.0 + (highest - 1.0) * jnp.arange(entries, dtype=jnp.float32) / (entries - 1)


def draw_images(key, part):
    key = jax.random.fold_in(key, 3)
    sample = jax.random.normal(key, (IMAGES, HGT, WID, C), jnp.float32)
    channel_scale = 0.5 * rising_scale(C, 3.0)
    return jnp.clip(sample * channel_scale, -4.0, 4.0).astype(jnp.bfloat16)


def draw_cotangent(key, part):
    key = jax.random.fold_in(key, 5)
    sample = jax.random.normal(key, (IMAGES, SEQ, D), jnp.float32)
    feature_scale = 0.5 * rising_scale(D, 3.0)
    return jnp.clip(sample * feature_scale, -4.0, 4.0).astype(jnp.bfloat16)


def draw_norm_params(key, part):
    gain_key = jax.random.fold_in(key, 11)
    bias_key = jax.random.fold_in(key, 23)
    ramp = jnp.arange(C, dtype=jnp.float32) / (C - 1)
    jitter = jax.random.uniform(gain_key, (C,), jnp.float32, 0.8, 1.25)
    gain = jnp.minimum((0.5 + ramp) * jitter, 1.6)
    bias = jnp.clip(0.5 * jax.random.normal(bias_key, (C,), jnp.float32), -1.0, 1.0)
    return jnp.stack([gain, bias])


def with_ends(values, key, low, largest):
    spot = [jax.random.randint(jax.random.fold_in(key, axis), (), 0, length) for axis, length in enumerate(values.shape)]
    longest = values.shape.index(max(values.shape))
    neighbour = spot[:longest] + [(spot[longest] + 1) % values.shape[longest]] + spot[longest + 1:]
    return values.at[tuple(spot)].set(low).at[tuple(neighbour)].set(largest)


def steps_of(stream_key, dims, pieces, smallest, largest):
    level, own = 1.0, jax.random.fold_in(stream_key, 6)
    for axis_at, parts in pieces:
        heights = jnp.exp(jax.random.uniform(jax.random.fold_in(own, axis_at), (parts,), jnp.float32, smallest / len(pieces), largest / len(pieces)))
        level = level * jnp.repeat(heights, dims[axis_at] // parts).reshape([-1 if axis == axis_at else 1 for axis in range(len(dims))])
    return level


def scatter_about(rng, dims, deviation, limit, cuts=(), kind=jnp.bfloat16):
    level = steps_of(rng, dims, cuts, -0.22, 0.18) if cuts else 1.0
    drawn = jax.random.normal(rng, dims, jnp.float32) * deviation * level
    return jnp.minimum(jnp.maximum(drawn, -limit), limit).astype(kind)


def setup_inputs(seed: int = 0) -> dict:
    seeds = jax.random.split(jax.random.key(seed), 34)
    images = draw_images(jax.random.fold_in(seeds[33], 71), 0)
    t_index = with_ends(jax.random.randint(seeds[1], (IMAGES,), 0, 1000), jax.random.fold_in(seeds[1], 1), 0, 999).astype(jnp.int32)
    cotangent = draw_cotangent(jax.random.fold_in(seeds[33], 71), 0)
    norm_params = draw_norm_params(jax.random.fold_in(seeds[33], 71), 0)
    norm_params_avg = scatter_about(seeds[4], (2, C), (1.3 / (76 * C * C + 81 * C * D + 7 * D * HEADS * HDIM + D * FF + 8 * FREQ * D + 4 * FREQ * C) ** 0.5), 0.0004272461, ((1, 16),), jnp.float32)
    norm_params_sq = jnp.clip(jnp.exp(math.log(2.246285113471913e-08) - 1.3862944 * jax.random.uniform(seeds[5], (2, C), jnp.float32) ** steps_of(seeds[5], (2, C), ((1, 16),), -0.2, 0.2)), 5.615712783679783e-09, 2.246285113471913e-08)
    first_conv = scatter_about(seeds[6], (3, 3, C, C), (9 * C) ** -0.5, 0.0625, ((2, 16), (3, 2)), jnp.float32)
    first_conv_avg = scatter_about(seeds[7], (3, 3, C, C), (1.8 / (76 * C * C + 81 * C * D + 7 * D * HEADS * HDIM + D * FF + 8 * FREQ * D + 4 * FREQ * C) ** 0.5), 0.00061035156, ((2, 16), (3, 2)), jnp.float32)
    first_conv_sq = jnp.clip(jnp.exp(math.log(4.306487610961085e-08) - 1.3862944 * jax.random.uniform(seeds[8], (3, 3, C, C), jnp.float32) ** steps_of(seeds[8], (3, 3, C, C), ((2, 16), (3, 2)), -0.2, 0.2)), 1.0766219027402713e-08, 4.306487610961085e-08)
    resnet_mod = scatter_about(seeds[9], (FREQ, 2, C), (4 * FREQ) ** -0.5, 0.1875, ((0, 16), (2, 2)), jnp.float32)
    resnet_mod_avg = scatter_about(seeds[10], (FREQ, 2, C), (1.3 / (76 * C * C + 81 * C * D + 7 * D * HEADS * HDIM + D * FF + 8 * FREQ * D + 4 * FREQ * C) ** 0.5), 0.0004272461, ((0, 16), (2, 2)), jnp.float32)
    resnet_mod_sq = jnp.clip(jnp.exp(math.log(2.246285113471913e-08) - 1.3862944 * jax.random.uniform(seeds[11], (FREQ, 2, C), jnp.float32) ** steps_of(seeds[11], (FREQ, 2, C), ((0, 16), (2, 2)), -0.2, 0.2)), 5.615712783679783e-09, 2.246285113471913e-08)
    second_conv = scatter_about(seeds[12], (3, 3, C, C), (9 * C) ** -0.5, 0.0625, ((2, 2), (3, 16)), jnp.float32)
    second_kernel_first_moment = scatter_about(seeds[13], (3, 3, C, C), (2.3 / (76 * C * C + 81 * C * D + 7 * D * HEADS * HDIM + D * FF + 8 * FREQ * D + 4 * FREQ * C) ** 0.5), 0.0008544922, ((2, 2), (3, 16)), jnp.float32)
    second_conv_sq = jnp.clip(jnp.exp(math.log(7.031271564983399e-08) - 1.3862944 * jax.random.uniform(seeds[14], (3, 3, C, C), jnp.float32) ** steps_of(seeds[14], (3, 3, C, C), ((2, 2), (3, 16)), -0.2, 0.2)), 1.7578178912458498e-08, 7.031271564983399e-08)
    down_conv = scatter_about(seeds[15], (3, 3, C, D), (9 * C) ** -0.5, 0.0625, ((2, 16), (3, 2)), jnp.float32)
    down_conv_avg = scatter_about(seeds[16], (3, 3, C, D), (3.0 / (76 * C * C + 81 * C * D + 7 * D * HEADS * HDIM + D * FF + 8 * FREQ * D + 4 * FREQ * C) ** 0.5), 0.0009765625, ((2, 16), (3, 2)), jnp.float32)
    down_conv_sq = jnp.clip(jnp.exp(math.log(1.196246586232519e-07) - 1.3862944 * jax.random.uniform(seeds[17], (3, 3, C, D), jnp.float32) ** steps_of(seeds[17], (3, 3, C, D), ((2, 16), (3, 2)), -0.2, 0.2)), 2.990616465581297e-08, 1.196246586232519e-07)
    ada_proj = scatter_about(seeds[18], (FREQ, 6, D), (4 * FREQ) ** -0.5, 0.1875, ((0, 16),), jnp.float32)
    ada_proj_avg = scatter_about(seeds[19], (FREQ, 6, D), (1.2 / (76 * C * C + 81 * C * D + 7 * D * HEADS * HDIM + D * FF + 8 * FREQ * D + 4 * FREQ * C) ** 0.5), 0.0004272461, ((0, 16),), jnp.float32)
    ada_proj_sq = jnp.clip(jnp.exp(math.log(1.913994474023184e-08) - 1.3862944 * jax.random.uniform(seeds[20], (FREQ, 6, D), jnp.float32) ** steps_of(seeds[20], (FREQ, 6, D), ((0, 16),), -0.2, 0.2)), 4.78498618505796e-09, 1.913994474023184e-08)
    qkv_proj = scatter_about(seeds[21], (D, 3, HEADS, HDIM), D ** -0.5, 0.125, ((0, 16), (2, 2)), jnp.float32)
    qkv_proj_avg = scatter_about(seeds[22], (D, 3, HEADS, HDIM), (1.5 / (76 * C * C + 81 * C * D + 7 * D * HEADS * HDIM + D * FF + 8 * FREQ * D + 4 * FREQ * C) ** 0.5), 0.00048828125, ((0, 16), (2, 2)), jnp.float32)
    qkv_proj_sq = jnp.clip(jnp.exp(math.log(2.990616465581297e-08) - 1.3862944 * jax.random.uniform(seeds[23], (D, 3, HEADS, HDIM), jnp.float32) ** steps_of(seeds[23], (D, 3, HEADS, HDIM), ((0, 16), (2, 2)), -0.2, 0.2)), 7.476541163953243e-09, 2.990616465581297e-08)
    out_proj = scatter_about(seeds[24], (HEADS, HDIM, D), (HEADS * HDIM // 32) ** -0.5, 0.75, ((0, 2), (2, 16)), jnp.float32)
    out_proj_avg = scatter_about(seeds[25], (HEADS, HDIM, D), (0.24 / (76 * C * C + 81 * C * D + 7 * D * HEADS * HDIM + D * FF + 8 * FREQ * D + 4 * FREQ * C) ** 0.5), 7.62939453125e-05, ((0, 2), (2, 16)), jnp.float32)
    out_proj_sq = jnp.clip(jnp.exp(math.log(7.655977518616908e-10) - 1.3862944 * jax.random.uniform(seeds[26], (HEADS, HDIM, D), jnp.float32) ** steps_of(seeds[26], (HEADS, HDIM, D), ((0, 2), (2, 16)), -0.2, 0.2)), 1.913994379654227e-10, 7.655977518616908e-10)
    hidden_in = scatter_about(seeds[27], (D, FF), D ** -0.5, 0.125, ((0, 16), (1, 2)), jnp.float32)
    hidden_in_avg = scatter_about(seeds[28], (D, FF), (0.5 / (76 * C * C + 81 * C * D + 7 * D * HEADS * HDIM + D * FF + 8 * FREQ * D + 4 * FREQ * C) ** 0.5), 0.00018310547, ((0, 16), (1, 2)), jnp.float32)
    hidden_in_sq = jnp.clip(jnp.exp(math.log(3.3229070606211053e-09) - 1.3862944 * jax.random.uniform(seeds[29], (D, FF), jnp.float32) ** steps_of(seeds[29], (D, FF), ((0, 16), (1, 2)), -0.2, 0.2)), 8.307267651552763e-10, 3.3229070606211053e-09)
    hidden_out = scatter_about(seeds[30], (FF, D), FF ** -0.5, 0.0625, ((0, 2), (1, 16)), jnp.float32)
    hidden_out_avg = scatter_about(seeds[31], (FF, D), (0.77 / (76 * C * C + 81 * C * D + 7 * D * HEADS * HDIM + D * FF + 8 * FREQ * D + 4 * FREQ * C) ** 0.5), 0.00024414062, ((0, 2), (1, 16)), jnp.float32)
    hidden_out_sq = jnp.clip(jnp.exp(math.log(7.880606389676359e-09) - 1.3862944 * jax.random.uniform(seeds[32], (FF, D), jnp.float32) ** steps_of(seeds[32], (FF, D), ((0, 2), (1, 16)), -0.2, 0.2)), 1.9701515974190897e-09, 7.880606389676359e-09)
    return {"images": images, "t_index": t_index, "cotangent": cotangent, "norm_params": norm_params, "norm_params_avg": norm_params_avg, "norm_params_sq": norm_params_sq, "first_conv": first_conv, "first_conv_avg": first_conv_avg, "first_conv_sq": first_conv_sq, "resnet_mod": resnet_mod, "resnet_mod_avg": resnet_mod_avg, "resnet_mod_sq": resnet_mod_sq, "second_conv": second_conv, "second_kernel_first_moment": second_kernel_first_moment, "second_conv_sq": second_conv_sq, "down_conv": down_conv, "down_conv_avg": down_conv_avg, "down_conv_sq": down_conv_sq, "ada_proj": ada_proj, "ada_proj_avg": ada_proj_avg, "ada_proj_sq": ada_proj_sq, "qkv_proj": qkv_proj, "qkv_proj_avg": qkv_proj_avg, "qkv_proj_sq": qkv_proj_sq, "out_proj": out_proj, "out_proj_avg": out_proj_avg, "out_proj_sq": out_proj_sq, "hidden_in": hidden_in, "hidden_in_avg": hidden_in_avg, "hidden_in_sq": hidden_in_sq, "hidden_out": hidden_out, "hidden_out_avg": hidden_out_avg, "hidden_out_sq": hidden_out_sq}


GN_EPS = 1e-05
LN_EPS = 1e-06
CLIP = 1.0
BETA_ONE = 0.5
BETA_TWO = 0.5
ADAM_EPS = 1e-08
DECAY = 0.1
LR_SCALE = 2.0
LR_NORM = 0.5
PLAN = 1000.0
HIGHEST = lax.Precision.HIGHEST

@jax.custom_vjp
def low(v):
    return lax.optimization_barrier(v.astype(jnp.bfloat16)).astype(jnp.float32)

@jax.custom_vjp
def low_back(v):
    return v

def low_keep(v):
    return (low(v), None)

def low_pass(kept, grad):
    return (grad,)

def back_keep(v):
    return (v, None)

def back_low(kept, grad):
    return (low(grad),)
low.defvjp(low_keep, low_pass)
low_back.defvjp(back_keep, back_low)

def embed_noise(t_index, emb_width):
    fraction = (t_index.astype(jnp.float32) + 0.5) / PLAN
    logsnr = -2.0 * jnp.log(jnp.tan(0.5 * math.pi * fraction)) + 2.0 * math.log(64.0 / 512.0)
    half_width = emb_width // 2
    frequencies = jnp.exp(-math.log(10000.0) * jnp.arange(half_width, dtype=jnp.float32) / half_width)
    angles = logsnr[:, None] * frequencies[None, :]
    return jnp.concatenate([jnp.sin(angles), jnp.cos(angles)], axis=1)

def group_norm(values, group_size):
    dims_of = values.shape
    grouped = values.reshape(dims_of[:-1] + (dims_of[-1] // group_size, group_size))
    center = lax.optimization_barrier(jnp.mean(grouped, axis=(1, 2, 4), keepdims=True))
    shifted = grouped - center
    spread = lax.optimization_barrier(jnp.mean(shifted * shifted, axis=(1, 2, 4), keepdims=True))
    return (shifted * lax.rsqrt(spread + GN_EPS)).reshape(dims_of)

def layer_norm(values):
    center = lax.optimization_barrier(jnp.mean(values, axis=-1, keepdims=True))
    shifted = values - center
    spread = lax.optimization_barrier(jnp.mean(shifted * shifted, axis=-1, keepdims=True))
    return shifted * lax.rsqrt(spread + LN_EPS)

def conv_same(inputs, kernel):
    return lax.conv_general_dilated(inputs, kernel, (1, 1), ((1, 1), (1, 1)), dimension_numbers=('NHWC', 'HWIO', 'NHWC'), precision=HIGHEST)

def conv_down(inputs, kernel):
    return lax.conv_general_dilated(inputs, kernel, (2, 2), ((1, 1), (1, 1)), dimension_numbers=('NHWC', 'HWIO', 'NHWC'), precision=HIGHEST)

def layer(params, pictures, emb_rows):
    gain_bias, first_conv, resnet_mod, second_conv, down_conv, ada_proj, qkv_proj, out_proj, hidden_in, hidden_out = [low(param_value) for param_value in params]
    batch_size = pictures.shape[0]
    emb_low = low(emb_rows)
    res_mods = jnp.dot(emb_low, resnet_mod.reshape(FREQ, 2 * C), precision=HIGHEST).reshape(batch_size, 2, C)
    ada_mods = jnp.dot(emb_low, ada_proj.reshape(FREQ, 6 * D), precision=HIGHEST).reshape(batch_size, 6, D)
    act_one = low(jax.nn.silu(group_norm(pictures, C // GROUPS) * gain_bias[0] + gain_bias[1]))
    middle = low_back(conv_same(act_one, first_conv))
    act_two = low(jax.nn.silu(group_norm(middle, C // GROUPS) * (1.0 + res_mods[:, None, None, 0]) + res_mods[:, None, None, 1]))
    branch = low_back(conv_same(act_two, second_conv))
    residual = pictures + branch
    shrunk = low_back(conv_down(low(residual), down_conv))
    tokens = shrunk.reshape(batch_size, SEQ, D)
    attn_in = low(layer_norm(tokens) * (1.0 + ada_mods[:, None, 1]) + ada_mods[:, None, 0])
    query_key_value_joined = low(low_back(jnp.dot(attn_in, qkv_proj.reshape(D, 3 * HEADS * HDIM), precision=HIGHEST)))
    query_key_value_joined = query_key_value_joined.reshape(batch_size, SEQ, 3, HEADS, HDIM)
    scores = low_back(jnp.einsum('bqhd,bkhd->bhqk', query_key_value_joined[:, :, 0], query_key_value_joined[:, :, 1], precision=HIGHEST) * HDIM ** (-0.5))
    attention = low(jax.nn.softmax(scores, axis=-1))
    mixed = jnp.einsum('bhqk,bkhd->bqhd', attention, query_key_value_joined[:, :, 2], precision=HIGHEST)
    mixed = low_back(low(mixed)).reshape(batch_size, SEQ, HEADS * HDIM)
    attended = low_back(jnp.dot(mixed, out_proj.reshape(HEADS * HDIM, D), precision=HIGHEST))
    after_attn = tokens + (1.0 + ada_mods[:, None, 2]) * attended
    mlp_in = low(layer_norm(after_attn) * (1.0 + ada_mods[:, None, 4]) + ada_mods[:, None, 3])
    pre_act = low_back(jnp.dot(mlp_in, hidden_in, precision=HIGHEST))
    hidden_act = low(jax.nn.gelu(pre_act, approximate=True))
    expanded = low_back(jnp.dot(hidden_act, hidden_out, precision=HIGHEST))
    return after_attn + (1.0 + ada_mods[:, None, 5]) * expanded

def learn_rates():
    conv_rate = LR_SCALE * (9 * C) ** (-0.5)
    mod_rate = LR_SCALE * (4 * FREQ) ** (-0.5)
    return (LR_NORM, conv_rate, mod_rate, conv_rate, conv_rate, mod_rate, LR_SCALE * D ** (-0.5), LR_SCALE * (HEADS * HDIM // 32) ** (-0.5), LR_SCALE * D ** (-0.5), LR_SCALE * FF ** (-0.5))

def reference(images, t_index, cotangent, norm_params, norm_params_avg, norm_params_sq, first_conv, first_conv_avg, first_conv_sq, resnet_mod, resnet_mod_avg, resnet_mod_sq, second_conv, second_kernel_first_moment, second_conv_sq, down_conv, down_conv_avg, down_conv_sq, ada_proj, ada_proj_avg, ada_proj_sq, qkv_proj, qkv_proj_avg, qkv_proj_sq, out_proj, out_proj_avg, out_proj_sq, hidden_in, hidden_in_avg, hidden_in_sq, hidden_out, hidden_out_avg, hidden_out_sq):
    masters = (norm_params, first_conv, resnet_mod, second_conv, down_conv, ada_proj, qkv_proj, out_proj, hidden_in, hidden_out)
    averages = (norm_params_avg, first_conv_avg, resnet_mod_avg, second_kernel_first_moment, down_conv_avg, ada_proj_avg, qkv_proj_avg, out_proj_avg, hidden_in_avg, hidden_out_avg)
    squares = (norm_params_sq, first_conv_sq, resnet_mod_sq, second_conv_sq, down_conv_sq, ada_proj_sq, qkv_proj_sq, out_proj_sq, hidden_in_sq, hidden_out_sq)
    noise_emb = embed_noise(t_index, FREQ)

    def one_image(totals, scanned):
        one_picture, emb_row, upstream = scanned

        def forward(params, inputs):
            return layer(params, inputs, emb_row[None])
        value_out, pullback = jax.vjp(forward, masters, one_picture.astype(jnp.float32)[None])
        param_grads, picture_grad = pullback(upstream.astype(jnp.float32)[None])
        totals = jax.tree.map(jnp.add, totals, param_grads)
        return (totals, (value_out[0].astype(jnp.bfloat16), picture_grad[0]))
    zeros_tree = jax.tree.map(jnp.zeros_like, masters)
    combined_total, (block_out, images_grad) = lax.scan(one_image, zeros_tree, (images, noise_emb, cotangent))
    square_sum = sum((jnp.sum(reduced * reduced) for reduced in combined_total))
    grad_norm = jnp.sqrt(square_sum)
    factor = jnp.minimum(1.0, CLIP / (grad_norm + 1e-06))
    correct_one = 1.0 - BETA_ONE ** STEP
    correct_two = 1.0 - BETA_TWO ** STEP
    results = []
    for master, average, square, reduced, learn_rate in zip(masters, averages, squares, combined_total, learn_rates()):
        clipped = reduced * factor
        new_avg = BETA_ONE * average + (1.0 - BETA_ONE) * clipped
        new_sq = BETA_TWO * square + (1.0 - BETA_TWO) * clipped * clipped
        step_dir = new_avg / correct_one / (jnp.sqrt(new_sq / correct_two) + ADAM_EPS)
        new_master = master - learn_rate * (step_dir + DECAY * master)
        results += [new_master, new_avg, new_sq]
    return (block_out, images_grad, grad_norm.reshape(1), results[0], results[1], results[2], results[3], results[4], results[5], results[6], results[7], results[8], results[9], results[10], results[11], results[12], results[13], results[14], results[15], results[16], results[17], results[18], results[19], results[20], results[21], results[22], results[23], results[24], results[25], results[26], results[27], results[28], results[29])
```

```python
import functools
import itertools
import math

import jax
import jax.numpy as jnp
from jax import lax
from jax.experimental import pallas as pl
from jax.experimental.pallas import tpu as pltpu
from jax.sharding import PartitionSpec as P

DP, TENSOR = ("dp", "tensor")
C = 1024
D = 2048
HEADS = 16
HDIM = 128
FF = 8192
GROUPS = 32
FREQ = 256
STEP = 5


GN_EPS = 1e-05
LN_EPS = 1e-06
CLIP = 1.0
BETA_ONE = 0.5
BETA_TWO = 0.5
ADAM_EPS = 1e-08
DECAY = 0.1
LR_SCALE = 2.0
LR_NORM = 0.5
PLAN = 1000.0
HIGHEST = lax.Precision.HIGHEST


def embed_noise(t_index, emb_width):
    fraction = (t_index.astype(jnp.float32) + 0.5) / PLAN
    logsnr = -2.0 * jnp.log(jnp.tan(0.5 * math.pi * fraction)) + 2.0 * math.log(64.0 / 512.0)
    half_width = emb_width // 2
    frequencies = jnp.exp(
        -math.log(10000.0) * jnp.arange(half_width, dtype=jnp.float32) / half_width
    )
    angles = logsnr[:, None] * frequencies[None, :]
    return jnp.concatenate([jnp.sin(angles), jnp.cos(angles)], axis=1)


def group_norm(values, group_size):
    dims_of = values.shape
    grouped = values.reshape(dims_of[:-1] + (dims_of[-1] // group_size, group_size))
    center = jnp.mean(grouped, axis=(1, 2, 4), keepdims=True)
    shifted = grouped - center
    spread = jnp.mean(shifted * shifted, axis=(1, 2, 4), keepdims=True)
    return (shifted * lax.rsqrt(spread + GN_EPS)).reshape(dims_of)


def layer_norm(values):
    center = jnp.mean(values, axis=-1, keepdims=True)
    shifted = values - center
    spread = jnp.mean(shifted * shifted, axis=-1, keepdims=True)
    return shifted * lax.rsqrt(spread + LN_EPS)


def leading_segment(picture, gain_bias):
    return jax.nn.silu(group_norm(picture, C // GROUPS) * gain_bias[0] + gain_bias[1])


def second_piece(middle, res_mods):
    return jax.nn.silu(
        group_norm(middle, C // GROUPS) * (1.0 + res_mods[:, None, None, 0])
        + res_mods[:, None, None, 1]
    )


def modulate(tokens, shift_scale):
    return layer_norm(tokens) * (1.0 + shift_scale[:, None, 1]) + shift_scale[:, None, 0]


def gelu_tanh(values):
    return jax.nn.gelu(values, approximate=True)


def conv_same(inputs, kernel):
    height, breadth = (inputs.shape[1], inputs.shape[2])
    padded = jnp.pad(inputs, ((0, 0), (1, 1), (1, 1), (0, 0)))
    summed_taps = jnp.zeros(inputs.shape[:3] + (kernel.shape[3],), jnp.float32)
    for row_tap in range(3):
        for col_tap in range(3):
            window = padded[:, row_tap : row_tap + height, col_tap : col_tap + breadth]
            summed_taps = summed_taps + jnp.einsum(
                "bhwc,cd->bhwd",
                window,
                kernel[row_tap, col_tap],
                preferred_element_type=jnp.float32,
            )
    return summed_taps


def conv_same_input(upstream, kernel):
    height, breadth = (upstream.shape[1], upstream.shape[2])
    padded = jnp.pad(upstream, ((0, 0), (1, 1), (1, 1), (0, 0)))
    summed_taps = jnp.zeros(upstream.shape[:3] + (kernel.shape[2],), jnp.float32)
    for row_tap in range(3):
        for col_tap in range(3):
            window = padded[
                :, 2 - row_tap : 2 - row_tap + height, 2 - col_tap : 2 - col_tap + breadth
            ]
            summed_taps = summed_taps + jnp.einsum(
                "bhwd,cd->bhwc",
                window,
                kernel[row_tap, col_tap],
                preferred_element_type=jnp.float32,
            )
    return summed_taps


def conv_same_kernel(inputs, upstream):
    height, breadth = (inputs.shape[1], inputs.shape[2])
    padded = jnp.pad(inputs, ((0, 0), (1, 1), (1, 1), (0, 0)))
    tap_list = []
    for row_tap in range(3):
        for col_tap in range(3):
            window = padded[:, row_tap : row_tap + height, col_tap : col_tap + breadth]
            tap_list.append(
                jnp.einsum("bhwc,bhwd->cd", window, upstream, preferred_element_type=jnp.float32)
            )
    return jnp.stack(tap_list).reshape(3, 3, inputs.shape[3], upstream.shape[3])


def conv_down(inputs, kernel):
    height, breadth = (inputs.shape[1], inputs.shape[2])
    padded = jnp.pad(inputs, ((0, 0), (1, 1), (1, 1), (0, 0)))
    summed_taps = jnp.zeros(
        (inputs.shape[0], height // 2, breadth // 2, kernel.shape[3]), jnp.float32
    )
    for row_tap in range(3):
        for col_tap in range(3):
            window = padded[:, row_tap : row_tap + height : 2, col_tap : col_tap + breadth : 2]
            summed_taps = summed_taps + jnp.einsum(
                "bhwc,cd->bhwd",
                window,
                kernel[row_tap, col_tap],
                preferred_element_type=jnp.float32,
            )
    return summed_taps


def conv_down_input(upstream, kernel, height, breadth):
    summed_taps = jnp.zeros(
        (upstream.shape[0], height + 2, breadth + 2, kernel.shape[2]), jnp.float32
    )
    for row_tap in range(3):
        for col_tap in range(3):
            spread_out = jnp.einsum(
                "bhwd,cd->bhwc",
                upstream,
                kernel[row_tap, col_tap],
                preferred_element_type=jnp.float32,
            )
            placed = lax.pad(
                spread_out,
                jnp.float32(0.0),
                ((0, 0, 0), (row_tap, 3 - row_tap, 1), (col_tap, 3 - col_tap, 1), (0, 0, 0)),
            )
            summed_taps = summed_taps + placed
    return summed_taps[:, 1 : height + 1, 1 : breadth + 1]


def conv_down_kernel(inputs, upstream):
    height, breadth = (inputs.shape[1], inputs.shape[2])
    padded = jnp.pad(inputs, ((0, 0), (1, 1), (1, 1), (0, 0)))
    tap_list = []
    for row_tap in range(3):
        for col_tap in range(3):
            window = padded[:, row_tap : row_tap + height : 2, col_tap : col_tap + breadth : 2]
            tap_list.append(
                jnp.einsum("bhwc,bhwd->cd", window, upstream, preferred_element_type=jnp.float32)
            )
    return jnp.stack(tap_list).reshape(3, 3, inputs.shape[3], upstream.shape[3])


def clipped_step(masters, averages, squares, combined_total, sum_all):
    local_sq = jnp.zeros((), jnp.float32)
    for position, reduced in enumerate(combined_total):
        shard_sq = jnp.sum(reduced * reduced)
        if position == 0 or position == 5:
            shard_sq = shard_sq / lax.axis_size(TENSOR)
        local_sq = local_sq + shard_sq
    square_sum = sum_all(local_sq)
    grad_norm = jnp.sqrt(square_sum)
    factor = jnp.minimum(1.0, CLIP / (grad_norm + 1e-06))
    conv_rate = LR_SCALE * (9 * C) ** (-0.5)
    mod_rate = LR_SCALE * (4 * FREQ) ** (-0.5)
    rates = (
        LR_NORM,
        conv_rate,
        mod_rate,
        conv_rate,
        conv_rate,
        mod_rate,
        LR_SCALE * D ** (-0.5),
        LR_SCALE * (HEADS * HDIM // 32) ** (-0.5),
        LR_SCALE * D ** (-0.5),
        LR_SCALE * FF ** (-0.5),
    )
    correct_one = 1.0 - BETA_ONE**STEP
    correct_two = 1.0 - BETA_TWO**STEP
    results = []
    for master, average, square, reduced, learn_rate in zip(
        masters, averages, squares, combined_total, rates
    ):
        clipped = reduced * factor
        new_avg = BETA_ONE * average + (1.0 - BETA_ONE) * clipped
        new_sq = BETA_TWO * square + (1.0 - BETA_TWO) * clipped * clipped
        step_dir = new_avg / correct_one / (jnp.sqrt(new_sq / correct_two) + ADAM_EPS)
        new_master = master - learn_rate * (step_dir + DECAY * master)
        results += [new_master, new_avg, new_sq]
    return (grad_norm.reshape(1),) + tuple(results)


def per_device(
    images,
    t_index,
    cotangent,
    norm_params,
    norm_params_avg,
    norm_params_sq,
    first_conv,
    first_conv_avg,
    first_conv_sq,
    resnet_mod,
    resnet_mod_avg,
    resnet_mod_sq,
    second_conv,
    second_kernel_first_moment,
    second_conv_sq,
    down_conv,
    down_conv_avg,
    down_conv_sq,
    ada_proj,
    ada_proj_avg,
    ada_proj_sq,
    qkv_proj,
    qkv_proj_avg,
    qkv_proj_sq,
    out_proj,
    out_proj_avg,
    out_proj_sq,
    hidden_in,
    hidden_in_avg,
    hidden_in_sq,
    hidden_out,
    hidden_out_avg,
    hidden_out_sq,
):
    masters = (
        norm_params,
        first_conv,
        resnet_mod,
        second_conv,
        down_conv,
        ada_proj,
        qkv_proj,
        out_proj,
        hidden_in,
        hidden_out,
    )
    averages = (
        norm_params_avg,
        first_conv_avg,
        resnet_mod_avg,
        second_kernel_first_moment,
        down_conv_avg,
        ada_proj_avg,
        qkv_proj_avg,
        out_proj_avg,
        hidden_in_avg,
        hidden_out_avg,
    )
    squares = (
        norm_params_sq,
        first_conv_sq,
        resnet_mod_sq,
        second_conv_sq,
        down_conv_sq,
        ada_proj_sq,
        qkv_proj_sq,
        out_proj_sq,
        hidden_in_sq,
        hidden_out_sq,
    )
    lowered = tuple((master.astype(jnp.bfloat16) for master in masters))
    gathered = (
        lax.all_gather(lowered[0], DP, axis=1, tiled=True),
        lax.all_gather(lowered[1], DP, axis=2, tiled=True),
        lax.all_gather(lowered[2], DP, axis=0, tiled=True),
        lax.all_gather(lowered[3], DP, axis=3, tiled=True),
        lax.all_gather(lowered[4], DP, axis=2, tiled=True),
        lax.all_gather(lowered[5], DP, axis=0, tiled=True),
        lax.all_gather(lowered[6], DP, axis=0, tiled=True),
        lax.all_gather(lowered[7], DP, axis=2, tiled=True),
        lax.all_gather(lowered[8], DP, axis=0, tiled=True),
        lax.all_gather(lowered[9], DP, axis=1, tiled=True),
    )
    (
        gain_bias,
        conv_one,
        res_table,
        conv_two,
        conv_half,
        ada_table,
        qkv_full,
        out_full,
        up_full,
        down_full,
    ) = gathered
    batch_size = images.shape[0]
    height, breadth = (images.shape[1], images.shape[2])
    local_c = conv_one.shape[3]
    local_d = conv_half.shape[3]
    heads_here = qkv_full.shape[2]
    tokens_len = height // 2 * (breadth // 2)
    tensor_pos = lax.axis_index(TENSOR)
    n_tensor = lax.axis_size(TENSOR)
    score_scale = HDIM ** (-0.5)
    noise_emb = embed_noise(t_index, FREQ)
    emb_low = noise_emb.astype(jnp.bfloat16)
    emb_back = emb_low.astype(jnp.float32)
    res_mods = jnp.dot(
        emb_low, res_table.reshape(FREQ, 2 * local_c), preferred_element_type=jnp.float32
    ).reshape(batch_size, 2, local_c)
    ada_mods = jnp.dot(
        emb_low, ada_table.reshape(FREQ, 6 * D), preferred_element_type=jnp.float32
    ).reshape(batch_size, 6, D)
    image_float = images.astype(jnp.float32)
    gain_float = gain_bias.astype(jnp.float32)
    act_one, first_back = jax.vjp(leading_segment, image_float, gain_float)
    act_one = act_one.astype(jnp.bfloat16)
    middle = conv_same(act_one, conv_one)
    act_two, second_back = jax.vjp(second_piece, middle, res_mods)
    act_two = act_two.astype(jnp.bfloat16)
    branch = lax.psum(conv_same(act_two, conv_two).astype(jnp.bfloat16), TENSOR).astype(
        jnp.float32
    )
    residual = image_float + branch
    resid_low = residual.astype(jnp.bfloat16)
    shrunk = conv_down(resid_low, conv_half)
    pieces = lax.all_gather(shrunk.astype(jnp.bfloat16), TENSOR, axis=3, tiled=True).astype(
        shrunk.dtype
    )
    tokens = pieces.reshape(batch_size, tokens_len, D)
    attn_in, attn_back = jax.vjp(modulate, tokens, ada_mods[:, 0:2])
    attn_low = attn_in.astype(jnp.bfloat16).reshape(batch_size * tokens_len, D)
    qkv_low = jnp.dot(
        attn_low, qkv_full.reshape(D, 3 * heads_here * HDIM), preferred_element_type=jnp.float32
    ).astype(jnp.bfloat16)
    qkv_low = qkv_low.reshape(batch_size, tokens_len, 3, heads_here, HDIM)
    query_low, key_low, value_low = (qkv_low[:, :, 0], qkv_low[:, :, 1], qkv_low[:, :, 2])
    scores = (
        jnp.einsum("bqhd,bkhd->bhqk", query_low, key_low, preferred_element_type=jnp.float32)
        * score_scale
    )
    row_max = jnp.max(scores, axis=-1, keepdims=True)
    log_total = row_max + jnp.log(jnp.sum(jnp.exp(scores - row_max), axis=-1, keepdims=True))
    attention_low = jnp.exp(scores - log_total).astype(jnp.bfloat16)
    mixed = jnp.einsum(
        "bhqk,bkhd->bqhd", attention_low, value_low, preferred_element_type=jnp.float32
    ).astype(jnp.bfloat16)
    mixed = mixed.reshape(batch_size * tokens_len, heads_here * HDIM)
    out_flat = out_full.reshape(heads_here * HDIM, D)
    attended = (
        lax.psum(
            jnp.dot(mixed, out_flat, preferred_element_type=jnp.float32).astype(jnp.bfloat16),
            TENSOR,
        )
        .astype(jnp.float32)
        .reshape(batch_size, tokens_len, D)
    )
    gate_one = 1.0 + ada_mods[:, None, 2]
    after_attn = tokens + gate_one * attended
    mlp_in, mlp_back = jax.vjp(modulate, after_attn, ada_mods[:, 3:5])
    mlp_low = mlp_in.astype(jnp.bfloat16).reshape(batch_size * tokens_len, D)
    pre_act = jnp.dot(mlp_low, up_full, preferred_element_type=jnp.float32)
    hidden_act, gelu_back = jax.vjp(gelu_tanh, pre_act)
    hidden_low = hidden_act.astype(jnp.bfloat16)
    expanded = (
        lax.psum(
            jnp.dot(hidden_low, down_full, preferred_element_type=jnp.float32).astype(jnp.bfloat16),
            TENSOR,
        )
        .astype(jnp.float32)
        .reshape(batch_size, tokens_len, D)
    )
    gate_two = 1.0 + ada_mods[:, None, 5]
    block_out = (after_attn + gate_two * expanded).astype(jnp.bfloat16)
    upstream = cotangent.astype(jnp.float32)
    grad_expanded = (gate_two * upstream).astype(jnp.bfloat16).reshape(batch_size * tokens_len, D)
    grad_gate_two = jnp.sum(upstream * expanded, axis=1)
    grad_down = jnp.einsum(
        "tf,td->fd", hidden_low, grad_expanded, preferred_element_type=jnp.float32
    )
    grad_hidden = jnp.einsum(
        "td,fd->tf", grad_expanded, down_full, preferred_element_type=jnp.float32
    )
    (grad_pre,) = gelu_back(grad_hidden)
    grad_pre_low = grad_pre.astype(jnp.bfloat16)
    grad_mlp_in = (
        lax.psum(
            jnp.einsum(
                "tf,df->td", grad_pre_low, up_full, preferred_element_type=jnp.float32
            ).astype(jnp.bfloat16),
            TENSOR,
        )
        .astype(jnp.float32)
        .reshape(batch_size, tokens_len, D)
    )
    grad_after_norm, grad_mods_two = mlp_back(grad_mlp_in)
    grad_after = upstream + grad_after_norm
    grad_attended = (gate_one * grad_after).astype(jnp.bfloat16).reshape(batch_size * tokens_len, D)
    grad_gate_one = jnp.sum(grad_after * attended, axis=1)
    grad_out = jnp.einsum("tk,td->kd", mixed, grad_attended, preferred_element_type=jnp.float32)
    grad_mixed = jnp.einsum(
        "td,kd->tk", grad_attended, out_flat, preferred_element_type=jnp.float32
    ).astype(jnp.bfloat16)
    grad_mixed = grad_mixed.reshape(batch_size, tokens_len, heads_here, HDIM)
    scores = (
        jnp.einsum("bqhd,bkhd->bhqk", query_low, key_low, preferred_element_type=jnp.float32)
        * score_scale
    )
    attention = jnp.exp(scores - log_total)
    attention_low = attention.astype(jnp.bfloat16)
    grad_probs = jnp.einsum(
        "bqhd,bkhd->bhqk", grad_mixed, value_low, preferred_element_type=jnp.float32
    )
    grad_values = jnp.einsum(
        "bhqk,bqhd->bkhd", attention_low, grad_mixed, preferred_element_type=jnp.float32
    )
    grad_scores = (
        attention * (grad_probs - jnp.sum(grad_probs * attention, axis=-1, keepdims=True))
    ).astype(jnp.bfloat16)
    query_gradient = (
        jnp.einsum("bhqk,bkhd->bqhd", grad_scores, key_low, preferred_element_type=jnp.float32)
        * score_scale
    )
    grad_keys = (
        jnp.einsum("bhqk,bqhd->bkhd", grad_scores, query_low, preferred_element_type=jnp.float32)
        * score_scale
    )
    grad_qkv = (
        jnp.stack([query_gradient, grad_keys, grad_values], axis=2)
        .astype(jnp.bfloat16)
        .reshape(batch_size * tokens_len, 3 * heads_here * HDIM)
    )
    grad_qkv_w = jnp.einsum(
        "td,tk->dk", attn_low, grad_qkv, preferred_element_type=jnp.float32
    ).reshape(D, 3, heads_here, HDIM)
    grad_attn_in = (
        lax.psum(
            jnp.einsum(
                "tk,dk->td",
                grad_qkv,
                qkv_full.reshape(D, 3 * heads_here * HDIM),
                preferred_element_type=jnp.float32,
            ).astype(jnp.bfloat16),
            TENSOR,
        )
        .astype(jnp.float32)
        .reshape(batch_size, tokens_len, D)
    )
    grad_tokens_norm, grad_mods_one = attn_back(grad_attn_in)
    grad_tokens = grad_after + grad_tokens_norm
    grad_mods = jnp.concatenate(
        [grad_mods_one, grad_gate_one[:, None], grad_mods_two, grad_gate_two[:, None]], axis=1
    )
    adaptive_gradient = jnp.einsum(
        "bf,bk->fk", emb_back, grad_mods.reshape(batch_size, 6 * D), precision=HIGHEST
    ).reshape(FREQ, 6, D)
    grad_out_w = grad_out.reshape(heads_here, HDIM, D)
    grad_up = jnp.einsum("td,tf->df", mlp_low, grad_pre_low, preferred_element_type=jnp.float32)
    transformer_gradient_total = (
        lax.psum_scatter(adaptive_gradient, DP, scatter_dimension=0, tiled=True),
        lax.psum_scatter(grad_qkv_w, DP, scatter_dimension=0, tiled=True),
        lax.psum_scatter(grad_out_w, DP, scatter_dimension=2, tiled=True),
        lax.psum_scatter(grad_up, DP, scatter_dimension=0, tiled=True),
        lax.psum_scatter(grad_down, DP, scatter_dimension=1, tiled=True),
    )
    grad_shrunk = lax.dynamic_slice_in_dim(
        grad_tokens.reshape(batch_size, height // 2, breadth // 2, D),
        tensor_pos * local_d,
        local_d,
        axis=3,
    ).astype(jnp.bfloat16)
    grad_half = conv_down_kernel(resid_low, grad_shrunk)
    grad_resid = lax.psum(
        conv_down_input(grad_shrunk, conv_half, height, breadth).astype(jnp.bfloat16), TENSOR
    ).astype(jnp.float32)
    grad_branch = grad_resid.astype(jnp.bfloat16)
    grad_conv_two = conv_same_kernel(act_two, grad_branch)
    grad_act_two = conv_same_input(grad_branch, conv_two)
    grad_middle, grad_res_mods = second_back(grad_act_two)
    grad_middle_low = grad_middle.astype(jnp.bfloat16)
    grad_conv_one = conv_same_kernel(act_one, grad_middle_low)
    grad_act_one = lax.psum(
        conv_same_input(grad_middle_low, conv_one).astype(jnp.bfloat16), TENSOR
    ).astype(jnp.float32)
    grad_image_norm, grad_gain = first_back(grad_act_one)
    images_grad = grad_resid + grad_image_norm
    grad_res_table = jnp.einsum(
        "bf,bk->fk", emb_back, grad_res_mods.reshape(batch_size, 2 * local_c), precision=HIGHEST
    ).reshape(FREQ, 2, local_c)
    resnet_gradient_total = (
        lax.psum_scatter(grad_gain, DP, scatter_dimension=1, tiled=True),
        lax.psum_scatter(grad_conv_one, DP, scatter_dimension=2, tiled=True),
        lax.psum_scatter(grad_res_table, DP, scatter_dimension=0, tiled=True),
        lax.psum_scatter(grad_conv_two, DP, scatter_dimension=3, tiled=True),
        lax.psum_scatter(grad_half, DP, scatter_dimension=2, tiled=True),
    )
    combined_total = tuple(resnet_gradient_total) + tuple(transformer_gradient_total)
    return (block_out, images_grad) + clipped_step(
        masters,
        averages,
        squares,
        combined_total,
        lambda local: lax.psum(local, (DP, TENSOR)),
    )


MESH = pl.DeviceIdType.MESH
ANYWHERE = pl.BlockSpec(memory_space=pl.ANY)
IN_VMEM = pl.BlockSpec(memory_space=pltpu.VMEM)
LAYERS = 4
ORDER = (3, 0, 2, 1)
VMEM_GRANT = 48 * 1024 * 1024


class Place:
    def __init__(self, wide):
        self.wide = wide
        self.dp = lax.axis_index(DP)
        self.core = lax.axis_index(TENSOR)
        self.z = self.dp // 4
        x = self.dp % 2
        y = (self.dp // 2) % 2
        x_mate = self.dp + 1 - 2 * x
        y_mate = self.dp + 2 - 4 * y
        if wide:
            self.first = x_mate * (1 - self.core) + y_mate * self.core
            self.second = y_mate * (1 - self.core) + x_mate * self.core
            self.stride = 4
            self.column = self.dp % 4
            self.first_column = self.first % 4
            self.second_column = self.second % 4
            self.far_column = 3 - self.column
        else:
            self.first = self.second = y_mate
            self.stride = 2
            self.column = y
            self.second_column = 1 - y
        self.slot = self.z * self.stride + self.column
        self.has_below = self.z > 0
        self.has_above = self.z < LAYERS - 1

    def greet(self, with_core):
        barrier = pltpu.get_barrier_semaphore()

        def signal(dp, core):
            pl.semaphore_signal(barrier, inc=1, device_id=(dp, core), device_id_type=MESH)

        signal(self.second, self.core)
        if self.wide:
            signal(self.first, self.core)
        if with_core:
            signal(self.dp, 1 - self.core)
        pl.when(self.has_below)(lambda: signal(self.dp - 4, self.core))
        pl.when(self.has_above)(lambda: signal(self.dp + 4, self.core))
        layers = (self.z + LAYERS - 1) // LAYERS + (2 * LAYERS - 2 - self.z) // LAYERS
        pl.semaphore_wait(barrier, 1 + self.wide + with_core + layers)


def params(number):
    return pltpu.CompilerParams(
        collective_id=number, has_side_effects=True, vmem_limit_bytes=VMEM_GRANT
    )


def gather_kernel(wide, both, block_ref, out_ref, send_sem, recv_sem, own_sem):
    at = Place(wide)

    def here(slot):
        return out_ref.at[slot, at.core] if both else out_ref.at[slot]

    def copy(sem, source, slot, mate):
        return pltpu.make_async_remote_copy(
            src_ref=source,
            dst_ref=here(slot),
            send_sem=send_sem.at[sem],
            recv_sem=recv_sem.at[sem],
            device_id=(mate, at.core),
            device_id_type=MESH,
        )

    def mirror(slot, source):
        return pltpu.make_async_remote_copy(
            src_ref=source,
            dst_ref=here(slot),
            send_sem=send_sem.at[18 + slot],
            recv_sem=recv_sem.at[18 + slot],
            device_id=(at.dp, 1 - at.core),
            device_id_type=MESH,
        )

    at.greet(both)
    keep = pltpu.make_async_copy(block_ref, here(at.slot), own_sem)
    keep.start()

    def place(layer, column):
        return layer * at.stride + column

    def spread(layer, source):
        slot = place(layer, at.column)
        if wide:
            copy(6 + layer, source, slot, at.first).start()
        copy(10 + layer, source, slot, at.second).start()
        if both:
            mirror(slot, source).start()

    def up(distance, source):
        return copy(distance, source, place(at.z - distance, at.column), at.dp + 4)

    def down(distance, source):
        return copy(3 + distance, source, place(at.z + distance, at.column), at.dp - 4)

    pl.when(at.has_above)(lambda: up(0, block_ref).start())
    pl.when(at.has_below)(lambda: down(0, block_ref).start())
    spread(at.z, block_ref)

    def onward(layer):
        slot = place(layer, at.first_column)
        copy(6 + layer, here(slot), slot, at.first).wait_recv()
        copy(14 + layer, here(slot), slot, at.second).start()
        if both:
            mirror(slot, here(slot)).start()

    for distance in range(1, LAYERS):
        below, above = at.z - distance, at.z + distance

        @pl.when(below >= 0)
        def _():
            slot = place(below, at.column)
            copy(distance - 1, here(slot), slot, at.dp).wait_recv()
            if distance < LAYERS - 1:
                pl.when(at.has_above)(lambda: up(distance, here(slot)).start())
            spread(below, here(slot))

        @pl.when(above < LAYERS)
        def _():
            slot = place(above, at.column)
            copy(3 + distance - 1, here(slot), slot, at.dp).wait_recv()
            if distance < LAYERS - 1:
                pl.when(at.has_below)(lambda: down(distance, here(slot)).start())
            spread(above, here(slot))

        if not wide:
            continue
        if distance == 1:
            onward(at.z)
        else:
            pl.when(at.z - distance + 1 >= 0)(lambda: onward(at.z - distance + 1))
            pl.when(at.z + distance - 1 < LAYERS)(lambda: onward(at.z + distance - 1))
    if wide:
        pl.when(at.z == LAYERS - 1)(lambda: onward(0))
        pl.when(at.z == 0)(lambda: onward(LAYERS - 1))

    keep.wait()
    own = here(at.slot)
    for layer in range(LAYERS):
        arriving = [(10, at.second_column)]
        if wide:
            arriving.append((14, at.far_column))
        for sem, column in arriving:
            slot = place(layer, column)
            copy(sem + layer, own, slot, at.second).wait_recv()
            if both:
                mirror(slot, here(slot)).start()
    if both:
        for slot in range(at.stride * LAYERS):
            pltpu.make_async_remote_copy(
                src_ref=own,
                dst_ref=out_ref.at[slot, 1 - at.core],
                send_sem=send_sem.at[18 + slot],
                recv_sem=recv_sem.at[18 + slot],
                device_id=(at.dp, 1 - at.core),
                device_id_type=MESH,
            ).wait_recv()
            mirror(slot, own).wait_send()
    for sem in range(6, 18) if wide else range(10, 14):
        copy(sem, own, at.slot, at.second).wait_send()
    for distance in range(LAYERS - 1):

        @pl.when(jnp.logical_and(at.has_above, at.z - distance >= 0))
        def _():
            up(distance, own).wait_send()

        @pl.when(jnp.logical_and(at.has_below, at.z + distance < LAYERS))
        def _():
            down(distance, own).wait_send()


def gather(number, block, wide=True, both=False):
    chips = 16 if wide else 8
    shape = (chips,) + ((2,) if both else ()) + block.shape
    count = 18 + both * chips
    return pl.pallas_call(
        functools.partial(gather_kernel, wide, both),
        out_shape=jax.ShapeDtypeStruct(shape, block.dtype),
        in_specs=[ANYWHERE],
        out_specs=ANYWHERE,
        scratch_shapes=[
            pltpu.SemaphoreType.DMA((count,)),
            pltpu.SemaphoreType.DMA((count,)),
            pltpu.SemaphoreType.DMA,
        ],
        compiler_params=params(number),
        name=f"gather_{chips}" + ("_both" if both else ""),
    )(block)


def reduce_kernel(wide, pair, share, in_ref, out_ref, *scratch):
    if pair:
        *scratch, paired, pair_send, pair_recv = scratch
    own, from_second, from_first, from_z, send_sem, recv_sem, own_sem = scratch
    at = Place(wide)

    def copy(sem, source, target, mate):
        return pltpu.make_async_remote_copy(
            src_ref=source,
            dst_ref=target,
            send_sem=send_sem.at[sem],
            recv_sem=recv_sem.at[sem],
            device_id=(mate, at.core),
            device_id_type=MESH,
        )

    def place(layer, column):
        return layer * at.stride + column

    def load(slot):
        source = in_ref.at[slot, at.core] if pair else in_ref.at[slot]
        return pltpu.make_async_copy(source, own.at[slot], own_sem.at[slot])

    def to_mate(slot):
        return pltpu.make_async_remote_copy(
            src_ref=in_ref.at[slot, 1 - at.core],
            dst_ref=paired.at[slot],
            send_sem=pair_send.at[slot],
            recv_sem=pair_recv.at[slot],
            device_id=(at.dp, 1 - at.core),
            device_id_type=MESH,
        )

    def to_second(half, layer):
        column = at.far_column if half == 0 else at.second_column
        source = own if pair else in_ref
        return copy(
            4 * half + layer,
            source.at[place(layer, column)],
            from_second.at[4 * half + layer],
            at.second,
        )

    def first_slot(layer):
        return place(layer, at.first_column)

    def own_slot(layer):
        return place(layer, at.column)

    def to_first(layer):
        return copy(8 + layer, own.at[first_slot(layer)], from_first.at[layer], at.first)

    def up(layer):
        return copy(12 + layer, own.at[own_slot(layer)], from_z.at[layer], at.dp + 4)

    def down(layer):
        return copy(16 + layer, own.at[own_slot(layer)], from_z.at[4 + layer], at.dp - 4)

    def value(ref, index):
        return ref[index].astype(jnp.float32)

    def join(slot):
        load(slot).wait()
        to_mate(slot).wait_recv()
        own[slot] = (value(own, slot) + value(paired, slot)).astype(own.dtype)

    at.greet(pair or share)
    halves = (0, 1) if wide else (1,)
    for half in halves:
        for layer in ORDER:
            away = place(layer, at.far_column if half == 0 else at.second_column)
            keep = first_slot(layer) if half == 0 else own_slot(layer)
            if pair:
                for slot in (away, keep):
                    to_mate(slot).start()
                    load(slot).start()
            else:
                to_second(half, layer).start()
                load(keep).start()
    if pair:
        for half in halves:
            for layer in ORDER:
                join(place(layer, at.far_column if half == 0 else at.second_column))
                to_second(half, layer).start()
        for layer in ORDER:
            if wide:
                join(first_slot(layer))
            join(own_slot(layer))

    if wide:
        for layer in ORDER:
            slot = first_slot(layer)
            if not pair:
                load(slot).wait()
            to_second(0, layer).wait_recv()
            own[slot] = (value(own, slot) + value(from_second, layer)).astype(own.dtype)
            to_first(layer).start()
    result = out_ref.at[at.core] if share else out_ref
    for layer in ORDER:
        slot = own_slot(layer)
        if not pair:
            load(slot).wait()
        to_second(1, layer).wait_recv()
        total = value(own, slot) + value(from_second, 4 + layer)
        if wide:
            to_first(layer).wait_recv()
            total = total + value(from_first, layer)
        own[slot] = total.astype(own.dtype)

        @pl.when(at.z < layer)
        def _():
            @pl.when(at.has_below)
            def _():
                up(layer).wait_recv()
                own[slot] = (value(own, slot) + value(from_z, layer)).astype(own.dtype)

            up(layer).start()

        @pl.when(at.z > layer)
        def _():
            @pl.when(at.has_above)
            def _():
                down(layer).wait_recv()
                own[slot] = (value(own, slot) + value(from_z, 4 + layer)).astype(own.dtype)

            down(layer).start()

        @pl.when(at.z == layer)
        def _():
            result[...] = total.astype(out_ref.dtype)

    for layer in range(LAYERS):

        @pl.when(at.z == layer)
        def _():
            @pl.when(at.has_below)
            def _():
                up(layer).wait_recv()
                result[...] = (result[...].astype(jnp.float32) + value(from_z, layer)).astype(
                    out_ref.dtype
                )

            @pl.when(at.has_above)
            def _():
                down(layer).wait_recv()
                result[...] = (result[...].astype(jnp.float32) + value(from_z, 4 + layer)).astype(
                    out_ref.dtype
                )

    if share:

        def give(core):
            return pltpu.make_async_remote_copy(
                src_ref=result,
                dst_ref=out_ref.at[core],
                send_sem=send_sem.at[20],
                recv_sem=recv_sem.at[20],
                device_id=(at.dp, 1 - at.core),
                device_id_type=MESH,
            )

        give(at.core).start()
        give(1 - at.core).wait_recv()
        give(at.core).wait_send()
    if pair:
        for slot in range(at.stride * LAYERS):
            to_mate(slot).wait_send()
    for layer in range(LAYERS):
        for half in halves:
            to_second(half, layer).wait_send()
        if wide:
            to_first(layer).wait_send()
        pl.when(at.z < layer)(lambda: up(layer).wait_send())
        pl.when(at.z > layer)(lambda: down(layer).wait_send())


def reduce(number, blocks, wide=True, pair=False, share=False):
    chips = 16 if wide else 8
    block = blocks.shape[-2:]
    kind = blocks.dtype
    scratch = [
        pltpu.VMEM((chips,) + block, kind),
        pltpu.VMEM((8,) + block, kind),
        pltpu.VMEM((4,) + block, kind),
        pltpu.VMEM((8,) + block, kind),
        pltpu.SemaphoreType.DMA((21,)),
        pltpu.SemaphoreType.DMA((21,)),
        pltpu.SemaphoreType.DMA((chips,)),
    ]
    if pair:
        scratch += [
            pltpu.VMEM((chips,) + block, kind),
            pltpu.SemaphoreType.DMA((chips,)),
            pltpu.SemaphoreType.DMA((chips,)),
        ]
    return pl.pallas_call(
        functools.partial(reduce_kernel, wide, pair, share),
        out_shape=jax.ShapeDtypeStruct(((2,) if share else ()) + block, jnp.float32),
        in_specs=[ANYWHERE],
        out_specs=IN_VMEM,
        scratch_shapes=scratch,
        compiler_params=params(number),
        name=f"reduce_{chips}" + ("_pair" if pair else "") + ("_share" if share else ""),
    )(blocks)


def trade_kernel(count, *refs):
    in_refs, out_refs = (refs[:count], refs[count : 2 * count])
    send_sem, recv_sem, own_sem = refs[2 * count :]
    dp, core = (lax.axis_index(DP), lax.axis_index(TENSOR))
    others = 4 * LAYERS - 1
    barrier = pltpu.get_barrier_semaphore()

    def peer(step):
        return (dp + step) % (4 * LAYERS)

    @pl.loop(1, others + 1)
    def _(step):
        pl.semaphore_signal(barrier, inc=1, device_id=(peer(step), core), device_id_type=MESH)

    pl.semaphore_wait(barrier, others)

    def copy(index, step):
        return pltpu.make_async_remote_copy(
            src_ref=in_refs[index].at[peer(step)],
            dst_ref=out_refs[index].at[dp],
            send_sem=send_sem.at[index, step - 1],
            recv_sem=recv_sem.at[index, step - 1],
            device_id=(peer(step), core),
            device_id_type=MESH,
        )

    def keep(index):
        return pltpu.make_async_copy(
            in_refs[index].at[dp], out_refs[index].at[dp], own_sem.at[index]
        )

    for index in range(count):
        keep(index).start()

        @pl.loop(1, others + 1)
        def _(step):
            copy(index, step).start()

    for index in range(count):
        keep(index).wait()

        @pl.loop(1, others + 1)
        def _(step):
            copy(index, step).wait()


def trade(number, *blocks):
    count = len(blocks)
    return pl.pallas_call(
        functools.partial(trade_kernel, count),
        out_shape=[jax.ShapeDtypeStruct(b.shape, b.dtype) for b in blocks],
        in_specs=[ANYWHERE] * count,
        out_specs=[ANYWHERE] * count,
        scratch_shapes=[
            pltpu.SemaphoreType.DMA((count, 15)),
            pltpu.SemaphoreType.DMA((count, 15)),
            pltpu.SemaphoreType.DMA((count,)),
        ],
        compiler_params=params(number),
        name="trade",
    )(*blocks)


def add_core_kernel(pieces, in_ref, out_ref, theirs, send_sem, recv_sem):
    dp, core = (lax.axis_index(DP), lax.axis_index(TENSOR))
    barrier = pltpu.get_barrier_semaphore()
    pl.semaphore_signal(barrier, inc=1, device_id=(dp, 1 - core), device_id_type=MESH)
    pl.semaphore_wait(barrier, 1)
    rows = in_ref.shape[0] // pieces

    def copy(piece):
        at = pl.ds(piece * rows, rows)
        return pltpu.make_async_remote_copy(
            src_ref=in_ref.at[at],
            dst_ref=theirs.at[at],
            send_sem=send_sem.at[piece],
            recv_sem=recv_sem.at[piece],
            device_id=(dp, 1 - core),
            device_id_type=MESH,
        )

    for piece in range(pieces):
        copy(piece).start()
    for piece in range(pieces):
        at = pl.ds(piece * rows, rows)
        copy(piece).wait_recv()
        out_ref[at] = in_ref[at].astype(jnp.float32) + theirs[at].astype(jnp.float32)
    for piece in range(pieces):
        copy(piece).wait_send()


def add_core(number, block):
    pieces = 4
    return pl.pallas_call(
        functools.partial(add_core_kernel, pieces),
        out_shape=jax.ShapeDtypeStruct(block.shape, jnp.float32),
        in_specs=[IN_VMEM],
        out_specs=IN_VMEM,
        scratch_shapes=[
            pltpu.VMEM(block.shape, block.dtype),
            pltpu.SemaphoreType.DMA((pieces,)),
            pltpu.SemaphoreType.DMA((pieces,)),
        ],
        compiler_params=params(number),
        name="add_core",
    )(block)


def total_kernel(in_ref, out_ref, tiles, held, send_sem, recv_sem):
    dp, core = (lax.axis_index(DP), lax.axis_index(TENSOR))
    others = 4 * LAYERS - 1
    barrier = pltpu.get_barrier_semaphore()

    def peer(step):
        return (dp + step) % (4 * LAYERS)

    pl.semaphore_signal(barrier, inc=1, device_id=(dp, 1 - core), device_id_type=MESH)

    @pl.loop(1, others + 1)
    def _(step):
        pl.semaphore_signal(barrier, inc=1, device_id=(peer(step), core), device_id_type=MESH)

    pl.semaphore_wait(barrier, others + 1)
    across = pltpu.make_async_remote_copy(
        src_ref=in_ref,
        dst_ref=tiles.at[0],
        send_sem=send_sem.at[0],
        recv_sem=recv_sem.at[0],
        device_id=(dp, 1 - core),
        device_id_type=MESH,
    )
    across.start()
    across.wait()
    held[...] = in_ref[...] + tiles[0]

    def copy(step):
        return pltpu.make_async_remote_copy(
            src_ref=held,
            dst_ref=tiles.at[step],
            send_sem=send_sem.at[step],
            recv_sem=recv_sem.at[step],
            device_id=(peer(step), core),
            device_id_type=MESH,
        )

    @pl.loop(1, others + 1)
    def _(step):
        copy(step).start()

    @pl.loop(1, others + 1)
    def _(step):
        copy(step).wait()

    total = jnp.zeros_like(held)
    for chip in range(4 * LAYERS):
        step = (dp - chip + 4 * LAYERS) % (4 * LAYERS)
        part = jnp.where(step == 0, held[...], tiles[step])
        total = total + part
    out_ref[...] = total


def total(number, tile):
    return pl.pallas_call(
        total_kernel,
        out_shape=jax.ShapeDtypeStruct(tile.shape, tile.dtype),
        in_specs=[IN_VMEM],
        out_specs=IN_VMEM,
        scratch_shapes=[
            pltpu.VMEM((16,) + tile.shape, tile.dtype),
            pltpu.VMEM(tile.shape, tile.dtype),
            pltpu.SemaphoreType.DMA((16,)),
            pltpu.SemaphoreType.DMA((16,)),
        ],
        compiler_params=params(number),
        name="total",
    )(tile)


def layer_order(step):
    odd = step % 2
    return (1 - odd) * (LAYERS - 1 - step // 2) + odd * (step // 2)


def remote(source, target, send_sem, recv_sem, device):
    return pltpu.make_async_remote_copy(
        src_ref=source,
        dst_ref=target,
        send_sem=send_sem,
        recv_sem=recv_sem,
        device_id=device,
        device_id_type=MESH,
    )


def by_distance(at, step):
    flip = at.z // 2
    inner = at.z * (1 - flip) + (LAYERS - 1 - at.z) * flip
    early = 1 - step // 2
    base = (1 - inner) * step + inner * (early * (1 - step) + (1 - early) * step)
    return (1 - flip) * base + flip * (LAYERS - 1 - base)


def gather_stage(at, out, use, send_sem, recv_sem):
    everyone = 4 * LAYERS

    def send(slot, sem, mate):
        return remote(
            out.at[slot], out.at[slot], send_sem.at[sem], recv_sem.at[slot], (mate, at.core)
        )

    @pl.loop(0, everyone)
    def _(step):
        late = step // 8
        rest = step % 8
        last = rest // 7
        even = 1 - rest % 2
        is_first = (1 - late) * (last + even * ((rest + 6) // 8))
        is_own = (1 - late) * (1 - is_first)
        near = is_own * ((rest + 1) // 2) + is_first * ((rest - 1) // 2)
        layer = by_distance(at, (1 - late) * near + late * (rest // 2))
        column = (
            is_own * at.column
            + is_first * at.first_column
            + late * ((1 - rest % 2) * at.second_column + rest % 2 * at.far_column)
        )
        slot = layer * 4 + column

        @pl.when(slot != at.slot)
        def _():
            send(slot, 0, at.dp).wait_recv()

        @pl.when(is_own == 1)
        def _():
            @pl.when(jnp.logical_and(layer <= at.z, at.has_above))
            def _():
                send(slot, layer, at.dp + 4).start()

            @pl.when(jnp.logical_and(layer >= at.z, at.has_below))
            def _():
                send(slot, 4 + layer, at.dp - 4).start()

            send(slot, 8 + layer, at.first).start()
            send(slot, 12 + layer, at.second).start()

        @pl.when(is_first == 1)
        def _():
            send(slot, 16 + layer, at.second).start()

        use(slot)

    @pl.loop(0, LAYERS)
    def _(layer):
        @pl.when(jnp.logical_and(layer <= at.z, at.has_above))
        def _():
            send(at.slot, layer, at.dp + 4).wait_send()

        @pl.when(jnp.logical_and(layer >= at.z, at.has_below))
        def _():
            send(at.slot, 4 + layer, at.dp - 4).wait_send()

        for group in (8, 12, 16):
            send(at.slot, group + layer, at.first).wait_send()


def reduce_stage(at, blocks, produce, pieces, result, from_second, from_first, from_z, send_sem, recv_sem, meanwhile=None):
    rows = blocks.shape[1] // pieces

    def part(ref, index, piece):
        return ref.at[index, pl.ds(piece * rows, rows)]

    def copy(sem, piece, source, target, mate):
        return remote(
            part(blocks, source, piece),
            part(target[0], target[1], piece),
            send_sem.at[sem, piece],
            recv_sem.at[sem, piece],
            (mate, at.core),
        )

    def to_second(half, layer, piece, slot):
        return copy(4 * half + layer, piece, slot, (from_second, 4 * half + layer), at.second)

    def to_first(layer, piece):
        return copy(
            8 + layer, piece, layer * 4 + at.first_column, (from_first, layer), at.first
        )

    def up(layer, piece):
        return copy(12 + layer, piece, layer * 4 + at.column, (from_z, layer), at.dp + 4)

    def down(layer, piece):
        return copy(16 + layer, piece, layer * 4 + at.column, (from_z, 4 + layer), at.dp - 4)

    def value(ref, index, piece):
        return part(ref, index, piece)[...].astype(jnp.float32)

    @pl.loop(0, 4 * LAYERS)
    def _(step):
        kind = step // LAYERS
        keep, second = (kind // 2, kind % 2)
        column = (1 - second) * ((1 - keep) * at.far_column + keep * at.first_column) + second * (
            (1 - keep) * at.second_column + keep * at.column
        )
        layer = layer_order(step % LAYERS)
        slot = layer * 4 + column
        produce(slot)

        @pl.when(keep == 0)
        def _():
            for piece in range(pieces):
                to_second(second, layer, piece, slot).start()

    if meanwhile is not None:
        meanwhile()

    @pl.loop(0, LAYERS * pieces)
    def _(step):
        layer, piece = (layer_order(step // pieces), step % pieces)
        slot = layer * 4 + at.first_column
        to_second(0, layer, piece, slot).wait_recv()
        part(blocks, slot, piece)[...] = (
            value(blocks, slot, piece) + value(from_second, layer, piece)
        ).astype(blocks.dtype)
        to_first(layer, piece).start()

    @pl.loop(0, LAYERS * pieces)
    def _(step):
        layer, piece = (layer_order(step // pieces), step % pieces)
        slot = layer * 4 + at.column
        to_second(1, layer, piece, slot).wait_recv()
        to_first(layer, piece).wait_recv()
        summed = (
            value(blocks, slot, piece)
            + value(from_second, 4 + layer, piece)
            + value(from_first, layer, piece)
        )

        @pl.when(at.z == layer)
        def _():
            result[pl.ds(piece * rows, rows)] = summed

        @pl.when(at.z < layer)
        def _():
            part(blocks, slot, piece)[...] = summed.astype(blocks.dtype)

            @pl.when(at.has_below)
            def _():
                up(layer, piece).wait_recv()
                part(blocks, slot, piece)[...] = (
                    value(blocks, slot, piece) + value(from_z, layer, piece)
                ).astype(blocks.dtype)

            up(layer, piece).start()

        @pl.when(at.z > layer)
        def _():
            part(blocks, slot, piece)[...] = summed.astype(blocks.dtype)

            @pl.when(at.has_above)
            def _():
                down(layer, piece).wait_recv()
                part(blocks, slot, piece)[...] = (
                    value(blocks, slot, piece) + value(from_z, 4 + layer, piece)
                ).astype(blocks.dtype)

            down(layer, piece).start()

    @pl.loop(0, pieces)
    def _(piece):
        @pl.when(at.has_below)
        def _():
            up(at.z, piece).wait_recv()
            result[pl.ds(piece * rows, rows)] += value(from_z, at.z, piece)

        @pl.when(at.has_above)
        def _():
            down(at.z, piece).wait_recv()
            result[pl.ds(piece * rows, rows)] += value(from_z, 4 + at.z, piece)

    @pl.loop(0, LAYERS * pieces)
    def _(step):
        layer, piece = (step // pieces, step % pieces)
        to_second(0, layer, piece, at.slot).wait_send()
        to_second(1, layer, piece, at.slot).wait_send()
        to_first(layer, piece).wait_send()
        pl.when(at.z < layer)(lambda: up(layer, piece).wait_send())
        pl.when(at.z > layer)(lambda: down(layer, piece).wait_send())


def reduce_scratch(block, pieces):
    kind = jnp.bfloat16
    return [
        pltpu.VMEM((4 * LAYERS,) + block, kind),
        pltpu.VMEM((8,) + block, kind),
        pltpu.VMEM((4,) + block, kind),
        pltpu.VMEM((8,) + block, kind),
        pltpu.SemaphoreType.DMA((20, pieces)),
        pltpu.SemaphoreType.DMA((20, pieces)),
    ]


def gather_scratch():
    return [pltpu.SemaphoreType.DMA((20,)), pltpu.SemaphoreType.DMA((16,))]


def mean_of_groups(sums, count):
    size = C // GROUPS
    channels = sums.shape[-1]
    row = lax.broadcasted_iota(jnp.int32, (channels, channels), 0) // size
    column = lax.broadcasted_iota(jnp.int32, (channels, channels), 1) // size
    same = jnp.where(row == column, 1.0 / (count * size), 0.0)
    return jnp.dot(sums, same, precision=HIGHEST, preferred_element_type=jnp.float32)


def side_by_side(maps, breadth, turned=False):
    positions = maps.shape[0]
    column = lax.broadcasted_iota(jnp.int32, maps.shape, 0) % breadth
    before = jnp.where(column == 0, 0.0, pltpu.roll(maps, 1, 0))
    after = jnp.where(column == breadth - 1, 0.0, pltpu.roll(maps, positions - 1, 0))
    three = (after, maps, before) if turned else (before, maps, after)
    return jnp.concatenate(three, axis=1)


def fold_three(products, breadth, turned=False):
    positions = products.shape[0]
    channels = products.shape[1] // 3
    left, middle, right = (products[:, tap * channels : (tap + 1) * channels] for tap in range(3))
    if turned:
        left, right = (right, left)
    column = lax.broadcasted_iota(jnp.int32, middle.shape, 0) % breadth
    before = jnp.where(column == 0, 0.0, pltpu.roll(left, 1, 0))
    after = jnp.where(column == breadth - 1, 0.0, pltpu.roll(right, positions - 1, 0))
    return before + middle + after


def fold_rows(above, same, below, breadth):
    edge = jnp.zeros((breadth, same.shape[1]), jnp.float32)
    count = same.shape[0] - breadth
    down = jnp.concatenate([edge, above[:count]], axis=0)
    up = jnp.concatenate([below[breadth:], edge], axis=0)
    return down + same + up


def silu(z):
    return z * jax.nn.sigmoid(z)


def store_padded(ref, index, maps, breadth):
    positions = maps.shape[0]
    edge = jnp.zeros((breadth, maps.shape[1]), ref.dtype)
    ref[index, pl.ds(0, breadth)] = edge
    ref[index, pl.ds(breadth, positions)] = maps.astype(ref.dtype)
    ref[index, pl.ds(breadth + positions, breadth)] = edge


def res_forward_kernel(
    breadth,
    pictures,
    gain_bias,
    conv_one,
    conv_two,
    conv_half,
    mods,
    picks,
    tokens,
    act_out,
    taps_one_out,
    taps_half,
    middle,
    stats,
    acts,
    taps_one,
    mine,
    theirs,
    pair_send,
    pair_recv,
    share_send,
    share_recv,
    out_sem,
    *scratch,
):
    first_reduce, (act_send, act_recv), last_reduce = (scratch[:6], scratch[6:8], scratch[8:])
    at = Place(True)
    at.greet(True)
    images, positions, channels = pictures.shape
    tokens_len = positions // 4

    @pl.loop(0, images)
    def _(i):
        x = pictures[i].astype(jnp.float32)
        stats[0, pl.ds(i, 1)] = jnp.sum(x, axis=0, keepdims=True)

    stats[0] = mean_of_groups(stats[0], positions)

    @pl.loop(0, images)
    def _(i):
        x = pictures[i].astype(jnp.float32) - stats[0, pl.ds(i, 1)]
        stats[1, pl.ds(i, 1)] = jnp.sum(x * x, axis=0, keepdims=True)

    stats[1] = lax.rsqrt(mean_of_groups(stats[1], positions) + GN_EPS)

    @pl.loop(0, images)
    def _(i):
        normed = (pictures[i].astype(jnp.float32) - stats[0, pl.ds(i, 1)]) * stats[1, pl.ds(i, 1)]
        act = silu(normed * gain_bias[0:1] + gain_bias[1:2])
        store_padded(taps_one, i, side_by_side(act, breadth), breadth)

    save_taps = pltpu.make_async_copy(taps_one, taps_one_out, out_sem.at[0])
    save_taps.start()

    def first_product(slot):
        total = jnp.zeros((positions, conv_one.shape[2]), jnp.float32)
        for a in range(3):
            total += dot(taps_one[slot, pl.ds(a * breadth, positions)], conv_one[a])
        first_reduce[0][slot] = total.astype(jnp.bfloat16)

    reduce_stage(at, first_reduce[0], first_product, 2, middle, *first_reduce[1:])

    x = middle[...]
    center = mean_of_groups(jnp.sum(x, axis=0, keepdims=True), positions)
    x = x - center
    scale = lax.rsqrt(mean_of_groups(jnp.sum(x * x, axis=0, keepdims=True), positions) + GN_EPS)
    acts[at.slot] = silu(x * scale * (1.0 + mods[0:1]) + mods[1:2]).astype(jnp.bfloat16)

    def swap(slot):
        return remote(
            mine.at[slot],
            theirs.at[slot],
            pair_send.at[slot],
            pair_recv.at[slot],
            (at.dp, 1 - at.core),
        )

    def second_product(slot):
        act = acts[slot]
        above, same, below = (dot(act, conv_two[a]) for a in range(3))
        folded = fold_three(fold_rows(above, same, below, breadth), breadth)
        mine[slot] = folded.astype(jnp.bfloat16)
        swap(slot).start()

    gather_stage(at, acts, second_product, act_send, act_recv)
    save_acts = pltpu.make_async_copy(acts, act_out, out_sem.at[1])
    save_acts.start()

    def half_product(slot):
        swap(slot).wait_recv()
        branch = mine[slot].astype(jnp.float32) + theirs[slot].astype(jnp.float32)
        resid = (pictures[slot].astype(jnp.float32) + branch).astype(jnp.bfloat16)
        three = side_by_side(resid.astype(jnp.float32), breadth).astype(jnp.bfloat16)
        picked = dot(picks[...], three).astype(jnp.bfloat16)
        total = jnp.zeros((tokens_len, conv_half.shape[2]), jnp.float32)
        for a in range(3):
            part = picked[a * tokens_len : (a + 1) * tokens_len]
            taps_half[a, slot] = part
            total += dot(part, conv_half[a])
        last_reduce[0][slot] = total.astype(jnp.bfloat16)

    own = tokens.at[at.core]
    reduce_stage(at, last_reduce[0], half_product, 1, own, *last_reduce[1:])

    def give(core):
        return remote(own, tokens.at[core], share_send, share_recv, (at.dp, 1 - at.core))

    give(at.core).start()
    give(1 - at.core).wait_recv()
    give(at.core).wait_send()

    @pl.loop(0, images)
    def _(slot):
        swap(slot).wait_send()

    save_taps.wait()
    save_acts.wait()


def res_forward(number, breadth, pictures, gain_bias, conv_one, conv_two, conv_half, mods, picks):
    images, positions, channels = pictures.shape
    half_c = conv_one.shape[2]
    half_d = conv_half.shape[2]
    tokens_len = positions // 4
    three = 3 * channels
    padded = (images, positions + 2 * breadth, three)
    low = jnp.bfloat16
    acts = (images, positions, half_c)
    return pl.pallas_call(
        functools.partial(res_forward_kernel, breadth),
        out_shape=[
            jax.ShapeDtypeStruct((2, tokens_len, half_d), jnp.float32),
            jax.ShapeDtypeStruct(acts, low),
            jax.ShapeDtypeStruct(padded, low),
            jax.ShapeDtypeStruct((3, images, tokens_len, three), low),
            jax.ShapeDtypeStruct((positions, half_c), jnp.float32),
            jax.ShapeDtypeStruct((2, images, channels), jnp.float32),
        ],
        in_specs=[IN_VMEM] * 7,
        out_specs=[IN_VMEM, ANYWHERE, ANYWHERE, IN_VMEM, IN_VMEM, IN_VMEM],
        scratch_shapes=[
            pltpu.VMEM(acts, low),
            pltpu.VMEM(padded, low),
            pltpu.VMEM(pictures.shape, low),
            pltpu.VMEM(pictures.shape, low),
            pltpu.SemaphoreType.DMA((images,)),
            pltpu.SemaphoreType.DMA((images,)),
            pltpu.SemaphoreType.DMA,
            pltpu.SemaphoreType.DMA,
            pltpu.SemaphoreType.DMA((2,)),
        ]
        + reduce_scratch((positions, half_c), 2)
        + gather_scratch()
        + reduce_scratch((tokens_len, half_d), 1),
        compiler_params=params(number),
        name="res_forward",
    )(pictures, gain_bias, conv_one, conv_two, conv_half, mods, picks)


def silu_slope(z):
    gate = jax.nn.sigmoid(z)
    return gate * (1.0 + z * (1.0 - gate))


def res_backward_kernel(
    breadth,
    shrunk,
    pictures,
    gain_bias,
    conv_one,
    conv_two,
    conv_half,
    mods,
    picks,
    taps_half,
    middle,
    stats,
    acts_in,
    taps_one_in,
    pictures_out,
    norm_out,
    mods_out,
    one_out,
    two_out,
    half_out,
    gathered,
    gathered_middle,
    acts,
    taps_one,
    taps_two,
    mine,
    theirs,
    back,
    back_theirs,
    held,
    sums,
    outgoing,
    acted,
    one_grad,
    two_grad,
    half_grad,
    pair_send,
    pair_recv,
    back_send,
    back_recv,
    trade_send,
    trade_recv,
    io_sem,
    *scratch,
):
    (shrunk_send, shrunk_recv), (middle_send, middle_recv) = (scratch[:2], scratch[2:4])
    reducing = scratch[4:]
    at = Place(True)
    images, positions, channels = pictures.shape
    others = images - 1
    tokens_len = positions // 4
    load_acts = pltpu.make_async_copy(acts_in, acts, io_sem.at[0])
    load_taps = pltpu.make_async_copy(taps_one_in, taps_one, io_sem.at[1])
    load_acts.start()
    load_taps.start()
    gathered[at.slot] = shrunk[...]

    barrier = pltpu.get_barrier_semaphore()

    def peer(step):
        return (at.dp + step) % images

    @pl.loop(1, others + 1)
    def _(step):
        pl.semaphore_signal(barrier, inc=1, device_id=(peer(step), at.core), device_id_type=MESH)

    pl.semaphore_signal(barrier, inc=1, device_id=(at.dp, 1 - at.core), device_id_type=MESH)
    pl.semaphore_wait(barrier, others + 1)

    def swap(slot):
        return remote(
            mine.at[slot],
            theirs.at[slot],
            pair_send.at[slot],
            pair_recv.at[slot],
            (at.dp, 1 - at.core),
        )

    def half_back(slot):
        products = [dot_nt(gathered[slot], conv_half[a]) for a in range(3)]
        products = jnp.concatenate(products, axis=0)
        coarse = products.astype(jnp.bfloat16)
        fine = (products - coarse.astype(jnp.float32)).astype(jnp.bfloat16)
        spread = dot_tn(picks[...], coarse) + dot_tn(picks[...], fine)
        mine[slot] = fold_three(spread, breadth, True).astype(jnp.bfloat16)
        swap(slot).start()

    gather_stage(at, gathered, half_back, shrunk_send, shrunk_recv)

    def resid(slot):
        return mine[slot].astype(jnp.float32) + theirs[slot].astype(jnp.float32)

    def second_back(slot):
        swap(slot).wait_recv()
        branch = resid(slot).astype(jnp.bfloat16).astype(jnp.float32)
        store_padded(taps_two, slot, side_by_side(branch, breadth, True), breadth)
        total = jnp.zeros((positions, conv_two.shape[1]), jnp.float32)
        for a in range(3):
            total += dot_nt(taps_two[slot, pl.ds((2 - a) * breadth, positions)], conv_two[a])
        reducing[0][slot] = total.astype(jnp.bfloat16)

    def weights_meanwhile():
        half_grad[...] = jnp.zeros_like(half_grad)
        two_grad[...] = jnp.zeros_like(two_grad)
        load_acts.wait()

        @pl.loop(0, images // 4)
        def _(i):
            right = gathered[pl.ds(4 * i, 4)].reshape(4 * tokens_len, -1)
            for a in range(3):
                left = taps_half[a, pl.ds(4 * i, 4)].reshape(4 * tokens_len, 3 * channels)
                half_grad[a] += dot_tn(left, right)

        @pl.loop(0, images)
        def _(i):
            right = acts[i]
            for a in range(3):
                left = taps_two[i, pl.ds((2 - a) * breadth, positions)]
                two_grad[a] += dot_tn(left, right)

        save(half_grad, half_out, 2).start()
        save(two_grad, two_out, 3).start()

    def save(source, target, sem):
        return pltpu.make_async_copy(source, target, io_sem.at[sem])

    reduce_stage(at, reducing[0], second_back, 2, acted, *reducing[1:], weights_meanwhile)

    x = middle[...]
    center = mean_of_groups(jnp.sum(x, axis=0, keepdims=True), positions)
    x = x - center
    scale = lax.rsqrt(mean_of_groups(jnp.sum(x * x, axis=0, keepdims=True), positions) + GN_EPS)
    normed = x * scale
    slope = 1.0 + mods[0:1]
    grad = acted[...] * silu_slope(normed * slope + mods[1:2])
    along = jnp.sum(grad * normed, axis=0, keepdims=True)
    level = jnp.sum(grad, axis=0, keepdims=True)
    mods_out[0:1] = along
    mods_out[1:2] = level
    along = mean_of_groups(slope * along, positions)
    level = mean_of_groups(slope * level, positions)
    gathered_middle[at.slot] = ((slope * grad - level - normed * along) * scale).astype(jnp.bfloat16)

    def swap_back(slot):
        return remote(
            back.at[slot],
            back_theirs.at[slot],
            back_send.at[slot],
            back_recv.at[slot],
            (at.dp, 1 - at.core),
        )

    def first_back(slot):
        below, same, above = (dot_nt(gathered_middle[slot], conv_one[a]) for a in range(3))
        folded = fold_three(fold_rows(above, same, below, breadth), breadth, True)
        back[slot] = folded.astype(jnp.bfloat16)
        swap_back(slot).start()

    gather_stage(at, gathered_middle, first_back, middle_send, middle_recv)

    gain, bias = (gain_bias[0:1], gain_bias[1:2])

    def normed_of(i):
        return (pictures[i].astype(jnp.float32) - stats[0, pl.ds(i, 1)]) * stats[1, pl.ds(i, 1)]

    @pl.loop(0, images)
    def _(i):
        swap_back(i).wait_recv()
        grad = back[i].astype(jnp.float32) + back_theirs[i].astype(jnp.float32)
        normed = normed_of(i)
        grad = grad * silu_slope(normed * gain + bias)
        held[i] = grad
        sums[0, pl.ds(i, 1)] = jnp.sum(grad * normed, axis=0, keepdims=True)
        sums[1, pl.ds(i, 1)] = jnp.sum(grad, axis=0, keepdims=True)

    norm_out[0:1] = jnp.sum(sums[0], axis=0, keepdims=True)
    norm_out[1:2] = jnp.sum(sums[1], axis=0, keepdims=True)
    sums[0] = mean_of_groups(gain * sums[0], positions)
    sums[1] = mean_of_groups(gain * sums[1], positions)

    def deliver(step):
        return remote(
            outgoing.at[peer(step)],
            pictures_out.at[at.dp],
            trade_send.at[step - 1],
            trade_recv.at[step - 1],
            (peer(step), at.core),
        )

    keep = save(outgoing.at[at.dp], pictures_out.at[at.dp], 5)

    @pl.loop(0, images)
    def _(step):
        i = peer(step)
        part = gain * held[i] - sums[1, pl.ds(i, 1)] - normed_of(i) * sums[0, pl.ds(i, 1)]
        part = resid(i) + part * stats[1, pl.ds(i, 1)]
        half = positions // 2
        outgoing[i] = jnp.concatenate([part[:half], part[half:]], axis=1).astype(jnp.bfloat16)
        pl.when(step == 0)(keep.start)
        pl.when(step > 0)(lambda: deliver(step).start())

    one_grad[...] = jnp.zeros_like(one_grad)
    load_taps.wait()

    @pl.loop(0, images)
    def _(i):
        right = gathered_middle[i]
        for a in range(3):
            one_grad[a] += dot_tn(taps_one[i, pl.ds(a * breadth, positions)], right)

    save(one_grad, one_out, 4).start()

    @pl.loop(0, images)
    def _(slot):
        swap(slot).wait_send()
        swap_back(slot).wait_send()

    keep.wait()

    @pl.loop(1, others + 1)
    def _(step):
        deliver(step).wait()

    save(half_grad, half_out, 2).wait()
    save(two_grad, two_out, 3).wait()
    save(one_grad, one_out, 4).wait()


def res_backward(number, breadth, *args):
    (shrunk, pictures, gain_bias, conv_one, conv_two, conv_half, mods, picks, taps_half, middle, stats, acts, taps_one) = args
    images, positions, channels = pictures.shape
    half_c = conv_one.shape[2]
    half_d = conv_half.shape[2]
    tokens_len = positions // 4
    three = 3 * channels
    low, full = (jnp.bfloat16, jnp.float32)
    grads = [(3, three, half_c), (3, three, half_c), (3, three, half_d)]
    traded = (images, positions // 2, 2 * channels)
    return pl.pallas_call(
        functools.partial(res_backward_kernel, breadth),
        out_shape=[
            jax.ShapeDtypeStruct(traded, low),
            jax.ShapeDtypeStruct((2, channels), full),
            jax.ShapeDtypeStruct((2, half_c), full),
        ]
        + [jax.ShapeDtypeStruct(shape, full) for shape in grads],
        in_specs=[IN_VMEM] * 11 + [ANYWHERE] * 2,
        out_specs=[ANYWHERE, IN_VMEM, IN_VMEM] + [ANYWHERE] * 3,
        scratch_shapes=[
            pltpu.VMEM((images, tokens_len, half_d), low),
            pltpu.VMEM((images, positions, half_c), low),
            pltpu.VMEM(acts.shape, low),
            pltpu.VMEM(taps_one.shape, low),
            pltpu.VMEM(taps_one.shape, low),
            pltpu.VMEM(pictures.shape, low),
            pltpu.VMEM(pictures.shape, low),
            pltpu.VMEM(pictures.shape, low),
            pltpu.VMEM(pictures.shape, low),
            pltpu.VMEM(pictures.shape, full),
            pltpu.VMEM((2, images, channels), full),
            pltpu.VMEM(traded, low),
            pltpu.VMEM((positions, half_c), full),
        ]
        + [pltpu.VMEM(shape, full) for shape in grads]
        + [pltpu.SemaphoreType.DMA((images,))] * 4
        + [pltpu.SemaphoreType.DMA((images - 1,))] * 2
        + [pltpu.SemaphoreType.DMA((6,))]
        + gather_scratch()
        + gather_scratch()
        + reduce_scratch((positions, half_c), 2),
        compiler_params=params(number),
        name="res_backward",
    )(*args)


def widen(block):
    return block.astype(jnp.float32)


def lower(block):
    return block.astype(jnp.bfloat16)


def paired_lanes(block):
    half = block.shape[-2] // 2
    return jnp.concatenate([block[..., :half, :], block[..., half:, :]], axis=-1)


def unpaired_lanes(block):
    half = block.shape[-1] // 2
    return jnp.concatenate([block[..., :half], block[..., half:]], axis=-2)


def trade_dp(blocks):
    return lax.all_to_all(blocks, DP, 0, 0)


def core_rows(block, tensor_pos):
    half = block.shape[0] // 2
    return lax.dynamic_slice_in_dim(block, tensor_pos * half, half, axis=0)


def layer_stats(values):
    center = jnp.mean(values, axis=-1, keepdims=True)
    shifted = values - center
    spread = jnp.mean(shifted * shifted, axis=-1, keepdims=True)
    scale = lax.rsqrt(spread + LN_EPS)
    return shifted * scale, scale


def layer_back(normed, scale, grad):
    first = jnp.mean(grad, axis=-1, keepdims=True)
    second = jnp.mean(grad * normed, axis=-1, keepdims=True)
    return (grad - first - normed * second) * scale


def half_picks(height, breadth):
    outputs = height * breadth // 4
    tap, out = (jnp.arange(3 * outputs) // outputs, jnp.arange(3 * outputs) % outputs)
    row = 2 * (out // (breadth // 2)) + tap - 1
    source = row * breadth + 2 * (out % (breadth // 2))
    place = jnp.arange(height * breadth)
    return ((place[None, :] == source[:, None]) & (row[:, None] >= 0)).astype(jnp.bfloat16)


def dot(left, right):
    return jnp.dot(left, right, preferred_element_type=jnp.float32)


def dot_tn(left, right):
    return lax.dot_general(left, right, (((0,), (0,)), ((), ())), preferred_element_type=jnp.float32)


def dot_nt(left, right):
    return lax.dot_general(left, right, (((1,), (1,)), ((), ())), preferred_element_type=jnp.float32)


def stationary(
    images,
    t_index,
    cotangent,
    norm_params,
    norm_params_avg,
    norm_params_sq,
    first_conv,
    first_conv_avg,
    first_conv_sq,
    resnet_mod,
    resnet_mod_avg,
    resnet_mod_sq,
    second_conv,
    second_kernel_first_moment,
    second_conv_sq,
    down_conv,
    down_conv_avg,
    down_conv_sq,
    ada_proj,
    ada_proj_avg,
    ada_proj_sq,
    qkv_proj,
    qkv_proj_avg,
    qkv_proj_sq,
    out_proj,
    out_proj_avg,
    out_proj_sq,
    hidden_in,
    hidden_in_avg,
    hidden_in_sq,
    hidden_out,
    hidden_out_avg,
    hidden_out_sq,
):
    masters = (
        norm_params,
        first_conv,
        resnet_mod,
        second_conv,
        down_conv,
        ada_proj,
        qkv_proj,
        out_proj,
        hidden_in,
        hidden_out,
    )
    averages = (
        norm_params_avg,
        first_conv_avg,
        resnet_mod_avg,
        second_kernel_first_moment,
        down_conv_avg,
        ada_proj_avg,
        qkv_proj_avg,
        out_proj_avg,
        hidden_in_avg,
        hidden_out_avg,
    )
    squares = (
        norm_params_sq,
        first_conv_sq,
        resnet_mod_sq,
        second_conv_sq,
        down_conv_sq,
        ada_proj_sq,
        qkv_proj_sq,
        out_proj_sq,
        hidden_in_sq,
        hidden_out_sq,
    )
    n_dp = lax.axis_size(DP)
    dp_pos = lax.axis_index(DP)
    tensor_pos = lax.axis_index(TENSOR)
    height, breadth = (images.shape[1], images.shape[2])
    positions = height * breadth
    tokens_len = positions // 4
    local_c = C // n_dp
    half_c = first_conv.shape[3]
    half_d = down_conv.shape[3]
    freq_rows = resnet_mod.shape[0]
    heads_here = out_proj.shape[0]
    hidden_cols = hidden_in.shape[1] // n_dp
    score_scale = HDIM ** (-0.5)
    as_maps = (n_dp, height, breadth, local_c)
    picks = half_picks(height, breadth)
    numbers = itertools.count()

    def gather_tokens(block, wide):
        gathered = gather(next(numbers), core_rows(block, tensor_pos), wide, True)
        return gathered.reshape(-1, D)

    def reduce_tokens(partial, wide):
        blocks = lower(partial).reshape(-1, 2, tokens_len // 2, D)
        return reduce(next(numbers), blocks, wide, True, True).reshape(tokens_len, D)

    def sum_cores(maps):
        return add_core(next(numbers), lower(maps).reshape(-1, local_c)).reshape(as_maps)

    def sum_all(local):
        return total(next(numbers), jnp.full((8, 128), local))[0, 0]

    gain_bias = widen(lower(norm_params))
    conv_one = lower(first_conv).reshape(3, 3 * local_c, half_c)
    conv_two = lower(second_conv).transpose(0, 2, 1, 3).reshape(3, half_c, 3 * local_c)
    conv_half = lower(down_conv).reshape(3, 3 * local_c, half_d)
    qkv_blocks = jnp.repeat(lower(qkv_proj).transpose(2, 0, 1, 3), n_dp // heads_here, axis=0)
    qkv_head = trade_dp(qkv_blocks).reshape(D, 3 * HDIM)
    out_blocks = jnp.repeat(lower(out_proj), n_dp // heads_here, axis=0)
    out_head = trade_dp(out_blocks).transpose(1, 0, 2).reshape(HDIM, D)
    up_blocks = lower(hidden_in).reshape(D // n_dp, n_dp, hidden_cols).transpose(1, 0, 2)
    up_here = trade_dp(up_blocks).reshape(D, hidden_cols)
    down_blocks = lower(hidden_out).reshape(n_dp, hidden_cols, D // n_dp)
    down_here = trade_dp(down_blocks).transpose(1, 0, 2).reshape(hidden_cols, D)

    emb = embed_noise(t_index, FREQ).reshape(FREQ // 128, 128)
    emb = jnp.broadcast_to(jnp.pad(emb, ((0, 8 - FREQ // 128), (0, 0))), (n_dp, 8, 128))
    image_blocks = images.reshape(positions, n_dp, local_c).transpose(1, 0, 2)
    pictures, emb = trade(next(numbers), paired_lanes(image_blocks), emb)
    pictures = unpaired_lanes(pictures)

    emb_low = lower(emb[:, : FREQ // 128].reshape(n_dp, FREQ))
    emb_rows = lax.dynamic_slice_in_dim(emb_low, dp_pos * freq_rows, freq_rows, axis=1)
    res_partial = dot(emb_rows, lower(resnet_mod).reshape(freq_rows, 2 * half_c))
    ada_partial = dot(emb_rows, lower(ada_proj).reshape(freq_rows, 6 * D))
    ada_partial = lax.dynamic_slice_in_dim(ada_partial, tensor_pos * 3 * D, 3 * D, axis=1)
    mods = jnp.concatenate([res_partial, ada_partial], axis=1).reshape(n_dp, -1, 128)
    mods = reduce(next(numbers), mods, True, False, True).reshape(2, -1)
    res_mods = lax.dynamic_index_in_dim(mods, tensor_pos, 0, keepdims=False)[: 2 * half_c]
    res_mods = res_mods.reshape(2, half_c)
    ada_mods = mods[:, 2 * half_c :].reshape(6, D)
    shift_one, scale_one, gate_one = (ada_mods[0], 1.0 + ada_mods[1], 1.0 + ada_mods[2])
    shift_two, scale_two, gate_two = (ada_mods[3], 1.0 + ada_mods[4], 1.0 + ada_mods[5])
    upstream = widen(cotangent).reshape(tokens_len, D)
    grad_expanded = gather_tokens(lower(gate_two * upstream), True)

    shrunk, act_two, taps_one, taps_half, middle, stats_one = res_forward(
        next(numbers), breadth, pictures, gain_bias, conv_one, conv_two, conv_half, res_mods, picks
    )
    tokens = jnp.concatenate([shrunk[0], shrunk[1]], axis=1)

    token_normed, token_spread = layer_stats(tokens)
    attn_in = gather_tokens(lower(token_normed * scale_one + shift_one), False)
    near = n_dp // 2
    qkv_low = lower(dot(attn_in, qkv_head)).reshape(near, tokens_len, 3, HDIM)
    query_low, key_low, value_low = (qkv_low[:, :, 0], qkv_low[:, :, 1], qkv_low[:, :, 2])
    scores = (
        jnp.einsum("bqd,bkd->bqk", query_low, key_low, preferred_element_type=jnp.float32) * score_scale
    )
    row_max = jnp.max(scores, axis=-1, keepdims=True)
    log_total = row_max + jnp.log(jnp.sum(jnp.exp(scores - row_max), axis=-1, keepdims=True))
    attention = jnp.exp(scores - log_total)
    attention_low = lower(attention)
    mixed = lower(
        jnp.einsum("bqk,bkd->bqd", attention_low, value_low, preferred_element_type=jnp.float32)
    ).reshape(near * tokens_len, HDIM)
    attended = reduce_tokens(dot(mixed, out_head), False)
    after_attn = tokens + gate_one * attended
    after_normed, after_spread = layer_stats(after_attn)
    mlp_in = gather_tokens(lower(after_normed * scale_two + shift_two), True)
    pre_act = dot(mlp_in, up_here)
    hidden_act, gelu_back = jax.vjp(gelu_tanh, pre_act)
    hidden_low = lower(hidden_act)
    expanded = reduce_tokens(dot(hidden_low, down_here), True)
    block_out = lower(after_attn + gate_two * expanded)

    grad_gate_two = jnp.sum(upstream * expanded, axis=0)
    grad_down = dot_tn(hidden_low, grad_expanded)
    (grad_pre,) = gelu_back(dot_nt(grad_expanded, down_here))
    grad_pre_low = lower(grad_pre)
    grad_mlp_in = reduce_tokens(dot_nt(grad_pre_low, up_here), True)
    grad_up = dot_tn(mlp_in, grad_pre_low)
    grad_after = upstream + layer_back(after_normed, after_spread, scale_two * grad_mlp_in)
    grad_attended = gather_tokens(lower(gate_one * grad_after), False)
    grad_out = dot_tn(mixed, grad_attended)
    grad_mixed = lower(dot_nt(grad_attended, out_head)).reshape(near, tokens_len, HDIM)
    grad_probs = jnp.einsum(
        "bqd,bkd->bqk", grad_mixed, value_low, preferred_element_type=jnp.float32
    )
    grad_values = jnp.einsum(
        "bqk,bqd->bkd", attention_low, grad_mixed, preferred_element_type=jnp.float32
    )
    grad_scores = lower(
        attention * (grad_probs - jnp.sum(grad_probs * attention, axis=-1, keepdims=True))
    )
    grad_query = (
        jnp.einsum("bqk,bkd->bqd", grad_scores, key_low, preferred_element_type=jnp.float32)
        * score_scale
    )
    grad_keys = (
        jnp.einsum("bqk,bqd->bkd", grad_scores, query_low, preferred_element_type=jnp.float32)
        * score_scale
    )
    grad_qkv = lower(jnp.concatenate([grad_query, grad_keys, grad_values], axis=2)).reshape(
        near * tokens_len, 3 * HDIM
    )
    grad_attn_in = reduce_tokens(dot_nt(grad_qkv, qkv_head), False)
    grad_qkv_w = dot_tn(attn_in, grad_qkv)
    grad_tokens = grad_after + layer_back(token_normed, token_spread, scale_one * grad_attn_in)

    grad_shrunk = lower(lax.dynamic_slice_in_dim(grad_tokens, tensor_pos * half_d, half_d, axis=1))
    images_grad, grad_norm_params, grad_res_mods, grad_conv_one, grad_conv_two, grad_half = res_backward(
        next(numbers),
        breadth,
        grad_shrunk,
        pictures,
        gain_bias,
        conv_one,
        conv_two,
        conv_half,
        res_mods,
        picks,
        taps_half,
        middle,
        stats_one,
        act_two,
        taps_one,
    )
    images_grad = widen(unpaired_lanes(images_grad))
    images_grad = images_grad.transpose(1, 0, 2).reshape((1, height, breadth, C))

    grad_ada = jnp.concatenate(
        [
            jnp.sum(grad_attn_in, axis=0),
            jnp.sum(grad_attn_in * token_normed, axis=0),
            jnp.sum(grad_after * attended, axis=0),
            jnp.sum(grad_mlp_in, axis=0),
            jnp.sum(grad_mlp_in * after_normed, axis=0),
            grad_gate_two,
        ]
    )
    grad_ada = lax.dynamic_slice_in_dim(grad_ada, tensor_pos * 3 * D, 3 * D, axis=0)
    grad_mods = jnp.concatenate([grad_res_mods.reshape(-1), grad_ada]).reshape(-1, 128)
    grad_mods = gather(next(numbers), grad_mods, True, True).reshape(n_dp, 2, -1)
    grad_ada = grad_mods[:, :, 2 * half_c :].reshape(n_dp, 6 * D)
    grad_mods = lax.dynamic_index_in_dim(grad_mods, tensor_pos, 1, keepdims=False)
    emb_cols = widen(emb_rows)
    grad_ada = jnp.einsum("bf,bk->fk", emb_cols, grad_ada, precision=HIGHEST)
    grad_res = jnp.einsum("bf,bk->fk", emb_cols, grad_mods[:, : 2 * half_c], precision=HIGHEST)

    grad_qkv_w = trade_dp(lower(grad_qkv_w).reshape(n_dp, D // n_dp, 3, HDIM))
    grad_qkv_w = jnp.sum(
        widen(grad_qkv_w).reshape((heads_here, n_dp // heads_here) + grad_qkv_w.shape[1:]), axis=1
    ).transpose(1, 2, 0, 3)
    grad_out = trade_dp(lower(grad_out).reshape(HDIM, n_dp, D // n_dp).transpose(1, 0, 2))
    grad_out = jnp.sum(
        widen(grad_out).reshape((heads_here, n_dp // heads_here) + grad_out.shape[1:]), axis=1
    )
    grad_up = widen(trade_dp(lower(grad_up).reshape(n_dp, D // n_dp, hidden_cols)))
    grad_up = grad_up.transpose(1, 0, 2).reshape(hidden_in.shape)
    grad_down = trade_dp(lower(grad_down).reshape(hidden_cols, n_dp, D // n_dp).transpose(1, 0, 2))
    grad_down = widen(grad_down).reshape(hidden_out.shape)

    combined_total = (
        grad_norm_params,
        grad_conv_one.reshape(first_conv.shape),
        grad_res.reshape(resnet_mod.shape),
        grad_conv_two.reshape(3, 3, local_c, half_c).transpose(0, 1, 3, 2),
        grad_half.reshape(down_conv.shape),
        grad_ada.reshape(ada_proj.shape),
        grad_qkv_w,
        grad_out,
        grad_up,
        grad_down,
    )
    results = clipped_step(masters, averages, squares, combined_total, sum_all)
    return (block_out[None], images_grad) + results


def solution(mesh):
    in_specs = (
        P(DP, None, None, None),
        P(DP),
        P(DP, None, None),
        P(None, DP),
        P(None, DP),
        P(None, DP),
        P(None, None, DP, TENSOR),
        P(None, None, DP, TENSOR),
        P(None, None, DP, TENSOR),
        P(DP, None, TENSOR),
        P(DP, None, TENSOR),
        P(DP, None, TENSOR),
        P(None, None, TENSOR, DP),
        P(None, None, TENSOR, DP),
        P(None, None, TENSOR, DP),
        P(None, None, DP, TENSOR),
        P(None, None, DP, TENSOR),
        P(None, None, DP, TENSOR),
        P(DP, None, None),
        P(DP, None, None),
        P(DP, None, None),
        P(DP, None, TENSOR, None),
        P(DP, None, TENSOR, None),
        P(DP, None, TENSOR, None),
        P(TENSOR, None, DP),
        P(TENSOR, None, DP),
        P(TENSOR, None, DP),
        P(DP, TENSOR),
        P(DP, TENSOR),
        P(DP, TENSOR),
        P(TENSOR, DP),
        P(TENSOR, DP),
        P(TENSOR, DP),
    )
    out_specs = (
        P(DP, None, None),
        P(DP, None, None, None),
        P(),
        P(None, DP),
        P(None, DP),
        P(None, DP),
        P(None, None, DP, TENSOR),
        P(None, None, DP, TENSOR),
        P(None, None, DP, TENSOR),
        P(DP, None, TENSOR),
        P(DP, None, TENSOR),
        P(DP, None, TENSOR),
        P(None, None, TENSOR, DP),
        P(None, None, TENSOR, DP),
        P(None, None, TENSOR, DP),
        P(None, None, DP, TENSOR),
        P(None, None, DP, TENSOR),
        P(None, None, DP, TENSOR),
        P(DP, None, None),
        P(DP, None, None),
        P(DP, None, None),
        P(DP, None, TENSOR, None),
        P(DP, None, TENSOR, None),
        P(DP, None, TENSOR, None),
        P(TENSOR, None, DP),
        P(TENSOR, None, DP),
        P(TENSOR, None, DP),
        P(DP, TENSOR),
        P(DP, TENSOR),
        P(DP, TENSOR),
        P(TENSOR, DP),
        P(TENSOR, DP),
        P(TENSOR, DP),
    )
    moves_activations = mesh.shape[DP] == 4 * LAYERS and mesh.shape[TENSOR] == 2
    return jax.shard_map(
        stationary if moves_activations else per_device, mesh=mesh, in_specs=in_specs, out_specs=out_specs, check_vma=False
    )
```

```python
import functools
import itertools
import math

import jax
import jax.numpy as jnp
from jax import lax
from jax.experimental import pallas as pl
from jax.experimental.pallas import tpu as pltpu
from jax.sharding import PartitionSpec as P

DP, TENSOR = ("dp", "tensor")
C = 1024
D = 2048
HEADS = 16
HDIM = 128
FF = 8192
GROUPS = 32
FREQ = 256
STEP = 5


GN_EPS = 1e-05
LN_EPS = 1e-06
CLIP = 1.0
BETA_ONE = 0.5
BETA_TWO = 0.5
ADAM_EPS = 1e-08
DECAY = 0.1
LR_SCALE = 2.0
LR_NORM = 0.5
PLAN = 1000.0
HIGHEST = lax.Precision.HIGHEST


def embed_noise(t_index, emb_width):
    fraction = (t_index.astype(jnp.float32) + 0.5) / PLAN
    logsnr = -2.0 * jnp.log(jnp.tan(0.5 * math.pi * fraction)) + 2.0 * math.log(64.0 / 512.0)
    half_width = emb_width // 2
    frequencies = jnp.exp(
        -math.log(10000.0) * jnp.arange(half_width, dtype=jnp.float32) / half_width
    )
    angles = logsnr[:, None] * frequencies[None, :]
    return jnp.concatenate([jnp.sin(angles), jnp.cos(angles)], axis=1)


def group_norm(values, group_size):
    dims_of = values.shape
    grouped = values.reshape(dims_of[:-1] + (dims_of[-1] // group_size, group_size))
    center = jnp.mean(grouped, axis=(1, 2, 4), keepdims=True)
    shifted = grouped - center
    spread = jnp.mean(shifted * shifted, axis=(1, 2, 4), keepdims=True)
    return (shifted * lax.rsqrt(spread + GN_EPS)).reshape(dims_of)


def layer_norm(values):
    center = jnp.mean(values, axis=-1, keepdims=True)
    shifted = values - center
    spread = jnp.mean(shifted * shifted, axis=-1, keepdims=True)
    return shifted * lax.rsqrt(spread + LN_EPS)


def leading_segment(picture, gain_bias):
    return jax.nn.silu(group_norm(picture, C // GROUPS) * gain_bias[0] + gain_bias[1])


def second_piece(middle, res_mods):
    return jax.nn.silu(
        group_norm(middle, C // GROUPS) * (1.0 + res_mods[:, None, None, 0])
        + res_mods[:, None, None, 1]
    )


def modulate(tokens, shift_scale):
    return layer_norm(tokens) * (1.0 + shift_scale[:, None, 1]) + shift_scale[:, None, 0]


def gelu_tanh(values):
    return jax.nn.gelu(values, approximate=True)


def conv_same(inputs, kernel):
    height, breadth = (inputs.shape[1], inputs.shape[2])
    padded = jnp.pad(inputs, ((0, 0), (1, 1), (1, 1), (0, 0)))
    summed_taps = jnp.zeros(inputs.shape[:3] + (kernel.shape[3],), jnp.float32)
    for row_tap in range(3):
        for col_tap in range(3):
            window = padded[:, row_tap : row_tap + height, col_tap : col_tap + breadth]
            summed_taps = summed_taps + jnp.einsum(
                "bhwc,cd->bhwd",
                window,
                kernel[row_tap, col_tap],
                preferred_element_type=jnp.float32,
            )
    return summed_taps


def conv_same_input(upstream, kernel):
    height, breadth = (upstream.shape[1], upstream.shape[2])
    padded = jnp.pad(upstream, ((0, 0), (1, 1), (1, 1), (0, 0)))
    summed_taps = jnp.zeros(upstream.shape[:3] + (kernel.shape[2],), jnp.float32)
    for row_tap in range(3):
        for col_tap in range(3):
            window = padded[
                :, 2 - row_tap : 2 - row_tap + height, 2 - col_tap : 2 - col_tap + breadth
            ]
            summed_taps = summed_taps + jnp.einsum(
                "bhwd,cd->bhwc",
                window,
                kernel[row_tap, col_tap],
                preferred_element_type=jnp.float32,
            )
    return summed_taps


def conv_same_kernel(inputs, upstream):
    height, breadth = (inputs.shape[1], inputs.shape[2])
    padded = jnp.pad(inputs, ((0, 0), (1, 1), (1, 1), (0, 0)))
    tap_list = []
    for row_tap in range(3):
        for col_tap in range(3):
            window = padded[:, row_tap : row_tap + height, col_tap : col_tap + breadth]
            tap_list.append(
                jnp.einsum("bhwc,bhwd->cd", window, upstream, preferred_element_type=jnp.float32)
            )
    return jnp.stack(tap_list).reshape(3, 3, inputs.shape[3], upstream.shape[3])


def conv_down(inputs, kernel):
    height, breadth = (inputs.shape[1], inputs.shape[2])
    padded = jnp.pad(inputs, ((0, 0), (1, 1), (1, 1), (0, 0)))
    summed_taps = jnp.zeros(
        (inputs.shape[0], height // 2, breadth // 2, kernel.shape[3]), jnp.float32
    )
    for row_tap in range(3):
        for col_tap in range(3):
            window = padded[:, row_tap : row_tap + height : 2, col_tap : col_tap + breadth : 2]
            summed_taps = summed_taps + jnp.einsum(
                "bhwc,cd->bhwd",
                window,
                kernel[row_tap, col_tap],
                preferred_element_type=jnp.float32,
            )
    return summed_taps


def conv_down_input(upstream, kernel, height, breadth):
    summed_taps = jnp.zeros(
        (upstream.shape[0], height + 2, breadth + 2, kernel.shape[2]), jnp.float32
    )
    for row_tap in range(3):
        for col_tap in range(3):
            spread_out = jnp.einsum(
                "bhwd,cd->bhwc",
                upstream,
                kernel[row_tap, col_tap],
                preferred_element_type=jnp.float32,
            )
            placed = lax.pad(
                spread_out,
                jnp.float32(0.0),
                ((0, 0, 0), (row_tap, 3 - row_tap, 1), (col_tap, 3 - col_tap, 1), (0, 0, 0)),
            )
            summed_taps = summed_taps + placed
    return summed_taps[:, 1 : height + 1, 1 : breadth + 1]


def conv_down_kernel(inputs, upstream):
    height, breadth = (inputs.shape[1], inputs.shape[2])
    padded = jnp.pad(inputs, ((0, 0), (1, 1), (1, 1), (0, 0)))
    tap_list = []
    for row_tap in range(3):
        for col_tap in range(3):
            window = padded[:, row_tap : row_tap + height : 2, col_tap : col_tap + breadth : 2]
            tap_list.append(
                jnp.einsum("bhwc,bhwd->cd", window, upstream, preferred_element_type=jnp.float32)
            )
    return jnp.stack(tap_list).reshape(3, 3, inputs.shape[3], upstream.shape[3])


def clipped_step(masters, averages, squares, combined_total, sum_all):
    local_sq = jnp.zeros((), jnp.float32)
    for position, reduced in enumerate(combined_total):
        shard_sq = jnp.sum(reduced * reduced)
        if position == 0 or position == 5:
            shard_sq = shard_sq / lax.axis_size(TENSOR)
        local_sq = local_sq + shard_sq
    square_sum = sum_all(local_sq)
    grad_norm = jnp.sqrt(square_sum)
    factor = jnp.minimum(1.0, CLIP / (grad_norm + 1e-06))
    conv_rate = LR_SCALE * (9 * C) ** (-0.5)
    mod_rate = LR_SCALE * (4 * FREQ) ** (-0.5)
    rates = (
        LR_NORM,
        conv_rate,
        mod_rate,
        conv_rate,
        conv_rate,
        mod_rate,
        LR_SCALE * D ** (-0.5),
        LR_SCALE * (HEADS * HDIM // 32) ** (-0.5),
        LR_SCALE * D ** (-0.5),
        LR_SCALE * FF ** (-0.5),
    )
    correct_one = 1.0 - BETA_ONE**STEP
    correct_two = 1.0 - BETA_TWO**STEP
    results = []
    for master, average, square, reduced, learn_rate in zip(
        masters, averages, squares, combined_total, rates
    ):
        clipped = reduced * factor
        new_avg = BETA_ONE * average + (1.0 - BETA_ONE) * clipped
        new_sq = BETA_TWO * square + (1.0 - BETA_TWO) * clipped * clipped
        step_dir = new_avg / correct_one / (jnp.sqrt(new_sq / correct_two) + ADAM_EPS)
        new_master = master - learn_rate * (step_dir + DECAY * master)
        results += [new_master, new_avg, new_sq]
    return (grad_norm.reshape(1),) + tuple(results)


def per_device(
    images,
    t_index,
    cotangent,
    norm_params,
    norm_params_avg,
    norm_params_sq,
    first_conv,
    first_conv_avg,
    first_conv_sq,
    resnet_mod,
    resnet_mod_avg,
    resnet_mod_sq,
    second_conv,
    second_kernel_first_moment,
    second_conv_sq,
    down_conv,
    down_conv_avg,
    down_conv_sq,
    ada_proj,
    ada_proj_avg,
    ada_proj_sq,
    qkv_proj,
    qkv_proj_avg,
    qkv_proj_sq,
    out_proj,
    out_proj_avg,
    out_proj_sq,
    hidden_in,
    hidden_in_avg,
    hidden_in_sq,
    hidden_out,
    hidden_out_avg,
    hidden_out_sq,
):
    masters = (
        norm_params,
        first_conv,
        resnet_mod,
        second_conv,
        down_conv,
        ada_proj,
        qkv_proj,
        out_proj,
        hidden_in,
        hidden_out,
    )
    averages = (
        norm_params_avg,
        first_conv_avg,
        resnet_mod_avg,
        second_kernel_first_moment,
        down_conv_avg,
        ada_proj_avg,
        qkv_proj_avg,
        out_proj_avg,
        hidden_in_avg,
        hidden_out_avg,
    )
    squares = (
        norm_params_sq,
        first_conv_sq,
        resnet_mod_sq,
        second_conv_sq,
        down_conv_sq,
        ada_proj_sq,
        qkv_proj_sq,
        out_proj_sq,
        hidden_in_sq,
        hidden_out_sq,
    )
    lowered = tuple((master.astype(jnp.bfloat16) for master in masters))
    gathered = (
        lax.all_gather(lowered[0], DP, axis=1, tiled=True),
        lax.all_gather(lowered[1], DP, axis=2, tiled=True),
        lax.all_gather(lowered[2], DP, axis=0, tiled=True),
        lax.all_gather(lowered[3], DP, axis=3, tiled=True),
        lax.all_gather(lowered[4], DP, axis=2, tiled=True),
        lax.all_gather(lowered[5], DP, axis=0, tiled=True),
        lax.all_gather(lowered[6], DP, axis=0, tiled=True),
        lax.all_gather(lowered[7], DP, axis=2, tiled=True),
        lax.all_gather(lowered[8], DP, axis=0, tiled=True),
        lax.all_gather(lowered[9], DP, axis=1, tiled=True),
    )
    (
        gain_bias,
        conv_one,
        res_table,
        conv_two,
        conv_half,
        ada_table,
        qkv_full,
        out_full,
        up_full,
        down_full,
    ) = gathered
    batch_size = images.shape[0]
    height, breadth = (images.shape[1], images.shape[2])
    local_c = conv_one.shape[3]
    local_d = conv_half.shape[3]
    heads_here = qkv_full.shape[2]
    tokens_len = height // 2 * (breadth // 2)
    tensor_pos = lax.axis_index(TENSOR)
    n_tensor = lax.axis_size(TENSOR)
    score_scale = HDIM ** (-0.5)
    noise_emb = embed_noise(t_index, FREQ)
    emb_low = noise_emb.astype(jnp.bfloat16)
    emb_back = emb_low.astype(jnp.float32)
    res_mods = jnp.dot(
        emb_low, res_table.reshape(FREQ, 2 * local_c), preferred_element_type=jnp.float32
    ).reshape(batch_size, 2, local_c)
    ada_mods = jnp.dot(
        emb_low, ada_table.reshape(FREQ, 6 * D), preferred_element_type=jnp.float32
    ).reshape(batch_size, 6, D)
    image_float = images.astype(jnp.float32)
    gain_float = gain_bias.astype(jnp.float32)
    act_one, first_back = jax.vjp(leading_segment, image_float, gain_float)
    act_one = act_one.astype(jnp.bfloat16)
    middle = conv_same(act_one, conv_one)
    act_two, second_back = jax.vjp(second_piece, middle, res_mods)
    act_two = act_two.astype(jnp.bfloat16)
    branch = lax.psum(conv_same(act_two, conv_two).astype(jnp.bfloat16), TENSOR).astype(
        jnp.float32
    )
    residual = image_float + branch
    resid_low = residual.astype(jnp.bfloat16)
    shrunk = conv_down(resid_low, conv_half)
    pieces = lax.all_gather(shrunk.astype(jnp.bfloat16), TENSOR, axis=3, tiled=True).astype(
        shrunk.dtype
    )
    tokens = pieces.reshape(batch_size, tokens_len, D)
    attn_in, attn_back = jax.vjp(modulate, tokens, ada_mods[:, 0:2])
    attn_low = attn_in.astype(jnp.bfloat16).reshape(batch_size * tokens_len, D)
    qkv_low = jnp.dot(
        attn_low, qkv_full.reshape(D, 3 * heads_here * HDIM), preferred_element_type=jnp.float32
    ).astype(jnp.bfloat16)
    qkv_low = qkv_low.reshape(batch_size, tokens_len, 3, heads_here, HDIM)
    query_low, key_low, value_low = (qkv_low[:, :, 0], qkv_low[:, :, 1], qkv_low[:, :, 2])
    scores = (
        jnp.einsum("bqhd,bkhd->bhqk", query_low, key_low, preferred_element_type=jnp.float32)
        * score_scale
    )
    row_max = jnp.max(scores, axis=-1, keepdims=True)
    log_total = row_max + jnp.log(jnp.sum(jnp.exp(scores - row_max), axis=-1, keepdims=True))
    attention_low = jnp.exp(scores - log_total).astype(jnp.bfloat16)
    mixed = jnp.einsum(
        "bhqk,bkhd->bqhd", attention_low, value_low, preferred_element_type=jnp.float32
    ).astype(jnp.bfloat16)
    mixed = mixed.reshape(batch_size * tokens_len, heads_here * HDIM)
    out_flat = out_full.reshape(heads_here * HDIM, D)
    attended = (
        lax.psum(
            jnp.dot(mixed, out_flat, preferred_element_type=jnp.float32).astype(jnp.bfloat16),
            TENSOR,
        )
        .astype(jnp.float32)
        .reshape(batch_size, tokens_len, D)
    )
    gate_one = 1.0 + ada_mods[:, None, 2]
    after_attn = tokens + gate_one * attended
    mlp_in, mlp_back = jax.vjp(modulate, after_attn, ada_mods[:, 3:5])
    mlp_low = mlp_in.astype(jnp.bfloat16).reshape(batch_size * tokens_len, D)
    pre_act = jnp.dot(mlp_low, up_full, preferred_element_type=jnp.float32)
    hidden_act, gelu_back = jax.vjp(gelu_tanh, pre_act)
    hidden_low = hidden_act.astype(jnp.bfloat16)
    expanded = (
        lax.psum(
            jnp.dot(hidden_low, down_full, preferred_element_type=jnp.float32).astype(jnp.bfloat16),
            TENSOR,
        )
        .astype(jnp.float32)
        .reshape(batch_size, tokens_len, D)
    )
    gate_two = 1.0 + ada_mods[:, None, 5]
    block_out = (after_attn + gate_two * expanded).astype(jnp.bfloat16)
    upstream = cotangent.astype(jnp.float32)
    grad_expanded = (gate_two * upstream).astype(jnp.bfloat16).reshape(batch_size * tokens_len, D)
    grad_gate_two = jnp.sum(upstream * expanded, axis=1)
    grad_down = jnp.einsum(
        "tf,td->fd", hidden_low, grad_expanded, preferred_element_type=jnp.float32
    )
    grad_hidden = jnp.einsum(
        "td,fd->tf", grad_expanded, down_full, preferred_element_type=jnp.float32
    )
    (grad_pre,) = gelu_back(grad_hidden)
    grad_pre_low = grad_pre.astype(jnp.bfloat16)
    grad_mlp_in = (
        lax.psum(
            jnp.einsum(
                "tf,df->td", grad_pre_low, up_full, preferred_element_type=jnp.float32
            ).astype(jnp.bfloat16),
            TENSOR,
        )
        .astype(jnp.float32)
        .reshape(batch_size, tokens_len, D)
    )
    grad_after_norm, grad_mods_two = mlp_back(grad_mlp_in)
    grad_after = upstream + grad_after_norm
    grad_attended = (gate_one * grad_after).astype(jnp.bfloat16).reshape(batch_size * tokens_len, D)
    grad_gate_one = jnp.sum(grad_after * attended, axis=1)
    grad_out = jnp.einsum("tk,td->kd", mixed, grad_attended, preferred_element_type=jnp.float32)
    grad_mixed = jnp.einsum(
        "td,kd->tk", grad_attended, out_flat, preferred_element_type=jnp.float32
    ).astype(jnp.bfloat16)
    grad_mixed = grad_mixed.reshape(batch_size, tokens_len, heads_here, HDIM)
    scores = (
        jnp.einsum("bqhd,bkhd->bhqk", query_low, key_low, preferred_element_type=jnp.float32)
        * score_scale
    )
    attention = jnp.exp(scores - log_total)
    attention_low = attention.astype(jnp.bfloat16)
    grad_probs = jnp.einsum(
        "bqhd,bkhd->bhqk", grad_mixed, value_low, preferred_element_type=jnp.float32
    )
    grad_values = jnp.einsum(
        "bhqk,bqhd->bkhd", attention_low, grad_mixed, preferred_element_type=jnp.float32
    )
    grad_scores = (
        attention * (grad_probs - jnp.sum(grad_probs * attention, axis=-1, keepdims=True))
    ).astype(jnp.bfloat16)
    query_gradient = (
        jnp.einsum("bhqk,bkhd->bqhd", grad_scores, key_low, preferred_element_type=jnp.float32)
        * score_scale
    )
    grad_keys = (
        jnp.einsum("bhqk,bqhd->bkhd", grad_scores, query_low, preferred_element_type=jnp.float32)
        * score_scale
    )
    grad_qkv = (
        jnp.stack([query_gradient, grad_keys, grad_values], axis=2)
        .astype(jnp.bfloat16)
        .reshape(batch_size * tokens_len, 3 * heads_here * HDIM)
    )
    grad_qkv_w = jnp.einsum(
        "td,tk->dk", attn_low, grad_qkv, preferred_element_type=jnp.float32
    ).reshape(D, 3, heads_here, HDIM)
    grad_attn_in = (
        lax.psum(
            jnp.einsum(
                "tk,dk->td",
                grad_qkv,
                qkv_full.reshape(D, 3 * heads_here * HDIM),
                preferred_element_type=jnp.float32,
            ).astype(jnp.bfloat16),
            TENSOR,
        )
        .astype(jnp.float32)
        .reshape(batch_size, tokens_len, D)
    )
    grad_tokens_norm, grad_mods_one = attn_back(grad_attn_in)
    grad_tokens = grad_after + grad_tokens_norm
    grad_mods = jnp.concatenate(
        [grad_mods_one, grad_gate_one[:, None], grad_mods_two, grad_gate_two[:, None]], axis=1
    )
    adaptive_gradient = jnp.einsum(
        "bf,bk->fk", emb_back, grad_mods.reshape(batch_size, 6 * D), precision=HIGHEST
    ).reshape(FREQ, 6, D)
    grad_out_w = grad_out.reshape(heads_here, HDIM, D)
    grad_up = jnp.einsum("td,tf->df", mlp_low, grad_pre_low, preferred_element_type=jnp.float32)
    transformer_gradient_total = (
        lax.psum_scatter(adaptive_gradient, DP, scatter_dimension=0, tiled=True),
        lax.psum_scatter(grad_qkv_w, DP, scatter_dimension=0, tiled=True),
        lax.psum_scatter(grad_out_w, DP, scatter_dimension=2, tiled=True),
        lax.psum_scatter(grad_up, DP, scatter_dimension=0, tiled=True),
        lax.psum_scatter(grad_down, DP, scatter_dimension=1, tiled=True),
    )
    grad_shrunk = lax.dynamic_slice_in_dim(
        grad_tokens.reshape(batch_size, height // 2, breadth // 2, D),
        tensor_pos * local_d,
        local_d,
        axis=3,
    ).astype(jnp.bfloat16)
    grad_half = conv_down_kernel(resid_low, grad_shrunk)
    grad_resid = lax.psum(
        conv_down_input(grad_shrunk, conv_half, height, breadth).astype(jnp.bfloat16), TENSOR
    ).astype(jnp.float32)
    grad_branch = grad_resid.astype(jnp.bfloat16)
    grad_conv_two = conv_same_kernel(act_two, grad_branch)
    grad_act_two = conv_same_input(grad_branch, conv_two)
    grad_middle, grad_res_mods = second_back(grad_act_two)
    grad_middle_low = grad_middle.astype(jnp.bfloat16)
    grad_conv_one = conv_same_kernel(act_one, grad_middle_low)
    grad_act_one = lax.psum(
        conv_same_input(grad_middle_low, conv_one).astype(jnp.bfloat16), TENSOR
    ).astype(jnp.float32)
    grad_image_norm, grad_gain = first_back(grad_act_one)
    images_grad = grad_resid + grad_image_norm
    grad_res_table = jnp.einsum(
        "bf,bk->fk", emb_back, grad_res_mods.reshape(batch_size, 2 * local_c), precision=HIGHEST
    ).reshape(FREQ, 2, local_c)
    resnet_gradient_total = (
        lax.psum_scatter(grad_gain, DP, scatter_dimension=1, tiled=True),
        lax.psum_scatter(grad_conv_one, DP, scatter_dimension=2, tiled=True),
        lax.psum_scatter(grad_res_table, DP, scatter_dimension=0, tiled=True),
        lax.psum_scatter(grad_conv_two, DP, scatter_dimension=3, tiled=True),
        lax.psum_scatter(grad_half, DP, scatter_dimension=2, tiled=True),
    )
    combined_total = tuple(resnet_gradient_total) + tuple(transformer_gradient_total)
    return (block_out, images_grad) + clipped_step(
        masters,
        averages,
        squares,
        combined_total,
        lambda local: lax.psum(local, (DP, TENSOR)),
    )


MESH = pl.DeviceIdType.MESH
ANYWHERE = pl.BlockSpec(memory_space=pl.ANY)
IN_VMEM = pl.BlockSpec(memory_space=pltpu.VMEM)
LAYERS = 4
ORDER = (3, 0, 2, 1)
VMEM_GRANT = 60 * 1024 * 1024


class Place:
    def __init__(self, wide):
        self.wide = wide
        self.dp = lax.axis_index(DP)
        self.core = lax.axis_index(TENSOR)
        self.z = self.dp // 4
        x = self.dp % 2
        y = (self.dp // 2) % 2
        x_mate = self.dp + 1 - 2 * x
        y_mate = self.dp + 2 - 4 * y
        self.x_mate = x_mate
        if wide:
            self.first = x_mate * (1 - self.core) + y_mate * self.core
            self.second = y_mate * (1 - self.core) + x_mate * self.core
            self.stride = 4
            self.column = self.dp % 4
            self.first_column = self.first % 4
            self.second_column = self.second % 4
            self.far_column = 3 - self.column
        else:
            self.first = self.second = y_mate
            self.stride = 2
            self.column = y
            self.second_column = 1 - y
        self.slot = self.z * self.stride + self.column
        self.has_below = self.z > 0
        self.has_above = self.z < LAYERS - 1

    def greet(self, with_core):
        barrier = pltpu.get_barrier_semaphore()

        def signal(dp, core):
            pl.semaphore_signal(barrier, inc=1, device_id=(dp, core), device_id_type=MESH)

        signal(self.second, self.core)
        if self.wide:
            signal(self.first, self.core)
        if with_core:
            signal(self.dp, 1 - self.core)
        pl.when(self.has_below)(lambda: signal(self.dp - 4, self.core))
        pl.when(self.has_above)(lambda: signal(self.dp + 4, self.core))
        layers = (self.z + LAYERS - 1) // LAYERS + (2 * LAYERS - 2 - self.z) // LAYERS
        pl.semaphore_wait(barrier, 1 + self.wide + with_core + layers)


def params(number):
    return pltpu.CompilerParams(
        collective_id=number, has_side_effects=True, vmem_limit_bytes=VMEM_GRANT
    )


def gather_kernel(wide, both, block_ref, out_ref, send_sem, recv_sem, own_sem):
    at = Place(wide)

    def here(slot):
        return out_ref.at[slot, at.core] if both else out_ref.at[slot]

    def copy(sem, source, slot, mate):
        return pltpu.make_async_remote_copy(
            src_ref=source,
            dst_ref=here(slot),
            send_sem=send_sem.at[sem],
            recv_sem=recv_sem.at[sem],
            device_id=(mate, at.core),
            device_id_type=MESH,
        )

    def mirror(slot, source):
        return pltpu.make_async_remote_copy(
            src_ref=source,
            dst_ref=here(slot),
            send_sem=send_sem.at[18 + slot],
            recv_sem=recv_sem.at[18 + slot],
            device_id=(at.dp, 1 - at.core),
            device_id_type=MESH,
        )

    at.greet(both)
    keep = pltpu.make_async_copy(block_ref, here(at.slot), own_sem)
    keep.start()

    def place(layer, column):
        return layer * at.stride + column

    def spread(layer, source):
        slot = place(layer, at.column)
        if wide:
            copy(6 + layer, source, slot, at.first).start()
        copy(10 + layer, source, slot, at.second).start()
        if both:
            mirror(slot, source).start()

    def up(distance, source):
        return copy(distance, source, place(at.z - distance, at.column), at.dp + 4)

    def down(distance, source):
        return copy(3 + distance, source, place(at.z + distance, at.column), at.dp - 4)

    pl.when(at.has_above)(lambda: up(0, block_ref).start())
    pl.when(at.has_below)(lambda: down(0, block_ref).start())
    spread(at.z, block_ref)

    def onward(layer):
        slot = place(layer, at.first_column)
        copy(6 + layer, here(slot), slot, at.first).wait_recv()
        copy(14 + layer, here(slot), slot, at.second).start()
        if both:
            mirror(slot, here(slot)).start()

    for distance in range(1, LAYERS):
        below, above = at.z - distance, at.z + distance

        @pl.when(below >= 0)
        def _():
            slot = place(below, at.column)
            copy(distance - 1, here(slot), slot, at.dp).wait_recv()
            if distance < LAYERS - 1:
                pl.when(at.has_above)(lambda: up(distance, here(slot)).start())
            spread(below, here(slot))

        @pl.when(above < LAYERS)
        def _():
            slot = place(above, at.column)
            copy(3 + distance - 1, here(slot), slot, at.dp).wait_recv()
            if distance < LAYERS - 1:
                pl.when(at.has_below)(lambda: down(distance, here(slot)).start())
            spread(above, here(slot))

        if not wide:
            continue
        if distance == 1:
            onward(at.z)
        else:
            pl.when(at.z - distance + 1 >= 0)(lambda: onward(at.z - distance + 1))
            pl.when(at.z + distance - 1 < LAYERS)(lambda: onward(at.z + distance - 1))
    if wide:
        pl.when(at.z == LAYERS - 1)(lambda: onward(0))
        pl.when(at.z == 0)(lambda: onward(LAYERS - 1))

    keep.wait()
    own = here(at.slot)
    for layer in range(LAYERS):
        arriving = [(10, at.second_column)]
        if wide:
            arriving.append((14, at.far_column))
        for sem, column in arriving:
            slot = place(layer, column)
            copy(sem + layer, own, slot, at.second).wait_recv()
            if both:
                mirror(slot, here(slot)).start()
    if both:
        for slot in range(at.stride * LAYERS):
            pltpu.make_async_remote_copy(
                src_ref=own,
                dst_ref=out_ref.at[slot, 1 - at.core],
                send_sem=send_sem.at[18 + slot],
                recv_sem=recv_sem.at[18 + slot],
                device_id=(at.dp, 1 - at.core),
                device_id_type=MESH,
            ).wait_recv()
            mirror(slot, own).wait_send()
    for sem in range(6, 18) if wide else range(10, 14):
        copy(sem, own, at.slot, at.second).wait_send()
    for distance in range(LAYERS - 1):

        @pl.when(jnp.logical_and(at.has_above, at.z - distance >= 0))
        def _():
            up(distance, own).wait_send()

        @pl.when(jnp.logical_and(at.has_below, at.z + distance < LAYERS))
        def _():
            down(distance, own).wait_send()


def gather(number, block, wide=True, both=False):
    chips = 16 if wide else 8
    shape = (chips,) + ((2,) if both else ()) + block.shape
    count = 18 + both * chips
    return pl.pallas_call(
        functools.partial(gather_kernel, wide, both),
        out_shape=jax.ShapeDtypeStruct(shape, block.dtype),
        in_specs=[ANYWHERE],
        out_specs=ANYWHERE,
        scratch_shapes=[
            pltpu.SemaphoreType.DMA((count,)),
            pltpu.SemaphoreType.DMA((count,)),
            pltpu.SemaphoreType.DMA,
        ],
        compiler_params=params(number),
        name=f"gather_{chips}" + ("_both" if both else ""),
    )(block)


def reduce_kernel(wide, pair, share, in_ref, out_ref, *scratch):
    if pair:
        *scratch, paired, pair_send, pair_recv = scratch
    own, from_second, from_first, from_z, send_sem, recv_sem, own_sem = scratch
    at = Place(wide)

    def copy(sem, source, target, mate):
        return pltpu.make_async_remote_copy(
            src_ref=source,
            dst_ref=target,
            send_sem=send_sem.at[sem],
            recv_sem=recv_sem.at[sem],
            device_id=(mate, at.core),
            device_id_type=MESH,
        )

    def place(layer, column):
        return layer * at.stride + column

    def load(slot):
        source = in_ref.at[slot, at.core] if pair else in_ref.at[slot]
        return pltpu.make_async_copy(source, own.at[slot], own_sem.at[slot])

    def to_mate(slot):
        return pltpu.make_async_remote_copy(
            src_ref=in_ref.at[slot, 1 - at.core],
            dst_ref=paired.at[slot],
            send_sem=pair_send.at[slot],
            recv_sem=pair_recv.at[slot],
            device_id=(at.dp, 1 - at.core),
            device_id_type=MESH,
        )

    def to_second(half, layer):
        column = at.far_column if half == 0 else at.second_column
        source = own if pair else in_ref
        return copy(
            4 * half + layer,
            source.at[place(layer, column)],
            from_second.at[4 * half + layer],
            at.second,
        )

    def first_slot(layer):
        return place(layer, at.first_column)

    def own_slot(layer):
        return place(layer, at.column)

    def to_first(layer):
        return copy(8 + layer, own.at[first_slot(layer)], from_first.at[layer], at.first)

    def up(layer):
        return copy(12 + layer, own.at[own_slot(layer)], from_z.at[layer], at.dp + 4)

    def down(layer):
        return copy(16 + layer, own.at[own_slot(layer)], from_z.at[4 + layer], at.dp - 4)

    def value(ref, index):
        return ref[index].astype(jnp.float32)

    def join(slot):
        load(slot).wait()
        to_mate(slot).wait_recv()
        own[slot] = (value(own, slot) + value(paired, slot)).astype(own.dtype)

    at.greet(pair or share)
    halves = (0, 1) if wide else (1,)
    for half in halves:
        for layer in ORDER:
            away = place(layer, at.far_column if half == 0 else at.second_column)
            keep = first_slot(layer) if half == 0 else own_slot(layer)
            if pair:
                for slot in (away, keep):
                    to_mate(slot).start()
                    load(slot).start()
            else:
                to_second(half, layer).start()
                load(keep).start()
    if pair:
        for half in halves:
            for layer in ORDER:
                join(place(layer, at.far_column if half == 0 else at.second_column))
                to_second(half, layer).start()
        for layer in ORDER:
            if wide:
                join(first_slot(layer))
            join(own_slot(layer))

    if wide:
        for layer in ORDER:
            slot = first_slot(layer)
            if not pair:
                load(slot).wait()
            to_second(0, layer).wait_recv()
            own[slot] = (value(own, slot) + value(from_second, layer)).astype(own.dtype)
            to_first(layer).start()
    result = out_ref.at[at.core] if share else out_ref
    for layer in ORDER:
        slot = own_slot(layer)
        if not pair:
            load(slot).wait()
        to_second(1, layer).wait_recv()
        total = value(own, slot) + value(from_second, 4 + layer)
        if wide:
            to_first(layer).wait_recv()
            total = total + value(from_first, layer)
        own[slot] = total.astype(own.dtype)

        @pl.when(at.z < layer)
        def _():
            @pl.when(at.has_below)
            def _():
                up(layer).wait_recv()
                own[slot] = (value(own, slot) + value(from_z, layer)).astype(own.dtype)

            up(layer).start()

        @pl.when(at.z > layer)
        def _():
            @pl.when(at.has_above)
            def _():
                down(layer).wait_recv()
                own[slot] = (value(own, slot) + value(from_z, 4 + layer)).astype(own.dtype)

            down(layer).start()

        @pl.when(at.z == layer)
        def _():
            result[...] = total.astype(out_ref.dtype)

    for layer in range(LAYERS):

        @pl.when(at.z == layer)
        def _():
            @pl.when(at.has_below)
            def _():
                up(layer).wait_recv()
                result[...] = (result[...].astype(jnp.float32) + value(from_z, layer)).astype(
                    out_ref.dtype
                )

            @pl.when(at.has_above)
            def _():
                down(layer).wait_recv()
                result[...] = (result[...].astype(jnp.float32) + value(from_z, 4 + layer)).astype(
                    out_ref.dtype
                )

    if share:

        def give(core):
            return pltpu.make_async_remote_copy(
                src_ref=result,
                dst_ref=out_ref.at[core],
                send_sem=send_sem.at[20],
                recv_sem=recv_sem.at[20],
                device_id=(at.dp, 1 - at.core),
                device_id_type=MESH,
            )

        give(at.core).start()
        give(1 - at.core).wait_recv()
        give(at.core).wait_send()
    if pair:
        for slot in range(at.stride * LAYERS):
            to_mate(slot).wait_send()
    for layer in range(LAYERS):
        for half in halves:
            to_second(half, layer).wait_send()
        if wide:
            to_first(layer).wait_send()
        pl.when(at.z < layer)(lambda: up(layer).wait_send())
        pl.when(at.z > layer)(lambda: down(layer).wait_send())


def reduce(number, blocks, wide=True, pair=False, share=False):
    chips = 16 if wide else 8
    block = blocks.shape[-2:]
    kind = blocks.dtype
    scratch = [
        pltpu.VMEM((chips,) + block, kind),
        pltpu.VMEM((8,) + block, kind),
        pltpu.VMEM((4,) + block, kind),
        pltpu.VMEM((8,) + block, kind),
        pltpu.SemaphoreType.DMA((21,)),
        pltpu.SemaphoreType.DMA((21,)),
        pltpu.SemaphoreType.DMA((chips,)),
    ]
    if pair:
        scratch += [
            pltpu.VMEM((chips,) + block, kind),
            pltpu.SemaphoreType.DMA((chips,)),
            pltpu.SemaphoreType.DMA((chips,)),
        ]
    return pl.pallas_call(
        functools.partial(reduce_kernel, wide, pair, share),
        out_shape=jax.ShapeDtypeStruct(((2,) if share else ()) + block, jnp.float32),
        in_specs=[ANYWHERE],
        out_specs=IN_VMEM,
        scratch_shapes=scratch,
        compiler_params=params(number),
        name=f"reduce_{chips}" + ("_pair" if pair else "") + ("_share" if share else ""),
    )(blocks)


def trade_kernel(count, *refs):
    in_refs, out_refs = (refs[:count], refs[count : 2 * count])
    send_sem, recv_sem, own_sem = refs[2 * count :]
    dp, core = (lax.axis_index(DP), lax.axis_index(TENSOR))
    others = 4 * LAYERS - 1
    barrier = pltpu.get_barrier_semaphore()

    def peer(step):
        return (dp + step) % (4 * LAYERS)

    @pl.loop(1, others + 1)
    def _(step):
        pl.semaphore_signal(barrier, inc=1, device_id=(peer(step), core), device_id_type=MESH)

    pl.semaphore_wait(barrier, others)

    def copy(index, step):
        return pltpu.make_async_remote_copy(
            src_ref=in_refs[index].at[peer(step)],
            dst_ref=out_refs[index].at[dp],
            send_sem=send_sem.at[index, step - 1],
            recv_sem=recv_sem.at[index, step - 1],
            device_id=(peer(step), core),
            device_id_type=MESH,
        )

    def keep(index):
        return pltpu.make_async_copy(
            in_refs[index].at[dp], out_refs[index].at[dp], own_sem.at[index]
        )

    for index in range(count):
        keep(index).start()

        @pl.loop(1, others + 1)
        def _(step):
            copy(index, step).start()

    for index in range(count):
        keep(index).wait()

        @pl.loop(1, others + 1)
        def _(step):
            copy(index, step).wait()


def trade(number, *blocks):
    count = len(blocks)
    return pl.pallas_call(
        functools.partial(trade_kernel, count),
        out_shape=[jax.ShapeDtypeStruct(b.shape, b.dtype) for b in blocks],
        in_specs=[ANYWHERE] * count,
        out_specs=[ANYWHERE] * count,
        scratch_shapes=[
            pltpu.SemaphoreType.DMA((count, 15)),
            pltpu.SemaphoreType.DMA((count, 15)),
            pltpu.SemaphoreType.DMA((count,)),
        ],
        compiler_params=params(number),
        name="trade",
    )(*blocks)


def add_core_kernel(pieces, in_ref, out_ref, theirs, send_sem, recv_sem):
    dp, core = (lax.axis_index(DP), lax.axis_index(TENSOR))
    barrier = pltpu.get_barrier_semaphore()
    pl.semaphore_signal(barrier, inc=1, device_id=(dp, 1 - core), device_id_type=MESH)
    pl.semaphore_wait(barrier, 1)
    rows = in_ref.shape[0] // pieces

    def copy(piece):
        at = pl.ds(piece * rows, rows)
        return pltpu.make_async_remote_copy(
            src_ref=in_ref.at[at],
            dst_ref=theirs.at[at],
            send_sem=send_sem.at[piece],
            recv_sem=recv_sem.at[piece],
            device_id=(dp, 1 - core),
            device_id_type=MESH,
        )

    for piece in range(pieces):
        copy(piece).start()
    for piece in range(pieces):
        at = pl.ds(piece * rows, rows)
        copy(piece).wait_recv()
        out_ref[at] = in_ref[at].astype(jnp.float32) + theirs[at].astype(jnp.float32)
    for piece in range(pieces):
        copy(piece).wait_send()


def add_core(number, block):
    pieces = 4
    return pl.pallas_call(
        functools.partial(add_core_kernel, pieces),
        out_shape=jax.ShapeDtypeStruct(block.shape, jnp.float32),
        in_specs=[IN_VMEM],
        out_specs=IN_VMEM,
        scratch_shapes=[
            pltpu.VMEM(block.shape, block.dtype),
            pltpu.SemaphoreType.DMA((pieces,)),
            pltpu.SemaphoreType.DMA((pieces,)),
        ],
        compiler_params=params(number),
        name="add_core",
    )(block)


def total_kernel(in_ref, out_ref, tiles, held, send_sem, recv_sem):
    dp, core = (lax.axis_index(DP), lax.axis_index(TENSOR))
    others = 4 * LAYERS - 1
    barrier = pltpu.get_barrier_semaphore()

    def peer(step):
        return (dp + step) % (4 * LAYERS)

    pl.semaphore_signal(barrier, inc=1, device_id=(dp, 1 - core), device_id_type=MESH)

    @pl.loop(1, others + 1)
    def _(step):
        pl.semaphore_signal(barrier, inc=1, device_id=(peer(step), core), device_id_type=MESH)

    pl.semaphore_wait(barrier, others + 1)
    across = pltpu.make_async_remote_copy(
        src_ref=in_ref,
        dst_ref=tiles.at[0],
        send_sem=send_sem.at[0],
        recv_sem=recv_sem.at[0],
        device_id=(dp, 1 - core),
        device_id_type=MESH,
    )
    across.start()
    across.wait()
    held[...] = in_ref[...] + tiles[0]

    def copy(step):
        return pltpu.make_async_remote_copy(
            src_ref=held,
            dst_ref=tiles.at[step],
            send_sem=send_sem.at[step],
            recv_sem=recv_sem.at[step],
            device_id=(peer(step), core),
            device_id_type=MESH,
        )

    @pl.loop(1, others + 1)
    def _(step):
        copy(step).start()

    @pl.loop(1, others + 1)
    def _(step):
        copy(step).wait()

    total = jnp.zeros_like(held)
    for chip in range(4 * LAYERS):
        step = (dp - chip + 4 * LAYERS) % (4 * LAYERS)
        part = jnp.where(step == 0, held[...], tiles[step])
        total = total + part
    out_ref[...] = total


def total(number, tile):
    return pl.pallas_call(
        total_kernel,
        out_shape=jax.ShapeDtypeStruct(tile.shape, tile.dtype),
        in_specs=[IN_VMEM],
        out_specs=IN_VMEM,
        scratch_shapes=[
            pltpu.VMEM((16,) + tile.shape, tile.dtype),
            pltpu.VMEM(tile.shape, tile.dtype),
            pltpu.SemaphoreType.DMA((16,)),
            pltpu.SemaphoreType.DMA((16,)),
        ],
        compiler_params=params(number),
        name="total",
    )(tile)


def layer_order(step):
    odd = step % 2
    return (1 - odd) * (LAYERS - 1 - step // 2) + odd * (step // 2)


def remote(source, target, send_sem, recv_sem, device):
    return pltpu.make_async_remote_copy(
        src_ref=source,
        dst_ref=target,
        send_sem=send_sem,
        recv_sem=recv_sem,
        device_id=device,
        device_id_type=MESH,
    )


def by_distance(at, step):
    flip = at.z // 2
    inner = at.z * (1 - flip) + (LAYERS - 1 - at.z) * flip
    early = 1 - step // 2
    base = (1 - inner) * step + inner * (early * (1 - step) + (1 - early) * step)
    return (1 - flip) * base + flip * (LAYERS - 1 - base)


def piece_of(block, index, pieces):
    rows, lanes = block.shape
    if rows >= 16 * pieces:
        return block.at[pl.ds(pl.multiple_of(index * (rows // pieces), rows // pieces), rows // pieces)]
    return block.at[:, pl.ds(pl.multiple_of(index * (lanes // pieces), lanes // pieces), lanes // pieces)]


def gather_stage(at, outs, use, pieces, send_sem, recv_sem, mirror=None):
    columns = at.stride
    arrays = range(len(outs))

    def here(index, slot, piece):
        block = outs[index].at[slot, at.core] if mirror else outs[index].at[slot]
        return piece_of(block, piece, pieces)

    def each(slot, piece, sem, mate, act):
        for index in arrays:
            act(
                remote(
                    here(index, slot, piece),
                    here(index, slot, piece),
                    send_sem.at[index, sem * pieces + piece],
                    recv_sem.at[index, slot * pieces + piece],
                    (mate, at.core),
                )
            )

    def start(copy):
        copy.start()

    def across(slot, piece, act, core):
        for index in arrays:
            block = piece_of(outs[index].at[slot, core], piece, pieces)
            act(
                remote(
                    block,
                    block,
                    mirror[0].at[index, slot * pieces + piece],
                    mirror[1].at[index, slot * pieces + piece],
                    (at.dp, 1 - at.core),
                )
            )

    @pl.loop(0, columns * LAYERS * pieces)
    def _(count):
        step, piece = (count // pieces, count % pieces)
        if at.wide:
            late = step // 8
            rest = step % 8
            last = rest // 7
            is_first = (1 - late) * (last + (1 - rest % 2) * ((rest + 6) // 8))
            is_own = (1 - late) * (1 - is_first)
            near = is_own * ((rest + 1) // 2) + is_first * ((rest - 1) // 2)
            layer = by_distance(at, (1 - late) * near + late * (rest // 2))
            column = (
                is_own * at.column
                + is_first * at.first_column
                + late * ((1 - rest % 2) * at.second_column + rest % 2 * at.far_column)
            )
        else:
            is_own = 1 - step // LAYERS
            layer = by_distance(at, step % LAYERS)
            column = is_own * at.column + (1 - is_own) * at.second_column
        slot = layer * columns + column

        @pl.when(slot != at.slot)
        def _():
            each(slot, piece, 0, at.dp, lambda copy: copy.wait_recv())

        @pl.when(is_own == 1)
        def _():
            @pl.when(jnp.logical_and(layer <= at.z, at.has_above))
            def _():
                each(slot, piece, layer, at.dp + 4, start)

            @pl.when(jnp.logical_and(layer >= at.z, at.has_below))
            def _():
                each(slot, piece, 4 + layer, at.dp - 4, start)

            if at.wide:
                each(slot, piece, 8 + layer, at.first, start)
            each(slot, piece, 12 + layer, at.second, start)

        if at.wide:

            @pl.when(is_first == 1)
            def _():
                each(slot, piece, 16 + layer, at.second, start)

        if mirror:
            across(slot, piece, start, at.core)
        if use is not None:
            pl.when(piece == pieces - 1)(lambda: use(slot))

    def sent(copy):
        copy.wait_send()

    @pl.loop(0, LAYERS * pieces)
    def _(count):
        layer, piece = (count // pieces, count % pieces)

        @pl.when(jnp.logical_and(layer <= at.z, at.has_above))
        def _():
            each(at.slot, piece, layer, at.dp + 4, sent)

        @pl.when(jnp.logical_and(layer >= at.z, at.has_below))
        def _():
            each(at.slot, piece, 4 + layer, at.dp - 4, sent)

        for group in (8, 12, 16) if at.wide else (12,):
            each(at.slot, piece, group + layer, at.second, sent)

    if mirror:

        @pl.loop(0, columns * LAYERS * pieces)
        def _(count):
            slot, piece = (count // pieces, count % pieces)
            across(slot, piece, lambda copy: copy.wait_recv(), 1 - at.core)
            across(slot, piece, sent, at.core)


def gather_scratch(pieces, arrays=1, wide=True, mirror=False):
    chips = 16 if wide else 8
    count = [20 * pieces, 16 * pieces] + [chips * pieces] * (2 * mirror)
    return [pltpu.SemaphoreType.DMA((arrays, n)) for n in count]


def reduce_stage(at, result, produce, pieces, scratch, pair=False, meanwhile=None):
    blocks, from_second, from_first, from_z, send_sem, recv_sem, *scratch = scratch
    columns = at.stride
    whole = columns * LAYERS
    lag = whole // 2 if pair else 0

    def part(ref, index, piece):
        return piece_of(ref.at[index], piece, pieces)

    def copy(sem, piece, source, target, mate):
        return remote(
            part(blocks, source, piece),
            part(target[0], target[1], piece),
            send_sem.at[sem, piece],
            recv_sem.at[sem, piece],
            (mate, at.core),
        )

    def to_second(half, layer, piece, slot):
        return copy(4 * half + layer, piece, slot, (from_second, 4 * half + layer), at.second)

    def to_first(layer, piece):
        return copy(
            8 + layer, piece, layer * columns + at.first_column, (from_first, layer), at.first
        )

    def up(layer, piece):
        return copy(12 + layer, piece, layer * columns + at.column, (from_z, layer), at.dp + 4)

    def down(layer, piece):
        return copy(16 + layer, piece, layer * columns + at.column, (from_z, 4 + layer), at.dp - 4)

    def value(ref, index, piece):
        return part(ref, index, piece)[...].astype(jnp.float32)

    def slot_of(step):
        if at.wide:
            keep, second, place = (step // 8, step % 2, step % 8 // 2)
            column = (1 - second) * (
                (1 - keep) * at.far_column + keep * at.first_column
            ) + second * ((1 - keep) * at.second_column + keep * at.column)
        else:
            keep, second, place = (step // LAYERS, 1, step % LAYERS)
            column = (1 - keep) * at.second_column + keep * at.column
        return layer_order(place) * columns + column, keep, second, place

    ahead = 2

    def send_layer(place, piece):
        layer = layer_order(place)
        if at.wide:
            to_second(0, layer, piece, layer * columns + at.far_column).start()
        to_second(1, layer, piece, layer * columns + at.second_column).start()

    def to_mate(slot):
        outbound, paired, pair_send, pair_recv = scratch
        return remote(
            outbound.at[slot],
            paired.at[slot],
            pair_send.at[slot],
            pair_recv.at[slot],
            (at.dp, 1 - at.core),
        )

    @pl.loop(0, whole + lag)
    def _(step):
        def make():
            slot = slot_of(step)[0]
            produce(slot)
            if pair:
                to_mate(slot).start()

        def pass_on():
            slot, keep, second, place = slot_of(step - lag)
            if pair:
                to_mate(slot).wait_recv()
                blocks[slot] = (
                    blocks[slot].astype(jnp.float32) + scratch[1][slot].astype(jnp.float32)
                ).astype(blocks.dtype)

            @pl.when(jnp.logical_and(keep == 0, place < ahead))
            def _():
                for piece in range(pieces):
                    to_second(second, layer_order(place), piece, slot).start()

        if pair:
            pl.when(step < whole)(make)
            pl.when(step >= lag)(pass_on)
        else:
            make()
            pass_on()

    if meanwhile is not None:
        meanwhile()

    def turn(place, piece):
        layer = layer_order(place)
        slot = layer * columns + at.first_column
        to_second(0, layer, piece, slot).wait_recv()
        part(blocks, slot, piece)[...] = (
            value(blocks, slot, piece) + value(from_second, layer, piece)
        ).astype(blocks.dtype)
        to_first(layer, piece).start()

    def rise(place, piece):
        layer = layer_order(place)
        slot = layer * columns + at.column
        to_second(1, layer, piece, slot).wait_recv()
        summed = value(blocks, slot, piece) + value(from_second, 4 + layer, piece)
        if at.wide:
            to_first(layer, piece).wait_recv()
            summed = summed + value(from_first, layer, piece)

        @pl.when(at.z == layer)
        def _():
            piece_of(result, piece, pieces)[...] = summed

        @pl.when(at.z < layer)
        def _():
            part(blocks, slot, piece)[...] = summed.astype(blocks.dtype)

            @pl.when(at.has_below)
            def _():
                up(layer, piece).wait_recv()
                part(blocks, slot, piece)[...] = (
                    value(blocks, slot, piece) + value(from_z, layer, piece)
                ).astype(blocks.dtype)

            up(layer, piece).start()

        @pl.when(at.z > layer)
        def _():
            part(blocks, slot, piece)[...] = summed.astype(blocks.dtype)

            @pl.when(at.has_above)
            def _():
                down(layer, piece).wait_recv()
                part(blocks, slot, piece)[...] = (
                    value(blocks, slot, piece) + value(from_z, 4 + layer, piece)
                ).astype(blocks.dtype)

            down(layer, piece).start()

    behind = 1 if at.wide else 0

    @pl.loop(0, (LAYERS + behind) * pieces)
    def _(step):
        place, piece = (step // pieces, step % pieces)
        pl.when(place + ahead < LAYERS)(lambda: send_layer(place + ahead, piece))
        if at.wide:
            pl.when(place < LAYERS)(lambda: turn(place, piece))
        pl.when(place >= behind)(lambda: rise(place - behind, piece))

    @pl.loop(0, pieces)
    def _(piece):
        @pl.when(at.has_below)
        def _():
            up(at.z, piece).wait_recv()
            piece_of(result, piece, pieces)[...] += value(from_z, at.z, piece)

        @pl.when(at.has_above)
        def _():
            down(at.z, piece).wait_recv()
            piece_of(result, piece, pieces)[...] += value(from_z, 4 + at.z, piece)

    @pl.loop(0, LAYERS * pieces)
    def _(step):
        layer, piece = (step // pieces, step % pieces)
        if at.wide:
            to_second(0, layer, piece, at.slot).wait_send()
            to_first(layer, piece).wait_send()
        to_second(1, layer, piece, at.slot).wait_send()
        pl.when(at.z < layer)(lambda: up(layer, piece).wait_send())
        pl.when(at.z > layer)(lambda: down(layer, piece).wait_send())

    if pair:

        @pl.loop(0, whole)
        def _(slot):
            to_mate(slot).wait_send()


def share_stage(at, result, send_sem, recv_sem):
    def give(core):
        return remote(result.at[core], result.at[core], send_sem, recv_sem, (at.dp, 1 - at.core))

    give(at.core).start()
    give(1 - at.core).wait_recv()
    give(at.core).wait_send()


def greet_all(at):
    everyone = 4 * LAYERS
    barrier = pltpu.get_barrier_semaphore()

    @pl.loop(1, everyone)
    def _(step):
        pl.semaphore_signal(
            barrier, inc=1, device_id=((at.dp + step) % everyone, at.core), device_id_type=MESH
        )

    pl.semaphore_signal(barrier, inc=1, device_id=(at.dp, 1 - at.core), device_id_type=MESH)
    pl.semaphore_wait(barrier, everyone)


class Ride:
    def __init__(self, at, parts, send_sem, recv_sem, own_sem):
        self.at, self.parts = (at, parts)
        self.send_sem, self.recv_sem, self.own_sem = (send_sem, recv_sem, own_sem)

    def copy(self, part, step):
        source, target = self.parts[part]
        peer = (self.at.dp + step) % (4 * LAYERS)
        return remote(
            source(peer),
            target(self.at.dp),
            self.send_sem.at[part, step - 1],
            self.recv_sem.at[part, step - 1],
            (peer, self.at.core),
        )

    def keep(self, part):
        source, target = self.parts[part]
        return pltpu.make_async_copy(
            source(self.at.dp), target(self.at.dp), self.own_sem.at[part]
        )

    def start(self, first=0, after=None):
        for part in range(len(self.parts))[first:after]:
            self.keep(part).start()

            @pl.loop(1, 4 * LAYERS)
            def _(step):
                self.copy(part, step).start()

    def wait_for(self, part):
        self.keep(part).wait()

        @pl.loop(1, 4 * LAYERS)
        def _(step):
            self.copy(part, step).wait()

    def wait(self, first=0):
        for part in range(first, len(self.parts)):
            self.wait_for(part)


def ride_scratch(parts):
    others = 4 * LAYERS - 1
    return [
        pltpu.SemaphoreType.DMA((parts, others)),
        pltpu.SemaphoreType.DMA((parts, others)),
        pltpu.SemaphoreType.DMA((parts,)),
    ]


class PairRide:
    def __init__(self, at, parts, send_sem, recv_sem, own_sem):
        self.at, self.parts = (at, parts)
        self.send_sem, self.recv_sem, self.own_sem = (send_sem, recv_sem, own_sem)
        self.steps = 2 * LAYERS

    def copy(self, part, step):
        source, target = self.parts[part]
        peer = (self.at.dp + 2 * step) % (4 * LAYERS)
        return remote(
            source(peer),
            target(self.at.dp),
            self.send_sem.at[part, step],
            self.recv_sem.at[part, step],
            (peer, self.at.core),
        )

    def keep(self, part):
        source, target = self.parts[part]
        return pltpu.make_async_copy(
            source(self.at.dp), target(self.at.dp), self.own_sem.at[part]
        )

    def onward(self, part, step):
        target = self.parts[part][1]
        chip = (self.at.dp + 4 * LAYERS - 2 * step) % (4 * LAYERS)
        return remote(
            target(chip),
            target(chip),
            self.send_sem.at[part, self.steps + step],
            self.recv_sem.at[part, self.steps + step],
            (self.at.x_mate, self.at.core),
        )

    def start(self):
        for part in range(len(self.parts)):
            self.keep(part).start()

            @pl.loop(1, self.steps)
            def _(step):
                self.copy(part, step).start()

    def forward(self):
        for part in range(len(self.parts)):
            self.keep(part).wait()

            @pl.loop(0, self.steps)
            def _(step):
                pl.when(step > 0)(lambda: self.copy(part, step).wait_recv())
                self.onward(part, step).start()

    def wait(self):
        for part in range(len(self.parts)):

            @pl.loop(0, self.steps)
            def _(step):
                self.onward(part, step).wait()
                pl.when(step > 0)(lambda: self.copy(part, step).wait_send())


def pair_ride_scratch(parts):
    return [
        pltpu.SemaphoreType.DMA((parts, 4 * LAYERS)),
        pltpu.SemaphoreType.DMA((parts, 4 * LAYERS)),
        pltpu.SemaphoreType.DMA((parts,)),
    ]


def strip(ref, axis, index, size):
    at = pl.ds(pl.multiple_of(index * size, size), size)
    return ref.at[at] if axis == 0 else ref.at[:, at]


def reduce_scratch(block, pieces, wide=True, pair=False):
    kind = jnp.bfloat16
    chips = 16 if wide else 8
    scratch = [
        pltpu.VMEM((chips,) + block, kind),
        pltpu.VMEM((8,) + block, kind),
        pltpu.VMEM((4,) + block, kind),
        pltpu.VMEM((8,) + block, kind),
        pltpu.SemaphoreType.DMA((20, pieces)),
        pltpu.SemaphoreType.DMA((20, pieces)),
    ]
    if pair:
        scratch += [pltpu.VMEM((chips,) + block, kind)] * 2
        scratch += [pltpu.SemaphoreType.DMA((chips,))] * 2
    return scratch


def mean_of_groups(sums, count):
    size = C // GROUPS
    channels = sums.shape[-1]
    row = lax.broadcasted_iota(jnp.int32, (channels, channels), 0) // size
    column = lax.broadcasted_iota(jnp.int32, (channels, channels), 1) // size
    same = jnp.where(row == column, 1.0 / (count * size), 0.0)
    return jnp.dot(sums, same, precision=HIGHEST, preferred_element_type=jnp.float32)


def side_by_side(maps, breadth, turned=False):
    positions = maps.shape[0]
    column = lax.broadcasted_iota(jnp.int32, maps.shape, 0) % breadth
    before = jnp.where(column == 0, 0.0, pltpu.roll(maps, 1, 0))
    after = jnp.where(column == breadth - 1, 0.0, pltpu.roll(maps, positions - 1, 0))
    three = (after, maps, before) if turned else (before, maps, after)
    return jnp.concatenate(three, axis=1)


def fold_three(products, breadth, turned=False):
    positions = products.shape[0]
    channels = products.shape[1] // 3
    left, middle, right = (products[:, tap * channels : (tap + 1) * channels] for tap in range(3))
    if turned:
        left, right = (right, left)
    column = lax.broadcasted_iota(jnp.int32, middle.shape, 0) % breadth
    before = jnp.where(column == 0, 0.0, pltpu.roll(left, 1, 0))
    after = jnp.where(column == breadth - 1, 0.0, pltpu.roll(right, positions - 1, 0))
    return before + middle + after


def fold_rows(above, same, below, breadth):
    edge = jnp.zeros((breadth, same.shape[1]), jnp.float32)
    count = same.shape[0] - breadth
    down = jnp.concatenate([edge, above[:count]], axis=0)
    up = jnp.concatenate([below[breadth:], edge], axis=0)
    return down + same + up


def silu(z):
    return z * jax.nn.sigmoid(z)


def store_padded(ref, index, maps, breadth):
    positions = maps.shape[0]
    edge = jnp.zeros((breadth, maps.shape[1]), ref.dtype)
    ref[index, pl.ds(0, breadth)] = edge
    ref[index, pl.ds(breadth, positions)] = maps.astype(ref.dtype)
    ref[index, pl.ds(breadth + positions, breadth)] = edge


def res_forward_kernel(
    breadth,
    gain_bias,
    conv_one,
    conv_two,
    conv_half,
    picks,
    res_table,
    ada_table,
    image_blocks,
    emb_blocks,
    qkv_blocks,
    out_blocks,
    up_rows,
    down_columns,
    pictures,
    emb,
    tokens,
    act_out,
    taps_one_out,
    taps_half,
    middle,
    stats,
    mods,
    qkv_head,
    out_head,
    up_here,
    down_here,
    arrived,
    mods_blocks,
    mods_terms,
    acts,
    taps_one,
    mine,
    theirs,
    pair_send,
    pair_recv,
    share_send,
    share_recv,
    out_sem,
    *scratch,
):
    first_reduce, (act_send, act_recv), last_reduce = (scratch[:6], scratch[6:8], scratch[8:14])
    at = Place(True)
    greet_all(at)

    rows, cols = (up_rows.shape[0], up_here.shape[1])
    near = 4 * LAYERS // qkv_blocks.shape[0]
    ride = Ride(
        at,
        [
            (lambda chip: emb_blocks.at[chip], lambda chip: emb.at[chip]),
            (lambda chip: image_blocks.at[chip], lambda chip: arrived.at[chip]),
            (lambda chip: strip(up_rows, 1, chip, cols), lambda chip: strip(up_here, 0, chip, rows)),
            (lambda chip: mods_blocks.at[chip], lambda chip: mods_terms.at[chip]),
            (lambda chip: strip(down_columns, 0, chip, cols), lambda chip: strip(down_here, 1, chip, rows)),
        ],
        *scratch[14:17],
    )
    attention = PairRide(
        at,
        [
            (lambda chip: qkv_blocks.at[chip // near], lambda chip: strip(qkv_head, 0, chip, rows)),
            (lambda chip: out_blocks.at[chip // near], lambda chip: strip(out_head, 1, chip, rows)),
        ],
        *scratch[17:20],
    )
    ride.start(0, 3)
    images, positions, channels = pictures.shape
    half_c = conv_one.shape[2]
    tokens_len = positions // 4

    ride.wait_for(0)
    emb_rows = emb[:, 0, : res_table.shape[0]].astype(jnp.bfloat16)
    lines = 0
    for table in (res_table, ada_table):
        terms = dot(emb_rows, table[...])
        for line in range(table.shape[1] // 128):
            mods_blocks[:, lines] = terms[:, 128 * line : 128 * (line + 1)]
            lines += 1
    ride.start(3, 4)
    ride.wait_for(1)

    @pl.loop(0, images)
    def _(i):
        both = arrived[i].astype(jnp.float32)
        sides = [both[:, :channels], both[:, channels:]]
        pictures[i] = jnp.concatenate(sides, axis=0).astype(jnp.bfloat16)

    attention.start()

    @pl.loop(0, images)
    def _(i):
        x = pictures[i].astype(jnp.float32)
        stats[0, pl.ds(i, 1)] = jnp.sum(x, axis=0, keepdims=True)

    stats[0] = mean_of_groups(stats[0], positions)

    @pl.loop(0, images)
    def _(i):
        x = pictures[i].astype(jnp.float32) - stats[0, pl.ds(i, 1)]
        stats[1, pl.ds(i, 1)] = jnp.sum(x * x, axis=0, keepdims=True)

    stats[1] = lax.rsqrt(mean_of_groups(stats[1], positions) + GN_EPS)

    @pl.loop(0, images)
    def _(i):
        normed = (pictures[i].astype(jnp.float32) - stats[0, pl.ds(i, 1)]) * stats[1, pl.ds(i, 1)]
        act = silu(normed * gain_bias[0:1] + gain_bias[1:2])
        store_padded(taps_one, i, side_by_side(act, breadth), breadth)

    save_taps = pltpu.make_async_copy(taps_one, taps_one_out, out_sem.at[0])
    save_taps.start()

    def first_product(slot):
        total = jnp.zeros((positions, conv_one.shape[2]), jnp.float32)
        for a in range(3):
            total += dot(taps_one[slot, pl.ds(a * breadth, positions)], conv_one[a])
        first_reduce[0][slot] = total.astype(jnp.bfloat16)

    reduce_stage(at, middle, first_product, 4, first_reduce)

    ride.start(4, 5)
    ride.wait_for(3)
    mods[at.core] = jnp.sum(mods_terms[...], axis=0)
    share_stage(at, mods, share_send.at[1], share_recv.at[1])

    def modulation(row):
        lines = half_c // 128
        parts = [mods[at.core, pl.ds(row * lines + i, 1)] for i in range(lines)]
        return jnp.concatenate(parts, axis=1)

    x = middle[...]
    center = mean_of_groups(jnp.sum(x, axis=0, keepdims=True), positions)
    x = x - center
    scale = lax.rsqrt(mean_of_groups(jnp.sum(x * x, axis=0, keepdims=True), positions) + GN_EPS)
    acts[at.slot] = silu(x * scale * (1.0 + modulation(0)) + modulation(1)).astype(jnp.bfloat16)

    def swap(slot):
        return remote(
            mine.at[slot],
            theirs.at[slot],
            pair_send.at[slot],
            pair_recv.at[slot],
            (at.dp, 1 - at.core),
        )

    def second_product(slot):
        act = acts[slot]
        above, same, below = (dot(act, conv_two[a]) for a in range(3))
        folded = fold_three(fold_rows(above, same, below, breadth), breadth)
        mine[slot] = folded.astype(jnp.bfloat16)
        swap(slot).start()

    gather_stage(at, [acts], second_product, 4, act_send, act_recv)
    save_acts = pltpu.make_async_copy(acts, act_out, out_sem.at[1])
    save_acts.start()
    attention.forward()

    def half_product(slot):
        swap(slot).wait_recv()
        branch = mine[slot].astype(jnp.float32) + theirs[slot].astype(jnp.float32)
        resid = (pictures[slot].astype(jnp.float32) + branch).astype(jnp.bfloat16)
        three = side_by_side(resid.astype(jnp.float32), breadth).astype(jnp.bfloat16)
        picked = dot(picks[...], three).astype(jnp.bfloat16)
        total = jnp.zeros((tokens_len, conv_half.shape[2]), jnp.float32)
        for a in range(3):
            part = picked[a * tokens_len : (a + 1) * tokens_len]
            taps_half[a, slot] = part
            total += dot(part, conv_half[a])
        last_reduce[0][slot] = total.astype(jnp.bfloat16)

    reduce_stage(at, tokens.at[at.core], half_product, 4, last_reduce)
    share_stage(at, tokens, share_send.at[0], share_recv.at[0])

    @pl.loop(0, images)
    def _(slot):
        swap(slot).wait_send()

    ride.wait_for(2)
    ride.wait_for(4)
    attention.wait()
    save_taps.wait()
    save_acts.wait()


def res_forward(number, height, breadth, *args):
    (gain_bias, conv_one, conv_two, conv_half, picks, res_table, ada_table, image_blocks, emb_blocks, qkv_blocks, out_blocks, up_rows, down_columns) = args
    images, positions, channels = (4 * LAYERS, height * breadth, gain_bias.shape[1])
    half_c = conv_one.shape[2]
    half_d = conv_half.shape[2]
    tokens_len = positions // 4
    three = 3 * channels
    rows, cols = (up_rows.shape[0], up_rows.shape[1] // images)
    low, full = (jnp.bfloat16, jnp.float32)
    pictures = (images, positions, channels)
    padded = (images, positions + 2 * breadth, three)
    acts = (images, positions, half_c)
    lines = (res_table.shape[1] + ada_table.shape[1]) // 128
    outs = [
        (pictures, low),
        (emb_blocks.shape, full),
        ((2, tokens_len, half_d), full),
        (acts, low),
        (padded, low),
        ((3, images, tokens_len, three), low),
        ((positions, half_c), full),
        ((2, images, channels), full),
        ((2, lines, 128), full),
        ((images * rows, qkv_blocks.shape[2]), low),
        ((out_blocks.shape[1], images * rows), low),
        ((images * rows, cols), low),
        ((cols, images * rows), low),
    ]
    return pl.pallas_call(
        functools.partial(res_forward_kernel, breadth),
        out_shape=[jax.ShapeDtypeStruct(shape, kind) for shape, kind in outs],
        in_specs=[IN_VMEM] * 7 + [ANYWHERE] * 6,
        out_specs=[IN_VMEM] * 3 + [ANYWHERE] * 2 + [IN_VMEM] * 4 + [ANYWHERE] * 4,
        scratch_shapes=[
            pltpu.VMEM(image_blocks.shape, low),
            pltpu.VMEM((images, lines, 128), full),
            pltpu.VMEM((images, lines, 128), full),
            pltpu.VMEM(acts, low),
            pltpu.VMEM(padded, low),
            pltpu.VMEM(pictures, low),
            pltpu.VMEM(pictures, low),
            pltpu.SemaphoreType.DMA((images,)),
            pltpu.SemaphoreType.DMA((images,)),
            pltpu.SemaphoreType.DMA((2,)),
            pltpu.SemaphoreType.DMA((2,)),
            pltpu.SemaphoreType.DMA((2,)),
        ]
        + reduce_scratch((positions, half_c), 4)
        + gather_scratch(4)
        + reduce_scratch((tokens_len, half_d), 4)
        + ride_scratch(5)
        + pair_ride_scratch(2),
        compiler_params=params(number),
        name="res_forward",
    )(*args)


def silu_slope(z):
    gate = jax.nn.sigmoid(z)
    return gate * (1.0 + z * (1.0 - gate))


def res_backward_kernel(
    breadth,
    shrunk,
    pictures,
    gain_bias,
    conv_one,
    conv_two,
    conv_half,
    mods,
    picks,
    taps_half,
    middle,
    stats,
    acts_in,
    taps_one_in,
    qkv_grad,
    out_grad,
    up_grad,
    ada_grad,
    pictures_out,
    norm_out,
    mods_back,
    ada_back,
    one_out,
    two_out,
    half_out,
    qkv_back,
    out_back,
    up_back,
    qkv_pair,
    out_pair,
    qkv_sums,
    out_sums,
    mods_block,
    gathered,
    gathered_middle,
    acts,
    taps_one,
    taps_two,
    mine,
    theirs,
    back,
    back_theirs,
    held,
    sums,
    outgoing,
    acted,
    one_grad,
    two_grad,
    half_grad,
    pair_send,
    pair_recv,
    back_send,
    back_recv,
    trade_send,
    trade_recv,
    io_sem,
    share_sem,
    neighbour_sem,
    store_sem,
    *scratch,
):
    (shrunk_send, shrunk_recv), (middle_send, middle_recv) = (scratch[:2], scratch[2:4])
    reducing = scratch[4:10]
    at = Place(True)
    images, positions, channels = pictures.shape
    others = images - 1
    tokens_len = positions // 4
    load_acts = pltpu.make_async_copy(acts_in, acts, io_sem.at[0])
    load_taps = pltpu.make_async_copy(taps_one_in, taps_one, io_sem.at[1])
    load_acts.start()
    load_taps.start()
    gathered[at.slot] = shrunk[at.core]

    greet_all(at)

    def peer(step):
        return (at.dp + step) % images

    rows, cols = (D // images, up_grad.shape[1])
    half = images // 2
    side = at.dp % 2

    def to_neighbour(part, place):
        chip = 2 * place + 1 - side
        source, target = (
            (strip(qkv_grad, 0, chip, rows), qkv_pair.at[place]),
            (strip(out_grad, 1, chip, rows), out_pair.at[place]),
        )[part]
        return remote(
            source,
            target,
            neighbour_sem.at[0, part, place],
            neighbour_sem.at[1, part, place],
            (at.x_mate, at.core),
        )

    def store(part, step):
        chip = (at.dp + 2 * step) % images
        source, target = ((qkv_sums, qkv_back), (out_sums, out_back))[part]
        return remote(
            source.at[chip // 2],
            target.at[at.dp // 2],
            store_sem.at[0, part, step],
            store_sem.at[1, part, step],
            (chip, at.core),
        )

    def store_own(part):
        source, target = ((qkv_sums, qkv_back), (out_sums, out_back))[part]
        return pltpu.make_async_copy(
            source.at[at.dp // 2], target.at[at.dp // 2], store_sem.at[0, part, 0]
        )

    def store_sums():
        @pl.loop(0, half)
        def _(place):
            chip = 2 * place + side
            to_neighbour(0, place).wait_recv()
            own = strip(qkv_grad, 0, chip, rows)[...].astype(jnp.float32)
            qkv_sums[place] = (own + qkv_pair[place].astype(jnp.float32)).astype(jnp.bfloat16)
            to_neighbour(1, place).wait_recv()
            own = strip(out_grad, 1, chip, rows)[...].astype(jnp.float32)
            out_sums[place] = (own + out_pair[place].astype(jnp.float32)).astype(jnp.bfloat16)

        for part in range(2):
            store_own(part).start()

            @pl.loop(1, half)
            def _(step):
                store(part, step).start()

    for part in range(2):

        @pl.loop(0, half)
        def _(place):
            to_neighbour(part, place).start()

    ride = Ride(
        at,
        [
            (lambda chip: ada_grad.at[at.core], lambda chip: ada_back.at[at.core, chip]),
            (lambda chip: mods_block, lambda chip: mods_back.at[chip]),
            (lambda chip: strip(up_grad, 0, chip, rows), lambda chip: strip(up_back, 1, chip, cols)),
        ],
        *scratch[10:],
    )
    ride.start(0, 1)

    def swap(slot):
        return remote(
            mine.at[slot],
            theirs.at[slot],
            pair_send.at[slot],
            pair_recv.at[slot],
            (at.dp, 1 - at.core),
        )

    def half_back(slot):
        products = [dot_nt(gathered[slot], conv_half[a]) for a in range(3)]
        products = jnp.concatenate(products, axis=0)
        coarse = products.astype(jnp.bfloat16)
        fine = (products - coarse.astype(jnp.float32)).astype(jnp.bfloat16)
        spread = dot_tn(picks[...], coarse) + dot_tn(picks[...], fine)
        mine[slot] = fold_three(spread, breadth, True).astype(jnp.bfloat16)
        swap(slot).start()

    gather_stage(at, [gathered], half_back, 4, shrunk_send, shrunk_recv)

    store_sums()

    def resid(slot):
        return mine[slot].astype(jnp.float32) + theirs[slot].astype(jnp.float32)

    def second_back(slot):
        swap(slot).wait_recv()
        branch = resid(slot).astype(jnp.bfloat16).astype(jnp.float32)
        store_padded(taps_two, slot, side_by_side(branch, breadth, True), breadth)
        total = jnp.zeros((positions, conv_two.shape[1]), jnp.float32)
        for a in range(3):
            total += dot_nt(taps_two[slot, pl.ds((2 - a) * breadth, positions)], conv_two[a])
        reducing[0][slot] = total.astype(jnp.bfloat16)

    def weights_meanwhile():
        half_grad[...] = jnp.zeros_like(half_grad)
        two_grad[...] = jnp.zeros_like(two_grad)
        load_acts.wait()

        @pl.loop(0, images // 4)
        def _(i):
            right = gathered[pl.ds(4 * i, 4)].reshape(4 * tokens_len, -1)
            for a in range(3):
                left = taps_half[a, pl.ds(4 * i, 4)].reshape(4 * tokens_len, 3 * channels)
                half_grad[a] += dot_tn(left, right)

        @pl.loop(0, images)
        def _(i):
            right = acts[i]
            for a in range(3):
                left = taps_two[i, pl.ds((2 - a) * breadth, positions)]
                two_grad[a] += dot_tn(left, right)

        save(half_grad, half_out, 2).start()
        save(two_grad, two_out, 3).start()

    def save(source, target, sem):
        return pltpu.make_async_copy(source, target, io_sem.at[sem])

    reduce_stage(at, acted, second_back, 4, reducing, False, weights_meanwhile)

    x = middle[...]
    center = mean_of_groups(jnp.sum(x, axis=0, keepdims=True), positions)
    x = x - center
    scale = lax.rsqrt(mean_of_groups(jnp.sum(x * x, axis=0, keepdims=True), positions) + GN_EPS)
    normed = x * scale
    slope = 1.0 + mods[0:1]
    grad = acted[...] * silu_slope(normed * slope + mods[1:2])
    along = jnp.sum(grad * normed, axis=0, keepdims=True)
    level = jnp.sum(grad, axis=0, keepdims=True)
    lines = along.shape[1] // 128
    for i in range(lines):
        mods_block[i : i + 1] = along[:, 128 * i : 128 * (i + 1)]
        mods_block[lines + i : lines + i + 1] = level[:, 128 * i : 128 * (i + 1)]
    ride.start(1, 2)
    ride.start(2, 3)
    along = mean_of_groups(slope * along, positions)
    level = mean_of_groups(slope * level, positions)
    gathered_middle[at.slot] = ((slope * grad - level - normed * along) * scale).astype(jnp.bfloat16)

    def swap_back(slot):
        return remote(
            back.at[slot],
            back_theirs.at[slot],
            back_send.at[slot],
            back_recv.at[slot],
            (at.dp, 1 - at.core),
        )

    def first_back(slot):
        below, same, above = (dot_nt(gathered_middle[slot], conv_one[a]) for a in range(3))
        folded = fold_three(fold_rows(above, same, below, breadth), breadth, True)
        back[slot] = folded.astype(jnp.bfloat16)
        swap_back(slot).start()

    gather_stage(at, [gathered_middle], first_back, 4, middle_send, middle_recv)

    gain, bias = (gain_bias[0:1], gain_bias[1:2])

    def normed_of(i):
        return (pictures[i].astype(jnp.float32) - stats[0, pl.ds(i, 1)]) * stats[1, pl.ds(i, 1)]

    @pl.loop(0, images)
    def _(i):
        swap_back(i).wait_recv()
        grad = back[i].astype(jnp.float32) + back_theirs[i].astype(jnp.float32)
        normed = normed_of(i)
        grad = grad * silu_slope(normed * gain + bias)
        held[i] = grad
        sums[0, pl.ds(i, 1)] = jnp.sum(grad * normed, axis=0, keepdims=True)
        sums[1, pl.ds(i, 1)] = jnp.sum(grad, axis=0, keepdims=True)

    norm_out[0:1] = jnp.sum(sums[0], axis=0, keepdims=True)
    norm_out[1:2] = jnp.sum(sums[1], axis=0, keepdims=True)
    sums[0] = mean_of_groups(gain * sums[0], positions)
    sums[1] = mean_of_groups(gain * sums[1], positions)

    def deliver(step):
        return remote(
            outgoing.at[peer(step)],
            pictures_out.at[at.dp],
            trade_send.at[step - 1],
            trade_recv.at[step - 1],
            (peer(step), at.core),
        )

    keep = save(outgoing.at[at.dp], pictures_out.at[at.dp], 5)

    @pl.loop(0, images)
    def _(step):
        i = peer(step)
        part = gain * held[i] - sums[1, pl.ds(i, 1)] - normed_of(i) * sums[0, pl.ds(i, 1)]
        part = resid(i) + part * stats[1, pl.ds(i, 1)]
        half = positions // 2
        outgoing[i] = jnp.concatenate([part[:half], part[half:]], axis=1).astype(jnp.bfloat16)
        pl.when(step == 0)(keep.start)
        pl.when(step > 0)(lambda: deliver(step).start())

    one_grad[...] = jnp.zeros_like(one_grad)
    load_taps.wait()

    @pl.loop(0, images)
    def _(i):
        right = gathered_middle[i]
        for a in range(3):
            one_grad[a] += dot_tn(taps_one[i, pl.ds(a * breadth, positions)], right)

    save(one_grad, one_out, 4).start()

    @pl.loop(0, images)
    def _(slot):
        swap(slot).wait_send()
        swap_back(slot).wait_send()

    keep.wait()

    ride.wait()
    for part in range(2):
        store_own(part).wait()

        @pl.loop(0, half)
        def _(step):
            to_neighbour(part, step).wait_send()
            pl.when(step > 0)(lambda: store(part, step).wait())

    share_stage(at, ada_back, share_sem.at[0], share_sem.at[1])

    @pl.loop(1, others + 1)
    def _(step):
        deliver(step).wait()

    save(half_grad, half_out, 2).wait()
    save(two_grad, two_out, 3).wait()
    save(one_grad, one_out, 4).wait()


def res_backward(number, breadth, *args):
    (shrunk, pictures, gain_bias, conv_one, conv_two, conv_half, mods, picks, taps_half, middle, stats, acts, taps_one, qkv_grad, out_grad, up_grad, ada_grad) = args
    images, positions, channels = pictures.shape
    half_c = conv_one.shape[2]
    half_d = conv_half.shape[2]
    tokens_len = positions // 4
    three = 3 * channels
    low, full = (jnp.bfloat16, jnp.float32)
    rows = qkv_grad.shape[0] // images
    grads = [(3, three, half_c), (3, three, half_c), (3, three, half_d)]
    traded = (images, positions // 2, 2 * channels)
    return pl.pallas_call(
        functools.partial(res_backward_kernel, breadth),
        out_shape=[
            jax.ShapeDtypeStruct(traded, low),
            jax.ShapeDtypeStruct((2, channels), full),
            jax.ShapeDtypeStruct((images, 2 * half_c // 128, 128), full),
            jax.ShapeDtypeStruct((2, images) + ada_grad.shape[1:], ada_grad.dtype),
        ]
        + [jax.ShapeDtypeStruct(shape, full) for shape in grads]
        + [
            jax.ShapeDtypeStruct((images // 2, rows, qkv_grad.shape[1]), low),
            jax.ShapeDtypeStruct((images // 2, out_grad.shape[0], rows), low),
            jax.ShapeDtypeStruct((rows, images * up_grad.shape[1]), low),
        ],
        in_specs=[IN_VMEM] * 11 + [ANYWHERE] * 2 + [IN_VMEM] * 2 + [ANYWHERE] * 2,
        out_specs=[ANYWHERE, IN_VMEM] + [ANYWHERE] * 8,
        scratch_shapes=[
            pltpu.VMEM((images // 2, rows, qkv_grad.shape[1]), low),
            pltpu.VMEM((images // 2, out_grad.shape[0], rows), low),
            pltpu.VMEM((images // 2, rows, qkv_grad.shape[1]), low),
            pltpu.VMEM((images // 2, out_grad.shape[0], rows), low),
            pltpu.VMEM((2 * half_c // 128, 128), full),
            pltpu.VMEM((images, tokens_len, half_d), low),
            pltpu.VMEM((images, positions, half_c), low),
            pltpu.VMEM(acts.shape, low),
            pltpu.VMEM(taps_one.shape, low),
            pltpu.VMEM(taps_one.shape, low),
            pltpu.VMEM(pictures.shape, low),
            pltpu.VMEM(pictures.shape, low),
            pltpu.VMEM(pictures.shape, low),
            pltpu.VMEM(pictures.shape, low),
            pltpu.VMEM(pictures.shape, full),
            pltpu.VMEM((2, images, channels), full),
            pltpu.VMEM(traded, low),
            pltpu.VMEM((positions, half_c), full),
        ]
        + [pltpu.VMEM(shape, full) for shape in grads]
        + [pltpu.SemaphoreType.DMA((images,))] * 4
        + [pltpu.SemaphoreType.DMA((images - 1,))] * 2
        + [pltpu.SemaphoreType.DMA((6,)), pltpu.SemaphoreType.DMA((2,))]
        + [pltpu.SemaphoreType.DMA((2, 2, images // 2))] * 2
        + gather_scratch(4)
        + gather_scratch(4)
        + reduce_scratch((positions, half_c), 4)
        + ride_scratch(3),
        compiler_params=params(number),
        name="res_backward",
    )(*args)


def gelu_of(z):
    inner = jnp.tanh(math.sqrt(2.0 / math.pi) * (z + 0.044715 * z * z * z))
    return 0.5 * z * (1.0 + inner)


def gelu_slope(z):
    rate = math.sqrt(2.0 / math.pi)
    inner = jnp.tanh(rate * (z + 0.044715 * z * z * z))
    return 0.5 * (1.0 + inner) + 0.5 * z * (1.0 - inner * inner) * rate * (1.0 + 3 * 0.044715 * z * z)


def transformer_kernel(
    shrunk,
    mods,
    cotangent,
    qkv_head,
    out_head,
    up_here,
    down_here,
    block_out,
    token_grad,
    mods_grad,
    qkv_grad,
    out_grad,
    up_grad,
    down_back,
    tokens,
    held,
    attn_in,
    qkv,
    probs,
    mixed,
    attended,
    mlp_in,
    expanded_grad,
    pre_act,
    hidden,
    pre_grad,
    expanded,
    mlp_grad,
    down_grad,
    attended_grad,
    mixed_grad,
    qkv_back,
    attn_grad,
    share_send,
    share_recv,
    *scratch,
):
    scratch = list(scratch)

    def take(count):
        taken = scratch[:count]
        del scratch[:count]
        return taken

    gather_one, gather_two, gather_three = (take(4), take(4), take(4))
    reduce_one, reduce_two, reduce_three, reduce_four = (take(10), take(10), take(10), take(10))
    ride_back = take(3)
    at, near = (Place(True), Place(False))
    greet_all(at)
    tokens_len = cotangent.shape[0]
    half = tokens_len // 2
    rows, cols = (D // (4 * LAYERS), up_here.shape[1])
    images = 4 * LAYERS
    score_scale = HDIM ** (-0.5)
    low, full = (jnp.bfloat16, jnp.float32)
    mine = pl.ds(pl.multiple_of(at.core * half, half), half)
    theirs = pl.ds(pl.multiple_of((1 - at.core) * half, half), half)

    def own_rows(value, out):
        held[...] = value.astype(low)
        out[...] = held[mine]

    def split(place, value, stage):
        held[...] = value.astype(low)
        stage[0][place] = held[mine]
        stage[6][place] = held[theirs]

    def image_rows(i):
        return pl.ds(pl.multiple_of(i * tokens_len, tokens_len), tokens_len)

    tokens[:, : shrunk.shape[2]] = shrunk[0]
    tokens[:, shrunk.shape[2] :] = shrunk[1]
    normed, _ = layer_stats(tokens[...])
    own_rows(normed * (1.0 + mods[1:2]) + mods[0:1], attn_in.at[near.slot, near.core])
    gather_stage(near, [attn_in], None, 4, *gather_one[:2], gather_one[2:])

    @pl.loop(0, images // 2)
    def _(i):
        rows_in = attn_in[i].reshape(tokens_len, D)
        low_qkv = dot(rows_in, qkv_head[...]).astype(low)
        qkv[image_rows(i)] = low_qkv
        query, key, value = (low_qkv[:, j * HDIM : (j + 1) * HDIM] for j in range(3))
        scores = dot_nt(query, key) * score_scale
        scores = scores - jnp.max(scores, axis=1, keepdims=True)
        weight = jnp.exp(scores)
        weight = weight / jnp.sum(weight, axis=1, keepdims=True)
        probs[i] = weight
        mixed[image_rows(i)] = dot(weight.astype(low), value).astype(low)

    def attention_term(place):
        split(place, dot(mixed[image_rows(place)], out_head[...]), reduce_one)

    reduce_stage(near, attended.at[at.core], attention_term, 4, reduce_one, True)
    share_stage(at, attended, share_send.at[0], share_recv.at[0])

    def whole(ref):
        return ref[...].reshape(tokens_len, D)

    after = tokens[...] + (1.0 + mods[2:3]) * whole(attended)
    normed, _ = layer_stats(after)
    own_rows(normed * (1.0 + mods[4:5]) + mods[3:4], mlp_in.at[at.slot, at.core])
    own_rows(
        (1.0 + mods[5:6]) * cotangent[...].astype(full), expanded_grad.at[at.slot, at.core]
    )
    gather_stage(at, [mlp_in, expanded_grad], None, 4, *gather_two[:2], gather_two[2:])

    @pl.loop(0, LAYERS)
    def _(i):
        here = pl.ds(pl.multiple_of(i * 4 * tokens_len, 4 * tokens_len), 4 * tokens_len)
        z = dot(mlp_in[pl.ds(4 * i, 4)].reshape(4 * tokens_len, D), up_here[...])
        pre_act[here] = z
        hidden[here] = gelu_of(z).astype(low)

    def hidden_term(place):
        split(place, dot(hidden[image_rows(place)], down_here[...]), reduce_two)

    def hidden_grads():
        @pl.loop(0, LAYERS)
        def _(i):
            here = pl.ds(pl.multiple_of(i * 4 * tokens_len, 4 * tokens_len), 4 * tokens_len)
            grad = dot_nt(expanded_grad[pl.ds(4 * i, 4)].reshape(4 * tokens_len, D), down_here[...])
            pre_grad[here] = (grad * gelu_slope(pre_act[here])).astype(low)

        @pl.loop(0, D // 512)
        def _(i):
            here = pl.ds(pl.multiple_of(i * 512, 512), 512)
            left = expanded_grad[:, :, :, here].reshape(images * tokens_len, 512)
            down_grad[:, here] = dot_tn(hidden[...], left).astype(low)
            right = mlp_in[:, :, :, here].reshape(images * tokens_len, 512)
            up_grad[here] = dot_tn(right, pre_grad[...]).astype(low)

    reduce_stage(at, expanded.at[at.core], hidden_term, 4, reduce_two, True, hidden_grads)
    back = Ride(
        at,
        [
            (lambda chip: strip(down_grad, 1, chip, rows), lambda chip: strip(down_back, 0, chip, cols)),
        ],
        *ride_back,
    )
    back.start()
    share_stage(at, expanded, share_send.at[1], share_recv.at[1])
    block_out[...] = (after + (1.0 + mods[5:6]) * whole(expanded)).astype(low)
    upstream = cotangent[...].astype(full)
    mods_grad[5:6] = jnp.sum(upstream * whole(expanded), axis=0, keepdims=True)

    def mlp_term(place):
        split(place, dot_nt(pre_grad[image_rows(place)], up_here[...]), reduce_three)

    reduce_stage(at, mlp_grad.at[at.core], mlp_term, 4, reduce_three, True)
    share_stage(at, mlp_grad, share_send.at[2], share_recv.at[2])
    after = tokens[...] + (1.0 + mods[2:3]) * whole(attended)
    normed, scale = layer_stats(after)
    grad = whole(mlp_grad)
    mods_grad[3:4] = jnp.sum(grad, axis=0, keepdims=True)
    mods_grad[4:5] = jnp.sum(grad * normed, axis=0, keepdims=True)
    grad_after = cotangent[...].astype(full) + layer_back(normed, scale, (1.0 + mods[4:5]) * grad)
    mods_grad[2:3] = jnp.sum(grad_after * whole(attended), axis=0, keepdims=True)

    own_rows((1.0 + mods[2:3]) * grad_after, attended_grad.at[near.slot, near.core])
    attended[...] = grad_after.reshape(attended.shape)
    gather_stage(near, [attended_grad], None, 4, *gather_three[:2], gather_three[2:])

    @pl.loop(0, images // 2)
    def _(i):
        grad = dot_nt(attended_grad[i].reshape(tokens_len, D), out_head[...]).astype(low)
        low_qkv = qkv[image_rows(i)]
        query, key, value = (low_qkv[:, j * HDIM : (j + 1) * HDIM] for j in range(3))
        weight = probs[i]
        grad_probs = dot_nt(grad, value)
        grad_value = dot_tn(weight.astype(low), grad)
        inner = jnp.sum(grad_probs * weight, axis=1, keepdims=True)
        grad_scores = (weight * (grad_probs - inner)).astype(low)
        grad_query = dot(grad_scores, key) * score_scale
        grad_key = dot_tn(grad_scores, query) * score_scale
        qkv_back[image_rows(i)] = jnp.concatenate(
            [grad_query, grad_key, grad_value], axis=1
        ).astype(low)

    def qkv_term(place):
        split(place, dot_nt(qkv_back[image_rows(place)], qkv_head[...]), reduce_four)

    def attention_grads():
        @pl.loop(0, D // 512)
        def _(i):
            here = pl.ds(pl.multiple_of(i * 512, 512), 512)
            right = attended_grad[:, :, :, here].reshape(images // 2 * tokens_len, 512)
            out_grad[:, here] = dot_tn(mixed[...], right).astype(low)
            left = attn_in[:, :, :, here].reshape(images // 2 * tokens_len, 512)
            qkv_grad[here] = dot_tn(left, qkv_back[...]).astype(low)

    reduce_stage(near, attn_grad.at[at.core], qkv_term, 4, reduce_four, True, attention_grads)
    share_stage(at, attn_grad, share_send.at[3], share_recv.at[3])
    normed, scale = layer_stats(tokens[...])
    grad = whole(attn_grad)
    mods_grad[0:1] = jnp.sum(grad, axis=0, keepdims=True)
    mods_grad[1:2] = jnp.sum(grad * normed, axis=0, keepdims=True)
    grad = whole(attended) + layer_back(normed, scale, (1.0 + mods[1:2]) * grad)
    token_grad[0] = grad[:, : shrunk.shape[2]].astype(low)
    token_grad[1] = grad[:, shrunk.shape[2] :].astype(low)
    back.wait()


def transformer(number, *args):
    shrunk, mods, cotangent, qkv_head, out_head, up_here, down_here = args
    tokens_len = cotangent.shape[0]
    images = 4 * LAYERS
    half = tokens_len // 2
    rows, cols = (D // images, up_here.shape[1])
    low, full = (jnp.bfloat16, jnp.float32)
    both = (2, half, D)
    near_tokens = images // 2 * tokens_len
    vmem = [
        ((tokens_len, D), full),
        ((tokens_len, D), low),
        ((images // 2,) + both, low),
        ((near_tokens, 3 * HDIM), low),
        ((images // 2, tokens_len, tokens_len), full),
        ((near_tokens, HDIM), low),
        (both, full),
        ((images,) + both, low),
        ((images,) + both, low),
        ((images * tokens_len, cols), full),
        ((images * tokens_len, cols), low),
        ((images * tokens_len, cols), low),
        (both, full),
        (both, full),
        ((cols, D), low),
        ((images // 2,) + both, low),
        ((near_tokens, HDIM), low),
        ((near_tokens, 3 * HDIM), low),
        (both, full),
    ]
    return pl.pallas_call(
        transformer_kernel,
        out_shape=[
            jax.ShapeDtypeStruct((tokens_len, D), low),
            jax.ShapeDtypeStruct(shrunk.shape, low),
            jax.ShapeDtypeStruct(mods.shape, full),
            jax.ShapeDtypeStruct(qkv_head.shape, low),
            jax.ShapeDtypeStruct(out_head.shape, low),
            jax.ShapeDtypeStruct((D, cols), low),
            jax.ShapeDtypeStruct((images * cols, rows), low),
        ],
        in_specs=[IN_VMEM] * 7,
        out_specs=[IN_VMEM] * 6 + [ANYWHERE],
        scratch_shapes=[pltpu.VMEM(shape, kind) for shape, kind in vmem]
        + [pltpu.SemaphoreType.DMA((4,))] * 2
        + gather_scratch(4, 1, False, True)
        + gather_scratch(4, 2, True, True)
        + gather_scratch(4, 1, False, True)
        + reduce_scratch((half, D), 4, False, True)
        + reduce_scratch((half, D), 4, True, True) * 2
        + reduce_scratch((half, D), 4, False, True)
        + ride_scratch(1),
        compiler_params=params(number),
        name="transformer",
    )(*args)


def layer_stats(values):
    center = jnp.mean(values, axis=-1, keepdims=True)
    shifted = values - center
    spread = jnp.mean(shifted * shifted, axis=-1, keepdims=True)
    scale = lax.rsqrt(spread + LN_EPS)
    return shifted * scale, scale


def layer_back(normed, scale, grad):
    first = jnp.mean(grad, axis=-1, keepdims=True)
    second = jnp.mean(grad * normed, axis=-1, keepdims=True)
    return (grad - first - normed * second) * scale


def widen(block):
    return block.astype(jnp.float32)


def lower(block):
    return block.astype(jnp.bfloat16)


def paired_lanes(block):
    half = block.shape[-2] // 2
    return jnp.concatenate([block[..., :half, :], block[..., half:, :]], axis=-1)


def unpaired_lanes(block):
    half = block.shape[-1] // 2
    return jnp.concatenate([block[..., :half], block[..., half:]], axis=-2)


def half_picks(height, breadth):
    outputs = height * breadth // 4
    tap, out = (jnp.arange(3 * outputs) // outputs, jnp.arange(3 * outputs) % outputs)
    row = 2 * (out // (breadth // 2)) + tap - 1
    source = row * breadth + 2 * (out % (breadth // 2))
    place = jnp.arange(height * breadth)
    return ((place[None, :] == source[:, None]) & (row[:, None] >= 0)).astype(jnp.bfloat16)


def dot(left, right):
    return jnp.dot(left, right, preferred_element_type=jnp.float32)


def dot_tn(left, right):
    return lax.dot_general(left, right, (((0,), (0,)), ((), ())), preferred_element_type=jnp.float32)


def dot_nt(left, right):
    return lax.dot_general(left, right, (((1,), (1,)), ((), ())), preferred_element_type=jnp.float32)


def stationary(
    images,
    t_index,
    cotangent,
    norm_params,
    norm_params_avg,
    norm_params_sq,
    first_conv,
    first_conv_avg,
    first_conv_sq,
    resnet_mod,
    resnet_mod_avg,
    resnet_mod_sq,
    second_conv,
    second_kernel_first_moment,
    second_conv_sq,
    down_conv,
    down_conv_avg,
    down_conv_sq,
    ada_proj,
    ada_proj_avg,
    ada_proj_sq,
    qkv_proj,
    qkv_proj_avg,
    qkv_proj_sq,
    out_proj,
    out_proj_avg,
    out_proj_sq,
    hidden_in,
    hidden_in_avg,
    hidden_in_sq,
    hidden_out,
    hidden_out_avg,
    hidden_out_sq,
):
    masters = (
        norm_params,
        first_conv,
        resnet_mod,
        second_conv,
        down_conv,
        ada_proj,
        qkv_proj,
        out_proj,
        hidden_in,
        hidden_out,
    )
    averages = (
        norm_params_avg,
        first_conv_avg,
        resnet_mod_avg,
        second_kernel_first_moment,
        down_conv_avg,
        ada_proj_avg,
        qkv_proj_avg,
        out_proj_avg,
        hidden_in_avg,
        hidden_out_avg,
    )
    squares = (
        norm_params_sq,
        first_conv_sq,
        resnet_mod_sq,
        second_conv_sq,
        down_conv_sq,
        ada_proj_sq,
        qkv_proj_sq,
        out_proj_sq,
        hidden_in_sq,
        hidden_out_sq,
    )
    n_dp = lax.axis_size(DP)
    dp_pos = lax.axis_index(DP)
    tensor_pos = lax.axis_index(TENSOR)
    height, breadth = (images.shape[1], images.shape[2])
    positions = height * breadth
    tokens_len = positions // 4
    local_c = C // n_dp
    half_c = first_conv.shape[3]
    half_d = down_conv.shape[3]
    freq_rows = resnet_mod.shape[0]
    heads_here = out_proj.shape[0]
    picks = half_picks(height, breadth)
    numbers = itertools.count()

    def sum_all(local):
        return total(next(numbers), jnp.full((8, 128), local))[0, 0]

    gain_bias = widen(lower(norm_params))
    conv_one = lower(first_conv).reshape(3, 3 * local_c, half_c)
    conv_two = lower(second_conv).transpose(0, 2, 1, 3).reshape(3, half_c, 3 * local_c)
    conv_half = lower(down_conv).reshape(3, 3 * local_c, half_d)
    qkv_blocks = lower(qkv_proj).transpose(2, 0, 1, 3).reshape(heads_here, D // n_dp, 3 * HDIM)

    emb = widen(lower(embed_noise(t_index, FREQ))).reshape(n_dp, 1, freq_rows)
    emb = jnp.pad(emb, ((0, 0), (0, 7), (0, 128 - freq_rows)))
    image_blocks = images.reshape(positions, n_dp, local_c).transpose(1, 0, 2)
    ada_half = lax.dynamic_slice_in_dim(ada_proj, tensor_pos * 3, 3, axis=1)
    convs = (conv_one, conv_two, conv_half)

    pictures, emb, shrunk, act_two, taps_one, taps_half, middle, stats_one, mods, *heads = res_forward(
        next(numbers),
        height,
        breadth,
        gain_bias,
        *convs,
        picks,
        lower(resnet_mod).reshape(freq_rows, 2 * half_c),
        lower(ada_half).reshape(freq_rows, 3 * D),
        paired_lanes(image_blocks),
        emb,
        qkv_blocks,
        lower(out_proj),
        lower(hidden_in),
        lower(hidden_out),
    )
    qkv_head, out_head, up_here, down_here = heads
    res_lines = 2 * half_c // 128
    res_mods = lax.dynamic_index_in_dim(mods, tensor_pos, 0, keepdims=False)[:res_lines]
    res_mods = res_mods.reshape(2, half_c)
    ada_mods = mods[:, res_lines:].reshape(6, D)

    block_out, grad_tokens, grad_ada, grad_qkv_w, grad_out, grad_up, grad_down = transformer(
        next(numbers),
        shrunk,
        ada_mods,
        cotangent.reshape(tokens_len, D),
        qkv_head,
        out_head,
        up_here,
        down_here,
    )
    grad_ada = lower(grad_ada).reshape(2, 3 * D // 128, 128)

    images_grad, grad_norm_params, grad_res, grad_ada, *returned = res_backward(
        next(numbers),
        breadth,
        grad_tokens,
        pictures,
        gain_bias,
        *convs,
        res_mods,
        picks,
        taps_half,
        middle,
        stats_one,
        act_two,
        taps_one,
        grad_qkv_w,
        grad_out,
        grad_up,
        grad_ada,
    )
    grad_conv_one, grad_conv_two, grad_half, grad_qkv_w, grad_out, grad_up = returned
    images_grad = widen(unpaired_lanes(images_grad))
    images_grad = images_grad.transpose(1, 0, 2).reshape((1, height, breadth, C))

    emb_cols = emb[:, 0, :freq_rows]
    grad_ada = widen(grad_ada).reshape(2, n_dp, 3 * D)
    grad_ada = jnp.einsum("bf,cbk->fck", emb_cols, grad_ada, precision=HIGHEST)
    grad_res = jnp.einsum("bf,bk->fk", emb_cols, grad_res.reshape(n_dp, -1), precision=HIGHEST)

    grad_qkv_w = widen(grad_qkv_w).reshape(heads_here, D // n_dp, 3, HDIM).transpose(1, 2, 0, 3)

    combined_total = (
        grad_norm_params,
        grad_conv_one.reshape(first_conv.shape),
        grad_res.reshape(resnet_mod.shape),
        grad_conv_two.reshape(3, 3, local_c, half_c).transpose(0, 1, 3, 2),
        grad_half.reshape(down_conv.shape),
        grad_ada.reshape(ada_proj.shape),
        grad_qkv_w,
        widen(grad_out),
        widen(grad_up),
        widen(grad_down),
    )
    results = clipped_step(masters, averages, squares, combined_total, sum_all)
    return (block_out[None], images_grad) + results


def solution(mesh):
    in_specs = (
        P(DP, None, None, None),
        P(DP),
        P(DP, None, None),
        P(None, DP),
        P(None, DP),
        P(None, DP),
        P(None, None, DP, TENSOR),
        P(None, None, DP, TENSOR),
        P(None, None, DP, TENSOR),
        P(DP, None, TENSOR),
        P(DP, None, TENSOR),
        P(DP, None, TENSOR),
        P(None, None, TENSOR, DP),
        P(None, None, TENSOR, DP),
        P(None, None, TENSOR, DP),
        P(None, None, DP, TENSOR),
        P(None, None, DP, TENSOR),
        P(None, None, DP, TENSOR),
        P(DP, None, None),
        P(DP, None, None),
        P(DP, None, None),
        P(DP, None, TENSOR, None),
        P(DP, None, TENSOR, None),
        P(DP, None, TENSOR, None),
        P(TENSOR, None, DP),
        P(TENSOR, None, DP),
        P(TENSOR, None, DP),
        P(DP, TENSOR),
        P(DP, TENSOR),
        P(DP, TENSOR),
        P(TENSOR, DP),
        P(TENSOR, DP),
        P(TENSOR, DP),
    )
    out_specs = (
        P(DP, None, None),
        P(DP, None, None, None),
        P(),
        P(None, DP),
        P(None, DP),
        P(None, DP),
        P(None, None, DP, TENSOR),
        P(None, None, DP, TENSOR),
        P(None, None, DP, TENSOR),
        P(DP, None, TENSOR),
        P(DP, None, TENSOR),
        P(DP, None, TENSOR),
        P(None, None, TENSOR, DP),
        P(None, None, TENSOR, DP),
        P(None, None, TENSOR, DP),
        P(None, None, DP, TENSOR),
        P(None, None, DP, TENSOR),
        P(None, None, DP, TENSOR),
        P(DP, None, None),
        P(DP, None, None),
        P(DP, None, None),
        P(DP, None, TENSOR, None),
        P(DP, None, TENSOR, None),
        P(DP, None, TENSOR, None),
        P(TENSOR, None, DP),
        P(TENSOR, None, DP),
        P(TENSOR, None, DP),
        P(DP, TENSOR),
        P(DP, TENSOR),
        P(DP, TENSOR),
        P(TENSOR, DP),
        P(TENSOR, DP),
        P(TENSOR, DP),
    )
    moves_activations = mesh.shape[DP] == 4 * LAYERS and mesh.shape[TENSOR] == 2
    return jax.shard_map(
        stationary if moves_activations else per_device, mesh=mesh, in_specs=in_specs, out_specs=out_specs, check_vma=False
    )
```

```python
import functools
import itertools
import math

import jax
import jax.numpy as jnp
from jax import lax
from jax.experimental import pallas as pl
from jax.experimental.pallas import tpu as pltpu
from jax.sharding import PartitionSpec as P

DP, TENSOR = ("dp", "tensor")
C = 1024
D = 2048
HEADS = 16
HDIM = 128
FF = 8192
GROUPS = 32
FREQ = 256
STEP = 5


GN_EPS = 1e-05
LN_EPS = 1e-06
CLIP = 1.0
BETA_ONE = 0.5
BETA_TWO = 0.5
ADAM_EPS = 1e-08
DECAY = 0.1
LR_SCALE = 2.0
LR_NORM = 0.5
PLAN = 1000.0
HIGHEST = lax.Precision.HIGHEST


def embed_noise(t_index, emb_width):
    fraction = (t_index.astype(jnp.float32) + 0.5) / PLAN
    logsnr = -2.0 * jnp.log(jnp.tan(0.5 * math.pi * fraction)) + 2.0 * math.log(64.0 / 512.0)
    half_width = emb_width // 2
    frequencies = jnp.exp(
        -math.log(10000.0) * jnp.arange(half_width, dtype=jnp.float32) / half_width
    )
    angles = logsnr[:, None] * frequencies[None, :]
    return jnp.concatenate([jnp.sin(angles), jnp.cos(angles)], axis=1)


def group_norm(values, group_size):
    dims_of = values.shape
    grouped = values.reshape(dims_of[:-1] + (dims_of[-1] // group_size, group_size))
    center = jnp.mean(grouped, axis=(1, 2, 4), keepdims=True)
    shifted = grouped - center
    spread = jnp.mean(shifted * shifted, axis=(1, 2, 4), keepdims=True)
    return (shifted * lax.rsqrt(spread + GN_EPS)).reshape(dims_of)


def layer_norm(values):
    center = jnp.mean(values, axis=-1, keepdims=True)
    shifted = values - center
    spread = jnp.mean(shifted * shifted, axis=-1, keepdims=True)
    return shifted * lax.rsqrt(spread + LN_EPS)


def leading_segment(picture, gain_bias):
    return jax.nn.silu(group_norm(picture, C // GROUPS) * gain_bias[0] + gain_bias[1])


def second_piece(middle, res_mods):
    return jax.nn.silu(
        group_norm(middle, C // GROUPS) * (1.0 + res_mods[:, None, None, 0])
        + res_mods[:, None, None, 1]
    )


def modulate(tokens, shift_scale):
    return layer_norm(tokens) * (1.0 + shift_scale[:, None, 1]) + shift_scale[:, None, 0]


def gelu_tanh(values):
    return jax.nn.gelu(values, approximate=True)


def conv_same(inputs, kernel):
    height, breadth = (inputs.shape[1], inputs.shape[2])
    padded = jnp.pad(inputs, ((0, 0), (1, 1), (1, 1), (0, 0)))
    summed_taps = jnp.zeros(inputs.shape[:3] + (kernel.shape[3],), jnp.float32)
    for row_tap in range(3):
        for col_tap in range(3):
            window = padded[:, row_tap : row_tap + height, col_tap : col_tap + breadth]
            summed_taps = summed_taps + jnp.einsum(
                "bhwc,cd->bhwd",
                window,
                kernel[row_tap, col_tap],
                preferred_element_type=jnp.float32,
            )
    return summed_taps


def conv_same_input(upstream, kernel):
    height, breadth = (upstream.shape[1], upstream.shape[2])
    padded = jnp.pad(upstream, ((0, 0), (1, 1), (1, 1), (0, 0)))
    summed_taps = jnp.zeros(upstream.shape[:3] + (kernel.shape[2],), jnp.float32)
    for row_tap in range(3):
        for col_tap in range(3):
            window = padded[
                :, 2 - row_tap : 2 - row_tap + height, 2 - col_tap : 2 - col_tap + breadth
            ]
            summed_taps = summed_taps + jnp.einsum(
                "bhwd,cd->bhwc",
                window,
                kernel[row_tap, col_tap],
                preferred_element_type=jnp.float32,
            )
    return summed_taps


def conv_same_kernel(inputs, upstream):
    height, breadth = (inputs.shape[1], inputs.shape[2])
    padded = jnp.pad(inputs, ((0, 0), (1, 1), (1, 1), (0, 0)))
    tap_list = []
    for row_tap in range(3):
        for col_tap in range(3):
            window = padded[:, row_tap : row_tap + height, col_tap : col_tap + breadth]
            tap_list.append(
                jnp.einsum("bhwc,bhwd->cd", window, upstream, preferred_element_type=jnp.float32)
            )
    return jnp.stack(tap_list).reshape(3, 3, inputs.shape[3], upstream.shape[3])


def conv_down(inputs, kernel):
    height, breadth = (inputs.shape[1], inputs.shape[2])
    padded = jnp.pad(inputs, ((0, 0), (1, 1), (1, 1), (0, 0)))
    summed_taps = jnp.zeros(
        (inputs.shape[0], height // 2, breadth // 2, kernel.shape[3]), jnp.float32
    )
    for row_tap in range(3):
        for col_tap in range(3):
            window = padded[:, row_tap : row_tap + height : 2, col_tap : col_tap + breadth : 2]
            summed_taps = summed_taps + jnp.einsum(
                "bhwc,cd->bhwd",
                window,
                kernel[row_tap, col_tap],
                preferred_element_type=jnp.float32,
            )
    return summed_taps


def conv_down_input(upstream, kernel, height, breadth):
    summed_taps = jnp.zeros(
        (upstream.shape[0], height + 2, breadth + 2, kernel.shape[2]), jnp.float32
    )
    for row_tap in range(3):
        for col_tap in range(3):
            spread_out = jnp.einsum(
                "bhwd,cd->bhwc",
                upstream,
                kernel[row_tap, col_tap],
                preferred_element_type=jnp.float32,
            )
            placed = lax.pad(
                spread_out,
                jnp.float32(0.0),
                ((0, 0, 0), (row_tap, 3 - row_tap, 1), (col_tap, 3 - col_tap, 1), (0, 0, 0)),
            )
            summed_taps = summed_taps + placed
    return summed_taps[:, 1 : height + 1, 1 : breadth + 1]


def conv_down_kernel(inputs, upstream):
    height, breadth = (inputs.shape[1], inputs.shape[2])
    padded = jnp.pad(inputs, ((0, 0), (1, 1), (1, 1), (0, 0)))
    tap_list = []
    for row_tap in range(3):
        for col_tap in range(3):
            window = padded[:, row_tap : row_tap + height : 2, col_tap : col_tap + breadth : 2]
            tap_list.append(
                jnp.einsum("bhwc,bhwd->cd", window, upstream, preferred_element_type=jnp.float32)
            )
    return jnp.stack(tap_list).reshape(3, 3, inputs.shape[3], upstream.shape[3])


def learn_rates():
    conv_rate = LR_SCALE * (9 * C) ** (-0.5)
    mod_rate = LR_SCALE * (4 * FREQ) ** (-0.5)
    return (
        LR_NORM,
        conv_rate,
        mod_rate,
        conv_rate,
        conv_rate,
        mod_rate,
        LR_SCALE * D ** (-0.5),
        LR_SCALE * (HEADS * HDIM // 32) ** (-0.5),
        LR_SCALE * D ** (-0.5),
        LR_SCALE * FF ** (-0.5),
    )


def clipped_step(masters, averages, squares, combined_total, sum_all):
    local_sq = jnp.zeros((), jnp.float32)
    for position, reduced in enumerate(combined_total):
        shard_sq = jnp.sum(reduced * reduced)
        if position == 0 or position == 5:
            shard_sq = shard_sq / lax.axis_size(TENSOR)
        local_sq = local_sq + shard_sq
    square_sum = sum_all(local_sq)
    grad_norm = jnp.sqrt(square_sum)
    factor = jnp.minimum(1.0, CLIP / (grad_norm + 1e-06))
    rates = learn_rates()
    correct_one = 1.0 - BETA_ONE**STEP
    correct_two = 1.0 - BETA_TWO**STEP
    results = []
    for master, average, square, reduced, learn_rate in zip(
        masters, averages, squares, combined_total, rates
    ):
        clipped = reduced * factor
        new_avg = BETA_ONE * average + (1.0 - BETA_ONE) * clipped
        new_sq = BETA_TWO * square + (1.0 - BETA_TWO) * clipped * clipped
        step_dir = new_avg / correct_one / (jnp.sqrt(new_sq / correct_two) + ADAM_EPS)
        new_master = master - learn_rate * (step_dir + DECAY * master)
        results += [new_master, new_avg, new_sq]
    return (grad_norm.reshape(1),) + tuple(results)


def per_device(
    images,
    t_index,
    cotangent,
    norm_params,
    norm_params_avg,
    norm_params_sq,
    first_conv,
    first_conv_avg,
    first_conv_sq,
    resnet_mod,
    resnet_mod_avg,
    resnet_mod_sq,
    second_conv,
    second_kernel_first_moment,
    second_conv_sq,
    down_conv,
    down_conv_avg,
    down_conv_sq,
    ada_proj,
    ada_proj_avg,
    ada_proj_sq,
    qkv_proj,
    qkv_proj_avg,
    qkv_proj_sq,
    out_proj,
    out_proj_avg,
    out_proj_sq,
    hidden_in,
    hidden_in_avg,
    hidden_in_sq,
    hidden_out,
    hidden_out_avg,
    hidden_out_sq,
):
    masters = (
        norm_params,
        first_conv,
        resnet_mod,
        second_conv,
        down_conv,
        ada_proj,
        qkv_proj,
        out_proj,
        hidden_in,
        hidden_out,
    )
    averages = (
        norm_params_avg,
        first_conv_avg,
        resnet_mod_avg,
        second_kernel_first_moment,
        down_conv_avg,
        ada_proj_avg,
        qkv_proj_avg,
        out_proj_avg,
        hidden_in_avg,
        hidden_out_avg,
    )
    squares = (
        norm_params_sq,
        first_conv_sq,
        resnet_mod_sq,
        second_conv_sq,
        down_conv_sq,
        ada_proj_sq,
        qkv_proj_sq,
        out_proj_sq,
        hidden_in_sq,
        hidden_out_sq,
    )
    lowered = tuple((master.astype(jnp.bfloat16) for master in masters))
    gathered = (
        lax.all_gather(lowered[0], DP, axis=1, tiled=True),
        lax.all_gather(lowered[1], DP, axis=2, tiled=True),
        lax.all_gather(lowered[2], DP, axis=0, tiled=True),
        lax.all_gather(lowered[3], DP, axis=3, tiled=True),
        lax.all_gather(lowered[4], DP, axis=2, tiled=True),
        lax.all_gather(lowered[5], DP, axis=0, tiled=True),
        lax.all_gather(lowered[6], DP, axis=0, tiled=True),
        lax.all_gather(lowered[7], DP, axis=2, tiled=True),
        lax.all_gather(lowered[8], DP, axis=0, tiled=True),
        lax.all_gather(lowered[9], DP, axis=1, tiled=True),
    )
    (
        gain_bias,
        conv_one,
        res_table,
        conv_two,
        conv_half,
        ada_table,
        qkv_full,
        out_full,
        up_full,
        down_full,
    ) = gathered
    batch_size = images.shape[0]
    height, breadth = (images.shape[1], images.shape[2])
    local_c = conv_one.shape[3]
    local_d = conv_half.shape[3]
    heads_here = qkv_full.shape[2]
    tokens_len = height // 2 * (breadth // 2)
    tensor_pos = lax.axis_index(TENSOR)
    n_tensor = lax.axis_size(TENSOR)
    score_scale = HDIM ** (-0.5)
    noise_emb = embed_noise(t_index, FREQ)
    emb_low = noise_emb.astype(jnp.bfloat16)
    emb_back = emb_low.astype(jnp.float32)
    res_mods = jnp.dot(
        emb_low, res_table.reshape(FREQ, 2 * local_c), preferred_element_type=jnp.float32
    ).reshape(batch_size, 2, local_c)
    ada_mods = jnp.dot(
        emb_low, ada_table.reshape(FREQ, 6 * D), preferred_element_type=jnp.float32
    ).reshape(batch_size, 6, D)
    image_float = images.astype(jnp.float32)
    gain_float = gain_bias.astype(jnp.float32)
    act_one, first_back = jax.vjp(leading_segment, image_float, gain_float)
    act_one = act_one.astype(jnp.bfloat16)
    middle = conv_same(act_one, conv_one)
    act_two, second_back = jax.vjp(second_piece, middle, res_mods)
    act_two = act_two.astype(jnp.bfloat16)
    branch = lax.psum(conv_same(act_two, conv_two).astype(jnp.bfloat16), TENSOR).astype(
        jnp.float32
    )
    residual = image_float + branch
    resid_low = residual.astype(jnp.bfloat16)
    shrunk = conv_down(resid_low, conv_half)
    pieces = lax.all_gather(shrunk.astype(jnp.bfloat16), TENSOR, axis=3, tiled=True).astype(
        shrunk.dtype
    )
    tokens = pieces.reshape(batch_size, tokens_len, D)
    attn_in, attn_back = jax.vjp(modulate, tokens, ada_mods[:, 0:2])
    attn_low = attn_in.astype(jnp.bfloat16).reshape(batch_size * tokens_len, D)
    qkv_low = jnp.dot(
        attn_low, qkv_full.reshape(D, 3 * heads_here * HDIM), preferred_element_type=jnp.float32
    ).astype(jnp.bfloat16)
    qkv_low = qkv_low.reshape(batch_size, tokens_len, 3, heads_here, HDIM)
    query_low, key_low, value_low = (qkv_low[:, :, 0], qkv_low[:, :, 1], qkv_low[:, :, 2])
    scores = (
        jnp.einsum("bqhd,bkhd->bhqk", query_low, key_low, preferred_element_type=jnp.float32)
        * score_scale
    )
    row_max = jnp.max(scores, axis=-1, keepdims=True)
    log_total = row_max + jnp.log(jnp.sum(jnp.exp(scores - row_max), axis=-1, keepdims=True))
    attention_low = jnp.exp(scores - log_total).astype(jnp.bfloat16)
    mixed = jnp.einsum(
        "bhqk,bkhd->bqhd", attention_low, value_low, preferred_element_type=jnp.float32
    ).astype(jnp.bfloat16)
    mixed = mixed.reshape(batch_size * tokens_len, heads_here * HDIM)
    out_flat = out_full.reshape(heads_here * HDIM, D)
    attended = (
        lax.psum(
            jnp.dot(mixed, out_flat, preferred_element_type=jnp.float32).astype(jnp.bfloat16),
            TENSOR,
        )
        .astype(jnp.float32)
        .reshape(batch_size, tokens_len, D)
    )
    gate_one = 1.0 + ada_mods[:, None, 2]
    after_attn = tokens + gate_one * attended
    mlp_in, mlp_back = jax.vjp(modulate, after_attn, ada_mods[:, 3:5])
    mlp_low = mlp_in.astype(jnp.bfloat16).reshape(batch_size * tokens_len, D)
    pre_act = jnp.dot(mlp_low, up_full, preferred_element_type=jnp.float32)
    hidden_act, gelu_back = jax.vjp(gelu_tanh, pre_act)
    hidden_low = hidden_act.astype(jnp.bfloat16)
    expanded = (
        lax.psum(
            jnp.dot(hidden_low, down_full, preferred_element_type=jnp.float32).astype(jnp.bfloat16),
            TENSOR,
        )
        .astype(jnp.float32)
        .reshape(batch_size, tokens_len, D)
    )
    gate_two = 1.0 + ada_mods[:, None, 5]
    block_out = (after_attn + gate_two * expanded).astype(jnp.bfloat16)
    upstream = cotangent.astype(jnp.float32)
    grad_expanded = (gate_two * upstream).astype(jnp.bfloat16).reshape(batch_size * tokens_len, D)
    grad_gate_two = jnp.sum(upstream * expanded, axis=1)
    grad_down = jnp.einsum(
        "tf,td->fd", hidden_low, grad_expanded, preferred_element_type=jnp.float32
    )
    grad_hidden = jnp.einsum(
        "td,fd->tf", grad_expanded, down_full, preferred_element_type=jnp.float32
    )
    (grad_pre,) = gelu_back(grad_hidden)
    grad_pre_low = grad_pre.astype(jnp.bfloat16)
    grad_mlp_in = (
        lax.psum(
            jnp.einsum(
                "tf,df->td", grad_pre_low, up_full, preferred_element_type=jnp.float32
            ).astype(jnp.bfloat16),
            TENSOR,
        )
        .astype(jnp.float32)
        .reshape(batch_size, tokens_len, D)
    )
    grad_after_norm, grad_mods_two = mlp_back(grad_mlp_in)
    grad_after = upstream + grad_after_norm
    grad_attended = (gate_one * grad_after).astype(jnp.bfloat16).reshape(batch_size * tokens_len, D)
    grad_gate_one = jnp.sum(grad_after * attended, axis=1)
    grad_out = jnp.einsum("tk,td->kd", mixed, grad_attended, preferred_element_type=jnp.float32)
    grad_mixed = jnp.einsum(
        "td,kd->tk", grad_attended, out_flat, preferred_element_type=jnp.float32
    ).astype(jnp.bfloat16)
    grad_mixed = grad_mixed.reshape(batch_size, tokens_len, heads_here, HDIM)
    scores = (
        jnp.einsum("bqhd,bkhd->bhqk", query_low, key_low, preferred_element_type=jnp.float32)
        * score_scale
    )
    attention = jnp.exp(scores - log_total)
    attention_low = attention.astype(jnp.bfloat16)
    grad_probs = jnp.einsum(
        "bqhd,bkhd->bhqk", grad_mixed, value_low, preferred_element_type=jnp.float32
    )
    grad_values = jnp.einsum(
        "bhqk,bqhd->bkhd", attention_low, grad_mixed, preferred_element_type=jnp.float32
    )
    grad_scores = (
        attention * (grad_probs - jnp.sum(grad_probs * attention, axis=-1, keepdims=True))
    ).astype(jnp.bfloat16)
    query_gradient = (
        jnp.einsum("bhqk,bkhd->bqhd", grad_scores, key_low, preferred_element_type=jnp.float32)
        * score_scale
    )
    grad_keys = (
        jnp.einsum("bhqk,bqhd->bkhd", grad_scores, query_low, preferred_element_type=jnp.float32)
        * score_scale
    )
    grad_qkv = (
        jnp.stack([query_gradient, grad_keys, grad_values], axis=2)
        .astype(jnp.bfloat16)
        .reshape(batch_size * tokens_len, 3 * heads_here * HDIM)
    )
    grad_qkv_w = jnp.einsum(
        "td,tk->dk", attn_low, grad_qkv, preferred_element_type=jnp.float32
    ).reshape(D, 3, heads_here, HDIM)
    grad_attn_in = (
        lax.psum(
            jnp.einsum(
                "tk,dk->td",
                grad_qkv,
                qkv_full.reshape(D, 3 * heads_here * HDIM),
                preferred_element_type=jnp.float32,
            ).astype(jnp.bfloat16),
            TENSOR,
        )
        .astype(jnp.float32)
        .reshape(batch_size, tokens_len, D)
    )
    grad_tokens_norm, grad_mods_one = attn_back(grad_attn_in)
    grad_tokens = grad_after + grad_tokens_norm
    grad_mods = jnp.concatenate(
        [grad_mods_one, grad_gate_one[:, None], grad_mods_two, grad_gate_two[:, None]], axis=1
    )
    adaptive_gradient = jnp.einsum(
        "bf,bk->fk", emb_back, grad_mods.reshape(batch_size, 6 * D), precision=HIGHEST
    ).reshape(FREQ, 6, D)
    grad_out_w = grad_out.reshape(heads_here, HDIM, D)
    grad_up = jnp.einsum("td,tf->df", mlp_low, grad_pre_low, preferred_element_type=jnp.float32)
    transformer_gradient_total = (
        lax.psum_scatter(adaptive_gradient, DP, scatter_dimension=0, tiled=True),
        lax.psum_scatter(grad_qkv_w, DP, scatter_dimension=0, tiled=True),
        lax.psum_scatter(grad_out_w, DP, scatter_dimension=2, tiled=True),
        lax.psum_scatter(grad_up, DP, scatter_dimension=0, tiled=True),
        lax.psum_scatter(grad_down, DP, scatter_dimension=1, tiled=True),
    )
    grad_shrunk = lax.dynamic_slice_in_dim(
        grad_tokens.reshape(batch_size, height // 2, breadth // 2, D),
        tensor_pos * local_d,
        local_d,
        axis=3,
    ).astype(jnp.bfloat16)
    grad_half = conv_down_kernel(resid_low, grad_shrunk)
    grad_resid = lax.psum(
        conv_down_input(grad_shrunk, conv_half, height, breadth).astype(jnp.bfloat16), TENSOR
    ).astype(jnp.float32)
    grad_branch = grad_resid.astype(jnp.bfloat16)
    grad_conv_two = conv_same_kernel(act_two, grad_branch)
    grad_act_two = conv_same_input(grad_branch, conv_two)
    grad_middle, grad_res_mods = second_back(grad_act_two)
    grad_middle_low = grad_middle.astype(jnp.bfloat16)
    grad_conv_one = conv_same_kernel(act_one, grad_middle_low)
    grad_act_one = lax.psum(
        conv_same_input(grad_middle_low, conv_one).astype(jnp.bfloat16), TENSOR
    ).astype(jnp.float32)
    grad_image_norm, grad_gain = first_back(grad_act_one)
    images_grad = grad_resid + grad_image_norm
    grad_res_table = jnp.einsum(
        "bf,bk->fk", emb_back, grad_res_mods.reshape(batch_size, 2 * local_c), precision=HIGHEST
    ).reshape(FREQ, 2, local_c)
    resnet_gradient_total = (
        lax.psum_scatter(grad_gain, DP, scatter_dimension=1, tiled=True),
        lax.psum_scatter(grad_conv_one, DP, scatter_dimension=2, tiled=True),
        lax.psum_scatter(grad_res_table, DP, scatter_dimension=0, tiled=True),
        lax.psum_scatter(grad_conv_two, DP, scatter_dimension=3, tiled=True),
        lax.psum_scatter(grad_half, DP, scatter_dimension=2, tiled=True),
    )
    combined_total = tuple(resnet_gradient_total) + tuple(transformer_gradient_total)
    return (block_out, images_grad) + clipped_step(
        masters,
        averages,
        squares,
        combined_total,
        lambda local: lax.psum(local, (DP, TENSOR)),
    )


MESH = pl.DeviceIdType.MESH
ANYWHERE = pl.BlockSpec(memory_space=pl.ANY)
IN_VMEM = pl.BlockSpec(memory_space=pltpu.VMEM)
LAYERS = 4
ORDER = (3, 0, 2, 1)
VMEM_GRANT = 60 * 1024 * 1024


class Place:
    def __init__(self, wide):
        self.wide = wide
        self.dp = lax.axis_index(DP)
        self.core = lax.axis_index(TENSOR)
        self.z = self.dp // 4
        x = self.dp % 2
        y = (self.dp // 2) % 2
        x_mate = self.dp + 1 - 2 * x
        y_mate = self.dp + 2 - 4 * y
        self.x_mate = x_mate
        if wide:
            self.first = x_mate * (1 - self.core) + y_mate * self.core
            self.second = y_mate * (1 - self.core) + x_mate * self.core
            self.stride = 4
            self.column = self.dp % 4
            self.first_column = self.first % 4
            self.second_column = self.second % 4
            self.far_column = 3 - self.column
        else:
            self.first = self.second = y_mate
            self.stride = 2
            self.column = y
            self.second_column = 1 - y
        self.slot = self.z * self.stride + self.column
        self.has_below = self.z > 0
        self.has_above = self.z < LAYERS - 1

    def greet(self, with_core):
        barrier = pltpu.get_barrier_semaphore()

        def signal(dp, core):
            pl.semaphore_signal(barrier, inc=1, device_id=(dp, core), device_id_type=MESH)

        signal(self.second, self.core)
        if self.wide:
            signal(self.first, self.core)
        if with_core:
            signal(self.dp, 1 - self.core)
        pl.when(self.has_below)(lambda: signal(self.dp - 4, self.core))
        pl.when(self.has_above)(lambda: signal(self.dp + 4, self.core))
        layers = (self.z + LAYERS - 1) // LAYERS + (2 * LAYERS - 2 - self.z) // LAYERS
        pl.semaphore_wait(barrier, 1 + self.wide + with_core + layers)


def params(number):
    return pltpu.CompilerParams(
        collective_id=number, has_side_effects=True, vmem_limit_bytes=VMEM_GRANT
    )


def layer_order(step):
    odd = step % 2
    return (1 - odd) * (LAYERS - 1 - step // 2) + odd * (step // 2)


def remote(source, target, send_sem, recv_sem, device):
    return pltpu.make_async_remote_copy(
        src_ref=source,
        dst_ref=target,
        send_sem=send_sem,
        recv_sem=recv_sem,
        device_id=device,
        device_id_type=MESH,
    )


def by_distance(at, step):
    flip = at.z // 2
    inner = at.z * (1 - flip) + (LAYERS - 1 - at.z) * flip
    early = 1 - step // 2
    base = (1 - inner) * step + inner * (early * (1 - step) + (1 - early) * step)
    return (1 - flip) * base + flip * (LAYERS - 1 - base)


def piece_of(block, index, pieces):
    rows, lanes = block.shape
    if rows >= 16 * pieces:
        return block.at[pl.ds(pl.multiple_of(index * (rows // pieces), rows // pieces), rows // pieces)]
    return block.at[:, pl.ds(pl.multiple_of(index * (lanes // pieces), lanes // pieces), lanes // pieces)]


def gather_steps(at, outs, use, pieces, send_sem, recv_sem, mirror=None, tick=None):
    columns = at.stride
    arrays = range(len(outs))

    def here(index, slot, piece):
        block = outs[index].at[slot, at.core] if mirror else outs[index].at[slot]
        return piece_of(block, piece, pieces)

    def each(slot, piece, sem, mate, act):
        for index in arrays:
            act(
                remote(
                    here(index, slot, piece),
                    here(index, slot, piece),
                    send_sem.at[index, sem * pieces + piece],
                    recv_sem.at[index, slot * pieces + piece],
                    (mate, at.core),
                )
            )

    def start(copy):
        copy.start()

    def across(slot, piece, act, core):
        for index in arrays:
            block = piece_of(outs[index].at[slot, core], piece, pieces)
            act(
                remote(
                    block,
                    block,
                    mirror[0].at[index, slot * pieces + piece],
                    mirror[1].at[index, slot * pieces + piece],
                    (at.dp, 1 - at.core),
                )
            )

    def turn(count):
        step, piece = (count // pieces, count % pieces)
        if at.wide:
            late = step // 8
            rest = step % 8
            last = rest // 7
            is_first = (1 - late) * (last + (1 - rest % 2) * ((rest + 6) // 8))
            is_own = (1 - late) * (1 - is_first)
            near = is_own * ((rest + 1) // 2) + is_first * ((rest - 1) // 2)
            layer = by_distance(at, (1 - late) * near + late * (rest // 2))
            column = (
                is_own * at.column
                + is_first * at.first_column
                + late * ((1 - rest % 2) * at.second_column + rest % 2 * at.far_column)
            )
        else:
            is_own = 1 - step // LAYERS
            layer = by_distance(at, step % LAYERS)
            column = is_own * at.column + (1 - is_own) * at.second_column
        slot = layer * columns + column

        @pl.when(slot != at.slot)
        def _():
            each(slot, piece, 0, at.dp, lambda copy: copy.wait_recv())

        @pl.when(is_own == 1)
        def _():
            @pl.when(jnp.logical_and(layer <= at.z, at.has_above))
            def _():
                each(slot, piece, layer, at.dp + 4, start)

            @pl.when(jnp.logical_and(layer >= at.z, at.has_below))
            def _():
                each(slot, piece, 4 + layer, at.dp - 4, start)

            if at.wide:
                each(slot, piece, 8 + layer, at.first, start)
            each(slot, piece, 12 + layer, at.second, start)

        if at.wide:

            @pl.when(is_first == 1)
            def _():
                each(slot, piece, 16 + layer, at.second, start)

        if mirror:
            across(slot, piece, start, at.core)
        if tick is not None:
            tick(count)
        if use is not None:
            pl.when(piece == pieces - 1)(lambda: use(slot))

    def sent(copy):
        copy.wait_send()

    def end():
        @pl.loop(0, LAYERS * pieces)
        def _(count):
            layer, piece = (count // pieces, count % pieces)

            @pl.when(jnp.logical_and(layer <= at.z, at.has_above))
            def _():
                each(at.slot, piece, layer, at.dp + 4, sent)

            @pl.when(jnp.logical_and(layer >= at.z, at.has_below))
            def _():
                each(at.slot, piece, 4 + layer, at.dp - 4, sent)

            for group in (8, 12, 16) if at.wide else (12,):
                each(at.slot, piece, group + layer, at.second, sent)

        if mirror:

            @pl.loop(0, columns * LAYERS * pieces)
            def _(count):
                slot, piece = (count // pieces, count % pieces)
                across(slot, piece, lambda copy: copy.wait_recv(), 1 - at.core)
                across(slot, piece, sent, at.core)

    return turn, columns * LAYERS * pieces, end


def gather_stage(*args, **options):
    turn, turns, end = gather_steps(*args, **options)
    pl.loop(0, turns)(turn)
    end()


def gather_scratch(pieces, arrays=1, wide=True, mirror=False):
    chips = 16 if wide else 8
    count = [20 * pieces, 16 * pieces] + [chips * pieces] * (2 * mirror)
    return [pltpu.SemaphoreType.DMA((arrays, n)) for n in count]


def reduce_stage(at, result, produce, pieces, scratch, pair=False, meanwhile=None, tick=None):
    blocks, from_second, from_first, from_z, send_sem, recv_sem, *scratch = scratch
    columns = at.stride
    whole = columns * LAYERS
    lag = whole // 2 if pair else 0

    def part(ref, index, piece):
        return piece_of(ref.at[index], piece, pieces)

    def copy(sem, piece, source, target, mate):
        return remote(
            part(blocks, source, piece),
            part(target[0], target[1], piece),
            send_sem.at[sem, piece],
            recv_sem.at[sem, piece],
            (mate, at.core),
        )

    def to_second(half, layer, piece, slot):
        return copy(4 * half + layer, piece, slot, (from_second, 4 * half + layer), at.second)

    def to_first(layer, piece):
        return copy(
            8 + layer, piece, layer * columns + at.first_column, (from_first, layer), at.first
        )

    def up(layer, piece):
        return copy(12 + layer, piece, layer * columns + at.column, (from_z, layer), at.dp + 4)

    def down(layer, piece):
        return copy(16 + layer, piece, layer * columns + at.column, (from_z, 4 + layer), at.dp - 4)

    def value(ref, index, piece):
        return part(ref, index, piece)[...].astype(jnp.float32)

    def slot_of(step):
        if at.wide:
            keep, second, place = (step // 8, step % 2, step % 8 // 2)
            column = (1 - second) * (
                (1 - keep) * at.far_column + keep * at.first_column
            ) + second * ((1 - keep) * at.second_column + keep * at.column)
        else:
            keep, second, place = (step // LAYERS, 1, step % LAYERS)
            column = (1 - keep) * at.second_column + keep * at.column
        return layer_order(place) * columns + column, keep, second, place

    ahead = 2

    def send_layer(place, piece):
        layer = layer_order(place)
        if at.wide:
            to_second(0, layer, piece, layer * columns + at.far_column).start()
        to_second(1, layer, piece, layer * columns + at.second_column).start()

    def to_mate(slot):
        outbound, paired, pair_send, pair_recv = scratch
        return remote(
            outbound.at[slot],
            paired.at[slot],
            pair_send.at[slot],
            pair_recv.at[slot],
            (at.dp, 1 - at.core),
        )

    @pl.loop(0, whole + lag)
    def _(step):
        def make():
            slot = slot_of(step)[0]
            produce(slot)
            if pair:
                to_mate(slot).start()

        def pass_on():
            slot, keep, second, place = slot_of(step - lag)
            if pair:
                to_mate(slot).wait_recv()
                blocks[slot] = (
                    blocks[slot].astype(jnp.float32) + scratch[1][slot].astype(jnp.float32)
                ).astype(blocks.dtype)

            @pl.when(jnp.logical_and(keep == 0, place < ahead))
            def _():
                for piece in range(pieces):
                    to_second(second, layer_order(place), piece, slot).start()

        if pair:
            pl.when(step < whole)(make)
            pl.when(step >= lag)(pass_on)
        else:
            make()
            pass_on()

    if meanwhile is not None:
        meanwhile()

    def turn(place, piece):
        layer = layer_order(place)
        slot = layer * columns + at.first_column
        to_second(0, layer, piece, slot).wait_recv()
        part(blocks, slot, piece)[...] = (
            value(blocks, slot, piece) + value(from_second, layer, piece)
        ).astype(blocks.dtype)
        to_first(layer, piece).start()

    def rise(place, piece):
        layer = layer_order(place)
        slot = layer * columns + at.column
        to_second(1, layer, piece, slot).wait_recv()
        summed = value(blocks, slot, piece) + value(from_second, 4 + layer, piece)
        if at.wide:
            to_first(layer, piece).wait_recv()
            summed = summed + value(from_first, layer, piece)

        @pl.when(at.z == layer)
        def _():
            piece_of(result, piece, pieces)[...] = summed

        @pl.when(at.z < layer)
        def _():
            part(blocks, slot, piece)[...] = summed.astype(blocks.dtype)

            @pl.when(at.has_below)
            def _():
                up(layer, piece).wait_recv()
                part(blocks, slot, piece)[...] = (
                    value(blocks, slot, piece) + value(from_z, layer, piece)
                ).astype(blocks.dtype)

            up(layer, piece).start()

        @pl.when(at.z > layer)
        def _():
            part(blocks, slot, piece)[...] = summed.astype(blocks.dtype)

            @pl.when(at.has_above)
            def _():
                down(layer, piece).wait_recv()
                part(blocks, slot, piece)[...] = (
                    value(blocks, slot, piece) + value(from_z, 4 + layer, piece)
                ).astype(blocks.dtype)

            down(layer, piece).start()

    behind = 1 if at.wide else 0

    @pl.loop(0, (LAYERS + behind) * pieces)
    def _(step):
        place, piece = (step // pieces, step % pieces)
        pl.when(place + ahead < LAYERS)(lambda: send_layer(place + ahead, piece))
        if at.wide:
            pl.when(place < LAYERS)(lambda: turn(place, piece))
        pl.when(place >= behind)(lambda: rise(place - behind, piece))
        if tick is not None:
            tick(step)

    @pl.loop(0, pieces)
    def _(piece):
        @pl.when(at.has_below)
        def _():
            up(at.z, piece).wait_recv()
            piece_of(result, piece, pieces)[...] += value(from_z, at.z, piece)

        @pl.when(at.has_above)
        def _():
            down(at.z, piece).wait_recv()
            piece_of(result, piece, pieces)[...] += value(from_z, 4 + at.z, piece)

    @pl.loop(0, LAYERS * pieces)
    def _(step):
        layer, piece = (step // pieces, step % pieces)
        if at.wide:
            to_second(0, layer, piece, at.slot).wait_send()
            to_first(layer, piece).wait_send()
        to_second(1, layer, piece, at.slot).wait_send()
        pl.when(at.z < layer)(lambda: up(layer, piece).wait_send())
        pl.when(at.z > layer)(lambda: down(layer, piece).wait_send())

    if pair:

        @pl.loop(0, whole)
        def _(slot):
            to_mate(slot).wait_send()


def share_stage(at, result, send_sem, recv_sem):
    def give(core):
        return remote(result.at[core], result.at[core], send_sem, recv_sem, (at.dp, 1 - at.core))

    give(at.core).start()
    give(1 - at.core).wait_recv()
    give(at.core).wait_send()


def greet_all(at):
    everyone = 4 * LAYERS
    barrier = pltpu.get_barrier_semaphore()

    @pl.loop(1, everyone)
    def _(step):
        pl.semaphore_signal(
            barrier, inc=1, device_id=((at.dp + step) % everyone, at.core), device_id_type=MESH
        )

    pl.semaphore_signal(barrier, inc=1, device_id=(at.dp, 1 - at.core), device_id_type=MESH)
    pl.semaphore_wait(barrier, everyone)


class Ride:
    def __init__(self, at, parts, send_sem, recv_sem, own_sem):
        self.at, self.parts = (at, parts)
        self.send_sem, self.recv_sem, self.own_sem = (send_sem, recv_sem, own_sem)

    def copy(self, part, step):
        source, target = self.parts[part]
        peer = (self.at.dp + step) % (4 * LAYERS)
        return remote(
            source(peer),
            target(self.at.dp),
            self.send_sem.at[part, step - 1],
            self.recv_sem.at[part, step - 1],
            (peer, self.at.core),
        )

    def keep(self, part):
        source, target = self.parts[part]
        return pltpu.make_async_copy(
            source(self.at.dp), target(self.at.dp), self.own_sem.at[part]
        )

    def start(self, first=0, after=None):
        for part in range(len(self.parts))[first:after]:
            self.keep(part).start()

            @pl.loop(1, 4 * LAYERS)
            def _(step):
                self.copy(part, step).start()

    def wait_for(self, part):
        self.keep(part).wait()

        @pl.loop(1, 4 * LAYERS)
        def _(step):
            self.copy(part, step).wait()

    def wait(self, first=0):
        for part in range(first, len(self.parts)):
            self.wait_for(part)


def ride_scratch(parts):
    others = 4 * LAYERS - 1
    return [
        pltpu.SemaphoreType.DMA((parts, others)),
        pltpu.SemaphoreType.DMA((parts, others)),
        pltpu.SemaphoreType.DMA((parts,)),
    ]


class PairRide:
    def __init__(self, at, parts, send_sem, recv_sem, own_sem):
        self.at, self.parts = (at, parts)
        self.send_sem, self.recv_sem, self.own_sem = (send_sem, recv_sem, own_sem)
        self.steps = 2 * LAYERS

    def copy(self, part, step):
        source, target = self.parts[part]
        peer = (self.at.dp + 2 * step) % (4 * LAYERS)
        return remote(
            source(peer),
            target(self.at.dp),
            self.send_sem.at[part, step],
            self.recv_sem.at[part, step],
            (peer, self.at.core),
        )

    def keep(self, part):
        source, target = self.parts[part]
        return pltpu.make_async_copy(
            source(self.at.dp), target(self.at.dp), self.own_sem.at[part]
        )

    def onward(self, part, step):
        target = self.parts[part][1]
        chip = (self.at.dp + 4 * LAYERS - 2 * step) % (4 * LAYERS)
        return remote(
            target(chip),
            target(chip),
            self.send_sem.at[part, self.steps + step],
            self.recv_sem.at[part, self.steps + step],
            (self.at.x_mate, self.at.core),
        )

    def start(self):
        for part in range(len(self.parts)):
            self.keep(part).start()

            @pl.loop(1, self.steps)
            def _(step):
                self.copy(part, step).start()

    def forward(self):
        for part in range(len(self.parts)):
            self.keep(part).wait()

            @pl.loop(0, self.steps)
            def _(step):
                pl.when(step > 0)(lambda: self.copy(part, step).wait_recv())
                self.onward(part, step).start()

    def wait(self):
        for part in range(len(self.parts)):

            @pl.loop(0, self.steps)
            def _(step):
                self.onward(part, step).wait()
                pl.when(step > 0)(lambda: self.copy(part, step).wait_send())


def pair_ride_scratch(parts):
    return [
        pltpu.SemaphoreType.DMA((parts, 4 * LAYERS)),
        pltpu.SemaphoreType.DMA((parts, 4 * LAYERS)),
        pltpu.SemaphoreType.DMA((parts,)),
    ]


def strip(ref, axis, index, size):
    at = pl.ds(pl.multiple_of(index * size, size), size)
    return ref.at[at] if axis == 0 else ref.at[:, at]


def reduce_scratch(block, pieces, wide=True, pair=False):
    kind = jnp.bfloat16
    chips = 16 if wide else 8
    scratch = [
        pltpu.VMEM((chips,) + block, kind),
        pltpu.VMEM((8,) + block, kind),
        pltpu.VMEM((4,) + block, kind),
        pltpu.VMEM((8,) + block, kind),
        pltpu.SemaphoreType.DMA((20, pieces)),
        pltpu.SemaphoreType.DMA((20, pieces)),
    ]
    if pair:
        scratch += [pltpu.VMEM((chips,) + block, kind)] * 2
        scratch += [pltpu.SemaphoreType.DMA((chips,))] * 2
    return scratch


def mean_of_groups(sums, count):
    size = C // GROUPS
    channels = sums.shape[-1]
    row = lax.broadcasted_iota(jnp.int32, (channels, channels), 0) // size
    column = lax.broadcasted_iota(jnp.int32, (channels, channels), 1) // size
    same = jnp.where(row == column, 1.0 / (count * size), 0.0)
    return jnp.dot(sums, same, precision=HIGHEST, preferred_element_type=jnp.float32)


def side_by_side(maps, breadth, turned=False):
    positions = maps.shape[0]
    column = lax.broadcasted_iota(jnp.int32, maps.shape, 0) % breadth
    before = jnp.where(column == 0, 0.0, pltpu.roll(maps, 1, 0))
    after = jnp.where(column == breadth - 1, 0.0, pltpu.roll(maps, positions - 1, 0))
    three = (after, maps, before) if turned else (before, maps, after)
    return jnp.concatenate(three, axis=1)


def fold_three(products, breadth, turned=False):
    positions = products.shape[0]
    channels = products.shape[1] // 3
    left, middle, right = (products[:, tap * channels : (tap + 1) * channels] for tap in range(3))
    if turned:
        left, right = (right, left)
    column = lax.broadcasted_iota(jnp.int32, middle.shape, 0) % breadth
    before = jnp.where(column == 0, 0.0, pltpu.roll(left, 1, 0))
    after = jnp.where(column == breadth - 1, 0.0, pltpu.roll(right, positions - 1, 0))
    return before + middle + after


def fold_rows(above, same, below, breadth):
    edge = jnp.zeros((breadth, same.shape[1]), jnp.float32)
    count = same.shape[0] - breadth
    down = jnp.concatenate([edge, above[:count]], axis=0)
    up = jnp.concatenate([below[breadth:], edge], axis=0)
    return down + same + up


def silu(z):
    return z * jax.nn.sigmoid(z)


def store_padded(ref, index, maps, breadth):
    positions = maps.shape[0]
    edge = jnp.zeros((breadth, maps.shape[1]), ref.dtype)
    ref[index, pl.ds(0, breadth)] = edge
    ref[index, pl.ds(breadth, positions)] = maps.astype(ref.dtype)
    ref[index, pl.ds(breadth + positions, breadth)] = edge


def res_forward_kernel(
    breadth,
    gain_bias,
    conv_one,
    conv_two,
    conv_half,
    picks,
    res_table,
    ada_table,
    image_blocks,
    emb_blocks,
    qkv_blocks,
    out_blocks,
    up_rows,
    down_columns,
    pictures,
    emb,
    tokens,
    act_out,
    taps_one_out,
    taps_half,
    middle,
    stats,
    mods,
    qkv_head,
    out_head,
    up_here,
    down_here,
    neighbour_sem,
    arrived,
    mods_blocks,
    mods_terms,
    acts,
    taps_one,
    mine,
    theirs,
    pair_send,
    pair_recv,
    share_send,
    share_recv,
    out_sem,
    *scratch,
):
    first_reduce, (act_send, act_recv), last_reduce = (scratch[:6], scratch[6:8], scratch[8:14])
    at = Place(True)
    greet_all(at)

    rows, cols = (up_rows.shape[0], up_here.shape[1])
    near = 4 * LAYERS // qkv_blocks.shape[0]
    ride = Ride(
        at,
        [
            (lambda chip: emb_blocks.at[chip], lambda chip: emb.at[chip]),
            (lambda chip: image_blocks.at[chip, at.core], lambda chip: arrived.at[chip, at.core]),
            (lambda chip: strip(up_rows, 1, chip, cols), lambda chip: strip(up_here, 0, chip, rows)),
            (lambda chip: mods_blocks.at[chip], lambda chip: mods_terms.at[chip]),
            (lambda chip: strip(down_columns, 0, chip, cols), lambda chip: strip(down_here, 1, chip, rows)),
        ],
        *scratch[14:17],
    )
    attention = PairRide(
        at,
        [
            (lambda chip: qkv_blocks.at[chip // near], lambda chip: strip(qkv_head, 0, chip, rows)),
            (lambda chip: out_blocks.at[chip // near], lambda chip: strip(out_head, 1, chip, rows)),
        ],
        *scratch[17:20],
    )
    ride.start(0, 3)
    images, positions, channels = pictures.shape
    half_c = conv_one.shape[2]
    tokens_len = positions // 4

    def hand_over(chip, core):
        return remote(
            arrived.at[chip, core],
            arrived.at[chip, core],
            neighbour_sem.at[0, chip],
            neighbour_sem.at[1, chip],
            (at.dp, 1 - at.core),
        )

    ride.keep(1).wait()
    hand_over(at.dp, at.core).start()

    @pl.loop(1, images)
    def _(step):
        ride.copy(1, step).wait()
        hand_over((at.dp + images - step) % images, at.core).start()

    @pl.loop(0, images)
    def _(i):
        hand_over(i, 1 - at.core).wait_recv()
        both = arrived[i].reshape(positions // 2, 2 * channels).astype(jnp.float32)
        sides = [both[:, :channels], both[:, channels:]]
        pictures[i] = jnp.concatenate(sides, axis=0).astype(jnp.bfloat16)

    attention.start()

    @pl.loop(0, images)
    def _(i):
        x = pictures[i].astype(jnp.float32)
        stats[0, pl.ds(i, 1)] = jnp.sum(x, axis=0, keepdims=True)

    stats[0] = mean_of_groups(stats[0], positions)

    @pl.loop(0, images)
    def _(i):
        x = pictures[i].astype(jnp.float32) - stats[0, pl.ds(i, 1)]
        stats[1, pl.ds(i, 1)] = jnp.sum(x * x, axis=0, keepdims=True)

    stats[1] = lax.rsqrt(mean_of_groups(stats[1], positions) + GN_EPS)

    @pl.loop(0, images)
    def _(i):
        normed = (pictures[i].astype(jnp.float32) - stats[0, pl.ds(i, 1)]) * stats[1, pl.ds(i, 1)]
        act = silu(normed * gain_bias[0:1] + gain_bias[1:2])
        store_padded(taps_one, i, side_by_side(act, breadth), breadth)

    save_taps = pltpu.make_async_copy(taps_one, taps_one_out, out_sem.at[0])
    save_taps.start()

    def first_product(slot):
        total = jnp.zeros((positions, conv_one.shape[2]), jnp.float32)
        for a in range(3):
            total += dot(taps_one[slot, pl.ds(a * breadth, positions)], conv_one[a])
        first_reduce[0][slot] = total.astype(jnp.bfloat16)

    def modulation_terms():
        ride.wait_for(0)
        emb_rows = emb[:, 0, : res_table.shape[0]].astype(jnp.bfloat16)
        lines = 0
        for table in [res_table] + [ada_table.at[row] for row in range(ada_table.shape[0])]:
            terms = dot(emb_rows, table[...])
            for line in range(table.shape[1] // 128):
                mods_blocks[:, lines] = terms[:, 128 * line : 128 * (line + 1)].astype(mods_blocks.dtype)
                lines += 1
        ride.start(3, 4)

    reduce_stage(at, middle, first_product, 2, first_reduce, meanwhile=modulation_terms)

    ride.start(4, 5)
    ride.wait_for(3)
    mods[at.core] = jnp.sum(mods_terms[...].astype(jnp.float32), axis=0)
    share_stage(at, mods, share_send.at[1], share_recv.at[1])

    def modulation(row):
        lines = half_c // 128
        parts = [mods[at.core, pl.ds(row * lines + i, 1)] for i in range(lines)]
        return jnp.concatenate(parts, axis=1)

    x = middle[...]
    center = mean_of_groups(jnp.sum(x, axis=0, keepdims=True), positions)
    x = x - center
    scale = lax.rsqrt(mean_of_groups(jnp.sum(x * x, axis=0, keepdims=True), positions) + GN_EPS)
    acts[at.slot] = silu(x * scale * (1.0 + modulation(0)) + modulation(1)).astype(jnp.bfloat16)

    def swap(slot):
        return remote(
            mine.at[slot],
            theirs.at[slot],
            pair_send.at[slot],
            pair_recv.at[slot],
            (at.dp, 1 - at.core),
        )

    def second_product(slot):
        act = acts[slot]
        above, same, below = (dot_nt(act, conv_two[a]) for a in range(3))
        folded = fold_three(fold_rows(above, same, below, breadth), breadth)
        mine[slot] = folded.astype(jnp.bfloat16)
        swap(slot).start()

    gather_stage(at, [acts], second_product, 2, act_send, act_recv)
    save_acts = pltpu.make_async_copy(acts, act_out, out_sem.at[1])
    save_acts.start()
    attention.forward()

    def half_product(slot):
        swap(slot).wait_recv()
        branch = mine[slot].astype(jnp.float32) + theirs[slot].astype(jnp.float32)
        resid = (pictures[slot].astype(jnp.float32) + branch).astype(jnp.bfloat16)
        three = side_by_side(resid.astype(jnp.float32), breadth).astype(jnp.bfloat16)
        picked = dot(picks[...], three).astype(jnp.bfloat16)
        total = jnp.zeros((tokens_len, conv_half.shape[2]), jnp.float32)
        for a in range(3):
            part = picked[a * tokens_len : (a + 1) * tokens_len]
            taps_half[a, slot] = part
            total += dot(part, conv_half[a])
        last_reduce[0][slot] = total.astype(jnp.bfloat16)

    reduce_stage(at, tokens.at[at.core], half_product, 2, last_reduce)
    share_stage(at, tokens, share_send.at[0], share_recv.at[0])

    @pl.loop(0, images)
    def _(slot):
        swap(slot).wait_send()
        hand_over(slot, at.core).wait_send()

    ride.wait_for(2)
    ride.wait_for(4)
    attention.wait()
    save_taps.wait()
    save_acts.wait()


def res_forward(number, height, breadth, *args):
    (gain_bias, conv_one, conv_two, conv_half, picks, res_table, ada_table, image_blocks, emb_blocks, qkv_blocks, out_blocks, up_rows, down_columns) = args
    images, positions, channels = (4 * LAYERS, height * breadth, gain_bias.shape[1])
    half_c = conv_one.shape[2]
    half_d = conv_half.shape[2]
    tokens_len = positions // 4
    three = 3 * channels
    rows, cols = (up_rows.shape[0], up_rows.shape[1] // images)
    low, full = (jnp.bfloat16, jnp.float32)
    pictures = (images, positions, channels)
    padded = (images, positions + 2 * breadth, three)
    acts = (images, positions, half_c)
    lines = (res_table.shape[1] + ada_table.shape[0] * ada_table.shape[2]) // 128
    outs = [
        (pictures, low),
        (emb_blocks.shape, full),
        ((2, tokens_len, half_d), full),
        (acts, low),
        (padded, low),
        ((3, images, tokens_len, three), low),
        ((positions, half_c), full),
        ((2, images, channels), full),
        ((2, lines, 128), full),
        ((images * rows, qkv_blocks.shape[2]), low),
        ((out_blocks.shape[1], images * rows), low),
        ((images * rows, cols), low),
        ((cols, images * rows), low),
    ]
    return pl.pallas_call(
        functools.partial(res_forward_kernel, breadth),
        out_shape=[jax.ShapeDtypeStruct(shape, kind) for shape, kind in outs],
        in_specs=[IN_VMEM] * 7 + [ANYWHERE] * 6,
        out_specs=[IN_VMEM] * 3 + [ANYWHERE] * 2 + [IN_VMEM] * 4 + [ANYWHERE] * 4,
        scratch_shapes=[
            pltpu.SemaphoreType.DMA((2, images)),
            pltpu.VMEM(image_blocks.shape, low),
            pltpu.VMEM((images, lines, 128), low),
            pltpu.VMEM((images, lines, 128), low),
            pltpu.VMEM(acts, low),
            pltpu.VMEM(padded, low),
            pltpu.VMEM(pictures, low),
            pltpu.VMEM(pictures, low),
            pltpu.SemaphoreType.DMA((images,)),
            pltpu.SemaphoreType.DMA((images,)),
            pltpu.SemaphoreType.DMA((2,)),
            pltpu.SemaphoreType.DMA((2,)),
            pltpu.SemaphoreType.DMA((2,)),
        ]
        + reduce_scratch((positions, half_c), 2)
        + gather_scratch(2)
        + reduce_scratch((tokens_len, half_d), 2)
        + ride_scratch(5)
        + pair_ride_scratch(2),
        compiler_params=params(number),
        name="res_forward",
    )(*args)


def silu_slope(z):
    gate = jax.nn.sigmoid(z)
    return gate * (1.0 + z * (1.0 - gate))


def res_backward_kernel(
    breadth,
    shrunk,
    pictures,
    gain_bias,
    conv_one,
    conv_two,
    conv_half,
    mods,
    picks,
    taps_half,
    middle,
    stats,
    acts_in,
    taps_one_in,
    qkv_grad,
    out_grad,
    up_grad,
    ada_grad,
    pictures_out,
    norm_out,
    mods_back,
    ada_back,
    one_out,
    two_out,
    half_out,
    qkv_back,
    out_back,
    up_back,
    qkv_pair,
    out_pair,
    qkv_sums,
    out_sums,
    mods_block,
    gathered,
    gathered_middle,
    acts,
    taps_one,
    taps_two,
    mine,
    theirs,
    back,
    back_theirs,
    held,
    sums,
    outgoing,
    acted,
    one_grad,
    two_grad,
    half_grad,
    pair_send,
    pair_recv,
    back_send,
    back_recv,
    trade_send,
    trade_recv,
    io_sem,
    share_sem,
    neighbour_sem,
    store_sem,
    *scratch,
):
    (shrunk_send, shrunk_recv), (middle_send, middle_recv) = (scratch[:2], scratch[2:4])
    reducing = scratch[4:10]
    at = Place(True)
    images, positions, channels = pictures.shape
    others = images - 1
    tokens_len = positions // 4
    load_acts = pltpu.make_async_copy(acts_in, acts, io_sem.at[0])
    load_taps = pltpu.make_async_copy(taps_one_in, taps_one, io_sem.at[1])
    load_acts.start()
    load_taps.start()
    gathered[at.slot] = shrunk[...]

    greet_all(at)

    def peer(step):
        return (at.dp + step) % images

    rows, cols = (D // images, up_grad.shape[1])
    half = images // 2
    side = at.dp % 2

    def to_neighbour(part, place):
        chip = 2 * place + 1 - side
        source, target = (
            (strip(qkv_grad, 0, chip, rows), qkv_pair.at[place]),
            (strip(out_grad, 1, chip, rows), out_pair.at[place]),
        )[part]
        return remote(
            source,
            target,
            neighbour_sem.at[0, part, place],
            neighbour_sem.at[1, part, place],
            (at.x_mate, at.core),
        )

    def store(part, step):
        chip = (at.dp + 2 * step) % images
        source, target = ((qkv_sums, qkv_back), (out_sums, out_back))[part]
        return remote(
            source.at[chip // 2],
            target.at[at.dp // 2],
            store_sem.at[0, part, step],
            store_sem.at[1, part, step],
            (chip, at.core),
        )

    def store_own(part):
        source, target = ((qkv_sums, qkv_back), (out_sums, out_back))[part]
        return pltpu.make_async_copy(
            source.at[at.dp // 2], target.at[at.dp // 2], store_sem.at[0, part, 0]
        )

    def store_sums():
        @pl.loop(0, half)
        def _(place):
            chip = 2 * place + side
            to_neighbour(0, place).wait_recv()
            own = strip(qkv_grad, 0, chip, rows)[...].astype(jnp.float32)
            qkv_sums[place] = (own + qkv_pair[place].astype(jnp.float32)).astype(jnp.bfloat16)
            to_neighbour(1, place).wait_recv()
            own = strip(out_grad, 1, chip, rows)[...].astype(jnp.float32)
            out_sums[place] = (own + out_pair[place].astype(jnp.float32)).astype(jnp.bfloat16)

        for part in range(2):
            store_own(part).start()

            @pl.loop(1, half)
            def _(step):
                store(part, step).start()

    for part in range(2):

        @pl.loop(0, half)
        def _(place):
            to_neighbour(part, place).start()

    ride = Ride(
        at,
        [
            (lambda chip: ada_grad.at[at.core], lambda chip: ada_back.at[at.core, chip]),
            (lambda chip: mods_block, lambda chip: mods_back.at[chip]),
            (lambda chip: strip(up_grad, 0, chip, rows), lambda chip: strip(up_back, 1, chip, cols)),
        ],
        *scratch[10:],
    )
    ride.start(0, 1)

    def swap(slot):
        return remote(
            mine.at[slot],
            theirs.at[slot],
            pair_send.at[slot],
            pair_recv.at[slot],
            (at.dp, 1 - at.core),
        )

    def half_back(slot):
        products = [dot_nt(gathered[slot], conv_half[a]) for a in range(3)]
        products = jnp.concatenate(products, axis=0)
        coarse = products.astype(jnp.bfloat16)
        fine = (products - coarse.astype(jnp.float32)).astype(jnp.bfloat16)
        spread = dot_tn(picks[...], coarse) + dot_tn(picks[...], fine)
        mine[slot] = fold_three(spread, breadth, True).astype(jnp.bfloat16)
        swap(slot).start()

    gather_stage(at, [gathered], half_back, 2, shrunk_send, shrunk_recv)

    store_sums()

    def resid(slot):
        return mine[slot].astype(jnp.float32) + theirs[slot].astype(jnp.float32)

    def second_back(slot):
        swap(slot).wait_recv()
        branch = resid(slot).astype(jnp.bfloat16).astype(jnp.float32)
        store_padded(taps_two, slot, side_by_side(branch, breadth, True), breadth)
        total = jnp.zeros((positions, conv_two.shape[2]), jnp.float32)
        for a in range(3):
            total += dot(taps_two[slot, pl.ds((2 - a) * breadth, positions)], conv_two[a])
        reducing[0][slot] = total.astype(jnp.bfloat16)

    def weights_meanwhile():
        half_grad[...] = jnp.zeros_like(half_grad)
        two_grad[...] = jnp.zeros_like(two_grad)
        load_acts.wait()

        @pl.loop(0, images // 4)
        def _(i):
            right = gathered[pl.ds(4 * i, 4)].reshape(4 * tokens_len, -1)
            for a in range(3):
                left = taps_half[a, pl.ds(4 * i, 4)].reshape(4 * tokens_len, 3 * channels)
                half_grad[a] += dot_tn(left, right)

        @pl.loop(0, images)
        def _(i):
            right = acts[i]
            for a in range(3):
                left = taps_two[i, pl.ds((2 - a) * breadth, positions)]
                two_grad[a] += dot_tn(left, right)

        save(half_grad, half_out, 2).start()
        save(two_grad, two_out, 3).start()

    def save(source, target, sem):
        return pltpu.make_async_copy(source, target, io_sem.at[sem])

    reduce_stage(at, acted, second_back, 2, reducing, False, weights_meanwhile)

    x = middle[...]
    center = mean_of_groups(jnp.sum(x, axis=0, keepdims=True), positions)
    x = x - center
    scale = lax.rsqrt(mean_of_groups(jnp.sum(x * x, axis=0, keepdims=True), positions) + GN_EPS)
    normed = x * scale
    slope = 1.0 + mods[0:1]
    grad = acted[...] * silu_slope(normed * slope + mods[1:2])
    along = jnp.sum(grad * normed, axis=0, keepdims=True)
    level = jnp.sum(grad, axis=0, keepdims=True)
    lines = along.shape[1] // 128
    for i in range(lines):
        mods_block[i : i + 1] = along[:, 128 * i : 128 * (i + 1)]
        mods_block[lines + i : lines + i + 1] = level[:, 128 * i : 128 * (i + 1)]
    ride.start(1, 2)
    ride.start(2, 3)
    along = mean_of_groups(slope * along, positions)
    level = mean_of_groups(slope * level, positions)
    gathered_middle[at.slot] = ((slope * grad - level - normed * along) * scale).astype(jnp.bfloat16)

    def swap_back(slot):
        return remote(
            back.at[slot],
            back_theirs.at[slot],
            back_send.at[slot],
            back_recv.at[slot],
            (at.dp, 1 - at.core),
        )

    def first_back(slot):
        below, same, above = (dot_nt(gathered_middle[slot], conv_one[a]) for a in range(3))
        folded = fold_three(fold_rows(above, same, below, breadth), breadth, True)
        back[slot] = folded.astype(jnp.bfloat16)
        swap_back(slot).start()

    gather_stage(at, [gathered_middle], first_back, 2, middle_send, middle_recv)

    gain, bias = (gain_bias[0:1], gain_bias[1:2])

    def normed_of(i):
        return (pictures[i].astype(jnp.float32) - stats[0, pl.ds(i, 1)]) * stats[1, pl.ds(i, 1)]

    @pl.loop(0, images)
    def _(i):
        swap_back(i).wait_recv()
        grad = back[i].astype(jnp.float32) + back_theirs[i].astype(jnp.float32)
        normed = normed_of(i)
        grad = grad * silu_slope(normed * gain + bias)
        held[i] = grad
        sums[0, pl.ds(i, 1)] = jnp.sum(grad * normed, axis=0, keepdims=True)
        sums[1, pl.ds(i, 1)] = jnp.sum(grad, axis=0, keepdims=True)

    norm_out[0:1] = jnp.sum(sums[0], axis=0, keepdims=True)
    norm_out[1:2] = jnp.sum(sums[1], axis=0, keepdims=True)
    sums[0] = mean_of_groups(gain * sums[0], positions)
    sums[1] = mean_of_groups(gain * sums[1], positions)

    def deliver(step):
        return remote(
            outgoing.at[peer(step)],
            pictures_out.at[at.dp],
            trade_send.at[step - 1],
            trade_recv.at[step - 1],
            (peer(step), at.core),
        )

    keep = save(outgoing.at[at.dp], pictures_out.at[at.dp], 5)

    @pl.loop(0, images)
    def _(step):
        i = peer(step)
        part = gain * held[i] - sums[1, pl.ds(i, 1)] - normed_of(i) * sums[0, pl.ds(i, 1)]
        part = resid(i) + part * stats[1, pl.ds(i, 1)]
        half = positions // 2
        outgoing[i] = jnp.concatenate([part[:half], part[half:]], axis=1).astype(jnp.bfloat16)
        pl.when(step == 0)(keep.start)
        pl.when(step > 0)(lambda: deliver(step).start())

    one_grad[...] = jnp.zeros_like(one_grad)
    load_taps.wait()

    @pl.loop(0, images)
    def _(i):
        right = gathered_middle[i]
        for a in range(3):
            one_grad[a] += dot_tn(taps_one[i, pl.ds(a * breadth, positions)], right)

    save(one_grad, one_out, 4).start()

    @pl.loop(0, images)
    def _(slot):
        swap(slot).wait_send()
        swap_back(slot).wait_send()

    keep.wait()

    ride.wait()
    for part in range(2):
        store_own(part).wait()

        @pl.loop(0, half)
        def _(step):
            to_neighbour(part, step).wait_send()
            pl.when(step > 0)(lambda: store(part, step).wait())

    share_stage(at, ada_back, share_sem.at[0], share_sem.at[1])

    @pl.loop(1, others + 1)
    def _(step):
        deliver(step).wait()

    save(half_grad, half_out, 2).wait()
    save(two_grad, two_out, 3).wait()
    save(one_grad, one_out, 4).wait()


def res_backward(number, breadth, *args):
    (shrunk, pictures, gain_bias, conv_one, conv_two, conv_half, mods, picks, taps_half, middle, stats, acts, taps_one, qkv_grad, out_grad, up_grad, ada_grad) = args
    images, positions, channels = pictures.shape
    half_c = conv_one.shape[2]
    half_d = conv_half.shape[2]
    tokens_len = positions // 4
    three = 3 * channels
    low, full = (jnp.bfloat16, jnp.float32)
    rows = qkv_grad.shape[0] // images
    grads = [(3, three, half_c), (3, three, half_c), (3, three, half_d)]
    traded = (images, positions // 2, 2 * channels)
    return pl.pallas_call(
        functools.partial(res_backward_kernel, breadth),
        out_shape=[
            jax.ShapeDtypeStruct(traded, low),
            jax.ShapeDtypeStruct((2, channels), full),
            jax.ShapeDtypeStruct((images, 2 * half_c // 128, 128), full),
            jax.ShapeDtypeStruct((2, images) + ada_grad.shape[1:], ada_grad.dtype),
        ]
        + [jax.ShapeDtypeStruct(shape, full) for shape in grads]
        + [
            jax.ShapeDtypeStruct((images // 2, rows, qkv_grad.shape[1]), low),
            jax.ShapeDtypeStruct((images // 2, out_grad.shape[0], rows), low),
            jax.ShapeDtypeStruct((rows, images * up_grad.shape[1]), low),
        ],
        in_specs=[IN_VMEM] * 11 + [ANYWHERE] * 2 + [IN_VMEM] * 2 + [ANYWHERE] * 2,
        out_specs=[ANYWHERE, IN_VMEM] + [ANYWHERE] * 8,
        scratch_shapes=[
            pltpu.VMEM((images // 2, rows, qkv_grad.shape[1]), low),
            pltpu.VMEM((images // 2, out_grad.shape[0], rows), low),
            pltpu.VMEM((images // 2, rows, qkv_grad.shape[1]), low),
            pltpu.VMEM((images // 2, out_grad.shape[0], rows), low),
            pltpu.VMEM((2 * half_c // 128, 128), full),
            pltpu.VMEM((images, tokens_len, half_d), low),
            pltpu.VMEM((images, positions, half_c), low),
            pltpu.VMEM(acts.shape, low),
            pltpu.VMEM(taps_one.shape, low),
            pltpu.VMEM(taps_one.shape, low),
            pltpu.VMEM(pictures.shape, low),
            pltpu.VMEM(pictures.shape, low),
            pltpu.VMEM(pictures.shape, low),
            pltpu.VMEM(pictures.shape, low),
            pltpu.VMEM(pictures.shape, full),
            pltpu.VMEM((2, images, channels), full),
            pltpu.VMEM(traded, low),
            pltpu.VMEM((positions, half_c), full),
        ]
        + [pltpu.VMEM(shape, full) for shape in grads]
        + [pltpu.SemaphoreType.DMA((images,))] * 4
        + [pltpu.SemaphoreType.DMA((images - 1,))] * 2
        + [pltpu.SemaphoreType.DMA((6,)), pltpu.SemaphoreType.DMA((2,))]
        + [pltpu.SemaphoreType.DMA((2, 2, images // 2))] * 2
        + gather_scratch(2)
        + gather_scratch(2)
        + reduce_scratch((positions, half_c), 2)
        + ride_scratch(3),
        compiler_params=params(number),
        name="res_backward",
    )(*args)


def gelu_of(z):
    inner = jnp.tanh(math.sqrt(2.0 / math.pi) * (z + 0.044715 * z * z * z))
    return 0.5 * z * (1.0 + inner)


def gelu_slope(z):
    rate = math.sqrt(2.0 / math.pi)
    inner = jnp.tanh(rate * (z + 0.044715 * z * z * z))
    return 0.5 * (1.0 + inner) + 0.5 * z * (1.0 - inner * inner) * rate * (1.0 + 3 * 0.044715 * z * z)


def transformer_kernel(
    shrunk,
    mods,
    cotangent,
    qkv_head,
    out_head,
    up_here,
    down_here,
    block_out,
    token_grad,
    mods_grad,
    qkv_grad,
    out_grad,
    up_grad,
    down_back,
    tokens,
    own_out,
    outgoing,
    mods_part,
    mods_theirs,
    attn_in,
    qkv,
    probs,
    mixed,
    attended,
    mlp_in,
    expanded_grad,
    pre_act,
    hidden,
    pre_grad,
    expanded,
    mlp_grad,
    down_grad,
    attended_grad,
    mixed_grad,
    qkv_back,
    attn_grad,
    share_send,
    share_recv,
    *scratch,
):
    scratch = list(scratch)

    def take(count):
        taken = scratch[:count]
        del scratch[:count]
        return taken

    gather_one, gather_two, gather_three, gather_four = (take(4), take(4), take(4), take(4))
    reduce_one, reduce_two, reduce_three, reduce_four = (take(10), take(10), take(10), take(10))
    ride_back = take(3)
    at, near = (Place(True), Place(False))
    greet_all(at)
    tokens_len = cotangent.shape[0]
    half = tokens_len // 2
    rows, cols = (D // (4 * LAYERS), up_here.shape[1])
    images = 4 * LAYERS
    score_scale = HDIM ** (-0.5)
    low, full = (jnp.bfloat16, jnp.float32)
    mine = pl.ds(pl.multiple_of(at.core * half, half), half)

    def split(place, value, stage):
        value = value.astype(low)
        for core in range(2):

            @pl.when(at.core == core)
            def _():
                stage[0][place] = value[core * half : (core + 1) * half]
                stage[6][place] = value[(1 - core) * half : (2 - core) * half]

    def image_rows(i):
        return pl.ds(pl.multiple_of(i * tokens_len, tokens_len), tokens_len)

    width = shrunk.shape[2]
    tokens[:, :width] = shrunk[0, mine]
    tokens[:, width:] = shrunk[1, mine]
    normed, _ = layer_stats(tokens[...])
    attn_in[near.slot, near.core] = (normed * (1.0 + mods[1:2]) + mods[0:1]).astype(low)
    upstream = cotangent[mine].astype(full)
    expanded_grad[at.slot, at.core] = ((1.0 + mods[5:6]) * upstream).astype(low)
    grad_turn, _, grad_end = gather_steps(
        at, [expanded_grad], None, 1, *gather_four[:2], gather_four[2:]
    )

    def in_gather(count):
        pl.when(count % 2 == 0)(lambda: grad_turn(count // 2))

    def in_sum(count):
        grad_turn(8 + count)

    gather_stage(near, [attn_in], None, 2, *gather_one[:2], gather_one[2:], tick=in_gather)

    @pl.loop(0, images // 2)
    def _(i):
        rows_in = attn_in[i].reshape(tokens_len, D)
        low_qkv = dot(rows_in, qkv_head[...]).astype(low)
        qkv[image_rows(i)] = low_qkv
        query, key, value = (low_qkv[:, j * HDIM : (j + 1) * HDIM] for j in range(3))
        scores = dot_nt(query, key) * score_scale
        scores = scores - jnp.max(scores, axis=1, keepdims=True)
        weight = jnp.exp(scores)
        weight = weight / jnp.sum(weight, axis=1, keepdims=True)
        probs[i] = weight
        mixed[image_rows(i)] = dot(weight.astype(low), value).astype(low)

    def attention_term(place):
        split(place, dot(mixed[image_rows(place)], out_head[...]), reduce_one)

    reduce_stage(near, attended, attention_term, 2, reduce_one, True, tick=in_sum)
    grad_end()

    after = tokens[...] + (1.0 + mods[2:3]) * attended[...]
    normed, _ = layer_stats(after)
    mlp_in[at.slot, at.core] = (normed * (1.0 + mods[4:5]) + mods[3:4]).astype(low)
    gather_stage(at, [mlp_in], None, 2, *gather_two[:2], gather_two[2:])

    @pl.loop(0, LAYERS)
    def _(i):
        here = pl.ds(pl.multiple_of(i * 4 * tokens_len, 4 * tokens_len), 4 * tokens_len)
        z = dot(mlp_in[pl.ds(4 * i, 4)].reshape(4 * tokens_len, D), up_here[...])
        pre_act[here] = z
        hidden[here] = gelu_of(z).astype(low)

    def hidden_term(place):
        split(place, dot(hidden[image_rows(place)], down_here[...]), reduce_two)

    def hidden_grads():
        @pl.loop(0, LAYERS)
        def _(i):
            here = pl.ds(pl.multiple_of(i * 4 * tokens_len, 4 * tokens_len), 4 * tokens_len)
            grad = dot_nt(expanded_grad[pl.ds(4 * i, 4)].reshape(4 * tokens_len, D), down_here[...])
            pre_grad[here] = (grad * gelu_slope(pre_act[here])).astype(low)

        @pl.loop(0, D // 512)
        def _(i):
            here = pl.ds(pl.multiple_of(i * 512, 512), 512)
            left = expanded_grad[:, :, :, here].reshape(images * tokens_len, 512)
            down_grad[:, here] = dot_tn(hidden[...], left).astype(low)
            right = mlp_in[:, :, :, here].reshape(images * tokens_len, 512)
            up_grad[here] = dot_tn(right, pre_grad[...]).astype(low)

    reduce_stage(at, expanded, hidden_term, 2, reduce_two, True, hidden_grads)
    back = Ride(
        at,
        [
            (lambda chip: strip(down_grad, 1, chip, rows), lambda chip: strip(down_back, 0, chip, cols)),
        ],
        *ride_back,
    )
    back.start()
    own_out[...] = (after + (1.0 + mods[5:6]) * expanded[...]).astype(low)
    block_out[mine] = own_out[...]
    mods_part[5:6] = jnp.sum(upstream * expanded[...], axis=0, keepdims=True)

    def exchange(index, source, target):
        return remote(
            source, target, share_send.at[index], share_recv.at[index], (at.dp, 1 - at.core)
        )

    give_out = exchange(0, own_out, block_out.at[mine])
    give_out.start()

    def mlp_term(place):
        split(place, dot_nt(pre_grad[image_rows(place)], up_here[...]), reduce_three)

    reduce_stage(at, mlp_grad, mlp_term, 2, reduce_three, True)
    after = tokens[...] + (1.0 + mods[2:3]) * attended[...]
    normed, scale = layer_stats(after)
    grad = mlp_grad[...]
    mods_part[3:4] = jnp.sum(grad, axis=0, keepdims=True)
    mods_part[4:5] = jnp.sum(grad * normed, axis=0, keepdims=True)
    grad_after = cotangent[mine].astype(full) + layer_back(normed, scale, (1.0 + mods[4:5]) * grad)
    mods_part[2:3] = jnp.sum(grad_after * attended[...], axis=0, keepdims=True)

    attended_grad[near.slot, near.core] = ((1.0 + mods[2:3]) * grad_after).astype(low)
    attended[...] = grad_after
    gather_stage(near, [attended_grad], None, 2, *gather_three[:2], gather_three[2:])

    @pl.loop(0, images // 2)
    def _(i):
        grad = dot_nt(attended_grad[i].reshape(tokens_len, D), out_head[...]).astype(low)
        low_qkv = qkv[image_rows(i)]
        query, key, value = (low_qkv[:, j * HDIM : (j + 1) * HDIM] for j in range(3))
        weight = probs[i]
        grad_probs = dot_nt(grad, value)
        grad_value = dot_tn(weight.astype(low), grad)
        inner = jnp.sum(grad_probs * weight, axis=1, keepdims=True)
        grad_scores = (weight * (grad_probs - inner)).astype(low)
        grad_query = dot(grad_scores, key) * score_scale
        grad_key = dot_tn(grad_scores, query) * score_scale
        qkv_back[image_rows(i)] = jnp.concatenate(
            [grad_query, grad_key, grad_value], axis=1
        ).astype(low)

    def qkv_term(place):
        split(place, dot_nt(qkv_back[image_rows(place)], qkv_head[...]), reduce_four)

    def attention_grads():
        @pl.loop(0, D // 512)
        def _(i):
            here = pl.ds(pl.multiple_of(i * 512, 512), 512)
            right = attended_grad[:, :, :, here].reshape(images // 2 * tokens_len, 512)
            out_grad[:, here] = dot_tn(mixed[...], right).astype(low)
            left = attn_in[:, :, :, here].reshape(images // 2 * tokens_len, 512)
            qkv_grad[here] = dot_tn(left, qkv_back[...]).astype(low)

    reduce_stage(near, attn_grad, qkv_term, 2, reduce_four, True, attention_grads)
    normed, scale = layer_stats(tokens[...])
    grad = attn_grad[...]
    mods_part[0:1] = jnp.sum(grad, axis=0, keepdims=True)
    mods_part[1:2] = jnp.sum(grad * normed, axis=0, keepdims=True)
    give_mods = exchange(1, mods_part, mods_theirs)
    give_mods.start()

    grad = (attended[...] + layer_back(normed, scale, (1.0 + mods[1:2]) * grad)).astype(low)
    for core in range(2):

        @pl.when(at.core == core)
        def _():
            token_grad[mine] = grad[:, core * width : (core + 1) * width]
            outgoing[...] = grad[:, (1 - core) * width : (2 - core) * width]

    give_tokens = exchange(2, outgoing, token_grad.at[mine])
    give_tokens.start()
    for give in (give_out, give_mods, give_tokens):
        give.wait()
    mods_grad[...] = mods_part[...] + mods_theirs[...]
    back.wait()


def transformer(number, *args):
    shrunk, mods, cotangent, qkv_head, out_head, up_here, down_here = args
    tokens_len = cotangent.shape[0]
    images = 4 * LAYERS
    half = tokens_len // 2
    rows, cols = (D // images, up_here.shape[1])
    low, full = (jnp.bfloat16, jnp.float32)
    both = (2, half, D)
    near_tokens = images // 2 * tokens_len
    vmem = [
        ((half, D), full),
        ((half, D), low),
        ((half, shrunk.shape[2]), low),
        (mods.shape, full),
        (mods.shape, full),
        ((images // 2,) + both, low),
        ((near_tokens, 3 * HDIM), low),
        ((images // 2, tokens_len, tokens_len), full),
        ((near_tokens, HDIM), low),
        ((half, D), full),
        ((images,) + both, low),
        ((images,) + both, low),
        ((images * tokens_len, cols), full),
        ((images * tokens_len, cols), low),
        ((images * tokens_len, cols), low),
        ((half, D), full),
        ((half, D), full),
        ((cols, D), low),
        ((images // 2,) + both, low),
        ((near_tokens, HDIM), low),
        ((near_tokens, 3 * HDIM), low),
        ((half, D), full),
    ]
    return pl.pallas_call(
        transformer_kernel,
        out_shape=[
            jax.ShapeDtypeStruct((tokens_len, D), low),
            jax.ShapeDtypeStruct(shrunk.shape[1:], low),
            jax.ShapeDtypeStruct(mods.shape, full),
            jax.ShapeDtypeStruct(qkv_head.shape, low),
            jax.ShapeDtypeStruct(out_head.shape, low),
            jax.ShapeDtypeStruct((D, cols), low),
            jax.ShapeDtypeStruct((images * cols, rows), low),
        ],
        in_specs=[IN_VMEM] * 7,
        out_specs=[IN_VMEM] * 6 + [ANYWHERE],
        scratch_shapes=[pltpu.VMEM(shape, kind) for shape, kind in vmem]
        + [pltpu.SemaphoreType.DMA((4,))] * 2
        + gather_scratch(2, 1, False, True)
        + gather_scratch(2, 1, True, True)
        + gather_scratch(2, 1, False, True)
        + gather_scratch(1, 1, True, True)
        + reduce_scratch((half, D), 2, False, True)
        + reduce_scratch((half, D), 2, True, True) * 2
        + reduce_scratch((half, D), 2, False, True)
        + ride_scratch(1),
        compiler_params=params(number),
        name="transformer",
    )(*args)


def rows_at_once(shape):
    size = math.prod(shape[1:-2] + tuple(-(-n // t) * t for n, t in zip(shape[-2:], (8, 128))))
    if len(shape) == 2:
        size = -(-shape[1] // 128) * 128
    step = shape[0]
    while step % 2 == 0 and step * size > 96 * 1024:
        step //= 2
    return step


def total_kernel(shared, *refs):
    count = len(shared)
    grads, out_ref, held = (refs[:count], refs[count], refs[count + 1 : 2 * count + 1])
    line, mine, tiles, send_sem, recv_sem, load_sem = refs[2 * count + 1 :]
    at = Place(True)

    def load(index):
        return pltpu.make_async_copy(grads[index], held[index], load_sem.at[index])

    for index in range(count):
        load(index).start()
    line[...] = jnp.zeros_like(line)
    for index in range(count):
        load(index).wait()
        ref = held[index]
        step = rows_at_once(ref.shape)

        @pl.loop(0, ref.shape[0] // step)
        def _(i):
            part = ref[pl.ds(i * step, step)].astype(jnp.float32)
            part = jnp.sum(part * part, axis=0, keepdims=len(ref.shape) == 2)
            if len(ref.shape) == 3:
                part = jnp.sum(part, axis=0, keepdims=True)
            weight = 0.5 if shared[index] else 1.0
            line[:, : ref.shape[-1]] += weight * part

    mine[...] = jnp.broadcast_to(jnp.sum(line[...], axis=1, keepdims=True), mine.shape)
    greet_all(at)
    across = remote(mine, tiles.at[0], send_sem.at[0], recv_sem.at[0], (at.dp, 1 - at.core))
    across.start()
    across.wait()
    mine[...] = mine[...] + tiles[0]
    others = 4 * LAYERS - 1

    def copy(step):
        peer = (at.dp + step) % (4 * LAYERS)
        return remote(
            mine, tiles.at[step], send_sem.at[step], recv_sem.at[step], (peer, at.core)
        )

    @pl.loop(1, others + 1)
    def _(step):
        copy(step).start()

    @pl.loop(1, others + 1)
    def _(step):
        copy(step).wait()

    total = jnp.zeros_like(mine)
    for chip in range(4 * LAYERS):
        step = (at.dp - chip + 4 * LAYERS) % (4 * LAYERS)
        total = total + jnp.where(step == 0, mine[...], tiles[step])
    out_ref[...] = total


def total_of_squares(number, grads, shared):
    tile = (8, 128)
    count = len(grads)
    longest = max(grad.shape[-1] for grad in grads)
    return pl.pallas_call(
        functools.partial(total_kernel, shared),
        out_shape=jax.ShapeDtypeStruct(tile, jnp.float32),
        in_specs=[ANYWHERE] * count,
        out_specs=IN_VMEM,
        scratch_shapes=[pltpu.VMEM(grad.shape, grad.dtype) for grad in grads]
        + [
            pltpu.VMEM((1, longest), jnp.float32),
            pltpu.VMEM(tile, jnp.float32),
            pltpu.VMEM((16,) + tile, jnp.float32),
            pltpu.SemaphoreType.DMA((16,)),
            pltpu.SemaphoreType.DMA((16,)),
            pltpu.SemaphoreType.DMA((count,)),
        ],
        compiler_params=params(number),
        name="total",
    )(*grads)


def update_kernel(rates, *refs):
    count = len(rates)
    total, refs = (refs[0], refs[1:])
    ins, outs = (refs[: 4 * count], refs[4 * count : 7 * count])
    held, (load_sem, store_sem) = (refs[7 * count : 11 * count], refs[11 * count :])

    def load(index):
        return pltpu.make_async_copy(ins[index], held[index], load_sem.at[index])

    for index in range(4 * count):
        load(index).start()
    factor = jnp.minimum(1.0, CLIP / (jnp.sqrt(total[0:1, 0:1]) + 1e-06))
    correct_one = 1.0 / (1.0 - BETA_ONE**STEP)
    correct_two = 1.0 / (1.0 - BETA_TWO**STEP)
    for index, rate in enumerate(rates):
        master, average, square, grad = held[4 * index : 4 * index + 4]
        for part in range(4):
            load(4 * index + part).wait()
        step = rows_at_once(master.shape)

        @pl.loop(0, master.shape[0] // step)
        def _(i):
            at = pl.ds(i * step, step)
            clipped = grad[at].astype(jnp.float32) * factor
            new_avg = BETA_ONE * average[at] + (1.0 - BETA_ONE) * clipped
            new_sq = BETA_TWO * square[at] + (1.0 - BETA_TWO) * clipped * clipped
            step_dir = new_avg * correct_one / (jnp.sqrt(new_sq * correct_two) + ADAM_EPS)
            old = master[at]
            master[at] = old - rate * (step_dir + DECAY * old)
            average[at] = new_avg
            square[at] = new_sq

        for part in range(3):
            pltpu.make_async_copy(
                held[4 * index + part], outs[3 * index + part], store_sem.at[3 * index + part]
            ).start()
    for index in range(count):
        for part in range(3):
            pltpu.make_async_copy(
                held[4 * index + part], outs[3 * index + part], store_sem.at[3 * index + part]
            ).wait()


def update(total, quads, rates):
    count = len(quads)
    flat = [array for quad in quads for array in quad]
    return pl.pallas_call(
        functools.partial(update_kernel, rates),
        out_shape=[
            jax.ShapeDtypeStruct(array.shape, array.dtype) for quad in quads for array in quad[:3]
        ],
        in_specs=[IN_VMEM] + [ANYWHERE] * (4 * count),
        out_specs=[ANYWHERE] * (3 * count),
        scratch_shapes=[pltpu.VMEM(array.shape, array.dtype) for array in flat]
        + [pltpu.SemaphoreType.DMA((4 * count,)), pltpu.SemaphoreType.DMA((3 * count,))],
        compiler_params=pltpu.CompilerParams(vmem_limit_bytes=VMEM_GRANT),
        name="update",
    )(total, *flat)


def layer_stats(values):
    center = jnp.mean(values, axis=-1, keepdims=True)
    shifted = values - center
    spread = jnp.mean(shifted * shifted, axis=-1, keepdims=True)
    scale = lax.rsqrt(spread + LN_EPS)
    return shifted * scale, scale


def layer_back(normed, scale, grad):
    first = jnp.mean(grad, axis=-1, keepdims=True)
    second = jnp.mean(grad * normed, axis=-1, keepdims=True)
    return (grad - first - normed * second) * scale


def widen(block):
    return block.astype(jnp.float32)


def lower(block):
    return block.astype(jnp.bfloat16)


def paired_lanes(block):
    half = block.shape[-2] // 2
    return jnp.concatenate([block[..., :half, :], block[..., half:, :]], axis=-1)


def unpaired_lanes(block):
    half = block.shape[-1] // 2
    return jnp.concatenate([block[..., :half], block[..., half:]], axis=-2)


def half_picks(height, breadth):
    outputs = height * breadth // 4
    tap, out = (jnp.arange(3 * outputs) // outputs, jnp.arange(3 * outputs) % outputs)
    row = 2 * (out // (breadth // 2)) + tap - 1
    source = row * breadth + 2 * (out % (breadth // 2))
    place = jnp.arange(height * breadth)
    return ((place[None, :] == source[:, None]) & (row[:, None] >= 0)).astype(jnp.bfloat16)


def dot(left, right):
    return jnp.dot(left, right, preferred_element_type=jnp.float32)


def dot_tn(left, right):
    return lax.dot_general(left, right, (((0,), (0,)), ((), ())), preferred_element_type=jnp.float32)


def dot_nt(left, right):
    return lax.dot_general(left, right, (((1,), (1,)), ((), ())), preferred_element_type=jnp.float32)


def stationary(
    images,
    t_index,
    cotangent,
    norm_params,
    norm_params_avg,
    norm_params_sq,
    first_conv,
    first_conv_avg,
    first_conv_sq,
    resnet_mod,
    resnet_mod_avg,
    resnet_mod_sq,
    second_conv,
    second_kernel_first_moment,
    second_conv_sq,
    down_conv,
    down_conv_avg,
    down_conv_sq,
    ada_proj,
    ada_proj_avg,
    ada_proj_sq,
    qkv_proj,
    qkv_proj_avg,
    qkv_proj_sq,
    out_proj,
    out_proj_avg,
    out_proj_sq,
    hidden_in,
    hidden_in_avg,
    hidden_in_sq,
    hidden_out,
    hidden_out_avg,
    hidden_out_sq,
):
    masters = (
        norm_params,
        first_conv,
        resnet_mod,
        second_conv,
        down_conv,
        ada_proj,
        qkv_proj,
        out_proj,
        hidden_in,
        hidden_out,
    )
    averages = (
        norm_params_avg,
        first_conv_avg,
        resnet_mod_avg,
        second_kernel_first_moment,
        down_conv_avg,
        ada_proj_avg,
        qkv_proj_avg,
        out_proj_avg,
        hidden_in_avg,
        hidden_out_avg,
    )
    squares = (
        norm_params_sq,
        first_conv_sq,
        resnet_mod_sq,
        second_conv_sq,
        down_conv_sq,
        ada_proj_sq,
        qkv_proj_sq,
        out_proj_sq,
        hidden_in_sq,
        hidden_out_sq,
    )
    n_dp = lax.axis_size(DP)
    dp_pos = lax.axis_index(DP)
    tensor_pos = lax.axis_index(TENSOR)
    height, breadth = (images.shape[1], images.shape[2])
    positions = height * breadth
    tokens_len = positions // 4
    local_c = C // n_dp
    half_c = first_conv.shape[3]
    half_d = down_conv.shape[3]
    freq_rows = resnet_mod.shape[0]
    heads_here = out_proj.shape[0]
    picks = half_picks(height, breadth)
    numbers = itertools.count()

    stored_order = {3: lambda array: array.transpose(0, 1, 3, 2), 5: lambda array: array.transpose(1, 0, 2)}

    gain_bias = widen(lower(norm_params))
    conv_one = lower(first_conv).reshape(3, 3 * local_c, half_c)
    conv_two = lower(stored_order[3](second_conv)).reshape(3, 3 * local_c, half_c)
    conv_half = lower(down_conv).reshape(3, 3 * local_c, half_d)
    qkv_blocks = lower(qkv_proj).transpose(2, 0, 1, 3).reshape(heads_here, D // n_dp, 3 * HDIM)

    emb = widen(lower(embed_noise(t_index, FREQ))).reshape(n_dp, 1, freq_rows)
    emb = jnp.pad(emb, ((0, 0), (0, 7), (0, 128 - freq_rows)))
    image_blocks = images.reshape(positions, n_dp, local_c).transpose(1, 0, 2)
    ada_half = lax.dynamic_slice_in_dim(stored_order[5](ada_proj), tensor_pos * 3, 3, axis=0)
    convs = (conv_one, conv_two, conv_half)

    pictures, emb, shrunk, act_two, taps_one, taps_half, middle, stats_one, mods, *heads = res_forward(
        next(numbers),
        height,
        breadth,
        gain_bias,
        *convs,
        picks,
        lower(resnet_mod).reshape(freq_rows, 2 * half_c),
        lower(ada_half),
        paired_lanes(image_blocks).reshape(n_dp, 2, positions // 4, 2 * local_c),
        emb,
        qkv_blocks,
        lower(out_proj),
        lower(hidden_in),
        lower(hidden_out),
    )
    qkv_head, out_head, up_here, down_here = heads
    res_lines = 2 * half_c // 128
    res_mods = lax.dynamic_index_in_dim(mods, tensor_pos, 0, keepdims=False)[:res_lines]
    res_mods = res_mods.reshape(2, half_c)
    ada_mods = mods[:, res_lines:].reshape(6, D)

    block_out, grad_tokens, grad_ada, grad_qkv_w, grad_out, grad_up, grad_down = transformer(
        next(numbers),
        shrunk,
        ada_mods,
        cotangent.reshape(tokens_len, D),
        qkv_head,
        out_head,
        up_here,
        down_here,
    )
    grad_ada = lower(grad_ada).reshape(2, 3 * D // 128, 128)

    images_grad, grad_norm_params, grad_res, grad_ada, *returned = res_backward(
        next(numbers),
        breadth,
        grad_tokens,
        pictures,
        gain_bias,
        *convs,
        res_mods,
        picks,
        taps_half,
        middle,
        stats_one,
        act_two,
        taps_one,
        grad_qkv_w,
        grad_out,
        grad_up,
        grad_ada,
    )
    grad_conv_one, grad_conv_two, grad_half, grad_qkv_w, grad_out, grad_up = returned
    images_grad = widen(unpaired_lanes(images_grad))
    images_grad = images_grad.transpose(1, 0, 2).reshape((1, height, breadth, C))

    emb_cols = emb[:, 0, :freq_rows]
    grad_ada = widen(grad_ada).reshape(2, n_dp, 3, D)
    grad_ada = jnp.einsum("bf,cbjk->cjfk", emb_cols, grad_ada, precision=HIGHEST)
    grad_res = jnp.einsum("bf,bk->fk", emb_cols, grad_res.reshape(n_dp, -1), precision=HIGHEST)

    grad_qkv_w = grad_qkv_w.reshape(heads_here, D // n_dp, 3, HDIM).transpose(1, 2, 0, 3)
    gradients = (
        grad_norm_params,
        grad_conv_one.reshape(9 * local_c, half_c),
        grad_res.reshape(resnet_mod.shape),
        grad_conv_two.reshape(9 * local_c, half_c),
        grad_half.reshape(9 * local_c, half_d),
        grad_ada.reshape((6, freq_rows, D)),
        grad_qkv_w.reshape(-1, HDIM),
        grad_out.reshape(heads_here * HDIM, -1),
        grad_up,
        grad_down,
    )
    shared = tuple(position in (0, 5) for position in range(len(gradients)))
    square_sum = total_of_squares(next(numbers), gradients, shared)
    quads = []
    for position, grad in enumerate(gradients):
        order = stored_order.get(position, lambda array: array)
        three = (masters[position], averages[position], squares[position])
        quads.append(tuple(order(array).reshape(grad.shape) for array in three) + (grad,))
    updated = update(square_sum, quads, learn_rates())
    results = []
    for position, array in enumerate(updated):
        order = stored_order.get(position // 3, lambda array: array)
        shape = jax.eval_shape(order, masters[position // 3]).shape
        results.append(order(array.reshape(shape)))
    return (block_out[None], images_grad, jnp.sqrt(square_sum[0, :1])) + tuple(results)


def solution(mesh):
    in_specs = (
        P(DP, None, None, None),
        P(DP),
        P(DP, None, None),
        P(None, DP),
        P(None, DP),
        P(None, DP),
        P(None, None, DP, TENSOR),
        P(None, None, DP, TENSOR),
        P(None, None, DP, TENSOR),
        P(DP, None, TENSOR),
        P(DP, None, TENSOR),
        P(DP, None, TENSOR),
        P(None, None, TENSOR, DP),
        P(None, None, TENSOR, DP),
        P(None, None, TENSOR, DP),
        P(None, None, DP, TENSOR),
        P(None, None, DP, TENSOR),
        P(None, None, DP, TENSOR),
        P(DP, None, None),
        P(DP, None, None),
        P(DP, None, None),
        P(DP, None, TENSOR, None),
        P(DP, None, TENSOR, None),
        P(DP, None, TENSOR, None),
        P(TENSOR, None, DP),
        P(TENSOR, None, DP),
        P(TENSOR, None, DP),
        P(DP, TENSOR),
        P(DP, TENSOR),
        P(DP, TENSOR),
        P(TENSOR, DP),
        P(TENSOR, DP),
        P(TENSOR, DP),
    )
    out_specs = (
        P(DP, None, None),
        P(DP, None, None, None),
        P(),
        P(None, DP),
        P(None, DP),
        P(None, DP),
        P(None, None, DP, TENSOR),
        P(None, None, DP, TENSOR),
        P(None, None, DP, TENSOR),
        P(DP, None, TENSOR),
        P(DP, None, TENSOR),
        P(DP, None, TENSOR),
        P(None, None, TENSOR, DP),
        P(None, None, TENSOR, DP),
        P(None, None, TENSOR, DP),
        P(None, None, DP, TENSOR),
        P(None, None, DP, TENSOR),
        P(None, None, DP, TENSOR),
        P(DP, None, None),
        P(DP, None, None),
        P(DP, None, None),
        P(DP, None, TENSOR, None),
        P(DP, None, TENSOR, None),
        P(DP, None, TENSOR, None),
        P(TENSOR, None, DP),
        P(TENSOR, None, DP),
        P(TENSOR, None, DP),
        P(DP, TENSOR),
        P(DP, TENSOR),
        P(DP, TENSOR),
        P(TENSOR, DP),
        P(TENSOR, DP),
        P(TENSOR, DP),
    )
    moves_activations = mesh.shape[DP] == 4 * LAYERS and mesh.shape[TENSOR] == 2
    return jax.shard_map(
        stationary if moves_activations else per_device, mesh=mesh, in_specs=in_specs, out_specs=out_specs, check_vma=False
    )
```

```python
import functools
import itertools
import math

import jax
import jax.numpy as jnp
from jax import lax
from jax.experimental import pallas as pl
from jax.experimental.pallas import tpu as pltpu
from jax.sharding import PartitionSpec as P

DP, TENSOR = ("dp", "tensor")
C = 1024
D = 2048
HEADS = 16
HDIM = 128
FF = 8192
GROUPS = 32
FREQ = 256
STEP = 5


GN_EPS = 1e-05
LN_EPS = 1e-06
CLIP = 1.0
BETA_ONE = 0.5
BETA_TWO = 0.5
ADAM_EPS = 1e-08
DECAY = 0.1
LR_SCALE = 2.0
LR_NORM = 0.5
PLAN = 1000.0
HIGHEST = lax.Precision.HIGHEST


def embed_noise(t_index, emb_width):
    fraction = (t_index.astype(jnp.float32) + 0.5) / PLAN
    logsnr = -2.0 * jnp.log(jnp.tan(0.5 * math.pi * fraction)) + 2.0 * math.log(64.0 / 512.0)
    half_width = emb_width // 2
    frequencies = jnp.exp(
        -math.log(10000.0) * jnp.arange(half_width, dtype=jnp.float32) / half_width
    )
    angles = logsnr[:, None] * frequencies[None, :]
    return jnp.concatenate([jnp.sin(angles), jnp.cos(angles)], axis=1)


def group_norm(values, group_size):
    dims_of = values.shape
    grouped = values.reshape(dims_of[:-1] + (dims_of[-1] // group_size, group_size))
    center = jnp.mean(grouped, axis=(1, 2, 4), keepdims=True)
    shifted = grouped - center
    spread = jnp.mean(shifted * shifted, axis=(1, 2, 4), keepdims=True)
    return (shifted * lax.rsqrt(spread + GN_EPS)).reshape(dims_of)


def layer_norm(values):
    center = jnp.mean(values, axis=-1, keepdims=True)
    shifted = values - center
    spread = jnp.mean(shifted * shifted, axis=-1, keepdims=True)
    return shifted * lax.rsqrt(spread + LN_EPS)


def leading_segment(picture, gain_bias):
    return jax.nn.silu(group_norm(picture, C // GROUPS) * gain_bias[0] + gain_bias[1])


def second_piece(middle, res_mods):
    return jax.nn.silu(
        group_norm(middle, C // GROUPS) * (1.0 + res_mods[:, None, None, 0])
        + res_mods[:, None, None, 1]
    )


def modulate(tokens, shift_scale):
    return layer_norm(tokens) * (1.0 + shift_scale[:, None, 1]) + shift_scale[:, None, 0]


def gelu_tanh(values):
    return jax.nn.gelu(values, approximate=True)


def conv_same(inputs, kernel):
    height, breadth = (inputs.shape[1], inputs.shape[2])
    padded = jnp.pad(inputs, ((0, 0), (1, 1), (1, 1), (0, 0)))
    summed_taps = jnp.zeros(inputs.shape[:3] + (kernel.shape[3],), jnp.float32)
    for row_tap in range(3):
        for col_tap in range(3):
            window = padded[:, row_tap : row_tap + height, col_tap : col_tap + breadth]
            summed_taps = summed_taps + jnp.einsum(
                "bhwc,cd->bhwd",
                window,
                kernel[row_tap, col_tap],
                preferred_element_type=jnp.float32,
            )
    return summed_taps


def conv_same_input(upstream, kernel):
    height, breadth = (upstream.shape[1], upstream.shape[2])
    padded = jnp.pad(upstream, ((0, 0), (1, 1), (1, 1), (0, 0)))
    summed_taps = jnp.zeros(upstream.shape[:3] + (kernel.shape[2],), jnp.float32)
    for row_tap in range(3):
        for col_tap in range(3):
            window = padded[
                :, 2 - row_tap : 2 - row_tap + height, 2 - col_tap : 2 - col_tap + breadth
            ]
            summed_taps = summed_taps + jnp.einsum(
                "bhwd,cd->bhwc",
                window,
                kernel[row_tap, col_tap],
                preferred_element_type=jnp.float32,
            )
    return summed_taps


def conv_same_kernel(inputs, upstream):
    height, breadth = (inputs.shape[1], inputs.shape[2])
    padded = jnp.pad(inputs, ((0, 0), (1, 1), (1, 1), (0, 0)))
    tap_list = []
    for row_tap in range(3):
        for col_tap in range(3):
            window = padded[:, row_tap : row_tap + height, col_tap : col_tap + breadth]
            tap_list.append(
                jnp.einsum("bhwc,bhwd->cd", window, upstream, preferred_element_type=jnp.float32)
            )
    return jnp.stack(tap_list).reshape(3, 3, inputs.shape[3], upstream.shape[3])


def conv_down(inputs, kernel):
    height, breadth = (inputs.shape[1], inputs.shape[2])
    padded = jnp.pad(inputs, ((0, 0), (1, 1), (1, 1), (0, 0)))
    summed_taps = jnp.zeros(
        (inputs.shape[0], height // 2, breadth // 2, kernel.shape[3]), jnp.float32
    )
    for row_tap in range(3):
        for col_tap in range(3):
            window = padded[:, row_tap : row_tap + height : 2, col_tap : col_tap + breadth : 2]
            summed_taps = summed_taps + jnp.einsum(
                "bhwc,cd->bhwd",
                window,
                kernel[row_tap, col_tap],
                preferred_element_type=jnp.float32,
            )
    return summed_taps


def conv_down_input(upstream, kernel, height, breadth):
    summed_taps = jnp.zeros(
        (upstream.shape[0], height + 2, breadth + 2, kernel.shape[2]), jnp.float32
    )
    for row_tap in range(3):
        for col_tap in range(3):
            spread_out = jnp.einsum(
                "bhwd,cd->bhwc",
                upstream,
                kernel[row_tap, col_tap],
                preferred_element_type=jnp.float32,
            )
            placed = lax.pad(
                spread_out,
                jnp.float32(0.0),
                ((0, 0, 0), (row_tap, 3 - row_tap, 1), (col_tap, 3 - col_tap, 1), (0, 0, 0)),
            )
            summed_taps = summed_taps + placed
    return summed_taps[:, 1 : height + 1, 1 : breadth + 1]


def conv_down_kernel(inputs, upstream):
    height, breadth = (inputs.shape[1], inputs.shape[2])
    padded = jnp.pad(inputs, ((0, 0), (1, 1), (1, 1), (0, 0)))
    tap_list = []
    for row_tap in range(3):
        for col_tap in range(3):
            window = padded[:, row_tap : row_tap + height : 2, col_tap : col_tap + breadth : 2]
            tap_list.append(
                jnp.einsum("bhwc,bhwd->cd", window, upstream, preferred_element_type=jnp.float32)
            )
    return jnp.stack(tap_list).reshape(3, 3, inputs.shape[3], upstream.shape[3])


def learn_rates():
    conv_rate = LR_SCALE * (9 * C) ** (-0.5)
    mod_rate = LR_SCALE * (4 * FREQ) ** (-0.5)
    return (
        LR_NORM,
        conv_rate,
        mod_rate,
        conv_rate,
        conv_rate,
        mod_rate,
        LR_SCALE * D ** (-0.5),
        LR_SCALE * (HEADS * HDIM // 32) ** (-0.5),
        LR_SCALE * D ** (-0.5),
        LR_SCALE * FF ** (-0.5),
    )


def clipped_step(masters, averages, squares, combined_total, sum_all):
    local_sq = jnp.zeros((), jnp.float32)
    for position, reduced in enumerate(combined_total):
        shard_sq = jnp.sum(reduced * reduced)
        if position == 0 or position == 5:
            shard_sq = shard_sq / lax.axis_size(TENSOR)
        local_sq = local_sq + shard_sq
    square_sum = sum_all(local_sq)
    grad_norm = jnp.sqrt(square_sum)
    factor = jnp.minimum(1.0, CLIP / (grad_norm + 1e-06))
    rates = learn_rates()
    correct_one = 1.0 - BETA_ONE**STEP
    correct_two = 1.0 - BETA_TWO**STEP
    results = []
    for master, average, square, reduced, learn_rate in zip(
        masters, averages, squares, combined_total, rates
    ):
        clipped = reduced * factor
        new_avg = BETA_ONE * average + (1.0 - BETA_ONE) * clipped
        new_sq = BETA_TWO * square + (1.0 - BETA_TWO) * clipped * clipped
        step_dir = new_avg / correct_one / (jnp.sqrt(new_sq / correct_two) + ADAM_EPS)
        new_master = master - learn_rate * (step_dir + DECAY * master)
        results += [new_master, new_avg, new_sq]
    return (grad_norm.reshape(1),) + tuple(results)


def per_device(
    images,
    t_index,
    cotangent,
    norm_params,
    norm_params_avg,
    norm_params_sq,
    first_conv,
    first_conv_avg,
    first_conv_sq,
    resnet_mod,
    resnet_mod_avg,
    resnet_mod_sq,
    second_conv,
    second_kernel_first_moment,
    second_conv_sq,
    down_conv,
    down_conv_avg,
    down_conv_sq,
    ada_proj,
    ada_proj_avg,
    ada_proj_sq,
    qkv_proj,
    qkv_proj_avg,
    qkv_proj_sq,
    out_proj,
    out_proj_avg,
    out_proj_sq,
    hidden_in,
    hidden_in_avg,
    hidden_in_sq,
    hidden_out,
    hidden_out_avg,
    hidden_out_sq,
):
    masters = (
        norm_params,
        first_conv,
        resnet_mod,
        second_conv,
        down_conv,
        ada_proj,
        qkv_proj,
        out_proj,
        hidden_in,
        hidden_out,
    )
    averages = (
        norm_params_avg,
        first_conv_avg,
        resnet_mod_avg,
        second_kernel_first_moment,
        down_conv_avg,
        ada_proj_avg,
        qkv_proj_avg,
        out_proj_avg,
        hidden_in_avg,
        hidden_out_avg,
    )
    squares = (
        norm_params_sq,
        first_conv_sq,
        resnet_mod_sq,
        second_conv_sq,
        down_conv_sq,
        ada_proj_sq,
        qkv_proj_sq,
        out_proj_sq,
        hidden_in_sq,
        hidden_out_sq,
    )
    lowered = tuple((master.astype(jnp.bfloat16) for master in masters))
    gathered = (
        lax.all_gather(lowered[0], DP, axis=1, tiled=True),
        lax.all_gather(lowered[1], DP, axis=2, tiled=True),
        lax.all_gather(lowered[2], DP, axis=0, tiled=True),
        lax.all_gather(lowered[3], DP, axis=3, tiled=True),
        lax.all_gather(lowered[4], DP, axis=2, tiled=True),
        lax.all_gather(lowered[5], DP, axis=0, tiled=True),
        lax.all_gather(lowered[6], DP, axis=0, tiled=True),
        lax.all_gather(lowered[7], DP, axis=2, tiled=True),
        lax.all_gather(lowered[8], DP, axis=0, tiled=True),
        lax.all_gather(lowered[9], DP, axis=1, tiled=True),
    )
    (
        gain_bias,
        conv_one,
        res_table,
        conv_two,
        conv_half,
        ada_table,
        qkv_full,
        out_full,
        up_full,
        down_full,
    ) = gathered
    batch_size = images.shape[0]
    height, breadth = (images.shape[1], images.shape[2])
    local_c = conv_one.shape[3]
    local_d = conv_half.shape[3]
    heads_here = qkv_full.shape[2]
    tokens_len = height // 2 * (breadth // 2)
    tensor_pos = lax.axis_index(TENSOR)
    n_tensor = lax.axis_size(TENSOR)
    score_scale = HDIM ** (-0.5)
    noise_emb = embed_noise(t_index, FREQ)
    emb_low = noise_emb.astype(jnp.bfloat16)
    emb_back = emb_low.astype(jnp.float32)
    res_mods = jnp.dot(
        emb_low, res_table.reshape(FREQ, 2 * local_c), preferred_element_type=jnp.float32
    ).reshape(batch_size, 2, local_c)
    ada_mods = jnp.dot(
        emb_low, ada_table.reshape(FREQ, 6 * D), preferred_element_type=jnp.float32
    ).reshape(batch_size, 6, D)
    image_float = images.astype(jnp.float32)
    gain_float = gain_bias.astype(jnp.float32)
    act_one, first_back = jax.vjp(leading_segment, image_float, gain_float)
    act_one = act_one.astype(jnp.bfloat16)
    middle = conv_same(act_one, conv_one)
    act_two, second_back = jax.vjp(second_piece, middle, res_mods)
    act_two = act_two.astype(jnp.bfloat16)
    branch = lax.psum(conv_same(act_two, conv_two).astype(jnp.bfloat16), TENSOR).astype(
        jnp.float32
    )
    residual = image_float + branch
    resid_low = residual.astype(jnp.bfloat16)
    shrunk = conv_down(resid_low, conv_half)
    pieces = lax.all_gather(shrunk.astype(jnp.bfloat16), TENSOR, axis=3, tiled=True).astype(
        shrunk.dtype
    )
    tokens = pieces.reshape(batch_size, tokens_len, D)
    attn_in, attn_back = jax.vjp(modulate, tokens, ada_mods[:, 0:2])
    attn_low = attn_in.astype(jnp.bfloat16).reshape(batch_size * tokens_len, D)
    qkv_low = jnp.dot(
        attn_low, qkv_full.reshape(D, 3 * heads_here * HDIM), preferred_element_type=jnp.float32
    ).astype(jnp.bfloat16)
    qkv_low = qkv_low.reshape(batch_size, tokens_len, 3, heads_here, HDIM)
    query_low, key_low, value_low = (qkv_low[:, :, 0], qkv_low[:, :, 1], qkv_low[:, :, 2])
    scores = (
        jnp.einsum("bqhd,bkhd->bhqk", query_low, key_low, preferred_element_type=jnp.float32)
        * score_scale
    )
    row_max = jnp.max(scores, axis=-1, keepdims=True)
    log_total = row_max + jnp.log(jnp.sum(jnp.exp(scores - row_max), axis=-1, keepdims=True))
    attention_low = jnp.exp(scores - log_total).astype(jnp.bfloat16)
    mixed = jnp.einsum(
        "bhqk,bkhd->bqhd", attention_low, value_low, preferred_element_type=jnp.float32
    ).astype(jnp.bfloat16)
    mixed = mixed.reshape(batch_size * tokens_len, heads_here * HDIM)
    out_flat = out_full.reshape(heads_here * HDIM, D)
    attended = (
        lax.psum(
            jnp.dot(mixed, out_flat, preferred_element_type=jnp.float32).astype(jnp.bfloat16),
            TENSOR,
        )
        .astype(jnp.float32)
        .reshape(batch_size, tokens_len, D)
    )
    gate_one = 1.0 + ada_mods[:, None, 2]
    after_attn = tokens + gate_one * attended
    mlp_in, mlp_back = jax.vjp(modulate, after_attn, ada_mods[:, 3:5])
    mlp_low = mlp_in.astype(jnp.bfloat16).reshape(batch_size * tokens_len, D)
    pre_act = jnp.dot(mlp_low, up_full, preferred_element_type=jnp.float32)
    hidden_act, gelu_back = jax.vjp(gelu_tanh, pre_act)
    hidden_low = hidden_act.astype(jnp.bfloat16)
    expanded = (
        lax.psum(
            jnp.dot(hidden_low, down_full, preferred_element_type=jnp.float32).astype(jnp.bfloat16),
            TENSOR,
        )
        .astype(jnp.float32)
        .reshape(batch_size, tokens_len, D)
    )
    gate_two = 1.0 + ada_mods[:, None, 5]
    block_out = (after_attn + gate_two * expanded).astype(jnp.bfloat16)
    upstream = cotangent.astype(jnp.float32)
    grad_expanded = (gate_two * upstream).astype(jnp.bfloat16).reshape(batch_size * tokens_len, D)
    grad_gate_two = jnp.sum(upstream * expanded, axis=1)
    grad_down = jnp.einsum(
        "tf,td->fd", hidden_low, grad_expanded, preferred_element_type=jnp.float32
    )
    grad_hidden = jnp.einsum(
        "td,fd->tf", grad_expanded, down_full, preferred_element_type=jnp.float32
    )
    (grad_pre,) = gelu_back(grad_hidden)
    grad_pre_low = grad_pre.astype(jnp.bfloat16)
    grad_mlp_in = (
        lax.psum(
            jnp.einsum(
                "tf,df->td", grad_pre_low, up_full, preferred_element_type=jnp.float32
            ).astype(jnp.bfloat16),
            TENSOR,
        )
        .astype(jnp.float32)
        .reshape(batch_size, tokens_len, D)
    )
    grad_after_norm, grad_mods_two = mlp_back(grad_mlp_in)
    grad_after = upstream + grad_after_norm
    grad_attended = (gate_one * grad_after).astype(jnp.bfloat16).reshape(batch_size * tokens_len, D)
    grad_gate_one = jnp.sum(grad_after * attended, axis=1)
    grad_out = jnp.einsum("tk,td->kd", mixed, grad_attended, preferred_element_type=jnp.float32)
    grad_mixed = jnp.einsum(
        "td,kd->tk", grad_attended, out_flat, preferred_element_type=jnp.float32
    ).astype(jnp.bfloat16)
    grad_mixed = grad_mixed.reshape(batch_size, tokens_len, heads_here, HDIM)
    scores = (
        jnp.einsum("bqhd,bkhd->bhqk", query_low, key_low, preferred_element_type=jnp.float32)
        * score_scale
    )
    attention = jnp.exp(scores - log_total)
    attention_low = attention.astype(jnp.bfloat16)
    grad_probs = jnp.einsum(
        "bqhd,bkhd->bhqk", grad_mixed, value_low, preferred_element_type=jnp.float32
    )
    grad_values = jnp.einsum(
        "bhqk,bqhd->bkhd", attention_low, grad_mixed, preferred_element_type=jnp.float32
    )
    grad_scores = (
        attention * (grad_probs - jnp.sum(grad_probs * attention, axis=-1, keepdims=True))
    ).astype(jnp.bfloat16)
    query_gradient = (
        jnp.einsum("bhqk,bkhd->bqhd", grad_scores, key_low, preferred_element_type=jnp.float32)
        * score_scale
    )
    grad_keys = (
        jnp.einsum("bhqk,bqhd->bkhd", grad_scores, query_low, preferred_element_type=jnp.float32)
        * score_scale
    )
    grad_qkv = (
        jnp.stack([query_gradient, grad_keys, grad_values], axis=2)
        .astype(jnp.bfloat16)
        .reshape(batch_size * tokens_len, 3 * heads_here * HDIM)
    )
    grad_qkv_w = jnp.einsum(
        "td,tk->dk", attn_low, grad_qkv, preferred_element_type=jnp.float32
    ).reshape(D, 3, heads_here, HDIM)
    grad_attn_in = (
        lax.psum(
            jnp.einsum(
                "tk,dk->td",
                grad_qkv,
                qkv_full.reshape(D, 3 * heads_here * HDIM),
                preferred_element_type=jnp.float32,
            ).astype(jnp.bfloat16),
            TENSOR,
        )
        .astype(jnp.float32)
        .reshape(batch_size, tokens_len, D)
    )
    grad_tokens_norm, grad_mods_one = attn_back(grad_attn_in)
    grad_tokens = grad_after + grad_tokens_norm
    grad_mods = jnp.concatenate(
        [grad_mods_one, grad_gate_one[:, None], grad_mods_two, grad_gate_two[:, None]], axis=1
    )
    adaptive_gradient = jnp.einsum(
        "bf,bk->fk", emb_back, grad_mods.reshape(batch_size, 6 * D), precision=HIGHEST
    ).reshape(FREQ, 6, D)
    grad_out_w = grad_out.reshape(heads_here, HDIM, D)
    grad_up = jnp.einsum("td,tf->df", mlp_low, grad_pre_low, preferred_element_type=jnp.float32)
    transformer_gradient_total = (
        lax.psum_scatter(adaptive_gradient, DP, scatter_dimension=0, tiled=True),
        lax.psum_scatter(grad_qkv_w, DP, scatter_dimension=0, tiled=True),
        lax.psum_scatter(grad_out_w, DP, scatter_dimension=2, tiled=True),
        lax.psum_scatter(grad_up, DP, scatter_dimension=0, tiled=True),
        lax.psum_scatter(grad_down, DP, scatter_dimension=1, tiled=True),
    )
    grad_shrunk = lax.dynamic_slice_in_dim(
        grad_tokens.reshape(batch_size, height // 2, breadth // 2, D),
        tensor_pos * local_d,
        local_d,
        axis=3,
    ).astype(jnp.bfloat16)
    grad_half = conv_down_kernel(resid_low, grad_shrunk)
    grad_resid = lax.psum(
        conv_down_input(grad_shrunk, conv_half, height, breadth).astype(jnp.bfloat16), TENSOR
    ).astype(jnp.float32)
    grad_branch = grad_resid.astype(jnp.bfloat16)
    grad_conv_two = conv_same_kernel(act_two, grad_branch)
    grad_act_two = conv_same_input(grad_branch, conv_two)
    grad_middle, grad_res_mods = second_back(grad_act_two)
    grad_middle_low = grad_middle.astype(jnp.bfloat16)
    grad_conv_one = conv_same_kernel(act_one, grad_middle_low)
    grad_act_one = lax.psum(
        conv_same_input(grad_middle_low, conv_one).astype(jnp.bfloat16), TENSOR
    ).astype(jnp.float32)
    grad_image_norm, grad_gain = first_back(grad_act_one)
    images_grad = grad_resid + grad_image_norm
    grad_res_table = jnp.einsum(
        "bf,bk->fk", emb_back, grad_res_mods.reshape(batch_size, 2 * local_c), precision=HIGHEST
    ).reshape(FREQ, 2, local_c)
    resnet_gradient_total = (
        lax.psum_scatter(grad_gain, DP, scatter_dimension=1, tiled=True),
        lax.psum_scatter(grad_conv_one, DP, scatter_dimension=2, tiled=True),
        lax.psum_scatter(grad_res_table, DP, scatter_dimension=0, tiled=True),
        lax.psum_scatter(grad_conv_two, DP, scatter_dimension=3, tiled=True),
        lax.psum_scatter(grad_half, DP, scatter_dimension=2, tiled=True),
    )
    combined_total = tuple(resnet_gradient_total) + tuple(transformer_gradient_total)
    return (block_out, images_grad) + clipped_step(
        masters,
        averages,
        squares,
        combined_total,
        lambda local: lax.psum(local, (DP, TENSOR)),
    )


MESH = pl.DeviceIdType.MESH
ANYWHERE = pl.BlockSpec(memory_space=pl.ANY)
IN_VMEM = pl.BlockSpec(memory_space=pltpu.VMEM)
LAYERS = 4
ORDER = (3, 0, 2, 1)
VMEM_GRANT = 60 * 1024 * 1024


class Place:
    def __init__(self, wide):
        self.wide = wide
        self.dp = lax.axis_index(DP)
        self.core = lax.axis_index(TENSOR)
        self.z = self.dp // 4
        x = self.dp % 2
        y = (self.dp // 2) % 2
        x_mate = self.dp + 1 - 2 * x
        y_mate = self.dp + 2 - 4 * y
        self.x_mate = x_mate
        if wide:
            self.first = x_mate * (1 - self.core) + y_mate * self.core
            self.second = y_mate * (1 - self.core) + x_mate * self.core
            self.stride = 4
            self.column = self.dp % 4
            self.first_column = self.first % 4
            self.second_column = self.second % 4
            self.far_column = 3 - self.column
        else:
            self.first = self.second = y_mate
            self.stride = 2
            self.column = y
            self.second_column = 1 - y
        self.slot = self.z * self.stride + self.column
        self.has_below = self.z > 0
        self.has_above = self.z < LAYERS - 1

    def greet(self, with_core):
        barrier = pltpu.get_barrier_semaphore()

        def signal(dp, core):
            pl.semaphore_signal(barrier, inc=1, device_id=(dp, core), device_id_type=MESH)

        signal(self.second, self.core)
        if self.wide:
            signal(self.first, self.core)
        if with_core:
            signal(self.dp, 1 - self.core)
        pl.when(self.has_below)(lambda: signal(self.dp - 4, self.core))
        pl.when(self.has_above)(lambda: signal(self.dp + 4, self.core))
        layers = (self.z + LAYERS - 1) // LAYERS + (2 * LAYERS - 2 - self.z) // LAYERS
        pl.semaphore_wait(barrier, 1 + self.wide + with_core + layers)


def params(number):
    return pltpu.CompilerParams(
        collective_id=number, has_side_effects=True, vmem_limit_bytes=VMEM_GRANT
    )


def layer_order(step):
    odd = step % 2
    return (1 - odd) * (LAYERS - 1 - step // 2) + odd * (step // 2)


def remote(source, target, send_sem, recv_sem, device):
    return pltpu.make_async_remote_copy(
        src_ref=source,
        dst_ref=target,
        send_sem=send_sem,
        recv_sem=recv_sem,
        device_id=device,
        device_id_type=MESH,
    )


def by_distance(at, step):
    flip = at.z // 2
    inner = at.z * (1 - flip) + (LAYERS - 1 - at.z) * flip
    early = 1 - step // 2
    base = (1 - inner) * step + inner * (early * (1 - step) + (1 - early) * step)
    return (1 - flip) * base + flip * (LAYERS - 1 - base)


def piece_of(block, index, pieces):
    rows, lanes = block.shape
    if rows >= 16 * pieces:
        return block.at[pl.ds(pl.multiple_of(index * (rows // pieces), rows // pieces), rows // pieces)]
    return block.at[:, pl.ds(pl.multiple_of(index * (lanes // pieces), lanes // pieces), lanes // pieces)]


def gather_steps(at, outs, use, pieces, send_sem, recv_sem, mirror=None, tick=None):
    columns = at.stride
    arrays = range(len(outs))

    def here(index, slot, piece):
        block = outs[index].at[slot, at.core] if mirror else outs[index].at[slot]
        return piece_of(block, piece, pieces)

    def each(slot, piece, sem, mate, act):
        for index in arrays:
            act(
                remote(
                    here(index, slot, piece),
                    here(index, slot, piece),
                    send_sem.at[index, sem * pieces + piece],
                    recv_sem.at[index, slot * pieces + piece],
                    (mate, at.core),
                )
            )

    def start(copy):
        copy.start()

    def across(slot, piece, act, core):
        for index in arrays:
            block = piece_of(outs[index].at[slot, core], piece, pieces)
            act(
                remote(
                    block,
                    block,
                    mirror[0].at[index, slot * pieces + piece],
                    mirror[1].at[index, slot * pieces + piece],
                    (at.dp, 1 - at.core),
                )
            )

    def turn(count):
        step, piece = (count // pieces, count % pieces)
        if at.wide:
            late = step // 8
            rest = step % 8
            last = rest // 7
            is_first = (1 - late) * (last + (1 - rest % 2) * ((rest + 6) // 8))
            is_own = (1 - late) * (1 - is_first)
            near = is_own * ((rest + 1) // 2) + is_first * ((rest - 1) // 2)
            layer = by_distance(at, (1 - late) * near + late * (rest // 2))
            column = (
                is_own * at.column
                + is_first * at.first_column
                + late * ((1 - rest % 2) * at.second_column + rest % 2 * at.far_column)
            )
        else:
            is_own = 1 - step // LAYERS
            layer = by_distance(at, step % LAYERS)
            column = is_own * at.column + (1 - is_own) * at.second_column
        slot = layer * columns + column

        @pl.when(slot != at.slot)
        def _():
            each(slot, piece, 0, at.dp, lambda copy: copy.wait_recv())

        @pl.when(is_own == 1)
        def _():
            @pl.when(jnp.logical_and(layer <= at.z, at.has_above))
            def _():
                each(slot, piece, layer, at.dp + 4, start)

            @pl.when(jnp.logical_and(layer >= at.z, at.has_below))
            def _():
                each(slot, piece, 4 + layer, at.dp - 4, start)

            if at.wide:
                each(slot, piece, 8 + layer, at.first, start)
            each(slot, piece, 12 + layer, at.second, start)

        if at.wide:

            @pl.when(is_first == 1)
            def _():
                each(slot, piece, 16 + layer, at.second, start)

        if mirror:
            across(slot, piece, start, at.core)
        if tick is not None:
            tick(count)
        if use is not None:
            pl.when(piece == pieces - 1)(lambda: use(slot))

    def sent(copy):
        copy.wait_send()

    def end():
        @pl.loop(0, LAYERS * pieces)
        def _(count):
            layer, piece = (count // pieces, count % pieces)

            @pl.when(jnp.logical_and(layer <= at.z, at.has_above))
            def _():
                each(at.slot, piece, layer, at.dp + 4, sent)

            @pl.when(jnp.logical_and(layer >= at.z, at.has_below))
            def _():
                each(at.slot, piece, 4 + layer, at.dp - 4, sent)

            for group in (8, 12, 16) if at.wide else (12,):
                each(at.slot, piece, group + layer, at.second, sent)

        if mirror:

            @pl.loop(0, columns * LAYERS * pieces)
            def _(count):
                slot, piece = (count // pieces, count % pieces)
                across(slot, piece, lambda copy: copy.wait_recv(), 1 - at.core)
                across(slot, piece, sent, at.core)

    return turn, columns * LAYERS * pieces, end


def gather_stage(*args, **options):
    turn, turns, end = gather_steps(*args, **options)
    pl.loop(0, turns)(turn)
    end()


def gather_scratch(pieces, arrays=1, wide=True, mirror=False):
    chips = 16 if wide else 8
    count = [20 * pieces, 16 * pieces] + [chips * pieces] * (2 * mirror)
    return [pltpu.SemaphoreType.DMA((arrays, n)) for n in count]


def reduce_stage(at, result, produce, pieces, scratch, pair=False, meanwhile=None, tick=None):
    blocks, from_second, from_first, from_z, send_sem, recv_sem, *scratch = scratch
    columns = at.stride
    whole = columns * LAYERS
    lag = whole // 2 if pair else 0

    def part(ref, index, piece):
        return piece_of(ref.at[index], piece, pieces)

    def copy(sem, piece, source, target, mate):
        return remote(
            part(blocks, source, piece),
            part(target[0], target[1], piece),
            send_sem.at[sem, piece],
            recv_sem.at[sem, piece],
            (mate, at.core),
        )

    def to_second(half, layer, piece, slot):
        return copy(4 * half + layer, piece, slot, (from_second, 4 * half + layer), at.second)

    def to_first(layer, piece):
        return copy(
            8 + layer, piece, layer * columns + at.first_column, (from_first, layer), at.first
        )

    def up(layer, piece):
        return copy(12 + layer, piece, layer * columns + at.column, (from_z, layer), at.dp + 4)

    def down(layer, piece):
        return copy(16 + layer, piece, layer * columns + at.column, (from_z, 4 + layer), at.dp - 4)

    def value(ref, index, piece):
        return part(ref, index, piece)[...].astype(jnp.float32)

    def slot_of(step):
        if at.wide:
            keep, second, place = (step // 8, step % 2, step % 8 // 2)
            column = (1 - second) * (
                (1 - keep) * at.far_column + keep * at.first_column
            ) + second * ((1 - keep) * at.second_column + keep * at.column)
        else:
            keep, second, place = (step // LAYERS, 1, step % LAYERS)
            column = (1 - keep) * at.second_column + keep * at.column
        return layer_order(place) * columns + column, keep, second, place

    ahead = 2

    def send_layer(place, piece):
        layer = layer_order(place)
        if at.wide:
            to_second(0, layer, piece, layer * columns + at.far_column).start()
        to_second(1, layer, piece, layer * columns + at.second_column).start()

    def to_mate(slot):
        outbound, paired, pair_send, pair_recv = scratch
        return remote(
            outbound.at[slot],
            paired.at[slot],
            pair_send.at[slot],
            pair_recv.at[slot],
            (at.dp, 1 - at.core),
        )

    @pl.loop(0, whole + lag)
    def _(step):
        def make():
            slot = slot_of(step)[0]
            produce(slot)
            if pair:
                to_mate(slot).start()

        def pass_on():
            slot, keep, second, place = slot_of(step - lag)
            if pair:
                to_mate(slot).wait_recv()
                blocks[slot] = (
                    blocks[slot].astype(jnp.float32) + scratch[1][slot].astype(jnp.float32)
                ).astype(blocks.dtype)

            @pl.when(jnp.logical_and(keep == 0, place < ahead))
            def _():
                for piece in range(pieces):
                    to_second(second, layer_order(place), piece, slot).start()

        if pair:
            pl.when(step < whole)(make)
            pl.when(step >= lag)(pass_on)
        else:
            make()
            pass_on()

    if meanwhile is not None:
        meanwhile()

    def turn(place, piece):
        layer = layer_order(place)
        slot = layer * columns + at.first_column
        to_second(0, layer, piece, slot).wait_recv()
        part(blocks, slot, piece)[...] = (
            value(blocks, slot, piece) + value(from_second, layer, piece)
        ).astype(blocks.dtype)
        to_first(layer, piece).start()

    def rise(place, piece):
        layer = layer_order(place)
        slot = layer * columns + at.column
        to_second(1, layer, piece, slot).wait_recv()
        summed = value(blocks, slot, piece) + value(from_second, 4 + layer, piece)
        if at.wide:
            to_first(layer, piece).wait_recv()
            summed = summed + value(from_first, layer, piece)

        @pl.when(at.z == layer)
        def _():
            piece_of(result, piece, pieces)[...] = summed

        @pl.when(at.z < layer)
        def _():
            part(blocks, slot, piece)[...] = summed.astype(blocks.dtype)

            @pl.when(at.has_below)
            def _():
                up(layer, piece).wait_recv()
                part(blocks, slot, piece)[...] = (
                    value(blocks, slot, piece) + value(from_z, layer, piece)
                ).astype(blocks.dtype)

            up(layer, piece).start()

        @pl.when(at.z > layer)
        def _():
            part(blocks, slot, piece)[...] = summed.astype(blocks.dtype)

            @pl.when(at.has_above)
            def _():
                down(layer, piece).wait_recv()
                part(blocks, slot, piece)[...] = (
                    value(blocks, slot, piece) + value(from_z, 4 + layer, piece)
                ).astype(blocks.dtype)

            down(layer, piece).start()

    behind = 1 if at.wide else 0

    @pl.loop(0, (LAYERS + behind) * pieces)
    def _(step):
        place, piece = (step // pieces, step % pieces)
        pl.when(place + ahead < LAYERS)(lambda: send_layer(place + ahead, piece))
        if at.wide:
            pl.when(place < LAYERS)(lambda: turn(place, piece))
        pl.when(place >= behind)(lambda: rise(place - behind, piece))
        if tick is not None:
            tick(step)

    @pl.loop(0, pieces)
    def _(piece):
        @pl.when(at.has_below)
        def _():
            up(at.z, piece).wait_recv()
            piece_of(result, piece, pieces)[...] += value(from_z, at.z, piece)

        @pl.when(at.has_above)
        def _():
            down(at.z, piece).wait_recv()
            piece_of(result, piece, pieces)[...] += value(from_z, 4 + at.z, piece)

    @pl.loop(0, LAYERS * pieces)
    def _(step):
        layer, piece = (step // pieces, step % pieces)
        if at.wide:
            to_second(0, layer, piece, at.slot).wait_send()
            to_first(layer, piece).wait_send()
        to_second(1, layer, piece, at.slot).wait_send()
        pl.when(at.z < layer)(lambda: up(layer, piece).wait_send())
        pl.when(at.z > layer)(lambda: down(layer, piece).wait_send())

    if pair:

        @pl.loop(0, whole)
        def _(slot):
            to_mate(slot).wait_send()


def share_stage(at, result, send_sem, recv_sem):
    def give(core):
        return remote(result.at[core], result.at[core], send_sem, recv_sem, (at.dp, 1 - at.core))

    give(at.core).start()
    give(1 - at.core).wait_recv()
    give(at.core).wait_send()


def greet_all(at):
    everyone = 4 * LAYERS
    barrier = pltpu.get_barrier_semaphore()

    @pl.loop(1, everyone)
    def _(step):
        pl.semaphore_signal(
            barrier, inc=1, device_id=((at.dp + step) % everyone, at.core), device_id_type=MESH
        )

    pl.semaphore_signal(barrier, inc=1, device_id=(at.dp, 1 - at.core), device_id_type=MESH)
    pl.semaphore_wait(barrier, everyone)


class Ride:
    def __init__(self, at, parts, send_sem, recv_sem, own_sem):
        self.at, self.parts = (at, parts)
        self.send_sem, self.recv_sem, self.own_sem = (send_sem, recv_sem, own_sem)

    def copy(self, part, step):
        source, target = self.parts[part]
        peer = (self.at.dp + step) % (4 * LAYERS)
        return remote(
            source(peer),
            target(self.at.dp),
            self.send_sem.at[part, step - 1],
            self.recv_sem.at[part, step - 1],
            (peer, self.at.core),
        )

    def keep(self, part):
        source, target = self.parts[part]
        return pltpu.make_async_copy(
            source(self.at.dp), target(self.at.dp), self.own_sem.at[part]
        )

    def start(self, first=0, after=None):
        for part in range(len(self.parts))[first:after]:
            self.keep(part).start()

            @pl.loop(1, 4 * LAYERS)
            def _(step):
                self.copy(part, step).start()

    def wait_for(self, part):
        self.keep(part).wait()

        @pl.loop(1, 4 * LAYERS)
        def _(step):
            self.copy(part, step).wait()

    def wait(self, first=0):
        for part in range(first, len(self.parts)):
            self.wait_for(part)


def ride_scratch(parts):
    others = 4 * LAYERS - 1
    return [
        pltpu.SemaphoreType.DMA((parts, others)),
        pltpu.SemaphoreType.DMA((parts, others)),
        pltpu.SemaphoreType.DMA((parts,)),
    ]


class PairRide:
    def __init__(self, at, parts, send_sem, recv_sem, own_sem):
        self.at, self.parts = (at, parts)
        self.send_sem, self.recv_sem, self.own_sem = (send_sem, recv_sem, own_sem)
        self.steps = 2 * LAYERS

    def copy(self, part, step):
        source, target = self.parts[part]
        peer = (self.at.dp + 2 * step) % (4 * LAYERS)
        return remote(
            source(peer),
            target(self.at.dp),
            self.send_sem.at[part, step],
            self.recv_sem.at[part, step],
            (peer, self.at.core),
        )

    def keep(self, part):
        source, target = self.parts[part]
        return pltpu.make_async_copy(
            source(self.at.dp), target(self.at.dp), self.own_sem.at[part]
        )

    def onward(self, part, step):
        target = self.parts[part][1]
        chip = (self.at.dp + 4 * LAYERS - 2 * step) % (4 * LAYERS)
        return remote(
            target(chip),
            target(chip),
            self.send_sem.at[part, self.steps + step],
            self.recv_sem.at[part, self.steps + step],
            (self.at.x_mate, self.at.core),
        )

    def start(self):
        for part in range(len(self.parts)):
            self.keep(part).start()

            @pl.loop(1, self.steps)
            def _(step):
                self.copy(part, step).start()

    def forward(self):
        for part in range(len(self.parts)):
            self.keep(part).wait()

            @pl.loop(0, self.steps)
            def _(step):
                pl.when(step > 0)(lambda: self.copy(part, step).wait_recv())
                self.onward(part, step).start()

    def wait(self):
        for part in range(len(self.parts)):

            @pl.loop(0, self.steps)
            def _(step):
                self.onward(part, step).wait()
                pl.when(step > 0)(lambda: self.copy(part, step).wait_send())


def pair_ride_scratch(parts):
    return [
        pltpu.SemaphoreType.DMA((parts, 4 * LAYERS)),
        pltpu.SemaphoreType.DMA((parts, 4 * LAYERS)),
        pltpu.SemaphoreType.DMA((parts,)),
    ]


def strip(ref, axis, index, size):
    at = pl.ds(pl.multiple_of(index * size, size), size)
    return ref.at[at] if axis == 0 else ref.at[:, at]


def reduce_scratch(block, pieces, wide=True, pair=False):
    kind = jnp.bfloat16
    chips = 16 if wide else 8
    scratch = [
        pltpu.VMEM((chips,) + block, kind),
        pltpu.VMEM((8,) + block, kind),
        pltpu.VMEM((4,) + block, kind),
        pltpu.VMEM((8,) + block, kind),
        pltpu.SemaphoreType.DMA((20, pieces)),
        pltpu.SemaphoreType.DMA((20, pieces)),
    ]
    if pair:
        scratch += [pltpu.VMEM((chips,) + block, kind)] * 2
        scratch += [pltpu.SemaphoreType.DMA((chips,))] * 2
    return scratch


def mean_of_groups(sums, count):
    size = C // GROUPS
    channels = sums.shape[-1]
    row = lax.broadcasted_iota(jnp.int32, (channels, channels), 0) // size
    column = lax.broadcasted_iota(jnp.int32, (channels, channels), 1) // size
    same = jnp.where(row == column, 1.0 / (count * size), 0.0)
    return jnp.dot(sums, same, precision=HIGHEST, preferred_element_type=jnp.float32)


def side_by_side(maps, breadth, turned=False):
    positions = maps.shape[0]
    column = lax.broadcasted_iota(jnp.int32, maps.shape, 0) % breadth
    before = jnp.where(column == 0, 0.0, pltpu.roll(maps, 1, 0))
    after = jnp.where(column == breadth - 1, 0.0, pltpu.roll(maps, positions - 1, 0))
    three = (after, maps, before) if turned else (before, maps, after)
    return jnp.concatenate(three, axis=1)


def fold_three(products, breadth, turned=False):
    positions = products.shape[0]
    channels = products.shape[1] // 3
    left, middle, right = (products[:, tap * channels : (tap + 1) * channels] for tap in range(3))
    if turned:
        left, right = (right, left)
    column = lax.broadcasted_iota(jnp.int32, middle.shape, 0) % breadth
    before = jnp.where(column == 0, 0.0, pltpu.roll(left, 1, 0))
    after = jnp.where(column == breadth - 1, 0.0, pltpu.roll(right, positions - 1, 0))
    return before + middle + after


def fold_rows(above, same, below, breadth):
    edge = jnp.zeros((breadth, same.shape[1]), jnp.float32)
    count = same.shape[0] - breadth
    down = jnp.concatenate([edge, above[:count]], axis=0)
    up = jnp.concatenate([below[breadth:], edge], axis=0)
    return down + same + up


def silu(z):
    return z * jax.nn.sigmoid(z)


def store_padded(ref, index, maps, breadth):
    positions = maps.shape[0]
    edge = jnp.zeros((breadth, maps.shape[1]), ref.dtype)
    ref[index, pl.ds(0, breadth)] = edge
    ref[index, pl.ds(breadth, positions)] = maps.astype(ref.dtype)
    ref[index, pl.ds(breadth + positions, breadth)] = edge


def res_forward_kernel(
    breadth,
    gain_bias,
    conv_one,
    conv_two,
    conv_half,
    picks,
    res_table,
    ada_table,
    image_blocks,
    emb_blocks,
    qkv_blocks,
    out_blocks,
    up_rows,
    down_columns,
    pictures,
    emb,
    tokens,
    act_out,
    taps_one_out,
    taps_half,
    middle,
    stats,
    mods,
    qkv_head,
    out_head,
    up_here,
    down_here,
    neighbour_sem,
    arrived,
    mods_blocks,
    mods_terms,
    acts,
    taps_one,
    mine,
    theirs,
    pair_send,
    pair_recv,
    share_send,
    share_recv,
    out_sem,
    *scratch,
):
    first_reduce, (act_send, act_recv), last_reduce = (scratch[:6], scratch[6:8], scratch[8:14])
    at = Place(True)
    greet_all(at)

    rows, cols = (up_rows.shape[0], up_here.shape[1])
    near = 4 * LAYERS // qkv_blocks.shape[0]
    ride = Ride(
        at,
        [
            (lambda chip: emb_blocks.at[chip], lambda chip: emb.at[chip]),
            (lambda chip: image_blocks.at[chip, at.core], lambda chip: arrived.at[chip, at.core]),
            (lambda chip: strip(up_rows, 1, chip, cols), lambda chip: strip(up_here, 0, chip, rows)),
            (lambda chip: mods_blocks.at[chip], lambda chip: mods_terms.at[chip]),
            (lambda chip: strip(down_columns, 0, chip, cols), lambda chip: strip(down_here, 1, chip, rows)),
        ],
        *scratch[14:17],
    )
    attention = PairRide(
        at,
        [
            (lambda chip: qkv_blocks.at[chip // near], lambda chip: strip(qkv_head, 0, chip, rows)),
            (lambda chip: out_blocks.at[chip // near], lambda chip: strip(out_head, 1, chip, rows)),
        ],
        *scratch[17:20],
    )
    ride.start(0, 3)
    images, positions, channels = pictures.shape
    half_c = conv_one.shape[2]
    tokens_len = positions // 4

    def hand_over(chip, core):
        return remote(
            arrived.at[chip, core],
            arrived.at[chip, core],
            neighbour_sem.at[0, chip],
            neighbour_sem.at[1, chip],
            (at.dp, 1 - at.core),
        )

    ride.keep(1).wait()
    hand_over(at.dp, at.core).start()

    @pl.loop(1, images)
    def _(step):
        ride.copy(1, step).wait()
        hand_over((at.dp + images - step) % images, at.core).start()

    @pl.loop(0, images)
    def _(i):
        hand_over(i, 1 - at.core).wait_recv()
        both = arrived[i].reshape(positions // 2, 2 * channels).astype(jnp.float32)
        sides = [both[:, :channels], both[:, channels:]]
        pictures[i] = jnp.concatenate(sides, axis=0).astype(jnp.bfloat16)

    attention.start()

    @pl.loop(0, images)
    def _(i):
        x = pictures[i].astype(jnp.float32)
        stats[0, pl.ds(i, 1)] = jnp.sum(x, axis=0, keepdims=True)

    stats[0] = mean_of_groups(stats[0], positions)

    @pl.loop(0, images)
    def _(i):
        x = pictures[i].astype(jnp.float32) - stats[0, pl.ds(i, 1)]
        stats[1, pl.ds(i, 1)] = jnp.sum(x * x, axis=0, keepdims=True)

    stats[1] = lax.rsqrt(mean_of_groups(stats[1], positions) + GN_EPS)

    @pl.loop(0, images)
    def _(i):
        normed = (pictures[i].astype(jnp.float32) - stats[0, pl.ds(i, 1)]) * stats[1, pl.ds(i, 1)]
        act = silu(normed * gain_bias[0:1] + gain_bias[1:2])
        store_padded(taps_one, i, side_by_side(act, breadth), breadth)

    save_taps = pltpu.make_async_copy(taps_one, taps_one_out, out_sem.at[0])
    save_taps.start()

    def first_product(slot):
        total = jnp.zeros((positions, conv_one.shape[2]), jnp.float32)
        for a in range(3):
            total += dot(taps_one[slot, pl.ds(a * breadth, positions)], conv_one[a])
        first_reduce[0][slot] = total.astype(jnp.bfloat16)

    def modulation_terms():
        ride.wait_for(0)
        emb_rows = emb[:, 0, : res_table.shape[0]].astype(jnp.bfloat16)
        lines = 0
        for table in [res_table] + [ada_table.at[row] for row in range(ada_table.shape[0])]:
            terms = dot(emb_rows, table[...])
            for line in range(table.shape[1] // 128):
                mods_blocks[:, lines] = terms[:, 128 * line : 128 * (line + 1)].astype(mods_blocks.dtype)
                lines += 1
        ride.start(3, 4)

    reduce_stage(at, middle, first_product, 2, first_reduce, meanwhile=modulation_terms)

    ride.start(4, 5)
    ride.wait_for(3)
    mods[at.core] = jnp.sum(mods_terms[...].astype(jnp.float32), axis=0)
    share_stage(at, mods, share_send.at[1], share_recv.at[1])

    def modulation(row):
        lines = half_c // 128
        parts = [mods[at.core, pl.ds(row * lines + i, 1)] for i in range(lines)]
        return jnp.concatenate(parts, axis=1)

    x = middle[...]
    center = mean_of_groups(jnp.sum(x, axis=0, keepdims=True), positions)
    x = x - center
    scale = lax.rsqrt(mean_of_groups(jnp.sum(x * x, axis=0, keepdims=True), positions) + GN_EPS)
    acts[at.slot] = silu(x * scale * (1.0 + modulation(0)) + modulation(1)).astype(jnp.bfloat16)

    def swap(slot):
        return remote(
            mine.at[slot],
            theirs.at[slot],
            pair_send.at[slot],
            pair_recv.at[slot],
            (at.dp, 1 - at.core),
        )

    def second_product(slot):
        act = acts[slot]
        above, same, below = (dot_nt(act, conv_two[a]) for a in range(3))
        folded = fold_three(fold_rows(above, same, below, breadth), breadth)
        mine[slot] = folded.astype(jnp.bfloat16)
        swap(slot).start()

    gather_stage(at, [acts], second_product, 2, act_send, act_recv)
    save_acts = pltpu.make_async_copy(acts, act_out, out_sem.at[1])
    save_acts.start()
    attention.forward()

    def half_product(slot):
        swap(slot).wait_recv()
        branch = mine[slot].astype(jnp.float32) + theirs[slot].astype(jnp.float32)
        resid = (pictures[slot].astype(jnp.float32) + branch).astype(jnp.bfloat16)
        three = side_by_side(resid.astype(jnp.float32), breadth).astype(jnp.bfloat16)
        picked = dot(picks[...], three).astype(jnp.bfloat16)
        total = jnp.zeros((tokens_len, conv_half.shape[2]), jnp.float32)
        for a in range(3):
            part = picked[a * tokens_len : (a + 1) * tokens_len]
            taps_half[a, slot] = part
            total += dot(part, conv_half[a])
        last_reduce[0][slot] = total.astype(jnp.bfloat16)

    reduce_stage(at, tokens.at[at.core], half_product, 2, last_reduce)
    share_stage(at, tokens, share_send.at[0], share_recv.at[0])

    @pl.loop(0, images)
    def _(slot):
        swap(slot).wait_send()
        hand_over(slot, at.core).wait_send()

    ride.wait_for(2)
    ride.wait_for(4)
    attention.wait()
    save_taps.wait()
    save_acts.wait()


def res_forward(number, height, breadth, *args):
    (gain_bias, conv_one, conv_two, conv_half, picks, res_table, ada_table, image_blocks, emb_blocks, qkv_blocks, out_blocks, up_rows, down_columns) = args
    images, positions, channels = (4 * LAYERS, height * breadth, gain_bias.shape[1])
    half_c = conv_one.shape[2]
    half_d = conv_half.shape[2]
    tokens_len = positions // 4
    three = 3 * channels
    rows, cols = (up_rows.shape[0], up_rows.shape[1] // images)
    low, full = (jnp.bfloat16, jnp.float32)
    pictures = (images, positions, channels)
    padded = (images, positions + 2 * breadth, three)
    acts = (images, positions, half_c)
    lines = (res_table.shape[1] + ada_table.shape[0] * ada_table.shape[2]) // 128
    outs = [
        (pictures, low),
        (emb_blocks.shape, full),
        ((2, tokens_len, half_d), full),
        (acts, low),
        (padded, low),
        ((3, images, tokens_len, three), low),
        ((positions, half_c), full),
        ((2, images, channels), full),
        ((2, lines, 128), full),
        ((images * rows, qkv_blocks.shape[2]), low),
        ((out_blocks.shape[1], images * rows), low),
        ((images * rows, cols), low),
        ((cols, images * rows), low),
    ]
    return pl.pallas_call(
        functools.partial(res_forward_kernel, breadth),
        out_shape=[jax.ShapeDtypeStruct(shape, kind) for shape, kind in outs],
        in_specs=[IN_VMEM] * 7 + [ANYWHERE] * 6,
        out_specs=[IN_VMEM] * 3 + [ANYWHERE] * 2 + [IN_VMEM] * 4 + [ANYWHERE] * 4,
        scratch_shapes=[
            pltpu.SemaphoreType.DMA((2, images)),
            pltpu.VMEM(image_blocks.shape, low),
            pltpu.VMEM((images, lines, 128), low),
            pltpu.VMEM((images, lines, 128), low),
            pltpu.VMEM(acts, low),
            pltpu.VMEM(padded, low),
            pltpu.VMEM(pictures, low),
            pltpu.VMEM(pictures, low),
            pltpu.SemaphoreType.DMA((images,)),
            pltpu.SemaphoreType.DMA((images,)),
            pltpu.SemaphoreType.DMA((2,)),
            pltpu.SemaphoreType.DMA((2,)),
            pltpu.SemaphoreType.DMA((2,)),
        ]
        + reduce_scratch((positions, half_c), 2)
        + gather_scratch(2)
        + reduce_scratch((tokens_len, half_d), 2)
        + ride_scratch(5)
        + pair_ride_scratch(2),
        compiler_params=params(number),
        name="res_forward",
    )(*args)


def silu_slope(z):
    gate = jax.nn.sigmoid(z)
    return gate * (1.0 + z * (1.0 - gate))


def res_backward_kernel(
    breadth,
    shrunk,
    pictures,
    gain_bias,
    conv_one,
    conv_two,
    conv_half,
    mods,
    picks,
    taps_half,
    middle,
    stats,
    acts_in,
    taps_one_in,
    qkv_grad,
    out_grad,
    up_grad,
    ada_grad,
    pictures_out,
    norm_out,
    mods_back,
    ada_back,
    one_out,
    two_out,
    half_out,
    qkv_back,
    out_back,
    up_back,
    qkv_pair,
    out_pair,
    qkv_sums,
    out_sums,
    mods_block,
    gathered,
    gathered_middle,
    acts,
    taps_one,
    taps_two,
    mine,
    theirs,
    back,
    back_theirs,
    held,
    sums,
    outgoing,
    acted,
    one_grad,
    two_grad,
    half_grad,
    pair_send,
    pair_recv,
    back_send,
    back_recv,
    trade_send,
    trade_recv,
    io_sem,
    share_sem,
    neighbour_sem,
    store_sem,
    *scratch,
):
    (shrunk_send, shrunk_recv), (middle_send, middle_recv) = (scratch[:2], scratch[2:4])
    reducing = scratch[4:10]
    at = Place(True)
    images, positions, channels = pictures.shape
    others = images - 1
    tokens_len = positions // 4
    load_acts = pltpu.make_async_copy(acts_in, acts, io_sem.at[0])
    load_taps = pltpu.make_async_copy(taps_one_in, taps_one, io_sem.at[1])
    load_acts.start()
    load_taps.start()
    gathered[at.slot] = shrunk[...]

    greet_all(at)

    def peer(step):
        return (at.dp + step) % images

    rows, cols = (D // images, up_grad.shape[1])
    half = images // 2
    side = at.dp % 2

    def to_neighbour(part, place):
        chip = 2 * place + 1 - side
        source, target = (
            (strip(qkv_grad, 0, chip, rows), qkv_pair.at[place]),
            (strip(out_grad, 1, chip, rows), out_pair.at[place]),
        )[part]
        return remote(
            source,
            target,
            neighbour_sem.at[0, part, place],
            neighbour_sem.at[1, part, place],
            (at.x_mate, at.core),
        )

    def store(part, step):
        chip = (at.dp + 2 * step) % images
        source, target = ((qkv_sums, qkv_back), (out_sums, out_back))[part]
        return remote(
            source.at[chip // 2],
            target.at[at.dp // 2],
            store_sem.at[0, part, step],
            store_sem.at[1, part, step],
            (chip, at.core),
        )

    def store_own(part):
        source, target = ((qkv_sums, qkv_back), (out_sums, out_back))[part]
        return pltpu.make_async_copy(
            source.at[at.dp // 2], target.at[at.dp // 2], store_sem.at[0, part, 0]
        )

    def store_sums():
        @pl.loop(0, half)
        def _(place):
            chip = 2 * place + side
            to_neighbour(0, place).wait_recv()
            own = strip(qkv_grad, 0, chip, rows)[...].astype(jnp.float32)
            qkv_sums[place] = (own + qkv_pair[place].astype(jnp.float32)).astype(jnp.bfloat16)
            to_neighbour(1, place).wait_recv()
            own = strip(out_grad, 1, chip, rows)[...].astype(jnp.float32)
            out_sums[place] = (own + out_pair[place].astype(jnp.float32)).astype(jnp.bfloat16)

        for part in range(2):
            store_own(part).start()

            @pl.loop(1, half)
            def _(step):
                store(part, step).start()

    for part in range(2):

        @pl.loop(0, half)
        def _(place):
            to_neighbour(part, place).start()

    ride = Ride(
        at,
        [
            (lambda chip: ada_grad.at[at.core], lambda chip: ada_back.at[at.core, chip]),
            (lambda chip: mods_block, lambda chip: mods_back.at[chip]),
            (lambda chip: strip(up_grad, 0, chip, rows), lambda chip: strip(up_back, 1, chip, cols)),
        ],
        *scratch[10:],
    )
    ride.start(0, 1)

    def swap(slot):
        return remote(
            mine.at[slot],
            theirs.at[slot],
            pair_send.at[slot],
            pair_recv.at[slot],
            (at.dp, 1 - at.core),
        )

    def half_back(slot):
        products = [dot_nt(gathered[slot], conv_half[a]) for a in range(3)]
        products = jnp.concatenate(products, axis=0)
        coarse = products.astype(jnp.bfloat16)
        fine = (products - coarse.astype(jnp.float32)).astype(jnp.bfloat16)
        spread = dot_tn(picks[...], coarse) + dot_tn(picks[...], fine)
        mine[slot] = fold_three(spread, breadth, True).astype(jnp.bfloat16)
        swap(slot).start()

    gather_stage(at, [gathered], half_back, 2, shrunk_send, shrunk_recv)

    store_sums()

    def resid(slot):
        return mine[slot].astype(jnp.float32) + theirs[slot].astype(jnp.float32)

    def second_back(slot):
        swap(slot).wait_recv()
        branch = resid(slot).astype(jnp.bfloat16).astype(jnp.float32)
        store_padded(taps_two, slot, side_by_side(branch, breadth, True), breadth)
        total = jnp.zeros((positions, conv_two.shape[2]), jnp.float32)
        for a in range(3):
            total += dot(taps_two[slot, pl.ds((2 - a) * breadth, positions)], conv_two[a])
        reducing[0][slot] = total.astype(jnp.bfloat16)

    def weights_meanwhile():
        half_grad[...] = jnp.zeros_like(half_grad)
        two_grad[...] = jnp.zeros_like(two_grad)
        load_acts.wait()

        @pl.loop(0, images // 4)
        def _(i):
            right = gathered[pl.ds(4 * i, 4)].reshape(4 * tokens_len, -1)
            for a in range(3):
                left = taps_half[a, pl.ds(4 * i, 4)].reshape(4 * tokens_len, 3 * channels)
                half_grad[a] += dot_tn(left, right)

        @pl.loop(0, images)
        def _(i):
            right = acts[i]
            for a in range(3):
                left = taps_two[i, pl.ds((2 - a) * breadth, positions)]
                two_grad[a] += dot_tn(left, right)

        save(half_grad, half_out, 2).start()
        save(two_grad, two_out, 3).start()

    def save(source, target, sem):
        return pltpu.make_async_copy(source, target, io_sem.at[sem])

    reduce_stage(at, acted, second_back, 2, reducing, False, weights_meanwhile)

    x = middle[...]
    center = mean_of_groups(jnp.sum(x, axis=0, keepdims=True), positions)
    x = x - center
    scale = lax.rsqrt(mean_of_groups(jnp.sum(x * x, axis=0, keepdims=True), positions) + GN_EPS)
    normed = x * scale
    slope = 1.0 + mods[0:1]
    grad = acted[...] * silu_slope(normed * slope + mods[1:2])
    along = jnp.sum(grad * normed, axis=0, keepdims=True)
    level = jnp.sum(grad, axis=0, keepdims=True)
    lines = along.shape[1] // 128
    for i in range(lines):
        mods_block[i : i + 1] = along[:, 128 * i : 128 * (i + 1)]
        mods_block[lines + i : lines + i + 1] = level[:, 128 * i : 128 * (i + 1)]
    ride.start(1, 2)
    ride.start(2, 3)
    along = mean_of_groups(slope * along, positions)
    level = mean_of_groups(slope * level, positions)
    gathered_middle[at.slot] = ((slope * grad - level - normed * along) * scale).astype(jnp.bfloat16)

    def swap_back(slot):
        return remote(
            back.at[slot],
            back_theirs.at[slot],
            back_send.at[slot],
            back_recv.at[slot],
            (at.dp, 1 - at.core),
        )

    def first_back(slot):
        below, same, above = (dot_nt(gathered_middle[slot], conv_one[a]) for a in range(3))
        folded = fold_three(fold_rows(above, same, below, breadth), breadth, True)
        back[slot] = folded.astype(jnp.bfloat16)
        swap_back(slot).start()

    gather_stage(at, [gathered_middle], first_back, 2, middle_send, middle_recv)

    gain, bias = (gain_bias[0:1], gain_bias[1:2])

    def normed_of(i):
        return (pictures[i].astype(jnp.float32) - stats[0, pl.ds(i, 1)]) * stats[1, pl.ds(i, 1)]

    @pl.loop(0, images)
    def _(i):
        swap_back(i).wait_recv()
        grad = back[i].astype(jnp.float32) + back_theirs[i].astype(jnp.float32)
        normed = normed_of(i)
        grad = grad * silu_slope(normed * gain + bias)
        held[i] = grad
        sums[0, pl.ds(i, 1)] = jnp.sum(grad * normed, axis=0, keepdims=True)
        sums[1, pl.ds(i, 1)] = jnp.sum(grad, axis=0, keepdims=True)

    norm_out[0:1] = jnp.sum(sums[0], axis=0, keepdims=True)
    norm_out[1:2] = jnp.sum(sums[1], axis=0, keepdims=True)
    sums[0] = mean_of_groups(gain * sums[0], positions)
    sums[1] = mean_of_groups(gain * sums[1], positions)

    def deliver(step):
        return remote(
            outgoing.at[peer(step)],
            pictures_out.at[at.dp],
            trade_send.at[step - 1],
            trade_recv.at[step - 1],
            (peer(step), at.core),
        )

    keep = save(outgoing.at[at.dp], pictures_out.at[at.dp], 5)

    @pl.loop(0, images)
    def _(step):
        i = peer(step)
        part = gain * held[i] - sums[1, pl.ds(i, 1)] - normed_of(i) * sums[0, pl.ds(i, 1)]
        part = resid(i) + part * stats[1, pl.ds(i, 1)]
        half = positions // 2
        outgoing[i] = jnp.concatenate([part[:half], part[half:]], axis=1).astype(jnp.bfloat16)
        pl.when(step == 0)(keep.start)
        pl.when(step > 0)(lambda: deliver(step).start())

    one_grad[...] = jnp.zeros_like(one_grad)
    load_taps.wait()

    @pl.loop(0, images)
    def _(i):
        right = gathered_middle[i]
        for a in range(3):
            one_grad[a] += dot_tn(taps_one[i, pl.ds(a * breadth, positions)], right)

    save(one_grad, one_out, 4).start()

    @pl.loop(0, images)
    def _(slot):
        swap(slot).wait_send()
        swap_back(slot).wait_send()

    keep.wait()

    ride.wait()
    for part in range(2):
        store_own(part).wait()

        @pl.loop(0, half)
        def _(step):
            to_neighbour(part, step).wait_send()
            pl.when(step > 0)(lambda: store(part, step).wait())

    share_stage(at, ada_back, share_sem.at[0], share_sem.at[1])

    @pl.loop(1, others + 1)
    def _(step):
        deliver(step).wait()

    save(half_grad, half_out, 2).wait()
    save(two_grad, two_out, 3).wait()
    save(one_grad, one_out, 4).wait()


def res_backward(number, breadth, *args):
    (shrunk, pictures, gain_bias, conv_one, conv_two, conv_half, mods, picks, taps_half, middle, stats, acts, taps_one, qkv_grad, out_grad, up_grad, ada_grad) = args
    images, positions, channels = pictures.shape
    half_c = conv_one.shape[2]
    half_d = conv_half.shape[2]
    tokens_len = positions // 4
    three = 3 * channels
    low, full = (jnp.bfloat16, jnp.float32)
    rows = qkv_grad.shape[0] // images
    grads = [(3, three, half_c), (3, three, half_c), (3, three, half_d)]
    traded = (images, positions // 2, 2 * channels)
    return pl.pallas_call(
        functools.partial(res_backward_kernel, breadth),
        out_shape=[
            jax.ShapeDtypeStruct(traded, low),
            jax.ShapeDtypeStruct((2, channels), full),
            jax.ShapeDtypeStruct((images, 2 * half_c // 128, 128), full),
            jax.ShapeDtypeStruct((2, images) + ada_grad.shape[1:], ada_grad.dtype),
        ]
        + [jax.ShapeDtypeStruct(shape, full) for shape in grads]
        + [
            jax.ShapeDtypeStruct((images // 2, rows, qkv_grad.shape[1]), low),
            jax.ShapeDtypeStruct((images // 2, out_grad.shape[0], rows), low),
            jax.ShapeDtypeStruct((rows, images * up_grad.shape[1]), low),
        ],
        in_specs=[IN_VMEM] * 11 + [ANYWHERE] * 2 + [IN_VMEM] * 2 + [ANYWHERE] * 2,
        out_specs=[ANYWHERE, IN_VMEM] + [ANYWHERE] * 8,
        scratch_shapes=[
            pltpu.VMEM((images // 2, rows, qkv_grad.shape[1]), low),
            pltpu.VMEM((images // 2, out_grad.shape[0], rows), low),
            pltpu.VMEM((images // 2, rows, qkv_grad.shape[1]), low),
            pltpu.VMEM((images // 2, out_grad.shape[0], rows), low),
            pltpu.VMEM((2 * half_c // 128, 128), full),
            pltpu.VMEM((images, tokens_len, half_d), low),
            pltpu.VMEM((images, positions, half_c), low),
            pltpu.VMEM(acts.shape, low),
            pltpu.VMEM(taps_one.shape, low),
            pltpu.VMEM(taps_one.shape, low),
            pltpu.VMEM(pictures.shape, low),
            pltpu.VMEM(pictures.shape, low),
            pltpu.VMEM(pictures.shape, low),
            pltpu.VMEM(pictures.shape, low),
            pltpu.VMEM(pictures.shape, full),
            pltpu.VMEM((2, images, channels), full),
            pltpu.VMEM(traded, low),
            pltpu.VMEM((positions, half_c), full),
        ]
        + [pltpu.VMEM(shape, full) for shape in grads]
        + [pltpu.SemaphoreType.DMA((images,))] * 4
        + [pltpu.SemaphoreType.DMA((images - 1,))] * 2
        + [pltpu.SemaphoreType.DMA((6,)), pltpu.SemaphoreType.DMA((2,))]
        + [pltpu.SemaphoreType.DMA((2, 2, images // 2))] * 2
        + gather_scratch(2)
        + gather_scratch(2)
        + reduce_scratch((positions, half_c), 2)
        + ride_scratch(3),
        compiler_params=params(number),
        name="res_backward",
    )(*args)


def gelu_of(z):
    inner = jnp.tanh(math.sqrt(2.0 / math.pi) * (z + 0.044715 * z * z * z))
    return 0.5 * z * (1.0 + inner)


def gelu_slope(z):
    rate = math.sqrt(2.0 / math.pi)
    inner = jnp.tanh(rate * (z + 0.044715 * z * z * z))
    return 0.5 * (1.0 + inner) + 0.5 * z * (1.0 - inner * inner) * rate * (1.0 + 3 * 0.044715 * z * z)


def transformer_kernel(
    shrunk,
    mods,
    cotangent,
    qkv_head,
    out_head,
    up_here,
    down_here,
    block_out,
    token_grad,
    mods_grad,
    qkv_grad,
    out_grad,
    up_grad,
    down_back,
    tokens,
    own_out,
    outgoing,
    mods_part,
    mods_theirs,
    attn_in,
    qkv,
    probs,
    mixed,
    attended,
    mlp_in,
    expanded_grad,
    pre_act,
    hidden,
    pre_grad,
    expanded,
    mlp_grad,
    down_grad,
    attended_grad,
    mixed_grad,
    qkv_back,
    attn_grad,
    share_send,
    share_recv,
    *scratch,
):
    scratch = list(scratch)

    def take(count):
        taken = scratch[:count]
        del scratch[:count]
        return taken

    gather_one, gather_two, gather_three, gather_four = (take(4), take(4), take(4), take(4))
    reduce_one, reduce_two, reduce_three, reduce_four = (take(10), take(10), take(10), take(10))
    ride_back = take(3)
    at, near = (Place(True), Place(False))
    greet_all(at)
    tokens_len = cotangent.shape[0]
    half = tokens_len // 2
    rows, cols = (D // (4 * LAYERS), up_here.shape[1])
    images = 4 * LAYERS
    score_scale = HDIM ** (-0.5)
    low, full = (jnp.bfloat16, jnp.float32)
    mine = pl.ds(pl.multiple_of(at.core * half, half), half)

    def split(place, value, stage):
        value = value.astype(low)
        for core in range(2):

            @pl.when(at.core == core)
            def _():
                stage[0][place] = value[core * half : (core + 1) * half]
                stage[6][place] = value[(1 - core) * half : (2 - core) * half]

    def image_rows(i):
        return pl.ds(pl.multiple_of(i * tokens_len, tokens_len), tokens_len)

    width = shrunk.shape[2]
    tokens[:, :width] = shrunk[0, mine]
    tokens[:, width:] = shrunk[1, mine]
    normed, _ = layer_stats(tokens[...])
    attn_in[near.slot, near.core] = (normed * (1.0 + mods[1:2]) + mods[0:1]).astype(low)
    upstream = cotangent[mine].astype(full)
    expanded_grad[at.slot, at.core] = ((1.0 + mods[5:6]) * upstream).astype(low)
    grad_turn, _, grad_end = gather_steps(
        at, [expanded_grad], None, 1, *gather_four[:2], gather_four[2:]
    )

    def in_gather(count):
        pl.when(count % 2 == 0)(lambda: grad_turn(count // 2))

    def in_sum(count):
        grad_turn(8 + count)

    gather_stage(near, [attn_in], None, 2, *gather_one[:2], gather_one[2:], tick=in_gather)

    def four_images(i):
        return pl.ds(pl.multiple_of(i * 4 * tokens_len, 4 * tokens_len), 4 * tokens_len)

    @pl.loop(0, images // 8)
    def _(i):
        rows_in = attn_in[pl.ds(4 * i, 4)].reshape(4 * tokens_len, D)
        qkv[four_images(i)] = dot(rows_in, qkv_head[...]).astype(low)

    @pl.loop(0, images // 2)
    def _(i):
        low_qkv = qkv[image_rows(i)]
        query, key, value = (low_qkv[:, j * HDIM : (j + 1) * HDIM] for j in range(3))
        scores = dot_nt(query, key) * score_scale
        scores = scores - jnp.max(scores, axis=1, keepdims=True)
        weight = jnp.exp(scores)
        weight = weight / jnp.sum(weight, axis=1, keepdims=True)
        probs[i] = weight
        mixed[image_rows(i)] = dot(weight.astype(low), value).astype(low)

    def attention_term(place):
        split(place, dot(mixed[image_rows(place)], out_head[...]), reduce_one)

    reduce_stage(near, attended, attention_term, 2, reduce_one, True, tick=in_sum)
    grad_end()

    after = tokens[...] + (1.0 + mods[2:3]) * attended[...]
    normed, _ = layer_stats(after)
    mlp_in[at.slot, at.core] = (normed * (1.0 + mods[4:5]) + mods[3:4]).astype(low)
    gather_stage(at, [mlp_in], None, 2, *gather_two[:2], gather_two[2:])

    @pl.loop(0, LAYERS)
    def _(i):
        here = pl.ds(pl.multiple_of(i * 4 * tokens_len, 4 * tokens_len), 4 * tokens_len)
        z = dot(mlp_in[pl.ds(4 * i, 4)].reshape(4 * tokens_len, D), up_here[...])
        pre_act[here] = z
        hidden[here] = gelu_of(z).astype(low)

    def hidden_term(place):
        split(place, dot(hidden[image_rows(place)], down_here[...]), reduce_two)

    def hidden_grads():
        @pl.loop(0, LAYERS)
        def _(i):
            here = pl.ds(pl.multiple_of(i * 4 * tokens_len, 4 * tokens_len), 4 * tokens_len)
            grad = dot_nt(expanded_grad[pl.ds(4 * i, 4)].reshape(4 * tokens_len, D), down_here[...])
            pre_grad[here] = (grad * gelu_slope(pre_act[here])).astype(low)

        @pl.loop(0, D // 512)
        def _(i):
            here = pl.ds(pl.multiple_of(i * 512, 512), 512)
            left = expanded_grad[:, :, :, here].reshape(images * tokens_len, 512)
            down_grad[:, here] = dot_tn(hidden[...], left).astype(low)
            right = mlp_in[:, :, :, here].reshape(images * tokens_len, 512)
            up_grad[here] = dot_tn(right, pre_grad[...]).astype(low)

    reduce_stage(at, expanded, hidden_term, 2, reduce_two, True, hidden_grads)
    back = Ride(
        at,
        [
            (lambda chip: strip(down_grad, 1, chip, rows), lambda chip: strip(down_back, 0, chip, cols)),
        ],
        *ride_back,
    )
    back.start()
    own_out[...] = (after + (1.0 + mods[5:6]) * expanded[...]).astype(low)
    block_out[mine] = own_out[...]
    mods_part[5:6] = jnp.sum(upstream * expanded[...], axis=0, keepdims=True)

    def exchange(index, source, target):
        return remote(
            source, target, share_send.at[index], share_recv.at[index], (at.dp, 1 - at.core)
        )

    give_out = exchange(0, own_out, block_out.at[mine])
    give_out.start()

    def mlp_term(place):
        split(place, dot_nt(pre_grad[image_rows(place)], up_here[...]), reduce_three)

    reduce_stage(at, mlp_grad, mlp_term, 2, reduce_three, True)
    after = tokens[...] + (1.0 + mods[2:3]) * attended[...]
    normed, scale = layer_stats(after)
    grad = mlp_grad[...]
    mods_part[3:4] = jnp.sum(grad, axis=0, keepdims=True)
    mods_part[4:5] = jnp.sum(grad * normed, axis=0, keepdims=True)
    grad_after = cotangent[mine].astype(full) + layer_back(normed, scale, (1.0 + mods[4:5]) * grad)
    mods_part[2:3] = jnp.sum(grad_after * attended[...], axis=0, keepdims=True)

    attended_grad[near.slot, near.core] = ((1.0 + mods[2:3]) * grad_after).astype(low)
    attended[...] = grad_after
    gather_stage(near, [attended_grad], None, 2, *gather_three[:2], gather_three[2:])

    @pl.loop(0, images // 8)
    def _(i):
        rows_in = attended_grad[pl.ds(4 * i, 4)].reshape(4 * tokens_len, D)
        mixed_grad[four_images(i)] = dot_nt(rows_in, out_head[...]).astype(low)

    @pl.loop(0, images // 2)
    def _(i):
        grad = mixed_grad[image_rows(i)]
        low_qkv = qkv[image_rows(i)]
        query, key, value = (low_qkv[:, j * HDIM : (j + 1) * HDIM] for j in range(3))
        weight = probs[i]
        grad_probs = dot_nt(grad, value)
        grad_value = dot_tn(weight.astype(low), grad)
        inner = jnp.sum(grad_probs * weight, axis=1, keepdims=True)
        grad_scores = (weight * (grad_probs - inner)).astype(low)
        grad_query = dot(grad_scores, key) * score_scale
        grad_key = dot_tn(grad_scores, query) * score_scale
        qkv_back[image_rows(i)] = jnp.concatenate(
            [grad_query, grad_key, grad_value], axis=1
        ).astype(low)

    def qkv_term(place):
        split(place, dot_nt(qkv_back[image_rows(place)], qkv_head[...]), reduce_four)

    def attention_grads():
        @pl.loop(0, D // 512)
        def _(i):
            here = pl.ds(pl.multiple_of(i * 512, 512), 512)
            right = attended_grad[:, :, :, here].reshape(images // 2 * tokens_len, 512)
            out_grad[:, here] = dot_tn(mixed[...], right).astype(low)
            left = attn_in[:, :, :, here].reshape(images // 2 * tokens_len, 512)
            qkv_grad[here] = dot_tn(left, qkv_back[...]).astype(low)

    reduce_stage(near, attn_grad, qkv_term, 2, reduce_four, True, attention_grads)
    normed, scale = layer_stats(tokens[...])
    grad = attn_grad[...]
    mods_part[0:1] = jnp.sum(grad, axis=0, keepdims=True)
    mods_part[1:2] = jnp.sum(grad * normed, axis=0, keepdims=True)
    give_mods = exchange(1, mods_part, mods_theirs)
    give_mods.start()

    grad = (attended[...] + layer_back(normed, scale, (1.0 + mods[1:2]) * grad)).astype(low)
    for core in range(2):

        @pl.when(at.core == core)
        def _():
            token_grad[mine] = grad[:, core * width : (core + 1) * width]
            outgoing[...] = grad[:, (1 - core) * width : (2 - core) * width]

    give_tokens = exchange(2, outgoing, token_grad.at[mine])
    give_tokens.start()
    for give in (give_out, give_mods, give_tokens):
        give.wait()
    mods_grad[...] = mods_part[...] + mods_theirs[...]
    back.wait()


def transformer(number, *args):
    shrunk, mods, cotangent, qkv_head, out_head, up_here, down_here = args
    tokens_len = cotangent.shape[0]
    images = 4 * LAYERS
    half = tokens_len // 2
    rows, cols = (D // images, up_here.shape[1])
    low, full = (jnp.bfloat16, jnp.float32)
    both = (2, half, D)
    near_tokens = images // 2 * tokens_len
    vmem = [
        ((half, D), full),
        ((half, D), low),
        ((half, shrunk.shape[2]), low),
        (mods.shape, full),
        (mods.shape, full),
        ((images // 2,) + both, low),
        ((near_tokens, 3 * HDIM), low),
        ((images // 2, tokens_len, tokens_len), full),
        ((near_tokens, HDIM), low),
        ((half, D), full),
        ((images,) + both, low),
        ((images,) + both, low),
        ((images * tokens_len, cols), full),
        ((images * tokens_len, cols), low),
        ((images * tokens_len, cols), low),
        ((half, D), full),
        ((half, D), full),
        ((cols, D), low),
        ((images // 2,) + both, low),
        ((near_tokens, HDIM), low),
        ((near_tokens, 3 * HDIM), low),
        ((half, D), full),
    ]
    return pl.pallas_call(
        transformer_kernel,
        out_shape=[
            jax.ShapeDtypeStruct((tokens_len, D), low),
            jax.ShapeDtypeStruct(shrunk.shape[1:], low),
            jax.ShapeDtypeStruct(mods.shape, full),
            jax.ShapeDtypeStruct(qkv_head.shape, low),
            jax.ShapeDtypeStruct(out_head.shape, low),
            jax.ShapeDtypeStruct((D, cols), low),
            jax.ShapeDtypeStruct((images * cols, rows), low),
        ],
        in_specs=[IN_VMEM] * 7,
        out_specs=[IN_VMEM] * 6 + [ANYWHERE],
        scratch_shapes=[pltpu.VMEM(shape, kind) for shape, kind in vmem]
        + [pltpu.SemaphoreType.DMA((4,))] * 2
        + gather_scratch(2, 1, False, True)
        + gather_scratch(2, 1, True, True)
        + gather_scratch(2, 1, False, True)
        + gather_scratch(1, 1, True, True)
        + reduce_scratch((half, D), 2, False, True)
        + reduce_scratch((half, D), 2, True, True) * 2
        + reduce_scratch((half, D), 2, False, True)
        + ride_scratch(1),
        compiler_params=params(number),
        name="transformer",
    )(*args)


def rows_at_once(shape):
    size = math.prod(shape[1:-2] + tuple(-(-n // t) * t for n, t in zip(shape[-2:], (8, 128))))
    if len(shape) == 2:
        size = -(-shape[1] // 128) * 128
    step = shape[0]
    while step % 2 == 0 and step * size > 96 * 1024:
        step //= 2
    return step


def total_kernel(shared, *refs):
    count = len(shared)
    grads, out_ref, held = (refs[:count], refs[count], refs[count + 1 : 2 * count + 1])
    line, mine, tiles, send_sem, recv_sem, load_sem = refs[2 * count + 1 :]
    at = Place(True)

    def load(index):
        return pltpu.make_async_copy(grads[index], held[index], load_sem.at[index])

    for index in range(count):
        load(index).start()
    line[...] = jnp.zeros_like(line)
    for index in range(count):
        load(index).wait()
        ref = held[index]
        step = rows_at_once(ref.shape)

        @pl.loop(0, ref.shape[0] // step)
        def _(i):
            part = ref[pl.ds(i * step, step)].astype(jnp.float32)
            part = jnp.sum(part * part, axis=0, keepdims=len(ref.shape) == 2)
            if len(ref.shape) == 3:
                part = jnp.sum(part, axis=0, keepdims=True)
            weight = 0.5 if shared[index] else 1.0
            line[:, : ref.shape[-1]] += weight * part

    mine[...] = jnp.broadcast_to(jnp.sum(line[...], axis=1, keepdims=True), mine.shape)
    greet_all(at)
    across = remote(mine, tiles.at[0], send_sem.at[0], recv_sem.at[0], (at.dp, 1 - at.core))
    across.start()
    across.wait()
    mine[...] = mine[...] + tiles[0]
    others = 4 * LAYERS - 1

    def copy(step):
        peer = (at.dp + step) % (4 * LAYERS)
        return remote(
            mine, tiles.at[step], send_sem.at[step], recv_sem.at[step], (peer, at.core)
        )

    @pl.loop(1, others + 1)
    def _(step):
        copy(step).start()

    @pl.loop(1, others + 1)
    def _(step):
        copy(step).wait()

    total = jnp.zeros_like(mine)
    for chip in range(4 * LAYERS):
        step = (at.dp - chip + 4 * LAYERS) % (4 * LAYERS)
        total = total + jnp.where(step == 0, mine[...], tiles[step])
    out_ref[...] = total


def total_of_squares(number, grads, shared):
    tile = (8, 128)
    count = len(grads)
    longest = max(grad.shape[-1] for grad in grads)
    return pl.pallas_call(
        functools.partial(total_kernel, shared),
        out_shape=jax.ShapeDtypeStruct(tile, jnp.float32),
        in_specs=[ANYWHERE] * count,
        out_specs=IN_VMEM,
        scratch_shapes=[pltpu.VMEM(grad.shape, grad.dtype) for grad in grads]
        + [
            pltpu.VMEM((1, longest), jnp.float32),
            pltpu.VMEM(tile, jnp.float32),
            pltpu.VMEM((16,) + tile, jnp.float32),
            pltpu.SemaphoreType.DMA((16,)),
            pltpu.SemaphoreType.DMA((16,)),
            pltpu.SemaphoreType.DMA((count,)),
        ],
        compiler_params=params(number),
        name="total",
    )(*grads)


def update_kernel(rates, *refs):
    count = len(rates)
    total, refs = (refs[0], refs[1:])
    ins, outs = (refs[: 4 * count], refs[4 * count : 7 * count])
    held, (load_sem, store_sem) = (refs[7 * count : 11 * count], refs[11 * count :])

    def load(index):
        return pltpu.make_async_copy(ins[index], held[index], load_sem.at[index])

    for index in range(4 * count):
        load(index).start()
    factor = jnp.minimum(1.0, CLIP / (jnp.sqrt(total[0:1, 0:1]) + 1e-06))
    correct_one = 1.0 / (1.0 - BETA_ONE**STEP)
    correct_two = 1.0 / (1.0 - BETA_TWO**STEP)
    for index, rate in enumerate(rates):
        master, average, square, grad = held[4 * index : 4 * index + 4]
        for part in range(4):
            load(4 * index + part).wait()
        step = rows_at_once(master.shape)

        @pl.loop(0, master.shape[0] // step)
        def _(i):
            at = pl.ds(i * step, step)
            clipped = grad[at].astype(jnp.float32) * factor
            new_avg = BETA_ONE * average[at] + (1.0 - BETA_ONE) * clipped
            new_sq = BETA_TWO * square[at] + (1.0 - BETA_TWO) * clipped * clipped
            step_dir = new_avg * correct_one / (jnp.sqrt(new_sq * correct_two) + ADAM_EPS)
            old = master[at]
            master[at] = old - rate * (step_dir + DECAY * old)
            average[at] = new_avg
            square[at] = new_sq

        for part in range(3):
            pltpu.make_async_copy(
                held[4 * index + part], outs[3 * index + part], store_sem.at[3 * index + part]
            ).start()
    for index in range(count):
        for part in range(3):
            pltpu.make_async_copy(
                held[4 * index + part], outs[3 * index + part], store_sem.at[3 * index + part]
            ).wait()


def update(total, quads, rates):
    count = len(quads)
    flat = [array for quad in quads for array in quad]
    return pl.pallas_call(
        functools.partial(update_kernel, rates),
        out_shape=[
            jax.ShapeDtypeStruct(array.shape, array.dtype) for quad in quads for array in quad[:3]
        ],
        in_specs=[IN_VMEM] + [ANYWHERE] * (4 * count),
        out_specs=[ANYWHERE] * (3 * count),
        scratch_shapes=[pltpu.VMEM(array.shape, array.dtype) for array in flat]
        + [pltpu.SemaphoreType.DMA((4 * count,)), pltpu.SemaphoreType.DMA((3 * count,))],
        compiler_params=pltpu.CompilerParams(vmem_limit_bytes=VMEM_GRANT),
        name="update",
    )(total, *flat)


def layer_stats(values):
    center = jnp.mean(values, axis=-1, keepdims=True)
    shifted = values - center
    spread = jnp.mean(shifted * shifted, axis=-1, keepdims=True)
    scale = lax.rsqrt(spread + LN_EPS)
    return shifted * scale, scale


def layer_back(normed, scale, grad):
    first = jnp.mean(grad, axis=-1, keepdims=True)
    second = jnp.mean(grad * normed, axis=-1, keepdims=True)
    return (grad - first - normed * second) * scale


def widen(block):
    return block.astype(jnp.float32)


def lower(block):
    return block.astype(jnp.bfloat16)


def paired_lanes(block):
    half = block.shape[-2] // 2
    return jnp.concatenate([block[..., :half, :], block[..., half:, :]], axis=-1)


def unpaired_lanes(block):
    half = block.shape[-1] // 2
    return jnp.concatenate([block[..., :half], block[..., half:]], axis=-2)


def half_picks(height, breadth):
    outputs = height * breadth // 4
    tap, out = (jnp.arange(3 * outputs) // outputs, jnp.arange(3 * outputs) % outputs)
    row = 2 * (out // (breadth // 2)) + tap - 1
    source = row * breadth + 2 * (out % (breadth // 2))
    place = jnp.arange(height * breadth)
    return ((place[None, :] == source[:, None]) & (row[:, None] >= 0)).astype(jnp.bfloat16)


def dot(left, right):
    return jnp.dot(left, right, preferred_element_type=jnp.float32)


def dot_tn(left, right):
    return lax.dot_general(left, right, (((0,), (0,)), ((), ())), preferred_element_type=jnp.float32)


def dot_nt(left, right):
    return lax.dot_general(left, right, (((1,), (1,)), ((), ())), preferred_element_type=jnp.float32)


def stationary(
    images,
    t_index,
    cotangent,
    norm_params,
    norm_params_avg,
    norm_params_sq,
    first_conv,
    first_conv_avg,
    first_conv_sq,
    resnet_mod,
    resnet_mod_avg,
    resnet_mod_sq,
    second_conv,
    second_kernel_first_moment,
    second_conv_sq,
    down_conv,
    down_conv_avg,
    down_conv_sq,
    ada_proj,
    ada_proj_avg,
    ada_proj_sq,
    qkv_proj,
    qkv_proj_avg,
    qkv_proj_sq,
    out_proj,
    out_proj_avg,
    out_proj_sq,
    hidden_in,
    hidden_in_avg,
    hidden_in_sq,
    hidden_out,
    hidden_out_avg,
    hidden_out_sq,
):
    masters = (
        norm_params,
        first_conv,
        resnet_mod,
        second_conv,
        down_conv,
        ada_proj,
        qkv_proj,
        out_proj,
        hidden_in,
        hidden_out,
    )
    averages = (
        norm_params_avg,
        first_conv_avg,
        resnet_mod_avg,
        second_kernel_first_moment,
        down_conv_avg,
        ada_proj_avg,
        qkv_proj_avg,
        out_proj_avg,
        hidden_in_avg,
        hidden_out_avg,
    )
    squares = (
        norm_params_sq,
        first_conv_sq,
        resnet_mod_sq,
        second_conv_sq,
        down_conv_sq,
        ada_proj_sq,
        qkv_proj_sq,
        out_proj_sq,
        hidden_in_sq,
        hidden_out_sq,
    )
    n_dp = lax.axis_size(DP)
    dp_pos = lax.axis_index(DP)
    tensor_pos = lax.axis_index(TENSOR)
    height, breadth = (images.shape[1], images.shape[2])
    positions = height * breadth
    tokens_len = positions // 4
    local_c = C // n_dp
    half_c = first_conv.shape[3]
    half_d = down_conv.shape[3]
    freq_rows = resnet_mod.shape[0]
    heads_here = out_proj.shape[0]
    picks = half_picks(height, breadth)
    numbers = itertools.count()

    stored_order = {3: lambda array: array.transpose(0, 1, 3, 2), 5: lambda array: array.transpose(1, 0, 2)}

    gain_bias = widen(lower(norm_params))
    conv_one = lower(first_conv).reshape(3, 3 * local_c, half_c)
    conv_two = lower(stored_order[3](second_conv)).reshape(3, 3 * local_c, half_c)
    conv_half = lower(down_conv).reshape(3, 3 * local_c, half_d)
    qkv_blocks = lower(qkv_proj).transpose(2, 0, 1, 3).reshape(heads_here, D // n_dp, 3 * HDIM)

    emb = widen(lower(embed_noise(t_index, FREQ))).reshape(n_dp, 1, freq_rows)
    emb = jnp.pad(emb, ((0, 0), (0, 7), (0, 128 - freq_rows)))
    image_blocks = images.reshape(positions, n_dp, local_c).transpose(1, 0, 2)
    ada_half = lax.dynamic_slice_in_dim(stored_order[5](ada_proj), tensor_pos * 3, 3, axis=0)
    convs = (conv_one, conv_two, conv_half)

    pictures, emb, shrunk, act_two, taps_one, taps_half, middle, stats_one, mods, *heads = res_forward(
        next(numbers),
        height,
        breadth,
        gain_bias,
        *convs,
        picks,
        lower(resnet_mod).reshape(freq_rows, 2 * half_c),
        lower(ada_half),
        paired_lanes(image_blocks).reshape(n_dp, 2, positions // 4, 2 * local_c),
        emb,
        qkv_blocks,
        lower(out_proj),
        lower(hidden_in),
        lower(hidden_out),
    )
    qkv_head, out_head, up_here, down_here = heads
    res_lines = 2 * half_c // 128
    res_mods = lax.dynamic_index_in_dim(mods, tensor_pos, 0, keepdims=False)[:res_lines]
    res_mods = res_mods.reshape(2, half_c)
    ada_mods = mods[:, res_lines:].reshape(6, D)

    block_out, grad_tokens, grad_ada, grad_qkv_w, grad_out, grad_up, grad_down = transformer(
        next(numbers),
        shrunk,
        ada_mods,
        cotangent.reshape(tokens_len, D),
        qkv_head,
        out_head,
        up_here,
        down_here,
    )
    grad_ada = lower(grad_ada).reshape(2, 3 * D // 128, 128)

    images_grad, grad_norm_params, grad_res, grad_ada, *returned = res_backward(
        next(numbers),
        breadth,
        grad_tokens,
        pictures,
        gain_bias,
        *convs,
        res_mods,
        picks,
        taps_half,
        middle,
        stats_one,
        act_two,
        taps_one,
        grad_qkv_w,
        grad_out,
        grad_up,
        grad_ada,
    )
    grad_conv_one, grad_conv_two, grad_half, grad_qkv_w, grad_out, grad_up = returned
    images_grad = widen(unpaired_lanes(images_grad))
    images_grad = images_grad.transpose(1, 0, 2).reshape((1, height, breadth, C))

    emb_cols = emb[:, 0, :freq_rows]
    grad_ada = widen(grad_ada).reshape(2, n_dp, 3, D)
    grad_ada = jnp.einsum("bf,cbjk->cjfk", emb_cols, grad_ada, precision=HIGHEST)
    grad_res = jnp.einsum("bf,bk->fk", emb_cols, grad_res.reshape(n_dp, -1), precision=HIGHEST)

    grad_qkv_w = grad_qkv_w.reshape(heads_here, D // n_dp, 3, HDIM).transpose(1, 2, 0, 3)
    gradients = (
        grad_norm_params,
        grad_conv_one.reshape(9 * local_c, half_c),
        grad_res.reshape(resnet_mod.shape),
        grad_conv_two.reshape(9 * local_c, half_c),
        grad_half.reshape(9 * local_c, half_d),
        grad_ada.reshape((6, freq_rows, D)),
        grad_qkv_w.reshape(-1, HDIM),
        grad_out.reshape(heads_here * HDIM, -1),
        grad_up,
        grad_down,
    )
    shared = tuple(position in (0, 5) for position in range(len(gradients)))
    square_sum = total_of_squares(next(numbers), gradients, shared)
    quads = []
    for position, grad in enumerate(gradients):
        order = stored_order.get(position, lambda array: array)
        three = (masters[position], averages[position], squares[position])
        quads.append(tuple(order(array).reshape(grad.shape) for array in three) + (grad,))
    updated = update(square_sum, quads, learn_rates())
    results = []
    for position, array in enumerate(updated):
        order = stored_order.get(position // 3, lambda array: array)
        shape = jax.eval_shape(order, masters[position // 3]).shape
        results.append(order(array.reshape(shape)))
    return (block_out[None], images_grad, jnp.sqrt(square_sum[0, :1])) + tuple(results)


def solution(mesh):
    in_specs = (
        P(DP, None, None, None),
        P(DP),
        P(DP, None, None),
        P(None, DP),
        P(None, DP),
        P(None, DP),
        P(None, None, DP, TENSOR),
        P(None, None, DP, TENSOR),
        P(None, None, DP, TENSOR),
        P(DP, None, TENSOR),
        P(DP, None, TENSOR),
        P(DP, None, TENSOR),
        P(None, None, TENSOR, DP),
        P(None, None, TENSOR, DP),
        P(None, None, TENSOR, DP),
        P(None, None, DP, TENSOR),
        P(None, None, DP, TENSOR),
        P(None, None, DP, TENSOR),
        P(DP, None, None),
        P(DP, None, None),
        P(DP, None, None),
        P(DP, None, TENSOR, None),
        P(DP, None, TENSOR, None),
        P(DP, None, TENSOR, None),
        P(TENSOR, None, DP),
        P(TENSOR, None, DP),
        P(TENSOR, None, DP),
        P(DP, TENSOR),
        P(DP, TENSOR),
        P(DP, TENSOR),
        P(TENSOR, DP),
        P(TENSOR, DP),
        P(TENSOR, DP),
    )
    out_specs = (
        P(DP, None, None),
        P(DP, None, None, None),
        P(),
        P(None, DP),
        P(None, DP),
        P(None, DP),
        P(None, None, DP, TENSOR),
        P(None, None, DP, TENSOR),
        P(None, None, DP, TENSOR),
        P(DP, None, TENSOR),
        P(DP, None, TENSOR),
        P(DP, None, TENSOR),
        P(None, None, TENSOR, DP),
        P(None, None, TENSOR, DP),
        P(None, None, TENSOR, DP),
        P(None, None, DP, TENSOR),
        P(None, None, DP, TENSOR),
        P(None, None, DP, TENSOR),
        P(DP, None, None),
        P(DP, None, None),
        P(DP, None, None),
        P(DP, None, TENSOR, None),
        P(DP, None, TENSOR, None),
        P(DP, None, TENSOR, None),
        P(TENSOR, None, DP),
        P(TENSOR, None, DP),
        P(TENSOR, None, DP),
        P(DP, TENSOR),
        P(DP, TENSOR),
        P(DP, TENSOR),
        P(TENSOR, DP),
        P(TENSOR, DP),
        P(TENSOR, DP),
    )
    moves_activations = mesh.shape[DP] == 4 * LAYERS and mesh.shape[TENSOR] == 2
    return jax.shard_map(
        stationary if moves_activations else per_device, mesh=mesh, in_specs=in_specs, out_specs=out_specs, check_vma=False
    )
```
